32 devices in a mesh: batch: 4 (over y, x), seq: 8 (over z, core).
Axes of the slice: x: 2, y: 2, z: 4, core: 2. Of those that a mesh axis runs over, the one named last changes fastest.
Arguments:
- tokens: bfloat16 [4, 1024, 768], P('batch', 'seq'), may hold values from -6 to 6
- doc_ids: int32 [4, 1024], P('batch', 'seq'), may hold values from 0 to 7, as said below
- w_query: bfloat16 [768, 768], replicated, may hold values from -0.21875 to 0.21875
- w_key: bfloat16 [768, 768], replicated, may hold values from -0.21875 to 0.21875
- w_value: bfloat16 [768, 768], replicated, may hold values from -0.21875 to 0.21875
- w_out: bfloat16 [768, 768], replicated, may hold values from -1.25 to 1.25
- w_gate: bfloat16 [768, 2048], replicated, may hold values from -0.21875 to 0.21875
- w_up: bfloat16 [768, 2048], replicated, may hold values from -0.21875 to 0.21875
- w_down: bfloat16 [2048, 768], replicated, may hold values from -0.125 to 0.125
- gain_attn: float32 [768], replicated, may hold values from 0.1 to 1.9
- gain_ffn: float32 [768], replicated, may hold values from 0.1 to 1.9
- cotangent: bfloat16 [4, 1024, 768], P('batch', 'seq'), may hold values from -6 to 6
Outputs:
- output: float32 [4, 1024, 768], P('batch', 'seq')
- grad_input: float32 [4, 1024, 768], P('batch', 'seq')
- grad_query: float32 [768, 768], P('seq')
- grad_key: float32 [768, 768], P('seq')
- value_weight_gradient: float32 [768, 768], P('seq')
- grad_out: float32 [768, 768], P('seq')
- grad_gate: float32 [768, 2048], P('seq')
- grad_up: float32 [768, 2048], P('seq')
- grad_down: float32 [2048, 768], P('seq')
- grad_gain_attn: float32 [768], P('seq')
- grad_gain_ffn: float32 [768], P('seq')
The draws below stay inside these ranges and needn't reach their ends.
Inputs may be any that keep to these rules, and one draw needn't show every extreme that they name: `doc_ids`: ids never fall along a row, and id 0 (padding) stands only at the start of a row.
All inputs are finite; a program needn't handle non-finite values.
Results may differ from the reference program's by a relative error of at most 0.019.
Values may be sent and summed in bfloat16 or wider, within the bound.
A program may use at most 320 MiB of HBM per device.

```python
import math
import jax
import jax.numpy as jnp
from jax import lax

D = 768
HEADS = 12
HD = 64
FF = 2048
TOK_DEV = 128
NSEG = 8
SEQS = 4
LENGTH = 1024


def draw_doc_ids(key, part):
    key = jax.random.fold_in(key, 11)

    def one_row(row_key):
        parts_keys = jax.random.split(row_key, 4)
        lead = jax.random.randint(parts_keys[0], (), 1, TOK_DEV // 2 + 1)
        first_end = lead + jax.random.randint(parts_keys[1], (), 1, TOK_DEV - lead)
        long_end = LENGTH - TOK_DEV + jax.random.randint(parts_keys[2], (), 1, TOK_DEV - 1)
        cuts = long_end + jax.random.randint(parts_keys[3], (NSEG - 4,), 1, LENGTH - long_end)
        places = jnp.arange(LENGTH, dtype=jnp.int32)
        labels = (places >= lead).astype(jnp.int32) + (places >= first_end).astype(jnp.int32) + (places >= long_end).astype(jnp.int32)
        labels = labels + jnp.sum((places[:, None] >= cuts[None, :]).astype(jnp.int32), 1)
        return labels.astype(jnp.int32)
    return jax.vmap(one_row)(jax.random.split(key, SEQS))


def block_scale(rng, shape, cuts, least, high):
    loudness = 1.0
    for axis_at, shards_of in cuts:
        heights = jax.random.uniform(jax.random.fold_in(jax.random.fold_in(rng, 6), axis_at), (shards_of,), jnp.float32, least / len(cuts), high / len(cuts))
        loudness = loudness * jnp.repeat(jnp.exp(heights), shape[axis_at] // shards_of).reshape((-1,) + (1,) * (len(shape) - 1 - axis_at))
    return loudness


def normal_values(rng, shape, deviation, reach, cuts=(), kind=jnp.bfloat16):
    drawn = deviation * jax.random.normal(rng, shape, jnp.float32)
    if cuts:
        drawn = drawn * block_scale(rng, shape, cuts, -0.22, 0.18)
    return jnp.clip(drawn, -reach, reach).astype(kind)


def setup_inputs(seed: int = 0) -> dict:
    streams_of = jax.random.split(jax.random.key(seed), 13)
    tokens = normal_values(streams_of[0], (SEQS, LENGTH, D), 1.0, 6.0, ((0, 4), (1, 8)))
    doc_ids = draw_doc_ids(jax.random.fold_in(streams_of[12], 71), 0)
    w_query = normal_values(streams_of[2], (D, D), D ** -0.5, 0.21875)
    w_key = normal_values(streams_of[3], (D, D), D ** -0.5, 0.21875)
    w_value = normal_values(streams_of[4], (D, D), D ** -0.5, 0.21875)
    w_out = normal_values(streams_of[5], (D, D), (max(D // 32, 1)) ** -0.5, 1.25)
    w_gate = normal_values(streams_of[6], (D, FF), D ** -0.5, 0.21875)
    w_up = normal_values(streams_of[7], (D, FF), D ** -0.5, 0.21875)
    w_down = normal_values(streams_of[8], (FF, D), FF ** -0.5, 0.125)
    gain_attn = jnp.clip(1.0 + 0.18 * jax.random.normal(streams_of[9], (D,), jnp.float32), 0.1, 1.9)
    gain_ffn = jnp.clip(1.0 + 0.18 * jax.random.normal(streams_of[10], (D,), jnp.float32), 0.1, 1.9)
    cotangent = normal_values(streams_of[11], (SEQS, LENGTH, D), 1.0, 6.0, ((0, 4), (1, 8)))
    return dict(tokens=tokens, doc_ids=doc_ids, w_query=w_query, w_key=w_key, w_value=w_value, w_out=w_out, w_gate=w_gate, w_up=w_up, w_down=w_down, gain_attn=gain_attn, gain_ffn=gain_ffn, cotangent=cotangent)


HIGH_ACCURACY = lax.Precision.HIGHEST
EPSILON = 1e-06
THETA = 10000.0
MASKED = -1e+30

@jax.custom_vjp
def low(v):
    return lax.optimization_barrier(v.astype(jnp.bfloat16)).astype(jnp.float32)

@jax.custom_vjp
def low_back(v):
    return v

def low_keep(v):
    return (low(v), None)

def low_pass(kept, grad):
    return (grad,)

def back_keep(v):
    return (v, None)

def back_low(kept, grad):
    return (low(grad),)
low.defvjp(low_keep, low_pass)
low_back.defvjp(back_keep, back_low)

def root_mean_square_norm(values, gain):
    return values * lax.rsqrt(lax.optimization_barrier(jnp.mean(values * values, -1, keepdims=True)) + EPSILON) * gain

def rope_tables(positions, head_dim):
    half_dim = head_dim // 2
    inverse = jnp.exp(-2.0 * math.log(THETA) / head_dim * jnp.arange(half_dim, dtype=jnp.float32))
    angle = positions.astype(jnp.float32)[..., None] * inverse
    return (jnp.concatenate([jnp.cos(angle), jnp.cos(angle)], -1), jnp.concatenate([jnp.sin(angle), jnp.sin(angle)], -1))

def rotate(values, cosine, sine):
    half_dim = values.shape[-1] // 2
    turned = jnp.concatenate([-values[..., half_dim:], values[..., :half_dim]], -1)
    return values * cosine + turned * sine

def doc_positions(doc_ids):
    labels = jnp.arange(NSEG, dtype=jnp.int32)
    member = doc_ids[:, :, None] == labels
    totals = lax.optimization_barrier(jnp.sum(member.astype(jnp.int32), 1))
    segment_begins = jnp.cumsum(totals, 1) - totals
    doc_start = lax.optimization_barrier(jnp.sum(jnp.where(member, segment_begins[:, None, :], 0), -1))
    places = jnp.arange(doc_ids.shape[1], dtype=jnp.int32)
    return places[None, :] - doc_start

def attend(queries, key_rows, value_rows, doc_ids):
    scale = 1.0 / math.sqrt(HD)

    def one_row(row_items):
        row_q, row_k, row_v, row_document_index = row_items
        row_len = row_q.shape[0]
        places = jnp.arange(row_len, dtype=jnp.int32)

        @jax.checkpoint
        def block_out(first_row):
            block_q = lax.dynamic_slice_in_dim(row_q, first_row, TOK_DEV, 0)
            block_ids = lax.dynamic_slice_in_dim(row_document_index, first_row, TOK_DEV, 0)
            query_at = first_row + jnp.arange(TOK_DEV, dtype=jnp.int32)
            scores = low_back(jnp.einsum('qhd,khd->hqk', block_q, row_k, precision=HIGH_ACCURACY) * scale)
            allowed = (block_ids[:, None] == row_document_index[None, :]) & (places[None, :] <= query_at[:, None]) & ((block_ids[:, None] != 0) | (places[None, :] == query_at[:, None]))
            scores = jnp.where(allowed[None], scores, MASKED)
            top = lax.optimization_barrier(jnp.max(scores, -1, keepdims=True))
            expo = jnp.exp(scores - top)
            probs = low(expo / lax.optimization_barrier(jnp.sum(expo, -1, keepdims=True)))
            return jnp.einsum('hqk,khd->qhd', probs, row_v, precision=HIGH_ACCURACY)
        firsts = jnp.arange(0, row_len, TOK_DEV, dtype=jnp.int32)
        blocks = lax.map(block_out, firsts)
        return blocks.reshape(row_len, row_q.shape[1], row_q.shape[2])
    return lax.map(one_row, (queries, key_rows, value_rows, doc_ids))

def layer(xf, w_query, w_key, w_value, w_out, w_gate, w_up, w_down, gain_attn, gain_ffn, cosine, sine, doc_ids):
    row_count, row_len, model_width = xf.shape
    shape_heads = (row_count, row_len, HEADS, model_width // HEADS)

    def project(remaining_tokens, weight_matrix):
        return jnp.einsum('ofv,vq->ofq', remaining_tokens, weight_matrix, precision=HIGH_ACCURACY)
    queries = low(rotate(low_back(project(xf, w_query)).reshape(shape_heads), cosine, sine))
    key_rows = low(rotate(low_back(project(xf, w_key)).reshape(shape_heads), cosine, sine))
    value_rows = low(low_back(project(xf, w_value))).reshape(shape_heads)
    attended = attend(queries, key_rows, value_rows, doc_ids)
    attended = low(low_back(attended.reshape(row_count, row_len, model_width)))
    first_sum = xf + low_back(project(attended, w_out))
    hidden = root_mean_square_norm(first_sum, gain_attn)
    hidden_low = low(hidden)
    gate = low_back(project(hidden_low, w_gate))
    up_part = low_back(project(hidden_low, w_up))
    active = low(jax.nn.silu(gate) * up_part)
    second_sum = hidden + low_back(project(active, w_down))
    return root_mean_square_norm(second_sum, gain_ffn)

def reference(tokens, doc_ids, w_query, w_key, w_value, w_out, w_gate, w_up, w_down, gain_attn, gain_ffn, cotangent):
    positions = doc_positions(doc_ids)
    cosine, sine = rope_tables(positions, HD)
    cosine = cosine[:, :, None, :]
    sine = sine[:, :, None, :]

    def forward(xf, wq, wk, wv, wo, wg, wu, wd, ga, gf):
        return layer(xf, wq, wk, wv, wo, wg, wu, wd, ga, gf, cosine, sine, doc_ids)
    inputs = (tokens, w_query, w_key, w_value, w_out, w_gate, w_up, w_down, gain_attn, gain_ffn)
    floats = tuple((item.astype(jnp.float32) for item in inputs))
    output, pullback = jax.vjp(forward, *floats)
    grads = pullback(cotangent.astype(jnp.float32))
    return (output, grads[0], grads[1], grads[2], grads[3], grads[4], grads[5], grads[6], grads[7], grads[8], grads[9])
```

```python
import functools
import math
import types

import jax
import jax.numpy as jnp
import numpy as np
from jax import lax
from jax.experimental import pallas as pl
from jax.experimental.pallas import tpu as pltpu
from jax.sharding import PartitionSpec as P

HEADS = 12
NSEG = 8


EPSILON = 1e-06
THETA = 10000.0
MASKED = -1e30


def root_mean_square_norm(values, gain):
    return values * lax.rsqrt(jnp.mean(values * values, -1, keepdims=True) + EPSILON) * gain


def swiglu(gate, up_part):
    return jax.nn.silu(gate) * up_part


def rope_tables(positions, head_dim):
    half_dim = head_dim // 2
    inverse = jnp.exp(-2.0 * math.log(THETA) / head_dim * jnp.arange(half_dim, dtype=jnp.float32))
    angle = positions.astype(jnp.float32)[..., None] * inverse
    return (
        jnp.concatenate([jnp.cos(angle), jnp.cos(angle)], -1),
        jnp.concatenate([jnp.sin(angle), jnp.sin(angle)], -1),
    )


def rotate(values, cosine, sine):
    half_dim = values.shape[-1] // 2
    turned = jnp.concatenate([-values[..., half_dim:], values[..., :half_dim]], -1)
    return values * cosine + turned * sine


def rotate_back(grads, cosine, sine):
    half_dim = grads.shape[-1] // 2
    turned = grads * sine
    return grads * cosine + jnp.concatenate([turned[..., half_dim:], -turned[..., :half_dim]], -1)


def block_size(total_rows):
    return max((d for d in range(1, min(total_rows, 2048) + 1) if total_rows % d == 0))


def doc_begin(segment_begins, where_at):
    earlier = segment_begins[:, None, :] <= where_at[:, :, None]
    return jnp.max(jnp.where(earlier, segment_begins[:, None, :], 0), -1)


def outer_sum(remaining_tokens, right):
    return lax.dot_general(
        remaining_tokens, right, (((0,), (0,)), ((), ())), preferred_element_type=jnp.float32
    )


def back_product(grads, weight_matrix):
    return lax.dot_general(
        grads, weight_matrix, (((1,), (1,)), ((), ())), preferred_element_type=jnp.float32
    )


def masked_scores(queries, key_block, key_at, query_at, query_begin):
    batch_rows, block_rows, model_width = key_block.shape
    head_count = queries.shape[2]
    head_dim = model_width // head_count
    key_heads = key_block.reshape(batch_rows, block_rows, head_count, head_dim)
    scores = jnp.einsum(
        "bqhd,bkhd->bhqk", queries, key_heads, preferred_element_type=jnp.float32
    ) * (1.0 / math.sqrt(head_dim))
    key_pos = key_at[None, None, :]
    query_pos = query_at[:, :, None]
    begin_pos = query_begin[:, :, None]
    allowed = (
        (key_pos <= query_pos) & (key_pos >= begin_pos) & ((begin_pos > 0) | (key_pos == query_pos))
    )
    return (scores, allowed[:, None], key_heads)


def grad_terms(
    queries, grad_heads, lse, delta, query_at, query_begin, key_block, value_block, key_at
):
    scores, allowed, key_heads = masked_scores(queries, key_block, key_at, query_at, query_begin)
    value_heads = value_block.reshape(key_heads.shape)
    probs = jnp.where(allowed, jnp.exp(scores - lse[..., None]), 0.0)
    dprob = jnp.einsum(
        "bqhd,bkhd->bhqk", grad_heads, value_heads, preferred_element_type=jnp.float32
    )
    dscore = (probs * (dprob - delta[..., None])).astype(jnp.bfloat16)
    return (probs.astype(jnp.bfloat16), dscore, key_heads, value_heads)


def over_rows(update, carried, arrays, first_row):
    total_rows = arrays[0].shape[1]
    block_rows = block_size(total_rows)

    def over_step(block_index, state):
        offset = block_index * block_rows
        blocks = tuple((lax.dynamic_slice_in_dim(item, offset, block_rows, 1) for item in arrays))
        key_at = first_row + offset + jnp.arange(block_rows, dtype=jnp.int32)
        return update(state, blocks, key_at)

    return lax.fori_loop(0, total_rows // block_rows, over_step, carried)


def local(
    tokens,
    doc_ids,
    w_query,
    w_key,
    w_value,
    w_out,
    w_gate,
    w_up,
    w_down,
    gain_attn,
    gain_ffn,
    cotangent,
):
    batch_rows, local_len, model_width = tokens.shape
    head_count = HEADS
    head_dim = model_width // head_count
    shape_heads = (batch_rows, local_len, head_count, head_dim)
    scale = 1.0 / math.sqrt(head_dim)
    labels = jnp.arange(NSEG, dtype=jnp.int32)
    member = (doc_ids[:, :, None] == labels).astype(jnp.int32)
    totals = lax.psum(jnp.sum(member, 1), "seq")
    segment_begins = jnp.cumsum(totals, 1) - totals
    local_at = lax.axis_index("seq") * local_len + jnp.arange(local_len, dtype=jnp.int32)
    query_at = jnp.broadcast_to(local_at, (batch_rows, local_len))
    query_begin = doc_begin(segment_begins, query_at)
    cosine, sine = rope_tables(query_at - query_begin, head_dim)
    cosine = cosine[:, :, None, :]
    sine = sine[:, :, None, :]
    flat_tokens = tokens.reshape(batch_rows * local_len, model_width)
    queries = rotate(
        jnp.dot(flat_tokens, w_query, preferred_element_type=jnp.float32).reshape(shape_heads),
        cosine,
        sine,
    ).astype(jnp.bfloat16)
    key_send = (
        rotate(
            jnp.dot(flat_tokens, w_key, preferred_element_type=jnp.float32).reshape(shape_heads),
            cosine,
            sine,
        )
        .astype(jnp.bfloat16)
        .reshape(batch_rows, local_len, model_width)
    )
    value_send = (
        jnp.dot(flat_tokens, w_value, preferred_element_type=jnp.float32)
        .astype(jnp.bfloat16)
        .reshape(batch_rows, local_len, model_width)
    )

    def stats_step(state, blocks, key_at):
        run_max, run_sum = state
        scores, allowed, key_heads = masked_scores(
            queries, blocks[0], key_at, query_at, query_begin
        )
        scores = jnp.where(allowed, scores, MASKED)
        new_max = jnp.maximum(run_max, jnp.max(scores, -1))
        weights = jnp.where(allowed, jnp.exp(scores - new_max[..., None]), 0.0)
        return (new_max, run_sum * jnp.exp(run_max - new_max) + jnp.sum(weights, -1))

    stats_init = (
        jnp.full((batch_rows, head_count, local_len), MASKED, jnp.float32),
        jnp.zeros((batch_rows, head_count, local_len), jnp.float32),
    )
    zero_heads = jnp.zeros(shape_heads, jnp.float32)
    run_max, run_sum = over_rows(
        stats_step, stats_init, (lax.all_gather(key_send, "seq", axis=1, tiled=True),), jnp.int32(0)
    )
    lse = run_max + jnp.log(run_sum)

    def output_step(state, blocks, key_at):
        scores, allowed, key_heads = masked_scores(
            queries, blocks[0], key_at, query_at, query_begin
        )
        value_heads = blocks[1].reshape(key_heads.shape)
        probs = jnp.where(allowed, jnp.exp(scores - lse[..., None]), 0.0).astype(jnp.bfloat16)
        return state + jnp.einsum(
            "bhqk,bkhd->bqhd", probs, value_heads, preferred_element_type=jnp.float32
        )

    attended = over_rows(
        output_step,
        zero_heads,
        (
            lax.all_gather(key_send, "seq", axis=1, tiled=True),
            lax.all_gather(value_send, "seq", axis=1, tiled=True),
        ),
        jnp.int32(0),
    )
    attended_low = attended.astype(jnp.bfloat16).reshape(batch_rows * local_len, model_width)
    first_sum = flat_tokens.astype(jnp.float32) + jnp.dot(
        attended_low, w_out, preferred_element_type=jnp.float32
    )
    hidden, norm_first_back = jax.vjp(root_mean_square_norm, first_sum, gain_attn)
    hidden_low = hidden.astype(jnp.bfloat16)
    gate = jnp.dot(hidden_low, w_gate, preferred_element_type=jnp.float32)
    up_part = jnp.dot(hidden_low, w_up, preferred_element_type=jnp.float32)
    active, swiglu_back = jax.vjp(swiglu, gate, up_part)
    active_low = active.astype(jnp.bfloat16)
    second_sum = hidden + jnp.dot(active_low, w_down, preferred_element_type=jnp.float32)
    output, norm_second_back = jax.vjp(root_mean_square_norm, second_sum, gain_ffn)
    second_grad, grad_gain_ffn = norm_second_back(
        cotangent.reshape(batch_rows * local_len, model_width).astype(jnp.float32)
    )
    branch_grad = second_grad.astype(jnp.bfloat16)
    grad_down = outer_sum(active_low, branch_grad)
    gate_grad, up_grad = swiglu_back(back_product(branch_grad, w_down))
    gate_low = gate_grad.astype(jnp.bfloat16)
    up_low = up_grad.astype(jnp.bfloat16)
    grad_gate = outer_sum(hidden_low, gate_low)
    grad_up = outer_sum(hidden_low, up_low)
    hidden_grad = second_grad + back_product(gate_low, w_gate) + back_product(up_low, w_up)
    first_grad, grad_gain_attn = norm_first_back(hidden_grad)
    attn_grad = first_grad.astype(jnp.bfloat16)
    grad_out = outer_sum(attended_low, attn_grad)
    grad_heads = back_product(attn_grad, w_out).astype(jnp.bfloat16).reshape(shape_heads)
    delta = jnp.swapaxes(jnp.sum(grad_heads.astype(jnp.float32) * attended, -1), 1, 2)

    def query_step(state, blocks, key_at):
        probs_low, dscore, key_heads, value_heads = grad_terms(
            queries, grad_heads, lse, delta, query_at, query_begin, blocks[0], blocks[1], key_at
        )
        return (
            state
            + jnp.einsum("bhqk,bkhd->bqhd", dscore, key_heads, preferred_element_type=jnp.float32)
            * scale
        )

    all_keys, all_values = (
        lax.all_gather(key_send, "seq", axis=1, tiled=True),
        lax.all_gather(value_send, "seq", axis=1, tiled=True),
    )
    query_grad = over_rows(query_step, zero_heads, (all_keys, all_values), 0)
    first_row = jnp.int32(0)
    span_rows = local_len * lax.axis_size("seq")
    block_rows = block_size(span_rows)
    empty = jnp.zeros((batch_rows, span_rows, head_count, head_dim), jnp.float32)

    def key_step(block_index, state):
        offset = block_index * block_rows
        key_block = lax.dynamic_slice_in_dim(all_keys, offset, block_rows, 1)
        value_block = lax.dynamic_slice_in_dim(all_values, offset, block_rows, 1)
        key_at = first_row + offset + jnp.arange(block_rows, dtype=jnp.int32)
        probs_low, dscore, key_heads, value_heads = grad_terms(
            queries, grad_heads, lse, delta, query_at, query_begin, key_block, value_block, key_at
        )
        key_part = (
            jnp.einsum("bhqk,bqhd->bkhd", dscore, queries, preferred_element_type=jnp.float32)
            * scale
        )
        value_part = jnp.einsum(
            "bhqk,bqhd->bkhd", probs_low, grad_heads, preferred_element_type=jnp.float32
        )
        return (
            lax.dynamic_update_slice_in_dim(state[0], key_part, offset, 1),
            lax.dynamic_update_slice_in_dim(state[1], value_part, offset, 1),
        )

    key_all, value_all = lax.fori_loop(0, span_rows // block_rows, key_step, (empty, empty))
    joined = jnp.concatenate(
        [
            key_all.reshape(batch_rows, span_rows, model_width),
            value_all.reshape(batch_rows, span_rows, model_width),
        ],
        -1,
    )
    summed_keys = jnp.swapaxes(
        lax.psum_scatter(jnp.swapaxes(joined, 0, 1), "seq", scatter_dimension=0, tiled=True), 0, 1
    )
    key_grad = summed_keys[..., :model_width].reshape(shape_heads)
    value_grad = summed_keys[..., model_width:]
    flat_len = batch_rows * local_len
    query_low = (
        rotate_back(query_grad, cosine, sine).astype(jnp.bfloat16).reshape(flat_len, model_width)
    )
    key_low = (
        rotate_back(key_grad, cosine, sine).astype(jnp.bfloat16).reshape(flat_len, model_width)
    )
    value_low = value_grad.astype(jnp.bfloat16).reshape(flat_len, model_width)
    grad_input = (
        first_grad
        + back_product(query_low, w_query)
        + back_product(key_low, w_key)
        + back_product(value_low, w_value)
    )
    grad_query = outer_sum(flat_tokens, query_low)
    grad_key = outer_sum(flat_tokens, key_low)
    value_weight_gradient = outer_sum(flat_tokens, value_low)
    shares = (
        lax.psum_scatter(grad_query, "seq", scatter_dimension=0, tiled=True),
        lax.psum_scatter(grad_key, "seq", scatter_dimension=0, tiled=True),
        lax.psum_scatter(value_weight_gradient, "seq", scatter_dimension=0, tiled=True),
        lax.psum_scatter(grad_out, "seq", scatter_dimension=0, tiled=True),
        lax.psum_scatter(grad_gate, "seq", scatter_dimension=0, tiled=True),
        lax.psum_scatter(grad_up, "seq", scatter_dimension=0, tiled=True),
        lax.psum_scatter(grad_down, "seq", scatter_dimension=0, tiled=True),
        lax.psum_scatter(grad_gain_attn, "seq", scatter_dimension=0, tiled=True),
        lax.psum_scatter(grad_gain_ffn, "seq", scatter_dimension=0, tiled=True),
    )
    results = (
        lax.psum(shares[0].astype(jnp.bfloat16), "batch").astype(jnp.float32),
        lax.psum(shares[1].astype(jnp.bfloat16), "batch").astype(jnp.float32),
        lax.psum(shares[2].astype(jnp.bfloat16), "batch").astype(jnp.float32),
        lax.psum(shares[3].astype(jnp.bfloat16), "batch").astype(jnp.float32),
        lax.psum(shares[4].astype(jnp.bfloat16), "batch").astype(jnp.float32),
        lax.psum(shares[5].astype(jnp.bfloat16), "batch").astype(jnp.float32),
        lax.psum(shares[6].astype(jnp.bfloat16), "batch").astype(jnp.float32),
        lax.psum(shares[7].astype(jnp.bfloat16), "batch").astype(jnp.float32),
        lax.psum(shares[8].astype(jnp.bfloat16), "batch").astype(jnp.float32),
    )
    output_rows = output.reshape(batch_rows, local_len, model_width)
    input_rows = grad_input.reshape(batch_rows, local_len, model_width)
    return (
        output_rows,
        input_rows,
        results[0],
        results[1],
        results[2],
        results[3],
        results[4],
        results[5],
        results[6],
        results[7],
        results[8],
    )


MESH = pl.DeviceIdType.MESH
F32 = jnp.float32
BF16 = jnp.bfloat16


def mm(a, b):
    return lax.dot_general(a, b, (((1,), (0,)), ((), ())), preferred_element_type=F32)


def mm_nt(a, b):
    return lax.dot_general(a, b, (((1,), (1,)), ((), ())), preferred_element_type=F32)


def scratch_plan(tok, d, f, n, nb):
    nz, plane, heads = n // 2, 2 * nb * tok, HEADS
    vm = pltpu.VMEM
    dma = lambda *shape: pltpu.SemaphoreType.DMA(shape)
    return dict(
        wq=vm((d, d), BF16), wk=vm((d, d), BF16), wv=vm((d, d), BF16), wo=vm((d, d), BF16),
        wg=vm((d, f), BF16), wu=vm((d, f), BF16), wd=vm((f, d), BF16),
        cos=vm((nz, 2 * tok, 128), F32), sin=vm((nz, 2 * tok, 128), F32),
        x_all=vm((n, tok, d), BF16), q_all=vm((n, tok, d), BF16), do_all=vm((n, tok, d), BF16),
        k_all=vm((nz, 2 * tok, d), BF16), v_all=vm((nz, 2 * tok, d), BF16),
        st_all=vm((n, 32, tok), F32), id_all=vm((n, 8, tok), jnp.int32),
        idcol=vm((tok, 128), F32), bias=vm((tok, 2 * tok), F32),
        m=vm((heads, tok, 128), F32), l=vm((heads, tok, 128), F32), delta=vm((heads, tok, 128), F32),
        acc=vm((tok, d), F32), acc2=vm((tok, d), F32),
        olow=vm((tok, d), BF16), hb=vm((tok, d), BF16), h1=vm((tok, d), F32), n1=vm((tok, d), F32),
        ri1=vm((tok, 128), F32), dr=vm((tok, d), F32),
        g32=vm((tok, f), F32), u32=vm((tok, f), F32), act=vm((tok, f), BF16),
        dg=vm((tok, f), BF16), du=vm((tok, f), BF16), dmo=vm((tok, d), BF16), dattn=vm((tok, d), BF16),
        dq=vm((tok, d), BF16), dk=vm((tok, d), BF16), dv=vm((tok, d), BF16),
        actT=vm((n, 2, tok, tok), BF16), hT=vm((d, tok), BF16), xT=vm((d, tok), BF16), oT=vm((d, tok), BF16),
        gl=vm((8, d), F32), out_v=vm((tok, d), F32), gin_v=vm((tok, d), F32),
        hT_b=vm((d, plane), BF16), dgu_b=vm((plane, 2 * f // nb), BF16),
        act_b=vm((n, tok, plane), BF16), dmo_b=vm((plane, d // 2), BF16),
        kT_b=vm((d, plane), BF16), nn_b=vm((plane, d), BF16), gl_b=vm((2 * nb, 8, d), F32),
        pgu=vm((d, 2 * f // nb), BF16), pdn=vm((n, tok, d // 2), BF16), pat=vm((d, d), BF16),
        rgu=vm((nz, d // nz, 2 * f // nb), BF16), rdn=vm((nz, 2, tok, d // 2), BF16), rat=vm((nz, d // nz, d), BF16),
        sgu=vm((d // nz, 2 * f // nb), BF16), sdn=vm((2, tok, d // 2), BF16), sat=vm((d // nz, d), BF16),
        gz=vm((nz, 8, d), F32), gsum=vm((8, d), F32),
        wsem=dma(9), osem=dma(2), ssem=dma(100), fsem=dma(4, n),
        rx=dma(n), rq=dma(n), rdo=dma(n), rst=dma(n), rid=dma(n),
        rh=dma(2 * nb), rdg=dma(2 * nb), rdu=dma(2 * nb), ract=dma(2 * nb), rdmo=dma(2 * nb),
        rkt=dma(2 * nb), rnn=dma(2 * nb), rgl=dma(2 * nb),
        zgu=dma(nz), zdn=dma(nz), zat=dma(nz), zgl=dma(nz),
        fgu=dma(nb), fdn=dma(nb), fat=dma(nb), fgl=dma(1),
    )


INPUTS = ("ids", "tok", "cot", "ga", "gf", "cos_h", "sin_h", "wq_h", "wk_h", "wv_h", "wo_h", "wg_h", "wu_h", "wd_h")
OUTPUTS = ("out_h", "gin_h", "oat_h", "ogu_h", "odn_h", "ogl_h")


def layer_kernel(plan_names, tok, d, f, n, nb, *refs):
    r = types.SimpleNamespace(**dict(zip(INPUTS + OUTPUTS + plan_names, refs)))
    nz, pairs = n // 2, d // 128
    fs, dh, blk = f // nb, d // 2, d // nz
    b, s = lax.axis_index("batch"), lax.axis_index("seq")
    z, c = s // 2, lax.rem(s, 2)
    by, bx = b // 2, lax.rem(b, 2)
    e = 2 * b + c
    sib = (b, s + 1 - 2 * c)
    pending, used = [], [0]

    def remote(src, dst, ssem, rsem, dev):
        return pltpu.make_async_remote_copy(
            src_ref=src, dst_ref=dst, send_sem=ssem, recv_sem=rsem, device_id=dev, device_id_type=MESH
        )

    def send(cond, src, dst, rsem, dev):
        ssem = r.ssem.at[used[0]]
        used[0] += 1
        pending.append((cond, src, dst, ssem, rsem, dev))

        @pl.when(cond)
        def _():
            remote(src, dst, ssem, rsem, dev).start()

    def plane_send(src, dst, rsem, to_b, to_c):
        here = (b == to_b) & (c == to_c)
        send(jnp.logical_not(here), src, dst, rsem, (to_b, 2 * z + to_c))

        @pl.when(here)
        def _():
            pltpu.make_async_copy(src, dst, rsem).start()

    def arrived(dst, rsem):
        remote(dst, dst, r.ssem.at[0], rsem, sib).wait_recv()

    loads = {}
    for i, name in enumerate(("wk", "wv", "wq", "cos", "sin", "wo", "wg", "wu", "wd")):
        loads[name] = pltpu.make_async_copy(getattr(r, name + "_h"), getattr(r, name), r.wsem.at[i])
        loads[name].start()

    r.x_all[s] = r.tok[0]
    r.id_all[s] = jnp.broadcast_to(r.ids[...], (8, tok))

    bar = pltpu.get_barrier_semaphore()
    for zz in range(nz):
        for cc in range(2):
            @pl.when(2 * zz + cc != s)
            def _(zz=zz, cc=cc):
                pl.semaphore_signal(bar, inc=1, device_id=(b, 2 * zz + cc), device_id_type=MESH)
    for bb in range(nb):
        for cc in range(2):
            @pl.when(bb != b)
            def _(bb=bb, cc=cc):
                pl.semaphore_signal(bar, inc=1, device_id=(bb, 2 * z + cc), device_id_type=MESH)
    pl.semaphore_wait(bar, n - 1 + 2 * (nb - 1))

    always = s >= 0
    send(always, r.x_all.at[s], r.x_all.at[s], r.rx.at[s], sib)
    for dz in range(1, nz):
        send(z + dz < nz, r.x_all.at[s], r.x_all.at[s], r.rx.at[s], (b, s + 2 * dz))
    for zz in range(nz):
        for cc in range(2):
            send(2 * zz + cc != s, r.id_all.at[s], r.id_all.at[s], r.rid.at[s], (b, 2 * zz + cc))

    lane = lax.broadcasted_iota(jnp.int32, (tok, 128), 1)
    first = lane < 64
    half_mask = (jnp.where(first, 1.0, 0.0).astype(BF16), jnp.where(first, 0.0, 1.0).astype(BF16))

    def turn(u):
        low = lax.rem(lax.broadcasted_iota(jnp.int32, u.shape, 1), 64) < 32
        return jnp.where(low, pltpu.roll(u, 96, 1), pltpu.roll(u, 32, 1))

    def twice(u):
        return jnp.concatenate([u, u], axis=1)

    own = pl.ds(pl.multiple_of(c * tok, tok), tok)

    loads["wq"].wait()
    loads["cos"].wait()
    loads["sin"].wait()

    def q_tile(i, _):
        at = pl.multiple_of(i * 256, 256)
        u = mm(r.tok[0], r.wq[:, pl.ds(at, 256)])
        co, si = r.cos[z, own, :], r.sin[z, own, :]
        for h in range(2):
            part = u[:, h * 128:(h + 1) * 128]
            part = (part * co + turn(part) * si) * 0.125
            r.q_all[s, :, pl.ds(at + h * 128, 128)] = part.astype(BF16)
        return 0

    lax.fori_loop(0, d // 256, q_tile, 0)
    send(always, r.q_all.at[s], r.q_all.at[s], r.rq.at[s], sib)
    for dz in range(1, nz):
        send(z - dz >= 0, r.q_all.at[s], r.q_all.at[s], r.rq.at[s], (b, s - 2 * dz))

    def transpose_into(dst, value):
        for p in range(d // 128):
            dst[p * 128:(p + 1) * 128, :] = value[:, p * 128:(p + 1) * 128].T.astype(BF16)

    tokens = pl.ds(pl.multiple_of(e * tok, tok), tok)
    transpose_into(r.xT, r.tok[0].astype(F32))
    for bb in range(3):
        plane_send(r.xT, r.kT_b.at[:, tokens], r.rkt.at[e], bb, 1)
    r.idcol[...] = jnp.broadcast_to(r.ids[...].astype(F32), (128, tok)).T

    def each_id(t, _):
        @pl.when(t != s)
        def _():
            arrived(r.id_all.at[t], r.rid.at[t])
        return 0

    lax.fori_loop(0, n, each_id, 0)

    def ids_of(block):
        return jnp.concatenate(
            [r.id_all[2 * block, 0:1, :], r.id_all[2 * block + 1, 0:1, :]], axis=1
        ).astype(F32)

    def set_bias(block, local_is_query):
        shape = (tok, 2 * tok)
        mine = s * tok + lax.broadcasted_iota(jnp.int32, shape, 0)
        theirs = block * (2 * tok) + lax.broadcasted_iota(jnp.int32, shape, 1)
        my_id = twice(r.idcol[...])
        their_id = jnp.broadcast_to(ids_of(block), shape)
        causal = (theirs <= mine) if local_is_query else (mine <= theirs)
        allowed = (my_id == their_id) & causal & ((my_id != 0.0) | (mine == theirs))
        r.bias[...] = jnp.where(allowed, 0.0, MASKED)

    r.m[...] = jnp.full(r.m.shape, MASKED, F32)
    r.l[...] = jnp.zeros(r.l.shape, F32)
    r.acc[...] = jnp.zeros(r.acc.shape, F32)
    loads["wk"].wait()
    loads["wv"].wait()

    def forward_step(j, _):
        kb = z - j
        mine, other = 2 * kb + c, 2 * kb + 1 - c

        @pl.when(j > 0)
        def _():
            arrived(r.x_all.at[mine], r.rx.at[mine])
            remote(r.x_all.at[mine], r.x_all.at[mine], r.fsem.at[0, mine], r.rx.at[mine], sib).start()

        arrived(r.x_all.at[other], r.rx.at[other])
        set_bias(kb, True)

        def kv_tile(i, _):
            at = pl.multiple_of(i * 256, 256)
            xb = r.x_all[pl.ds(2 * kb, 2)].reshape(2 * tok, d)
            u = mm(xb, r.wk[:, pl.ds(at, 256)])
            co, si = r.cos[kb], r.sin[kb]
            for h in range(2):
                part = u[:, h * 128:(h + 1) * 128]
                r.k_all[kb, :, pl.ds(at + h * 128, 128)] = (part * co + turn(part) * si).astype(BF16)
            r.v_all[kb, :, pl.ds(at, 256)] = mm(xb, r.wv[:, pl.ds(at, 256)]).astype(BF16)
            return 0

        lax.fori_loop(0, d // 256, kv_tile, 0)

        def pair(p, _):
            lanes = pl.ds(pl.multiple_of(p * 128, 128), 128)
            qp, kp, vp = r.q_all[s, :, lanes], r.k_all[kb, :, lanes], r.v_all[kb, :, lanes]
            alphas, outs = [], []
            for h in range(2):
                sc = mm_nt(qp * half_mask[h], kp) + r.bias[...]
                m_old = r.m[2 * p + h]
                m_new = jnp.maximum(m_old, jnp.max(sc, axis=1, keepdims=True))
                alpha = jnp.exp(m_old - m_new)
                ex = jnp.exp(sc - twice(m_new))
                r.m[2 * p + h] = m_new
                r.l[2 * p + h] = r.l[2 * p + h] * alpha + jnp.sum(ex, axis=1, keepdims=True)
                alphas.append(alpha)
                outs.append(mm(ex.astype(BF16), vp))
            r.acc[:, lanes] = r.acc[:, lanes] * jnp.where(first, alphas[0], alphas[1]) + jnp.where(
                first, outs[0], outs[1]
            )
            return 0

        lax.fori_loop(0, pairs, pair, 0)
        return 0

    lax.fori_loop(0, z + 1, forward_step, 0)

    def finish(p, _):
        lanes = pl.ds(pl.multiple_of(p * 128, 128), 128)
        l0, l1 = r.l[2 * p], r.l[2 * p + 1]
        r.acc[:, lanes] = r.acc[:, lanes] / jnp.where(first, l0, l1)
        r.m[2 * p] = r.m[2 * p] + jnp.log(l0)
        r.m[2 * p + 1] = r.m[2 * p + 1] + jnp.log(l1)
        return 0

    lax.fori_loop(0, pairs, finish, 0)
    r.olow[...] = r.acc[...].astype(BF16)

    loads["wo"].wait()
    r1 = r.tok[0].astype(F32) + mm(r.olow[...], r.wo[...])
    ri1 = lax.rsqrt(jnp.mean(r1 * r1, axis=1, keepdims=True) + EPSILON)
    r.ri1[...] = jnp.broadcast_to(ri1, (tok, 128))
    n1 = r1 * ri1
    r.n1[...] = n1
    h1 = n1 * r.ga[...]
    r.h1[...] = h1
    r.hb[...] = h1.astype(BF16)
    transpose_into(r.hT, h1)
    for bb in range(nb):
        plane_send(r.hT, r.hT_b.at[:, tokens], r.rh.at[e], bb, 0)
    transpose_into(r.oT, r.acc[...])
    plane_send(r.oT, r.kT_b.at[:, tokens], r.rkt.at[e], 3, 1)
    loads["wg"].wait()
    loads["wu"].wait()

    def up_tile(i, _):
        at = pl.ds(pl.multiple_of(i * 256, 256), 256)
        g = mm(r.hb[...], r.wg[:, at])
        u = mm(r.hb[...], r.wu[:, at])
        r.g32[:, at] = g
        r.u32[:, at] = u
        a = g / (1.0 + jnp.exp(-g)) * u
        r.act[:, at] = a.astype(BF16)
        r.actT[i, 0] = a[:, :128].T.astype(BF16)
        r.actT[i, 1] = a[:, 128:].T.astype(BF16)
        return 0

    lax.fori_loop(0, f // 256, up_tile, 0)
    for bb in range(nb):
        plane_send(r.actT.at[:, bb // 2], r.act_b.at[:, :, tokens], r.ract.at[e], bb, 1)
    loads["wd"].wait()
    r2 = r.h1[...] + mm(r.act[...], r.wd[...])
    ri2 = lax.rsqrt(jnp.mean(r2 * r2, axis=1, keepdims=True) + EPSILON)
    n2 = r2 * ri2
    r.out_v[...] = n2 * r.gf[...]
    out_copy = pltpu.make_async_copy(r.out_v, r.out_h, r.osem.at[0])
    out_copy.start()
    ct = r.cot[0].astype(F32)
    gain_ffn = jnp.sum(ct * n2, axis=0, keepdims=True)
    t2 = ct * r.gf[...]
    dr2 = ri2 * (t2 - n2 * jnp.mean(n2 * t2, axis=1, keepdims=True))
    r.dr[...] = dr2
    r.dmo[...] = dr2.astype(BF16)
    for bb in range(nb):
        plane_send(
            r.dmo.at[:, pl.ds((bb % 2) * dh, dh)], r.dmo_b.at[tokens, :], r.rdmo.at[e], bb, 1
        )

    def down_tile(i, _):
        at = pl.ds(pl.multiple_of(i * 256, 256), 256)
        da = mm_nt(r.dmo[...], r.wd[at, :])
        g, u = r.g32[:, at], r.u32[:, at]
        sg = 1.0 / (1.0 + jnp.exp(-g))
        r.dg[:, at] = (da * u * (sg * (1.0 + g * (1.0 - sg)))).astype(BF16)
        r.du[:, at] = (da * (g * sg)).astype(BF16)
        return 0

    lax.fori_loop(0, f // 256, down_tile, 0)
    for bb in range(nb):
        cols = pl.ds(bb * fs, fs)
        plane_send(r.dg.at[:, cols], r.dgu_b.at[tokens, pl.ds(0, fs)], r.rdg.at[e], bb, 0)
        plane_send(r.du.at[:, cols], r.dgu_b.at[tokens, pl.ds(fs, fs)], r.rdu.at[e], bb, 0)
    dh1 = r.dr[...] + mm_nt(r.dg[...], r.wg[...]) + mm_nt(r.du[...], r.wu[...])
    n1 = r.n1[...]
    gain_attn = jnp.sum(dh1 * n1, axis=0, keepdims=True)
    t1 = dh1 * r.ga[...]
    dr1 = r.ri1[:, 0:1] * (t1 - n1 * jnp.mean(n1 * t1, axis=1, keepdims=True))
    r.dr[...] = dr1
    r.dattn[...] = dr1.astype(BF16)
    r.gl[...] = jnp.concatenate([gain_attn, gain_ffn, jnp.zeros((6, d), F32)], axis=0)
    plane_send(r.dattn, r.nn_b.at[tokens, :], r.rnn.at[e], 3, 1)
    plane_send(r.gl, r.gl_b.at[e], r.rgl.at[e], 0, 0)
    r.do_all[s] = mm_nt(r.dattn[...], r.wo[...]).astype(BF16)
    send(always, r.do_all.at[s], r.do_all.at[s], r.rdo.at[s], sib)
    for dz in range(1, nz):
        send(z - dz >= 0, r.do_all.at[s], r.do_all.at[s], r.rdo.at[s], (b, s - 2 * dz))

    stats = jnp.zeros((tok, 128), F32)
    for p in range(pairs):
        prod = r.do_all[s, :, p * 128:(p + 1) * 128].astype(F32) * r.acc[:, p * 128:(p + 1) * 128]
        for h in range(2):
            head = 2 * p + h
            part = jnp.sum(jnp.where(first == (h == 0), prod, 0.0), axis=1, keepdims=True)
            part = jnp.broadcast_to(part, (tok, 128))
            r.delta[head] = part
            stats = jnp.where(lane == head, r.m[head], stats)
            stats = jnp.where(lane == 16 + head, part, stats)
    r.st_all[s] = stats.T[0:32, :]
    send(always, r.st_all.at[s], r.st_all.at[s], r.rst.at[s], sib)
    for dz in range(1, nz):
        send(z - dz >= 0, r.st_all.at[s], r.st_all.at[s], r.rst.at[s], (b, s - 2 * dz))

    r.acc[...] = jnp.zeros(r.acc.shape, F32)

    def query_step(kb, _):
        set_bias(kb, True)

        def pair(p, _):
            lanes = pl.ds(pl.multiple_of(p * 128, 128), 128)
            qp, kp, vp = r.q_all[s, :, lanes], r.k_all[kb, :, lanes], r.v_all[kb, :, lanes]
            dop = r.do_all[s, :, lanes]
            outs = []
            for h in range(2):
                sc = mm_nt(qp * half_mask[h], kp) + r.bias[...]
                pf = jnp.exp(sc - twice(r.m[2 * p + h]))
                dp = mm_nt(dop * half_mask[h], vp)
                ds = (pf * (dp - twice(r.delta[2 * p + h]))).astype(BF16)
                outs.append(mm(ds, kp))
            r.acc[:, lanes] += jnp.where(first, outs[0], outs[1])
            return 0

        lax.fori_loop(0, pairs, pair, 0)
        return 0

    lax.fori_loop(0, z + 1, query_step, 0)

    def turn_back(src, dst, factor):
        co, si = r.cos[z, own, :], r.sin[z, own, :]
        for p in range(pairs):
            g = src[:, p * 128:(p + 1) * 128] * factor
            dst[:, p * 128:(p + 1) * 128] = (g * co - turn(g) * si).astype(BF16)

    turn_back(r.acc, r.dq, 0.125)
    plane_send(r.dq, r.nn_b.at[tokens, :], r.rnn.at[e], 0, 1)

    r.acc[...] = jnp.zeros(r.acc.shape, F32)
    r.acc2[...] = jnp.zeros(r.acc2.shape, F32)

    def key_step(j, _):
        qb = z + j
        mine, other = 2 * qb + c, 2 * qb + 1 - c
        moved = ((1, r.q_all, r.rq), (2, r.do_all, r.rdo), (3, r.st_all, r.rst))

        @pl.when(j > 0)
        def _():
            for i, ref, sem in moved:
                arrived(ref.at[mine], sem.at[mine])
                remote(ref.at[mine], ref.at[mine], r.fsem.at[i, mine], sem.at[mine], sib).start()

        for i, ref, sem in moved:
            arrived(ref.at[other], sem.at[other])
        set_bias(qb, False)

        def pair(p, _):
            lanes = pl.ds(pl.multiple_of(p * 128, 128), 128)
            kp, vp = r.k_all[z, own, lanes], r.v_all[z, own, lanes]
            qp = r.q_all[pl.ds(2 * qb, 2), :, lanes].reshape(2 * tok, 128)
            dop = r.do_all[pl.ds(2 * qb, 2), :, lanes].reshape(2 * tok, 128)
            dks, dvs = [], []
            for h in range(2):
                head = 2 * p + h
                lse = jnp.concatenate(
                    [r.st_all[2 * qb, pl.ds(head, 1), :], r.st_all[2 * qb + 1, pl.ds(head, 1), :]], axis=1
                )
                dlt = jnp.concatenate(
                    [r.st_all[2 * qb, pl.ds(16 + head, 1), :], r.st_all[2 * qb + 1, pl.ds(16 + head, 1), :]],
                    axis=1,
                )
                sc = mm_nt(kp * half_mask[h], qp) + r.bias[...]
                pf = jnp.exp(sc - lse)
                dvs.append(mm(pf.astype(BF16), dop))
                dp = mm_nt(vp * half_mask[h], dop)
                ds = (pf * (dp - dlt)).astype(BF16)
                dks.append(mm(ds, qp))
            r.acc[:, lanes] += jnp.where(first, dks[0], dks[1])
            r.acc2[:, lanes] += jnp.where(first, dvs[0], dvs[1])
            return 0

        lax.fori_loop(0, pairs, pair, 0)
        return 0

    lax.fori_loop(0, nz - z, key_step, 0)
    turn_back(r.acc, r.dk, 1.0)
    plane_send(r.dk, r.nn_b.at[tokens, :], r.rnn.at[e], 1, 1)
    r.dv[...] = r.acc2[...].astype(BF16)
    plane_send(r.dv, r.nn_b.at[tokens, :], r.rnn.at[e], 2, 1)
    r.gin_v[...] = (
        r.dr[...] + mm_nt(r.dq[...], r.wq[...]) + mm_nt(r.dk[...], r.wk[...]) + mm_nt(r.dv[...], r.wv[...])
    )
    gin_copy = pltpu.make_async_copy(r.gin_v, r.gin_h, r.osem.at[1])
    gin_copy.start()

    def each_source(dst_of, rsem):
        for i in range(2 * nb):
            arrived(dst_of(i), rsem.at[i])

    def share(src_of, dst, rsem, to_c):
        for zz in range(nz):
            send((c == to_c) & (z != zz), src_of(zz), dst.at[z], rsem.at[z], (b, 2 * zz + to_c))

    def others(recv, rsem):
        total = None
        for dz in range(1, nz):
            at = lax.rem(z + dz, nz)
            arrived(recv.at[at], rsem.at[at])
            total = recv[at].astype(F32) if total is None else total + recv[at].astype(F32)
        return total

    def spread(src_of, dst, rsem, from_c):
        for bb in range(nb):
            for cc in range(2):
                here = (b == bb) & (s == 2 * z + cc)
                send(
                    (c == from_c) & jnp.logical_not(here), src_of(cc), dst, rsem, (bb, 2 * z + cc)
                )

                @pl.when((c == from_c) & here)
                def _(cc=cc):
                    pltpu.make_async_copy(src_of(cc), dst, rsem).start()

    span = 2 * tok * nb

    @pl.when(c == 0)
    def _():
        each_source(lambda i: r.hT_b.at[:, pl.ds(i * tok, tok)], r.rh)
        each_source(lambda i: r.dgu_b.at[pl.ds(i * tok, tok), pl.ds(0, fs)], r.rdg)
        each_source(lambda i: r.dgu_b.at[pl.ds(i * tok, tok), pl.ds(fs, fs)], r.rdu)

        def tile(i, _):
            at = pl.ds(pl.multiple_of(i * 256, 256), 256)
            r.pgu[:, at] = mm(r.hT_b[...], r.dgu_b[:, at]).astype(BF16)
            return 0

        lax.fori_loop(0, 2 * fs // 256, tile, 0)

    share(lambda zz: r.pgu.at[pl.ds(zz * blk, blk), :], r.rgu, r.zgu, 0)

    @pl.when(c == 1)
    def _():
        each_source(lambda i: r.act_b.at[:, :, pl.ds(i * tok, tok)], r.ract)
        each_source(lambda i: r.dmo_b.at[pl.ds(i * tok, tok), :], r.rdmo)

        def tile(i, _):
            left = r.act_b[pl.ds(2 * i, 2)].reshape(2 * tok, span)
            r.pdn[pl.ds(2 * i, 2)] = mm(left, r.dmo_b[...]).astype(BF16).reshape(2, tok, dh)
            return 0

        lax.fori_loop(0, n // 2, tile, 0)

    share(lambda zz: r.pdn.at[pl.ds(2 * zz, 2)], r.rdn, r.zdn, 1)

    @pl.when(c == 1)
    def _():
        each_source(lambda i: r.kT_b.at[:, pl.ds(i * tok, tok)], r.rkt)
        each_source(lambda i: r.nn_b.at[pl.ds(i * tok, tok), :], r.rnn)

        def tile(i, _):
            at = pl.ds(pl.multiple_of(i * 256, 256), 256)
            r.pat[:, at] = mm(r.kT_b[...], r.nn_b[:, at]).astype(BF16)
            return 0

        lax.fori_loop(0, d // 256, tile, 0)

    share(lambda zz: r.pat.at[pl.ds(zz * blk, blk), :], r.rat, r.zat, 1)

    adds = (b == 0) & (c == 0)

    @pl.when(adds)
    def _():
        total = None
        for i in range(2 * nb):
            arrived(r.gl_b.at[i], r.rgl.at[i])
            total = r.gl_b[i] if total is None else total + r.gl_b[i]
        r.gz[z] = total

    for zz in range(nz):
        send(adds & (z != zz), r.gz.at[z], r.gz.at[z], r.zgl.at[z], (0, 2 * zz))

    @pl.when(adds)
    def _():
        total = r.gz[z]
        for dz in range(1, nz):
            at = lax.rem(z + dz, nz)
            arrived(r.gz.at[at], r.zgl.at[at])
            total = total + r.gz[at]
        r.gsum[...] = total

    for bb in range(nb):
        for cc in range(2):
            here = (bb == 0) and (cc == 0)
            if not here:
                send(adds, r.gsum, r.ogl_h, r.fgl.at[0], (bb, 2 * z + cc))

    @pl.when(adds)
    def _():
        pltpu.make_async_copy(r.gsum, r.ogl_h, r.fgl.at[0]).start()

    rows = pl.ds(pl.multiple_of(z * blk, blk), blk)

    @pl.when(c == 0)
    def _():
        r.sgu[...] = (r.pgu[rows, :].astype(F32) + others(r.rgu, r.zgu)).astype(BF16)

    spread(lambda cc: r.sgu.at[pl.ds(cc * (blk // 2), blk // 2), :], r.ogu_h.at[b], r.fgu.at[b], 0)

    @pl.when(c == 1)
    def _():
        r.sdn[...] = (r.pdn[pl.ds(2 * z, 2)].astype(F32) + others(r.rdn, r.zdn)).astype(BF16)

    spread(lambda cc: r.sdn.at[cc], r.odn_h.at[b], r.fdn.at[b], 1)

    @pl.when(c == 1)
    def _():
        r.sat[...] = (r.pat[rows, :].astype(F32) + others(r.rat, r.zat)).astype(BF16)

    spread(lambda cc: r.sat.at[pl.ds(cc * (blk // 2), blk // 2), :], r.oat_h.at[b], r.fat.at[b], 1)

    for bb in range(nb):
        arrived(r.ogu_h.at[bb], r.fgu.at[bb])
        arrived(r.odn_h.at[bb], r.fdn.at[bb])
        arrived(r.oat_h.at[bb], r.fat.at[bb])
    arrived(r.ogl_h, r.fgl.at[0])
    out_copy.wait()
    gin_copy.wait()
    assert used[0] == r.ssem.shape[0]
    for cond, src, dst, ssem, rsem, dev in pending:
        @pl.when(cond)
        def _(args=(src, dst, ssem, rsem, dev)):
            remote(*args).wait_send()

    def sent_on(t, _):
        @pl.when((lax.rem(t, 2) == c) & (t < s))
        def _():
            remote(r.x_all.at[t], r.x_all.at[t], r.fsem.at[0, t], r.rx.at[t], sib).wait_send()

        @pl.when((lax.rem(t, 2) == c) & (t > s))
        def _():
            remote(r.q_all.at[t], r.q_all.at[t], r.fsem.at[1, t], r.rq.at[t], sib).wait_send()
            remote(r.do_all.at[t], r.do_all.at[t], r.fsem.at[2, t], r.rdo.at[t], sib).wait_send()
            remote(r.st_all.at[t], r.st_all.at[t], r.fsem.at[3, t], r.rst.at[t], sib).wait_send()
        return 0

    lax.fori_loop(0, n, sent_on, 0)


def unpack_kernel(n, nb, out_in, gin_in, oat, ogu, odn, ogl, out, gin, gq, gk, gv, go, gg, gu, gd, g1, g2):
    s = lax.axis_index("seq")
    fs = ogu.shape[2] // 2
    tok, dh = odn.shape[1], odn.shape[2]
    out[0] = out_in[...]
    gin[0] = gin_in[...]
    for m, ref in enumerate((gq, gk, gv, go)):
        ref[...] = oat[m].astype(F32)
    for bb in range(nb):
        gg[:, bb * fs:(bb + 1) * fs] = ogu[bb, :, :fs].astype(F32)
        gu[:, bb * fs:(bb + 1) * fs] = ogu[bb, :, fs:].astype(F32)
        gd[(bb // 2) * tok:(bb // 2 + 1) * tok, (bb % 2) * dh:(bb % 2 + 1) * dh] = odn[bb].astype(F32)
    d = ogl.shape[1]
    own = d // n
    gains = pltpu.roll(ogl[...], lax.rem(d - s * own, d), 1)
    g1[...] = gains[0:1, :own]
    g2[...] = gains[1:2, :own]


def rope_constants(length, head_dim):
    half = head_dim // 2
    inverse = np.exp(-2.0 * math.log(THETA) / head_dim * np.arange(half)).astype(np.float32)
    angle = np.arange(length, dtype=np.float32)[:, None] * inverse
    cos, sin = np.cos(angle.astype(np.float64)), np.sin(angle.astype(np.float64))
    return (
        np.concatenate([cos, cos, cos, cos], 1).astype(np.float32),
        np.concatenate([-sin, sin, -sin, sin], 1).astype(np.float32),
    )


def fused_local(n, nb, tokens, doc_ids, w_query, w_key, w_value, w_out, w_gate, w_up, w_down, gain_attn, gain_ffn, cotangent):
    _, tok, d = tokens.shape
    f = w_gate.shape[1]
    nz = n // 2
    cos, sin = rope_constants(n * tok, d // HEADS)
    cos = jnp.asarray(cos.reshape(nz, 2 * tok, 128))
    sin = jnp.asarray(sin.reshape(nz, 2 * tok, 128))
    plan = scratch_plan(tok, d, f, n, nb)
    vmem, anywhere = pl.BlockSpec(memory_space=pltpu.VMEM), pl.BlockSpec(memory_space=pl.ANY)
    shape = jax.ShapeDtypeStruct
    parts = pl.pallas_call(
        functools.partial(layer_kernel, tuple(plan), tok, d, f, n, nb),
        out_shape=(
            shape((tok, d), F32), shape((tok, d), F32), shape((nb, d // n, d), BF16),
            shape((nb, d // n, 2 * f // nb), BF16), shape((nb, tok, d // 2), BF16), shape((8, d), F32),
        ),
        in_specs=[vmem] * 5 + [anywhere] * 9,
        out_specs=[anywhere] * 6,
        scratch_shapes=list(plan.values()),
        compiler_params=pltpu.CompilerParams(
            collective_id=0, has_side_effects=True, vmem_limit_bytes=62 * 2**20
        ),
        name="layer",
    )(
        doc_ids, tokens, cotangent, gain_attn.reshape(1, d), gain_ffn.reshape(1, d), cos, sin,
        w_query, w_key, w_value, w_out, w_gate, w_up, w_down,
    )
    own = d // n
    results = pl.pallas_call(
        functools.partial(unpack_kernel, n, nb),
        out_shape=(
            shape((1, tok, d), F32), shape((1, tok, d), F32),
            shape((own, d), F32), shape((own, d), F32), shape((own, d), F32), shape((own, d), F32),
            shape((own, f), F32), shape((own, f), F32), shape((f // n, d), F32),
            shape((1, own), F32), shape((1, own), F32),
        ),
        in_specs=[vmem] * 6,
        out_specs=[vmem] * 11,
        compiler_params=pltpu.CompilerParams(vmem_limit_bytes=32 * 2**20),
        name="unpack",
    )(*parts)
    return results[:9] + (results[9].reshape(own), results[10].reshape(own))


def fits(shapes, n, nb):
    (_, tok, d), f = shapes[0], shapes[6][1]
    return (
        nb == 4 and n % 2 == 0 and n * tok <= 1024 and tok == 128 and shapes[0][0] == 1
        and d == HEADS * 64 and d % 256 == 0 and d % (16 * n) == 0 and f == 2 * tok * n and f % 1024 == 0
    )


def solution(mesh):
    nb, n = mesh.shape["batch"], mesh.shape["seq"]

    def either(*args):
        shapes = [a.shape for a in args]
        if fits(shapes, n, nb):
            return fused_local(n, nb, *args)
        return local(*args)

    return jax.shard_map(
        either,
        mesh=mesh,
        in_specs=(
            P("batch", "seq", None),
            P("batch", "seq"),
            P(),
            P(),
            P(),
            P(),
            P(),
            P(),
            P(),
            P(),
            P(),
            P("batch", "seq", None),
        ),
        out_specs=(
            P("batch", "seq", None),
            P("batch", "seq", None),
            P("seq", None),
            P("seq", None),
            P("seq", None),
            P("seq", None),
            P("seq", None),
            P("seq", None),
            P("seq", None),
            P("seq"),
            P("seq"),
        ),
        check_vma=False,
    )
```

```python
import functools
import math
import types

import jax
import jax.numpy as jnp
import numpy as np
from jax import lax
from jax.experimental import pallas as pl
from jax.experimental.pallas import tpu as pltpu
from jax.sharding import PartitionSpec as P

HEADS = 12
NSEG = 8


EPSILON = 1e-06
THETA = 10000.0
MASKED = -1e30


def root_mean_square_norm(values, gain):
    return values * lax.rsqrt(jnp.mean(values * values, -1, keepdims=True) + EPSILON) * gain


def swiglu(gate, up_part):
    return jax.nn.silu(gate) * up_part


def rope_tables(positions, head_dim):
    half_dim = head_dim // 2
    inverse = jnp.exp(-2.0 * math.log(THETA) / head_dim * jnp.arange(half_dim, dtype=jnp.float32))
    angle = positions.astype(jnp.float32)[..., None] * inverse
    return (
        jnp.concatenate([jnp.cos(angle), jnp.cos(angle)], -1),
        jnp.concatenate([jnp.sin(angle), jnp.sin(angle)], -1),
    )


def rotate(values, cosine, sine):
    half_dim = values.shape[-1] // 2
    turned = jnp.concatenate([-values[..., half_dim:], values[..., :half_dim]], -1)
    return values * cosine + turned * sine


def rotate_back(grads, cosine, sine):
    half_dim = grads.shape[-1] // 2
    turned = grads * sine
    return grads * cosine + jnp.concatenate([turned[..., half_dim:], -turned[..., :half_dim]], -1)


def block_size(total_rows):
    return max((d for d in range(1, min(total_rows, 2048) + 1) if total_rows % d == 0))


def doc_begin(segment_begins, where_at):
    earlier = segment_begins[:, None, :] <= where_at[:, :, None]
    return jnp.max(jnp.where(earlier, segment_begins[:, None, :], 0), -1)


def outer_sum(remaining_tokens, right):
    return lax.dot_general(
        remaining_tokens, right, (((0,), (0,)), ((), ())), preferred_element_type=jnp.float32
    )


def back_product(grads, weight_matrix):
    return lax.dot_general(
        grads, weight_matrix, (((1,), (1,)), ((), ())), preferred_element_type=jnp.float32
    )


def masked_scores(queries, key_block, key_at, query_at, query_begin):
    batch_rows, block_rows, model_width = key_block.shape
    head_count = queries.shape[2]
    head_dim = model_width // head_count
    key_heads = key_block.reshape(batch_rows, block_rows, head_count, head_dim)
    scores = jnp.einsum(
        "bqhd,bkhd->bhqk", queries, key_heads, preferred_element_type=jnp.float32
    ) * (1.0 / math.sqrt(head_dim))
    key_pos = key_at[None, None, :]
    query_pos = query_at[:, :, None]
    begin_pos = query_begin[:, :, None]
    allowed = (
        (key_pos <= query_pos) & (key_pos >= begin_pos) & ((begin_pos > 0) | (key_pos == query_pos))
    )
    return (scores, allowed[:, None], key_heads)


def grad_terms(
    queries, grad_heads, lse, delta, query_at, query_begin, key_block, value_block, key_at
):
    scores, allowed, key_heads = masked_scores(queries, key_block, key_at, query_at, query_begin)
    value_heads = value_block.reshape(key_heads.shape)
    probs = jnp.where(allowed, jnp.exp(scores - lse[..., None]), 0.0)
    dprob = jnp.einsum(
        "bqhd,bkhd->bhqk", grad_heads, value_heads, preferred_element_type=jnp.float32
    )
    dscore = (probs * (dprob - delta[..., None])).astype(jnp.bfloat16)
    return (probs.astype(jnp.bfloat16), dscore, key_heads, value_heads)


def over_rows(update, carried, arrays, first_row):
    total_rows = arrays[0].shape[1]
    block_rows = block_size(total_rows)

    def over_step(block_index, state):
        offset = block_index * block_rows
        blocks = tuple((lax.dynamic_slice_in_dim(item, offset, block_rows, 1) for item in arrays))
        key_at = first_row + offset + jnp.arange(block_rows, dtype=jnp.int32)
        return update(state, blocks, key_at)

    return lax.fori_loop(0, total_rows // block_rows, over_step, carried)


def local(
    tokens,
    doc_ids,
    w_query,
    w_key,
    w_value,
    w_out,
    w_gate,
    w_up,
    w_down,
    gain_attn,
    gain_ffn,
    cotangent,
):
    batch_rows, local_len, model_width = tokens.shape
    head_count = HEADS
    head_dim = model_width // head_count
    shape_heads = (batch_rows, local_len, head_count, head_dim)
    scale = 1.0 / math.sqrt(head_dim)
    labels = jnp.arange(NSEG, dtype=jnp.int32)
    member = (doc_ids[:, :, None] == labels).astype(jnp.int32)
    totals = lax.psum(jnp.sum(member, 1), "seq")
    segment_begins = jnp.cumsum(totals, 1) - totals
    local_at = lax.axis_index("seq") * local_len + jnp.arange(local_len, dtype=jnp.int32)
    query_at = jnp.broadcast_to(local_at, (batch_rows, local_len))
    query_begin = doc_begin(segment_begins, query_at)
    cosine, sine = rope_tables(query_at - query_begin, head_dim)
    cosine = cosine[:, :, None, :]
    sine = sine[:, :, None, :]
    flat_tokens = tokens.reshape(batch_rows * local_len, model_width)
    queries = rotate(
        jnp.dot(flat_tokens, w_query, preferred_element_type=jnp.float32).reshape(shape_heads),
        cosine,
        sine,
    ).astype(jnp.bfloat16)
    key_send = (
        rotate(
            jnp.dot(flat_tokens, w_key, preferred_element_type=jnp.float32).reshape(shape_heads),
            cosine,
            sine,
        )
        .astype(jnp.bfloat16)
        .reshape(batch_rows, local_len, model_width)
    )
    value_send = (
        jnp.dot(flat_tokens, w_value, preferred_element_type=jnp.float32)
        .astype(jnp.bfloat16)
        .reshape(batch_rows, local_len, model_width)
    )

    def stats_step(state, blocks, key_at):
        run_max, run_sum = state
        scores, allowed, key_heads = masked_scores(
            queries, blocks[0], key_at, query_at, query_begin
        )
        scores = jnp.where(allowed, scores, MASKED)
        new_max = jnp.maximum(run_max, jnp.max(scores, -1))
        weights = jnp.where(allowed, jnp.exp(scores - new_max[..., None]), 0.0)
        return (new_max, run_sum * jnp.exp(run_max - new_max) + jnp.sum(weights, -1))

    stats_init = (
        jnp.full((batch_rows, head_count, local_len), MASKED, jnp.float32),
        jnp.zeros((batch_rows, head_count, local_len), jnp.float32),
    )
    zero_heads = jnp.zeros(shape_heads, jnp.float32)
    run_max, run_sum = over_rows(
        stats_step, stats_init, (lax.all_gather(key_send, "seq", axis=1, tiled=True),), jnp.int32(0)
    )
    lse = run_max + jnp.log(run_sum)

    def output_step(state, blocks, key_at):
        scores, allowed, key_heads = masked_scores(
            queries, blocks[0], key_at, query_at, query_begin
        )
        value_heads = blocks[1].reshape(key_heads.shape)
        probs = jnp.where(allowed, jnp.exp(scores - lse[..., None]), 0.0).astype(jnp.bfloat16)
        return state + jnp.einsum(
            "bhqk,bkhd->bqhd", probs, value_heads, preferred_element_type=jnp.float32
        )

    attended = over_rows(
        output_step,
        zero_heads,
        (
            lax.all_gather(key_send, "seq", axis=1, tiled=True),
            lax.all_gather(value_send, "seq", axis=1, tiled=True),
        ),
        jnp.int32(0),
    )
    attended_low = attended.astype(jnp.bfloat16).reshape(batch_rows * local_len, model_width)
    first_sum = flat_tokens.astype(jnp.float32) + jnp.dot(
        attended_low, w_out, preferred_element_type=jnp.float32
    )
    hidden, norm_first_back = jax.vjp(root_mean_square_norm, first_sum, gain_attn)
    hidden_low = hidden.astype(jnp.bfloat16)
    gate = jnp.dot(hidden_low, w_gate, preferred_element_type=jnp.float32)
    up_part = jnp.dot(hidden_low, w_up, preferred_element_type=jnp.float32)
    active, swiglu_back = jax.vjp(swiglu, gate, up_part)
    active_low = active.astype(jnp.bfloat16)
    second_sum = hidden + jnp.dot(active_low, w_down, preferred_element_type=jnp.float32)
    output, norm_second_back = jax.vjp(root_mean_square_norm, second_sum, gain_ffn)
    second_grad, grad_gain_ffn = norm_second_back(
        cotangent.reshape(batch_rows * local_len, model_width).astype(jnp.float32)
    )
    branch_grad = second_grad.astype(jnp.bfloat16)
    grad_down = outer_sum(active_low, branch_grad)
    gate_grad, up_grad = swiglu_back(back_product(branch_grad, w_down))
    gate_low = gate_grad.astype(jnp.bfloat16)
    up_low = up_grad.astype(jnp.bfloat16)
    grad_gate = outer_sum(hidden_low, gate_low)
    grad_up = outer_sum(hidden_low, up_low)
    hidden_grad = second_grad + back_product(gate_low, w_gate) + back_product(up_low, w_up)
    first_grad, grad_gain_attn = norm_first_back(hidden_grad)
    attn_grad = first_grad.astype(jnp.bfloat16)
    grad_out = outer_sum(attended_low, attn_grad)
    grad_heads = back_product(attn_grad, w_out).astype(jnp.bfloat16).reshape(shape_heads)
    delta = jnp.swapaxes(jnp.sum(grad_heads.astype(jnp.float32) * attended, -1), 1, 2)

    def query_step(state, blocks, key_at):
        probs_low, dscore, key_heads, value_heads = grad_terms(
            queries, grad_heads, lse, delta, query_at, query_begin, blocks[0], blocks[1], key_at
        )
        return (
            state
            + jnp.einsum("bhqk,bkhd->bqhd", dscore, key_heads, preferred_element_type=jnp.float32)
            * scale
        )

    all_keys, all_values = (
        lax.all_gather(key_send, "seq", axis=1, tiled=True),
        lax.all_gather(value_send, "seq", axis=1, tiled=True),
    )
    query_grad = over_rows(query_step, zero_heads, (all_keys, all_values), 0)
    first_row = jnp.int32(0)
    span_rows = local_len * lax.axis_size("seq")
    block_rows = block_size(span_rows)
    empty = jnp.zeros((batch_rows, span_rows, head_count, head_dim), jnp.float32)

    def key_step(block_index, state):
        offset = block_index * block_rows
        key_block = lax.dynamic_slice_in_dim(all_keys, offset, block_rows, 1)
        value_block = lax.dynamic_slice_in_dim(all_values, offset, block_rows, 1)
        key_at = first_row + offset + jnp.arange(block_rows, dtype=jnp.int32)
        probs_low, dscore, key_heads, value_heads = grad_terms(
            queries, grad_heads, lse, delta, query_at, query_begin, key_block, value_block, key_at
        )
        key_part = (
            jnp.einsum("bhqk,bqhd->bkhd", dscore, queries, preferred_element_type=jnp.float32)
            * scale
        )
        value_part = jnp.einsum(
            "bhqk,bqhd->bkhd", probs_low, grad_heads, preferred_element_type=jnp.float32
        )
        return (
            lax.dynamic_update_slice_in_dim(state[0], key_part, offset, 1),
            lax.dynamic_update_slice_in_dim(state[1], value_part, offset, 1),
        )

    key_all, value_all = lax.fori_loop(0, span_rows // block_rows, key_step, (empty, empty))
    joined = jnp.concatenate(
        [
            key_all.reshape(batch_rows, span_rows, model_width),
            value_all.reshape(batch_rows, span_rows, model_width),
        ],
        -1,
    )
    summed_keys = jnp.swapaxes(
        lax.psum_scatter(jnp.swapaxes(joined, 0, 1), "seq", scatter_dimension=0, tiled=True), 0, 1
    )
    key_grad = summed_keys[..., :model_width].reshape(shape_heads)
    value_grad = summed_keys[..., model_width:]
    flat_len = batch_rows * local_len
    query_low = (
        rotate_back(query_grad, cosine, sine).astype(jnp.bfloat16).reshape(flat_len, model_width)
    )
    key_low = (
        rotate_back(key_grad, cosine, sine).astype(jnp.bfloat16).reshape(flat_len, model_width)
    )
    value_low = value_grad.astype(jnp.bfloat16).reshape(flat_len, model_width)
    grad_input = (
        first_grad
        + back_product(query_low, w_query)
        + back_product(key_low, w_key)
        + back_product(value_low, w_value)
    )
    grad_query = outer_sum(flat_tokens, query_low)
    grad_key = outer_sum(flat_tokens, key_low)
    value_weight_gradient = outer_sum(flat_tokens, value_low)
    shares = (
        lax.psum_scatter(grad_query, "seq", scatter_dimension=0, tiled=True),
        lax.psum_scatter(grad_key, "seq", scatter_dimension=0, tiled=True),
        lax.psum_scatter(value_weight_gradient, "seq", scatter_dimension=0, tiled=True),
        lax.psum_scatter(grad_out, "seq", scatter_dimension=0, tiled=True),
        lax.psum_scatter(grad_gate, "seq", scatter_dimension=0, tiled=True),
        lax.psum_scatter(grad_up, "seq", scatter_dimension=0, tiled=True),
        lax.psum_scatter(grad_down, "seq", scatter_dimension=0, tiled=True),
        lax.psum_scatter(grad_gain_attn, "seq", scatter_dimension=0, tiled=True),
        lax.psum_scatter(grad_gain_ffn, "seq", scatter_dimension=0, tiled=True),
    )
    results = (
        lax.psum(shares[0].astype(jnp.bfloat16), "batch").astype(jnp.float32),
        lax.psum(shares[1].astype(jnp.bfloat16), "batch").astype(jnp.float32),
        lax.psum(shares[2].astype(jnp.bfloat16), "batch").astype(jnp.float32),
        lax.psum(shares[3].astype(jnp.bfloat16), "batch").astype(jnp.float32),
        lax.psum(shares[4].astype(jnp.bfloat16), "batch").astype(jnp.float32),
        lax.psum(shares[5].astype(jnp.bfloat16), "batch").astype(jnp.float32),
        lax.psum(shares[6].astype(jnp.bfloat16), "batch").astype(jnp.float32),
        lax.psum(shares[7].astype(jnp.bfloat16), "batch").astype(jnp.float32),
        lax.psum(shares[8].astype(jnp.bfloat16), "batch").astype(jnp.float32),
    )
    output_rows = output.reshape(batch_rows, local_len, model_width)
    input_rows = grad_input.reshape(batch_rows, local_len, model_width)
    return (
        output_rows,
        input_rows,
        results[0],
        results[1],
        results[2],
        results[3],
        results[4],
        results[5],
        results[6],
        results[7],
        results[8],
    )


MESH = pl.DeviceIdType.MESH
F32 = jnp.float32
BF16 = jnp.bfloat16


def mm(a, b):
    return lax.dot_general(a, b, (((1,), (0,)), ((), ())), preferred_element_type=F32)


def mm_nt(a, b):
    return lax.dot_general(a, b, (((1,), (1,)), ((), ())), preferred_element_type=F32)


def scratch_plan(tok, d, f, n, nb):
    nz, plane, heads = n // 2, 2 * nb * tok, HEADS
    vm = pltpu.VMEM
    dma = lambda *shape: pltpu.SemaphoreType.DMA(shape)
    return dict(
        wq=vm((d, d), BF16), wk=vm((d, d), BF16), wv=vm((d, d), BF16), wo=vm((d, d), BF16),
        wg=vm((d, f), BF16), wu=vm((d, f), BF16), wd=vm((f, d), BF16),
        cos=vm((nz, 2 * tok, 128), F32), sin=vm((nz, 2 * tok, 128), F32),
        x_all=vm((n, tok, d), BF16), q_all=vm((n, tok, d), BF16), do_all=vm((n, tok, d), BF16),
        k_all=vm((nz, 2 * tok, d), BF16), v_all=vm((nz, 2 * tok, d), BF16),
        st_all=vm((n, 32, tok), F32), id_all=vm((n, 8, tok), jnp.int32),
        idcol=vm((tok, 128), F32), bias=vm((tok, 2 * tok), F32),
        m=vm((heads, tok, 128), F32), l=vm((heads, tok, 128), F32), delta=vm((heads, tok, 128), F32),
        acc=vm((tok, d), F32), acc2=vm((tok, d), F32),
        olow=vm((tok, d), BF16), hb=vm((tok, d), BF16), h1=vm((tok, d), F32), n1=vm((tok, d), F32),
        ri1=vm((tok, 128), F32), dr=vm((tok, d), F32),
        g32=vm((tok, f), F32), u32=vm((tok, f), F32), act=vm((tok, f), BF16),
        dg=vm((tok, f), BF16), du=vm((tok, f), BF16), dmo=vm((tok, d), BF16), dattn=vm((tok, d), BF16),
        dq=vm((tok, d), BF16), dk=vm((tok, d), BF16), dv=vm((tok, d), BF16),
        actT=vm((n, 2, tok, tok), BF16), hT=vm((d, tok), BF16), xT=vm((d, tok), BF16), oT=vm((d, tok), BF16),
        gl=vm((8, d), F32), out_v=vm((tok, d), F32), gin_v=vm((tok, d), F32),
        hT_b=vm((d, plane), BF16), dgu_b=vm((plane, 2 * f // nb), BF16),
        act_b=vm((n, tok, plane), BF16), dmo_b=vm((plane, d // 2), BF16),
        kT_b=vm((d, plane), BF16), nn_b=vm((plane, d), BF16), gl_b=vm((2 * nb, 8, d), F32),
        pgu=vm((d, 2 * f // nb), BF16), pdn=vm((n, tok, d // 2), BF16), pat=vm((d, d), BF16),
        rgu=vm((nz, d // nz, 2 * f // nb), BF16), rdn=vm((nz, 2, tok, d // 2), BF16), rat=vm((nz, d // nz, d), BF16),
        sgu=vm((d // nz, 2 * f // nb), BF16), sdn=vm((2, tok, d // 2), BF16), sat=vm((d // nz, d), BF16),
        gz=vm((nz, 8, d), F32), gsum=vm((8, d), F32),
        wsem=dma(9), osem=dma(2), ssem=dma(100), fsem=dma(4, n),
        rx=dma(n), rq=dma(n), rdo=dma(n), rst=dma(n), rid=dma(n),
        rh=dma(2 * nb), rdg=dma(2 * nb), rdu=dma(2 * nb), ract=dma(2 * nb), rdmo=dma(2 * nb),
        rkt=dma(2 * nb), rnn=dma(2 * nb), rgl=dma(2 * nb),
        zgu=dma(nz), zdn=dma(nz), zat=dma(nz), zgl=dma(nz),
        fgu=dma(nb), fdn=dma(nb), fat=dma(nb), fgl=dma(1),
    )


INPUTS = ("ids", "tok", "cot", "ga", "gf", "cos_h", "sin_h", "wq_h", "wk_h", "wv_h", "wo_h", "wg_h", "wu_h", "wd_h")
OUTPUTS = ("out_h", "gin_h", "oat_h", "ogu_h", "odn_h", "ogl_h")


def layer_kernel(plan_names, tok, d, f, n, nb, *refs):
    r = types.SimpleNamespace(**dict(zip(INPUTS + OUTPUTS + plan_names, refs)))
    nz, pairs = n // 2, d // 128
    fs, dh, blk = f // nb, d // 2, d // nz
    b, s = lax.axis_index("batch"), lax.axis_index("seq")
    z, c = s // 2, lax.rem(s, 2)
    by, bx = b // 2, lax.rem(b, 2)
    e = 2 * b + c
    sib = (b, s + 1 - 2 * c)
    gain_a, gain_f = r.ga[...].reshape(1, d), r.gf[...].reshape(1, d)
    pending, used = [], [0]

    def remote(src, dst, ssem, rsem, dev):
        return pltpu.make_async_remote_copy(
            src_ref=src, dst_ref=dst, send_sem=ssem, recv_sem=rsem, device_id=dev, device_id_type=MESH
        )

    def send(cond, src, dst, rsem, dev):
        ssem = r.ssem.at[used[0]]
        used[0] += 1
        pending.append((cond, src, dst, ssem, rsem, dev))

        @pl.when(cond)
        def _():
            remote(src, dst, ssem, rsem, dev).start()

    def plane_send(src, dst, rsem, to_b, to_c):
        here = (b == to_b) & (c == to_c)
        send(jnp.logical_not(here), src, dst, rsem, (to_b, 2 * z + to_c))

        @pl.when(here)
        def _():
            pltpu.make_async_copy(src, dst, rsem).start()

    def arrived(dst, rsem):
        remote(dst, dst, r.ssem.at[0], rsem, sib).wait_recv()

    loads = {}
    for i, name in enumerate(("wk", "wv", "wq", "cos", "sin", "wo", "wg", "wu", "wd")):
        loads[name] = pltpu.make_async_copy(getattr(r, name + "_h"), getattr(r, name), r.wsem.at[i])
        loads[name].start()

    r.x_all[s] = r.tok[0]
    r.id_all[s] = jnp.broadcast_to(r.ids[...], (8, tok))

    bar = pltpu.get_barrier_semaphore()
    for zz in range(nz):
        for cc in range(2):
            @pl.when(2 * zz + cc != s)
            def _(zz=zz, cc=cc):
                pl.semaphore_signal(bar, inc=1, device_id=(b, 2 * zz + cc), device_id_type=MESH)
    for bb in range(nb):
        for cc in range(2):
            @pl.when(bb != b)
            def _(bb=bb, cc=cc):
                pl.semaphore_signal(bar, inc=1, device_id=(bb, 2 * z + cc), device_id_type=MESH)
    pl.semaphore_wait(bar, n - 1 + 2 * (nb - 1))

    always = s >= 0
    send(always, r.x_all.at[s], r.x_all.at[s], r.rx.at[s], sib)
    for dz in range(1, nz):
        send(z + dz < nz, r.x_all.at[s], r.x_all.at[s], r.rx.at[s], (b, s + 2 * dz))
    for zz in range(nz):
        for cc in range(2):
            send(2 * zz + cc != s, r.id_all.at[s], r.id_all.at[s], r.rid.at[s], (b, 2 * zz + cc))

    lane = lax.broadcasted_iota(jnp.int32, (tok, 128), 1)
    first = lane < 64
    half_mask = (jnp.where(first, 1.0, 0.0).astype(BF16), jnp.where(first, 0.0, 1.0).astype(BF16))

    def turn(u):
        low = lax.rem(lax.broadcasted_iota(jnp.int32, u.shape, 1), 64) < 32
        return jnp.where(low, pltpu.roll(u, 96, 1), pltpu.roll(u, 32, 1))

    def twice(u):
        return jnp.concatenate([u, u], axis=1)

    own = pl.ds(pl.multiple_of(c * tok, tok), tok)

    loads["wq"].wait()
    loads["cos"].wait()
    loads["sin"].wait()

    u = mm(r.tok[0], r.wq[...])
    co, si = r.cos[z, own, :], r.sin[z, own, :]
    for p in range(pairs):
        part = u[:, p * 128:(p + 1) * 128]
        r.q_all[s, :, p * 128:(p + 1) * 128] = ((part * co + turn(part) * si) * 0.125).astype(BF16)
    send(always, r.q_all.at[s], r.q_all.at[s], r.rq.at[s], sib)
    for dz in range(1, nz):
        send(z - dz >= 0, r.q_all.at[s], r.q_all.at[s], r.rq.at[s], (b, s - 2 * dz))

    def transpose_into(dst, value):
        for p in range(d // 128):
            dst[p * 128:(p + 1) * 128, :] = value[:, p * 128:(p + 1) * 128].T.astype(BF16)

    tokens = pl.ds(pl.multiple_of(e * tok, tok), tok)
    transpose_into(r.xT, r.tok[0].astype(F32))
    for bb in range(3):
        plane_send(r.xT, r.kT_b.at[:, tokens], r.rkt.at[e], bb, 1)
    r.idcol[...] = jnp.broadcast_to(r.ids[...].astype(F32), (128, tok)).T

    def each_id(t, _):
        @pl.when(t != s)
        def _():
            arrived(r.id_all.at[t], r.rid.at[t])
        return 0

    lax.fori_loop(0, n, each_id, 0)

    def ids_of(block):
        return jnp.concatenate(
            [r.id_all[2 * block, 0:1, :], r.id_all[2 * block + 1, 0:1, :]], axis=1
        ).astype(F32)

    def set_bias(block, local_is_query):
        shape = (tok, 2 * tok)
        mine = s * tok + lax.broadcasted_iota(jnp.int32, shape, 0)
        theirs = block * (2 * tok) + lax.broadcasted_iota(jnp.int32, shape, 1)
        my_id = twice(r.idcol[...])
        their_id = jnp.broadcast_to(ids_of(block), shape)
        causal = (theirs <= mine) if local_is_query else (mine <= theirs)
        allowed = (my_id == their_id) & causal & ((my_id != 0.0) | (mine == theirs))
        r.bias[...] = jnp.where(allowed, 0.0, MASKED)

    r.m[...] = jnp.full(r.m.shape, MASKED, F32)
    r.l[...] = jnp.zeros(r.l.shape, F32)
    r.acc[...] = jnp.zeros(r.acc.shape, F32)
    loads["wk"].wait()
    loads["wv"].wait()

    def forward_step(j, _):
        kb = z - j
        mine, other = 2 * kb + c, 2 * kb + 1 - c

        @pl.when(j > 0)
        def _():
            arrived(r.x_all.at[mine], r.rx.at[mine])
            remote(r.x_all.at[mine], r.x_all.at[mine], r.fsem.at[0, mine], r.rx.at[mine], sib).start()

        arrived(r.x_all.at[other], r.rx.at[other])
        set_bias(kb, True)

        xb = r.x_all[pl.ds(2 * kb, 2)].reshape(2 * tok, d)
        u = mm(xb, r.wk[...])
        co, si = r.cos[kb], r.sin[kb]
        for p in range(pairs):
            part = u[:, p * 128:(p + 1) * 128]
            r.k_all[kb, :, p * 128:(p + 1) * 128] = (part * co + turn(part) * si).astype(BF16)
        r.v_all[kb] = mm(xb, r.wv[...]).astype(BF16)

        def pair(p, _):
            lanes = pl.ds(pl.multiple_of(p * 128, 128), 128)
            qp, kp, vp = r.q_all[s, :, lanes], r.k_all[kb, :, lanes], r.v_all[kb, :, lanes]
            alphas, outs = [], []
            for h in range(2):
                sc = mm_nt(qp * half_mask[h], kp) + r.bias[...]
                m_old = r.m[2 * p + h]
                m_new = jnp.maximum(m_old, jnp.max(sc, axis=1, keepdims=True))
                alpha = jnp.exp(m_old - m_new)
                ex = jnp.exp(sc - twice(m_new))
                r.m[2 * p + h] = m_new
                r.l[2 * p + h] = r.l[2 * p + h] * alpha + jnp.sum(ex, axis=1, keepdims=True)
                alphas.append(alpha)
                outs.append(mm(ex.astype(BF16), vp))
            r.acc[:, lanes] = r.acc[:, lanes] * jnp.where(first, alphas[0], alphas[1]) + jnp.where(
                first, outs[0], outs[1]
            )
            return 0

        lax.fori_loop(0, pairs, pair, 0, unroll=True)
        return 0

    lax.fori_loop(0, z + 1, forward_step, 0)

    def finish(p, _):
        lanes = pl.ds(pl.multiple_of(p * 128, 128), 128)
        l0, l1 = r.l[2 * p], r.l[2 * p + 1]
        r.acc[:, lanes] = r.acc[:, lanes] / jnp.where(first, l0, l1)
        r.m[2 * p] = r.m[2 * p] + jnp.log(l0)
        r.m[2 * p + 1] = r.m[2 * p + 1] + jnp.log(l1)
        return 0

    lax.fori_loop(0, pairs, finish, 0, unroll=True)
    r.olow[...] = r.acc[...].astype(BF16)

    loads["wo"].wait()
    r1 = r.tok[0].astype(F32) + mm(r.olow[...], r.wo[...])
    ri1 = lax.rsqrt(jnp.mean(r1 * r1, axis=1, keepdims=True) + EPSILON)
    r.ri1[...] = jnp.broadcast_to(ri1, (tok, 128))
    n1 = r1 * ri1
    r.n1[...] = n1
    h1 = n1 * gain_a
    r.h1[...] = h1
    r.hb[...] = h1.astype(BF16)
    transpose_into(r.hT, h1)
    for bb in range(nb):
        plane_send(r.hT, r.hT_b.at[:, tokens], r.rh.at[e], bb, 0)
    transpose_into(r.oT, r.acc[...])
    plane_send(r.oT, r.kT_b.at[:, tokens], r.rkt.at[e], 3, 1)
    loads["wg"].wait()
    loads["wu"].wait()

    def up_tile(i, _):
        at = pl.ds(pl.multiple_of(i * 256, 256), 256)
        g = mm(r.hb[...], r.wg[:, at])
        u = mm(r.hb[...], r.wu[:, at])
        r.g32[:, at] = g
        r.u32[:, at] = u
        a = g / (1.0 + jnp.exp(-g)) * u
        r.act[:, at] = a.astype(BF16)
        r.actT[i, 0] = a[:, :128].T.astype(BF16)
        r.actT[i, 1] = a[:, 128:].T.astype(BF16)
        return 0

    lax.fori_loop(0, f // 256, up_tile, 0)
    for bb in range(nb):
        plane_send(r.actT.at[:, bb // 2], r.act_b.at[:, :, tokens], r.ract.at[e], bb, 1)
    loads["wd"].wait()
    r2 = r.h1[...] + mm(r.act[...], r.wd[...])
    ri2 = lax.rsqrt(jnp.mean(r2 * r2, axis=1, keepdims=True) + EPSILON)
    n2 = r2 * ri2
    r.out_v[...] = n2 * gain_f
    out_copy = pltpu.make_async_copy(r.out_v, r.out_h, r.osem.at[0])
    out_copy.start()
    ct = r.cot[0].astype(F32)
    gain_ffn = jnp.sum(ct * n2, axis=0, keepdims=True)
    t2 = ct * gain_f
    dr2 = ri2 * (t2 - n2 * jnp.mean(n2 * t2, axis=1, keepdims=True))
    r.dr[...] = dr2
    r.dmo[...] = dr2.astype(BF16)
    for bb in range(nb):
        plane_send(
            r.dmo.at[:, pl.ds((bb % 2) * dh, dh)], r.dmo_b.at[tokens, :], r.rdmo.at[e], bb, 1
        )

    def down_tile(i, _):
        at = pl.ds(pl.multiple_of(i * 256, 256), 256)
        da = mm_nt(r.dmo[...], r.wd[at, :])
        g, u = r.g32[:, at], r.u32[:, at]
        sg = 1.0 / (1.0 + jnp.exp(-g))
        r.dg[:, at] = (da * u * (sg * (1.0 + g * (1.0 - sg)))).astype(BF16)
        r.du[:, at] = (da * (g * sg)).astype(BF16)
        return 0

    lax.fori_loop(0, f // 256, down_tile, 0)
    for bb in range(nb):
        cols = pl.ds(bb * fs, fs)
        plane_send(r.dg.at[:, cols], r.dgu_b.at[tokens, pl.ds(0, fs)], r.rdg.at[e], bb, 0)
        plane_send(r.du.at[:, cols], r.dgu_b.at[tokens, pl.ds(fs, fs)], r.rdu.at[e], bb, 0)
    dh1 = r.dr[...] + mm_nt(r.dg[...], r.wg[...]) + mm_nt(r.du[...], r.wu[...])
    n1 = r.n1[...]
    gain_attn = jnp.sum(dh1 * n1, axis=0, keepdims=True)
    t1 = dh1 * gain_a
    dr1 = r.ri1[:, 0:1] * (t1 - n1 * jnp.mean(n1 * t1, axis=1, keepdims=True))
    r.dr[...] = dr1
    r.dattn[...] = dr1.astype(BF16)
    r.gl[...] = jnp.concatenate([gain_attn, gain_ffn, jnp.zeros((6, d), F32)], axis=0)
    plane_send(r.dattn, r.nn_b.at[tokens, :], r.rnn.at[e], 3, 1)
    plane_send(r.gl, r.gl_b.at[e], r.rgl.at[e], 0, 0)
    r.do_all[s] = mm_nt(r.dattn[...], r.wo[...]).astype(BF16)
    send(always, r.do_all.at[s], r.do_all.at[s], r.rdo.at[s], sib)
    for dz in range(1, nz):
        send(z - dz >= 0, r.do_all.at[s], r.do_all.at[s], r.rdo.at[s], (b, s - 2 * dz))

    stats = jnp.zeros((tok, 128), F32)
    for p in range(pairs):
        prod = r.do_all[s, :, p * 128:(p + 1) * 128].astype(F32) * r.acc[:, p * 128:(p + 1) * 128]
        for h in range(2):
            head = 2 * p + h
            part = jnp.sum(jnp.where(first == (h == 0), prod, 0.0), axis=1, keepdims=True)
            part = jnp.broadcast_to(part, (tok, 128))
            r.delta[head] = part
            stats = jnp.where(lane == head, r.m[head], stats)
            stats = jnp.where(lane == 16 + head, part, stats)
    r.st_all[s] = stats.T[0:32, :]
    send(always, r.st_all.at[s], r.st_all.at[s], r.rst.at[s], sib)
    for dz in range(1, nz):
        send(z - dz >= 0, r.st_all.at[s], r.st_all.at[s], r.rst.at[s], (b, s - 2 * dz))

    r.acc[...] = jnp.zeros(r.acc.shape, F32)

    def query_step(kb, _):
        set_bias(kb, True)

        def pair(p, _):
            lanes = pl.ds(pl.multiple_of(p * 128, 128), 128)
            qp, kp, vp = r.q_all[s, :, lanes], r.k_all[kb, :, lanes], r.v_all[kb, :, lanes]
            dop = r.do_all[s, :, lanes]
            outs = []
            for h in range(2):
                sc = mm_nt(qp * half_mask[h], kp) + r.bias[...]
                pf = jnp.exp(sc - twice(r.m[2 * p + h]))
                dp = mm_nt(dop * half_mask[h], vp)
                ds = (pf * (dp - twice(r.delta[2 * p + h]))).astype(BF16)
                outs.append(mm(ds, kp))
            r.acc[:, lanes] += jnp.where(first, outs[0], outs[1])
            return 0

        lax.fori_loop(0, pairs, pair, 0, unroll=True)
        return 0

    lax.fori_loop(0, z + 1, query_step, 0)

    def turn_back(src, dst, factor):
        co, si = r.cos[z, own, :], r.sin[z, own, :]
        for p in range(pairs):
            g = src[:, p * 128:(p + 1) * 128] * factor
            dst[:, p * 128:(p + 1) * 128] = (g * co - turn(g) * si).astype(BF16)

    turn_back(r.acc, r.dq, 0.125)
    plane_send(r.dq, r.nn_b.at[tokens, :], r.rnn.at[e], 0, 1)

    r.acc[...] = jnp.zeros(r.acc.shape, F32)
    r.acc2[...] = jnp.zeros(r.acc2.shape, F32)

    def key_step(j, _):
        qb = z + j
        mine, other = 2 * qb + c, 2 * qb + 1 - c
        moved = ((1, r.q_all, r.rq), (2, r.do_all, r.rdo), (3, r.st_all, r.rst))

        @pl.when(j > 0)
        def _():
            for i, ref, sem in moved:
                arrived(ref.at[mine], sem.at[mine])
                remote(ref.at[mine], ref.at[mine], r.fsem.at[i, mine], sem.at[mine], sib).start()

        for i, ref, sem in moved:
            arrived(ref.at[other], sem.at[other])
        set_bias(qb, False)

        def pair(p, _):
            lanes = pl.ds(pl.multiple_of(p * 128, 128), 128)
            kp, vp = r.k_all[z, own, lanes], r.v_all[z, own, lanes]
            qp = r.q_all[pl.ds(2 * qb, 2), :, lanes].reshape(2 * tok, 128)
            dop = r.do_all[pl.ds(2 * qb, 2), :, lanes].reshape(2 * tok, 128)
            dks, dvs = [], []
            for h in range(2):
                head = 2 * p + h
                lse = jnp.concatenate(
                    [r.st_all[2 * qb, pl.ds(head, 1), :], r.st_all[2 * qb + 1, pl.ds(head, 1), :]], axis=1
                )
                dlt = jnp.concatenate(
                    [r.st_all[2 * qb, pl.ds(16 + head, 1), :], r.st_all[2 * qb + 1, pl.ds(16 + head, 1), :]],
                    axis=1,
                )
                sc = mm_nt(kp * half_mask[h], qp) + r.bias[...]
                pf = jnp.exp(sc - lse)
                dvs.append(mm(pf.astype(BF16), dop))
                dp = mm_nt(vp * half_mask[h], dop)
                ds = (pf * (dp - dlt)).astype(BF16)
                dks.append(mm(ds, qp))
            r.acc[:, lanes] += jnp.where(first, dks[0], dks[1])
            r.acc2[:, lanes] += jnp.where(first, dvs[0], dvs[1])
            return 0

        lax.fori_loop(0, pairs, pair, 0, unroll=True)
        return 0

    lax.fori_loop(0, nz - z, key_step, 0)
    turn_back(r.acc, r.dk, 1.0)
    plane_send(r.dk, r.nn_b.at[tokens, :], r.rnn.at[e], 1, 1)
    r.dv[...] = r.acc2[...].astype(BF16)
    plane_send(r.dv, r.nn_b.at[tokens, :], r.rnn.at[e], 2, 1)
    r.gin_v[...] = (
        r.dr[...] + mm_nt(r.dq[...], r.wq[...]) + mm_nt(r.dk[...], r.wk[...]) + mm_nt(r.dv[...], r.wv[...])
    )
    gin_copy = pltpu.make_async_copy(r.gin_v, r.gin_h, r.osem.at[1])
    gin_copy.start()

    def each_source(dst_of, rsem):
        for i in range(2 * nb):
            arrived(dst_of(i), rsem.at[i])

    def share(src_of, dst, rsem, to_c):
        for zz in range(nz):
            send((c == to_c) & (z != zz), src_of(zz), dst.at[z], rsem.at[z], (b, 2 * zz + to_c))

    def others(recv, rsem):
        total = None
        for dz in range(1, nz):
            at = lax.rem(z + dz, nz)
            arrived(recv.at[at], rsem.at[at])
            total = recv[at].astype(F32) if total is None else total + recv[at].astype(F32)
        return total

    def spread(src_of, dst, rsem, from_c):
        for bb in range(nb):
            for cc in range(2):
                here = (b == bb) & (s == 2 * z + cc)
                send(
                    (c == from_c) & jnp.logical_not(here), src_of(cc), dst, rsem, (bb, 2 * z + cc)
                )

                @pl.when((c == from_c) & here)
                def _(cc=cc):
                    pltpu.make_async_copy(src_of(cc), dst, rsem).start()

    span = 2 * tok * nb

    @pl.when(c == 0)
    def _():
        each_source(lambda i: r.hT_b.at[:, pl.ds(i * tok, tok)], r.rh)
        each_source(lambda i: r.dgu_b.at[pl.ds(i * tok, tok), pl.ds(0, fs)], r.rdg)
        each_source(lambda i: r.dgu_b.at[pl.ds(i * tok, tok), pl.ds(fs, fs)], r.rdu)

        def tile(i, _):
            at = pl.ds(pl.multiple_of(i * 256, 256), 256)
            r.pgu[:, at] = mm(r.hT_b[...], r.dgu_b[:, at]).astype(BF16)
            return 0

        lax.fori_loop(0, 2 * fs // 256, tile, 0)

    share(lambda zz: r.pgu.at[pl.ds(zz * blk, blk), :], r.rgu, r.zgu, 0)

    @pl.when(c == 1)
    def _():
        each_source(lambda i: r.act_b.at[:, :, pl.ds(i * tok, tok)], r.ract)
        each_source(lambda i: r.dmo_b.at[pl.ds(i * tok, tok), :], r.rdmo)

        def tile(i, _):
            left = r.act_b[pl.ds(2 * i, 2)].reshape(2 * tok, span)
            r.pdn[pl.ds(2 * i, 2)] = mm(left, r.dmo_b[...]).astype(BF16).reshape(2, tok, dh)
            return 0

        lax.fori_loop(0, n // 2, tile, 0)

    share(lambda zz: r.pdn.at[pl.ds(2 * zz, 2)], r.rdn, r.zdn, 1)

    @pl.when(c == 1)
    def _():
        each_source(lambda i: r.kT_b.at[:, pl.ds(i * tok, tok)], r.rkt)
        each_source(lambda i: r.nn_b.at[pl.ds(i * tok, tok), :], r.rnn)

        def tile(i, _):
            at = pl.ds(pl.multiple_of(i * 256, 256), 256)
            r.pat[:, at] = mm(r.kT_b[...], r.nn_b[:, at]).astype(BF16)
            return 0

        lax.fori_loop(0, d // 256, tile, 0)

    share(lambda zz: r.pat.at[pl.ds(zz * blk, blk), :], r.rat, r.zat, 1)

    adds = (b == 0) & (c == 0)

    @pl.when(adds)
    def _():
        total = None
        for i in range(2 * nb):
            arrived(r.gl_b.at[i], r.rgl.at[i])
            total = r.gl_b[i] if total is None else total + r.gl_b[i]
        r.gz[z] = total

    for zz in range(nz):
        send(adds & (z != zz), r.gz.at[z], r.gz.at[z], r.zgl.at[z], (0, 2 * zz))

    @pl.when(adds)
    def _():
        total = r.gz[z]
        for dz in range(1, nz):
            at = lax.rem(z + dz, nz)
            arrived(r.gz.at[at], r.zgl.at[at])
            total = total + r.gz[at]
        r.gsum[...] = total

    for bb in range(nb):
        for cc in range(2):
            here = (bb == 0) and (cc == 0)
            if not here:
                send(adds, r.gsum, r.ogl_h, r.fgl.at[0], (bb, 2 * z + cc))

    @pl.when(adds)
    def _():
        pltpu.make_async_copy(r.gsum, r.ogl_h, r.fgl.at[0]).start()

    rows = pl.ds(pl.multiple_of(z * blk, blk), blk)

    @pl.when(c == 0)
    def _():
        r.sgu[...] = (r.pgu[rows, :].astype(F32) + others(r.rgu, r.zgu)).astype(BF16)

    spread(lambda cc: r.sgu.at[pl.ds(cc * (blk // 2), blk // 2), :], r.ogu_h.at[b], r.fgu.at[b], 0)

    @pl.when(c == 1)
    def _():
        r.sdn[...] = (r.pdn[pl.ds(2 * z, 2)].astype(F32) + others(r.rdn, r.zdn)).astype(BF16)

    spread(lambda cc: r.sdn.at[cc], r.odn_h.at[b], r.fdn.at[b], 1)

    @pl.when(c == 1)
    def _():
        r.sat[...] = (r.pat[rows, :].astype(F32) + others(r.rat, r.zat)).astype(BF16)

    spread(lambda cc: r.sat.at[pl.ds(cc * (blk // 2), blk // 2), :], r.oat_h.at[b], r.fat.at[b], 1)

    for bb in range(nb):
        arrived(r.ogu_h.at[bb], r.fgu.at[bb])
        arrived(r.odn_h.at[bb], r.fdn.at[bb])
        arrived(r.oat_h.at[bb], r.fat.at[bb])
    arrived(r.ogl_h, r.fgl.at[0])
    out_copy.wait()
    gin_copy.wait()
    assert used[0] == r.ssem.shape[0]
    for cond, src, dst, ssem, rsem, dev in pending:
        @pl.when(cond)
        def _(args=(src, dst, ssem, rsem, dev)):
            remote(*args).wait_send()

    def sent_on(t, _):
        @pl.when((lax.rem(t, 2) == c) & (t < s))
        def _():
            remote(r.x_all.at[t], r.x_all.at[t], r.fsem.at[0, t], r.rx.at[t], sib).wait_send()

        @pl.when((lax.rem(t, 2) == c) & (t > s))
        def _():
            remote(r.q_all.at[t], r.q_all.at[t], r.fsem.at[1, t], r.rq.at[t], sib).wait_send()
            remote(r.do_all.at[t], r.do_all.at[t], r.fsem.at[2, t], r.rdo.at[t], sib).wait_send()
            remote(r.st_all.at[t], r.st_all.at[t], r.fsem.at[3, t], r.rst.at[t], sib).wait_send()
        return 0

    lax.fori_loop(0, n, sent_on, 0)


def unpack_kernel(
    n, nb, out_in, gin_in, oat_h, ogu_h, odn_h, ogl_h,
    out, gin, gq_h, gk_h, gv_h, go_h, gg_h, gu_h, gd_h, g1, g2,
    oat, ogu, odn, ogl, gq, gk, gv, go, gg, gu, gd, out_v, gin_v, isem, osem,
):
    s = lax.axis_index("seq")
    fs = ogu.shape[2] // 2
    tok, dh = odn.shape[1], odn.shape[2]
    copy = pltpu.make_async_copy
    loads = [copy(a, b, isem.at[i]) for i, (a, b) in enumerate(
        ((ogu_h, ogu), (oat_h, oat), (odn_h, odn), (ogl_h, ogl), (out_in, out_v), (gin_in, gin_v)))]
    stores = [copy(a, b, osem.at[i]) for i, (a, b) in enumerate(
        ((gg, gg_h), (gu, gu_h), (gq, gq_h), (gk, gk_h), (gv, gv_h), (go, go_h), (gd, gd_h),
         (out_v, out.at[0]), (gin_v, gin.at[0])))]
    for load in loads:
        load.start()
    loads[0].wait()
    for bb in range(nb):
        gg[:, bb * fs:(bb + 1) * fs] = ogu[bb, :, :fs].astype(F32)
    stores[0].start()
    for bb in range(nb):
        gu[:, bb * fs:(bb + 1) * fs] = ogu[bb, :, fs:].astype(F32)
    stores[1].start()
    loads[1].wait()
    for m, ref in enumerate((gq, gk, gv, go)):
        ref[...] = oat[m].astype(F32)
        stores[2 + m].start()
    loads[2].wait()
    for bb in range(nb):
        gd[(bb // 2) * tok:(bb // 2 + 1) * tok, (bb % 2) * dh:(bb % 2 + 1) * dh] = odn[bb].astype(F32)
    stores[6].start()
    for i in (4, 5):
        loads[i].wait()
        stores[3 + i].start()
    loads[3].wait()
    d = ogl.shape[1]
    own = d // n
    gains = pltpu.roll(ogl[...], lax.rem(d - s * own, d), 1)
    g1[...] = gains[0:1, :own]
    g2[...] = gains[1:2, :own]
    for store in stores:
        store.wait()


def rope_constants(length, head_dim):
    half = head_dim // 2
    inverse = np.exp(-2.0 * math.log(THETA) / head_dim * np.arange(half)).astype(np.float32)
    angle = np.arange(length, dtype=np.float32)[:, None] * inverse
    cos, sin = np.cos(angle.astype(np.float64)), np.sin(angle.astype(np.float64))
    return (
        np.concatenate([cos, cos, cos, cos], 1).astype(np.float32),
        np.concatenate([-sin, sin, -sin, sin], 1).astype(np.float32),
    )


def fused_local(n, nb, tokens, doc_ids, w_query, w_key, w_value, w_out, w_gate, w_up, w_down, gain_attn, gain_ffn, cotangent):
    _, tok, d = tokens.shape
    f = w_gate.shape[1]
    nz = n // 2
    cos, sin = rope_constants(n * tok, d // HEADS)
    cos = jnp.asarray(cos.reshape(nz, 2 * tok, 128))
    sin = jnp.asarray(sin.reshape(nz, 2 * tok, 128))
    plan = scratch_plan(tok, d, f, n, nb)
    vmem, anywhere = pl.BlockSpec(memory_space=pltpu.VMEM), pl.BlockSpec(memory_space=pl.ANY)
    shape = jax.ShapeDtypeStruct
    parts = pl.pallas_call(
        functools.partial(layer_kernel, tuple(plan), tok, d, f, n, nb),
        out_shape=(
            shape((tok, d), F32), shape((tok, d), F32), shape((nb, d // n, d), BF16),
            shape((nb, d // n, 2 * f // nb), BF16), shape((nb, tok, d // 2), BF16), shape((8, d), F32),
        ),
        in_specs=[vmem] * 5 + [anywhere] * 9,
        out_specs=[anywhere] * 6,
        scratch_shapes=list(plan.values()),
        compiler_params=pltpu.CompilerParams(
            collective_id=0, has_side_effects=True, vmem_limit_bytes=62 * 2**20
        ),
        name="layer",
    )(
        doc_ids, tokens, cotangent, gain_attn, gain_ffn, cos, sin,
        w_query, w_key, w_value, w_out, w_gate, w_up, w_down,
    )
    own = d // n
    grads = [shape((own, d), F32)] * 4 + [shape((own, f), F32)] * 2 + [shape((f // n, d), F32)]
    results = pl.pallas_call(
        functools.partial(unpack_kernel, n, nb),
        out_shape=(shape((1, tok, d), F32), shape((1, tok, d), F32), *grads, shape((1, own), F32), shape((1, own), F32)),
        in_specs=[pl.BlockSpec(memory_space=pltpu.HBM)] * 6,
        out_specs=[anywhere] * 9 + [vmem] * 2,
        scratch_shapes=[pltpu.VMEM(parts[i].shape, parts[i].dtype) for i in (2, 3, 4, 5)]
        + [pltpu.VMEM(g.shape, g.dtype) for g in grads]
        + [pltpu.VMEM((tok, d), F32)] * 2
        + [pltpu.SemaphoreType.DMA((6,)), pltpu.SemaphoreType.DMA((9,))],
        compiler_params=pltpu.CompilerParams(vmem_limit_bytes=62 * 2**20),
        name="unpack",
    )(*parts)
    return results[:9] + (results[9].reshape(own), results[10].reshape(own))


def fits(shapes, n, nb):
    (_, tok, d), f = shapes[0], shapes[6][1]
    return (
        nb == 4 and n % 2 == 0 and n * tok <= 1024 and tok == 128 and shapes[0][0] == 1
        and d == HEADS * 64 and d % 256 == 0 and d % (16 * n) == 0 and f == 2 * tok * n and f % 1024 == 0
    )


def solution(mesh):
    nb, n = mesh.shape["batch"], mesh.shape["seq"]

    def either(*args):
        shapes = [a.shape for a in args]
        if fits(shapes, n, nb):
            return fused_local(n, nb, *args)
        return local(*args)

    return jax.shard_map(
        either,
        mesh=mesh,
        in_specs=(
            P("batch", "seq", None),
            P("batch", "seq"),
            P(),
            P(),
            P(),
            P(),
            P(),
            P(),
            P(),
            P(),
            P(),
            P("batch", "seq", None),
        ),
        out_specs=(
            P("batch", "seq", None),
            P("batch", "seq", None),
            P("seq", None),
            P("seq", None),
            P("seq", None),
            P("seq", None),
            P("seq", None),
            P("seq", None),
            P("seq", None),
            P("seq"),
            P("seq"),
        ),
        check_vma=False,
    )
```

```python
import functools
import math
import types

import jax
import jax.numpy as jnp
import numpy as np
from jax import lax
from jax.experimental import pallas as pl
from jax.experimental.pallas import tpu as pltpu
from jax.sharding import PartitionSpec as P

HEADS = 12
NSEG = 8


EPSILON = 1e-06
THETA = 10000.0
MASKED = -1e30


def root_mean_square_norm(values, gain):
    return values * lax.rsqrt(jnp.mean(values * values, -1, keepdims=True) + EPSILON) * gain


def swiglu(gate, up_part):
    return jax.nn.silu(gate) * up_part


def rope_tables(positions, head_dim):
    half_dim = head_dim // 2
    inverse = jnp.exp(-2.0 * math.log(THETA) / head_dim * jnp.arange(half_dim, dtype=jnp.float32))
    angle = positions.astype(jnp.float32)[..., None] * inverse
    return (
        jnp.concatenate([jnp.cos(angle), jnp.cos(angle)], -1),
        jnp.concatenate([jnp.sin(angle), jnp.sin(angle)], -1),
    )


def rotate(values, cosine, sine):
    half_dim = values.shape[-1] // 2
    turned = jnp.concatenate([-values[..., half_dim:], values[..., :half_dim]], -1)
    return values * cosine + turned * sine


def rotate_back(grads, cosine, sine):
    half_dim = grads.shape[-1] // 2
    turned = grads * sine
    return grads * cosine + jnp.concatenate([turned[..., half_dim:], -turned[..., :half_dim]], -1)


def block_size(total_rows):
    return max((d for d in range(1, min(total_rows, 2048) + 1) if total_rows % d == 0))


def doc_begin(segment_begins, where_at):
    earlier = segment_begins[:, None, :] <= where_at[:, :, None]
    return jnp.max(jnp.where(earlier, segment_begins[:, None, :], 0), -1)


def outer_sum(remaining_tokens, right):
    return lax.dot_general(
        remaining_tokens, right, (((0,), (0,)), ((), ())), preferred_element_type=jnp.float32
    )


def back_product(grads, weight_matrix):
    return lax.dot_general(
        grads, weight_matrix, (((1,), (1,)), ((), ())), preferred_element_type=jnp.float32
    )


def masked_scores(queries, key_block, key_at, query_at, query_begin):
    batch_rows, block_rows, model_width = key_block.shape
    head_count = queries.shape[2]
    head_dim = model_width // head_count
    key_heads = key_block.reshape(batch_rows, block_rows, head_count, head_dim)
    scores = jnp.einsum(
        "bqhd,bkhd->bhqk", queries, key_heads, preferred_element_type=jnp.float32
    ) * (1.0 / math.sqrt(head_dim))
    key_pos = key_at[None, None, :]
    query_pos = query_at[:, :, None]
    begin_pos = query_begin[:, :, None]
    allowed = (
        (key_pos <= query_pos) & (key_pos >= begin_pos) & ((begin_pos > 0) | (key_pos == query_pos))
    )
    return (scores, allowed[:, None], key_heads)


def grad_terms(
    queries, grad_heads, lse, delta, query_at, query_begin, key_block, value_block, key_at
):
    scores, allowed, key_heads = masked_scores(queries, key_block, key_at, query_at, query_begin)
    value_heads = value_block.reshape(key_heads.shape)
    probs = jnp.where(allowed, jnp.exp(scores - lse[..., None]), 0.0)
    dprob = jnp.einsum(
        "bqhd,bkhd->bhqk", grad_heads, value_heads, preferred_element_type=jnp.float32
    )
    dscore = (probs * (dprob - delta[..., None])).astype(jnp.bfloat16)
    return (probs.astype(jnp.bfloat16), dscore, key_heads, value_heads)


def over_rows(update, carried, arrays, first_row):
    total_rows = arrays[0].shape[1]
    block_rows = block_size(total_rows)

    def over_step(block_index, state):
        offset = block_index * block_rows
        blocks = tuple((lax.dynamic_slice_in_dim(item, offset, block_rows, 1) for item in arrays))
        key_at = first_row + offset + jnp.arange(block_rows, dtype=jnp.int32)
        return update(state, blocks, key_at)

    return lax.fori_loop(0, total_rows // block_rows, over_step, carried)


def local(
    tokens,
    doc_ids,
    w_query,
    w_key,
    w_value,
    w_out,
    w_gate,
    w_up,
    w_down,
    gain_attn,
    gain_ffn,
    cotangent,
):
    batch_rows, local_len, model_width = tokens.shape
    head_count = HEADS
    head_dim = model_width // head_count
    shape_heads = (batch_rows, local_len, head_count, head_dim)
    scale = 1.0 / math.sqrt(head_dim)
    labels = jnp.arange(NSEG, dtype=jnp.int32)
    member = (doc_ids[:, :, None] == labels).astype(jnp.int32)
    totals = lax.psum(jnp.sum(member, 1), "seq")
    segment_begins = jnp.cumsum(totals, 1) - totals
    local_at = lax.axis_index("seq") * local_len + jnp.arange(local_len, dtype=jnp.int32)
    query_at = jnp.broadcast_to(local_at, (batch_rows, local_len))
    query_begin = doc_begin(segment_begins, query_at)
    cosine, sine = rope_tables(query_at - query_begin, head_dim)
    cosine = cosine[:, :, None, :]
    sine = sine[:, :, None, :]
    flat_tokens = tokens.reshape(batch_rows * local_len, model_width)
    queries = rotate(
        jnp.dot(flat_tokens, w_query, preferred_element_type=jnp.float32).reshape(shape_heads),
        cosine,
        sine,
    ).astype(jnp.bfloat16)
    key_send = (
        rotate(
            jnp.dot(flat_tokens, w_key, preferred_element_type=jnp.float32).reshape(shape_heads),
            cosine,
            sine,
        )
        .astype(jnp.bfloat16)
        .reshape(batch_rows, local_len, model_width)
    )
    value_send = (
        jnp.dot(flat_tokens, w_value, preferred_element_type=jnp.float32)
        .astype(jnp.bfloat16)
        .reshape(batch_rows, local_len, model_width)
    )

    def stats_step(state, blocks, key_at):
        run_max, run_sum = state
        scores, allowed, key_heads = masked_scores(
            queries, blocks[0], key_at, query_at, query_begin
        )
        scores = jnp.where(allowed, scores, MASKED)
        new_max = jnp.maximum(run_max, jnp.max(scores, -1))
        weights = jnp.where(allowed, jnp.exp(scores - new_max[..., None]), 0.0)
        return (new_max, run_sum * jnp.exp(run_max - new_max) + jnp.sum(weights, -1))

    stats_init = (
        jnp.full((batch_rows, head_count, local_len), MASKED, jnp.float32),
        jnp.zeros((batch_rows, head_count, local_len), jnp.float32),
    )
    zero_heads = jnp.zeros(shape_heads, jnp.float32)
    run_max, run_sum = over_rows(
        stats_step, stats_init, (lax.all_gather(key_send, "seq", axis=1, tiled=True),), jnp.int32(0)
    )
    lse = run_max + jnp.log(run_sum)

    def output_step(state, blocks, key_at):
        scores, allowed, key_heads = masked_scores(
            queries, blocks[0], key_at, query_at, query_begin
        )
        value_heads = blocks[1].reshape(key_heads.shape)
        probs = jnp.where(allowed, jnp.exp(scores - lse[..., None]), 0.0).astype(jnp.bfloat16)
        return state + jnp.einsum(
            "bhqk,bkhd->bqhd", probs, value_heads, preferred_element_type=jnp.float32
        )

    attended = over_rows(
        output_step,
        zero_heads,
        (
            lax.all_gather(key_send, "seq", axis=1, tiled=True),
            lax.all_gather(value_send, "seq", axis=1, tiled=True),
        ),
        jnp.int32(0),
    )
    attended_low = attended.astype(jnp.bfloat16).reshape(batch_rows * local_len, model_width)
    first_sum = flat_tokens.astype(jnp.float32) + jnp.dot(
        attended_low, w_out, preferred_element_type=jnp.float32
    )
    hidden, norm_first_back = jax.vjp(root_mean_square_norm, first_sum, gain_attn)
    hidden_low = hidden.astype(jnp.bfloat16)
    gate = jnp.dot(hidden_low, w_gate, preferred_element_type=jnp.float32)
    up_part = jnp.dot(hidden_low, w_up, preferred_element_type=jnp.float32)
    active, swiglu_back = jax.vjp(swiglu, gate, up_part)
    active_low = active.astype(jnp.bfloat16)
    second_sum = hidden + jnp.dot(active_low, w_down, preferred_element_type=jnp.float32)
    output, norm_second_back = jax.vjp(root_mean_square_norm, second_sum, gain_ffn)
    second_grad, grad_gain_ffn = norm_second_back(
        cotangent.reshape(batch_rows * local_len, model_width).astype(jnp.float32)
    )
    branch_grad = second_grad.astype(jnp.bfloat16)
    grad_down = outer_sum(active_low, branch_grad)
    gate_grad, up_grad = swiglu_back(back_product(branch_grad, w_down))
    gate_low = gate_grad.astype(jnp.bfloat16)
    up_low = up_grad.astype(jnp.bfloat16)
    grad_gate = outer_sum(hidden_low, gate_low)
    grad_up = outer_sum(hidden_low, up_low)
    hidden_grad = second_grad + back_product(gate_low, w_gate) + back_product(up_low, w_up)
    first_grad, grad_gain_attn = norm_first_back(hidden_grad)
    attn_grad = first_grad.astype(jnp.bfloat16)
    grad_out = outer_sum(attended_low, attn_grad)
    grad_heads = back_product(attn_grad, w_out).astype(jnp.bfloat16).reshape(shape_heads)
    delta = jnp.swapaxes(jnp.sum(grad_heads.astype(jnp.float32) * attended, -1), 1, 2)

    def query_step(state, blocks, key_at):
        probs_low, dscore, key_heads, value_heads = grad_terms(
            queries, grad_heads, lse, delta, query_at, query_begin, blocks[0], blocks[1], key_at
        )
        return (
            state
            + jnp.einsum("bhqk,bkhd->bqhd", dscore, key_heads, preferred_element_type=jnp.float32)
            * scale
        )

    all_keys, all_values = (
        lax.all_gather(key_send, "seq", axis=1, tiled=True),
        lax.all_gather(value_send, "seq", axis=1, tiled=True),
    )
    query_grad = over_rows(query_step, zero_heads, (all_keys, all_values), 0)
    first_row = jnp.int32(0)
    span_rows = local_len * lax.axis_size("seq")
    block_rows = block_size(span_rows)
    empty = jnp.zeros((batch_rows, span_rows, head_count, head_dim), jnp.float32)

    def key_step(block_index, state):
        offset = block_index * block_rows
        key_block = lax.dynamic_slice_in_dim(all_keys, offset, block_rows, 1)
        value_block = lax.dynamic_slice_in_dim(all_values, offset, block_rows, 1)
        key_at = first_row + offset + jnp.arange(block_rows, dtype=jnp.int32)
        probs_low, dscore, key_heads, value_heads = grad_terms(
            queries, grad_heads, lse, delta, query_at, query_begin, key_block, value_block, key_at
        )
        key_part = (
            jnp.einsum("bhqk,bqhd->bkhd", dscore, queries, preferred_element_type=jnp.float32)
            * scale
        )
        value_part = jnp.einsum(
            "bhqk,bqhd->bkhd", probs_low, grad_heads, preferred_element_type=jnp.float32
        )
        return (
            lax.dynamic_update_slice_in_dim(state[0], key_part, offset, 1),
            lax.dynamic_update_slice_in_dim(state[1], value_part, offset, 1),
        )

    key_all, value_all = lax.fori_loop(0, span_rows // block_rows, key_step, (empty, empty))
    joined = jnp.concatenate(
        [
            key_all.reshape(batch_rows, span_rows, model_width),
            value_all.reshape(batch_rows, span_rows, model_width),
        ],
        -1,
    )
    summed_keys = jnp.swapaxes(
        lax.psum_scatter(jnp.swapaxes(joined, 0, 1), "seq", scatter_dimension=0, tiled=True), 0, 1
    )
    key_grad = summed_keys[..., :model_width].reshape(shape_heads)
    value_grad = summed_keys[..., model_width:]
    flat_len = batch_rows * local_len
    query_low = (
        rotate_back(query_grad, cosine, sine).astype(jnp.bfloat16).reshape(flat_len, model_width)
    )
    key_low = (
        rotate_back(key_grad, cosine, sine).astype(jnp.bfloat16).reshape(flat_len, model_width)
    )
    value_low = value_grad.astype(jnp.bfloat16).reshape(flat_len, model_width)
    grad_input = (
        first_grad
        + back_product(query_low, w_query)
        + back_product(key_low, w_key)
        + back_product(value_low, w_value)
    )
    grad_query = outer_sum(flat_tokens, query_low)
    grad_key = outer_sum(flat_tokens, key_low)
    value_weight_gradient = outer_sum(flat_tokens, value_low)
    shares = (
        lax.psum_scatter(grad_query, "seq", scatter_dimension=0, tiled=True),
        lax.psum_scatter(grad_key, "seq", scatter_dimension=0, tiled=True),
        lax.psum_scatter(value_weight_gradient, "seq", scatter_dimension=0, tiled=True),
        lax.psum_scatter(grad_out, "seq", scatter_dimension=0, tiled=True),
        lax.psum_scatter(grad_gate, "seq", scatter_dimension=0, tiled=True),
        lax.psum_scatter(grad_up, "seq", scatter_dimension=0, tiled=True),
        lax.psum_scatter(grad_down, "seq", scatter_dimension=0, tiled=True),
        lax.psum_scatter(grad_gain_attn, "seq", scatter_dimension=0, tiled=True),
        lax.psum_scatter(grad_gain_ffn, "seq", scatter_dimension=0, tiled=True),
    )
    results = (
        lax.psum(shares[0].astype(jnp.bfloat16), "batch").astype(jnp.float32),
        lax.psum(shares[1].astype(jnp.bfloat16), "batch").astype(jnp.float32),
        lax.psum(shares[2].astype(jnp.bfloat16), "batch").astype(jnp.float32),
        lax.psum(shares[3].astype(jnp.bfloat16), "batch").astype(jnp.float32),
        lax.psum(shares[4].astype(jnp.bfloat16), "batch").astype(jnp.float32),
        lax.psum(shares[5].astype(jnp.bfloat16), "batch").astype(jnp.float32),
        lax.psum(shares[6].astype(jnp.bfloat16), "batch").astype(jnp.float32),
        lax.psum(shares[7].astype(jnp.bfloat16), "batch").astype(jnp.float32),
        lax.psum(shares[8].astype(jnp.bfloat16), "batch").astype(jnp.float32),
    )
    output_rows = output.reshape(batch_rows, local_len, model_width)
    input_rows = grad_input.reshape(batch_rows, local_len, model_width)
    return (
        output_rows,
        input_rows,
        results[0],
        results[1],
        results[2],
        results[3],
        results[4],
        results[5],
        results[6],
        results[7],
        results[8],
    )


MESH = pl.DeviceIdType.MESH
F32 = jnp.float32
BF16 = jnp.bfloat16


def mm(a, b):
    return lax.dot_general(a, b, (((1,), (0,)), ((), ())), preferred_element_type=F32)


def mm_nt(a, b):
    return lax.dot_general(a, b, (((1,), (1,)), ((), ())), preferred_element_type=F32)


def scratch_plan(tok, d, f, n, nb):
    nz, plane, pair, heads = n // 2, 2 * nb * tok, 4 * tok, HEADS
    vm = pltpu.VMEM
    dma = lambda *shape: pltpu.SemaphoreType.DMA(shape)
    return dict(
        wq=vm((d, d), BF16), wk=vm((d, d), BF16), wv=vm((d, d), BF16), wo=vm((d, d), BF16),
        wg=vm((d, f), BF16), wu=vm((d, f), BF16), wd=vm((f, d), BF16),
        cos=vm((nz, 2 * tok, 128), F32), sin=vm((nz, 2 * tok, 128), F32),
        x_all=vm((n, tok, d), BF16), q_all=vm((n, tok, d), BF16), do_all=vm((n, tok, d), BF16),
        k_all=vm((nz, 2 * tok, d), BF16), v_all=vm((nz, 2 * tok, d), BF16),
        st_all=vm((n, 32, tok), F32), id_all=vm((n, 8, tok), jnp.int32),
        idcol=vm((tok, 128), F32), bias=vm((2 * tok, 2 * tok), F32),
        m=vm((heads // 2, 2 * tok, 128), F32), l=vm((heads // 2, 2 * tok, 128), F32),
        delta=vm((heads // 2, 2 * tok, 128), F32),
        acc=vm((tok, d), F32), acc2=vm((tok, d), F32),
        olow=vm((tok, d), BF16), hb=vm((tok, d), BF16), h1=vm((tok, d), F32), n1=vm((tok, d), F32),
        ri1=vm((tok, 128), F32), dr=vm((tok, d), F32),
        g32=vm((tok, f), F32), u32=vm((tok, f), F32), act=vm((tok, f), BF16),
        dg=vm((tok, f), BF16), du=vm((tok, f), BF16), dmo=vm((tok, d), BF16), dattn=vm((tok, d), BF16),
        dq=vm((tok, d), BF16), dk=vm((tok, d), BF16), dv=vm((tok, d), BF16),
        actT=vm((n, 2, tok, tok), BF16), hT=vm((d, tok), BF16), xT=vm((d, tok), BF16), oT=vm((d, tok), BF16),
        gl=vm((8, d), F32), out_v=vm((tok, d), F32), gin_v=vm((tok, d), F32),
        hT_b=vm((d, pair), BF16), dgu_b=vm((2, 2, pair, f // nb), BF16),
        act_b=vm((n, tok, pair), BF16), dmo_b=vm((pair, d), BF16),
        xT_b=vm((d, plane), BF16), oT_b=vm((d, plane), BF16), at_b=vm((2, plane, d // 2), BF16), gl_b=vm((2 * nb, 8, d), F32),
        pyu=vm((2, d, f // nb), BF16), ryu=vm((2, d, f // nb), BF16), pgu=vm((2, d, f // nb), BF16),
        pxd=vm((n, tok, d // 2), BF16), rxd=vm((n, tok, d // 2), BF16), pdn=vm((n, tok, d // 2), BF16),
        pat=vm((2, d, d // 2), BF16),
        ugu=vm((2, d // nz, f // nb), BF16), udn=vm((2, tok, d // 2), BF16), uat=vm((2, d // nz, d // 2), BF16),
        rgu=vm((2, nz, d // nz, f // nb), BF16), rdn=vm((nz, 2, tok, d // 2), BF16), rat=vm((2, nz, d // nz, d // 2), BF16),
        sgu=vm((2, d // nz, f // nb), BF16), sdn=vm((2, tok, d // 2), BF16), sat=vm((2, d // nz, d // 2), BF16),
        gz=vm((nz, 8, d), F32), gsum=vm((8, d), F32),
        wsem=dma(9), osem=dma(2), usem=dma(1), ssem=dma(134), fsem=dma(5, n), bsem=dma(6, n),
        rx=dma(2, n), rq=dma(n), rdo=dma(2, n), rst=dma(n), rid=dma(n),
        rh=dma(4), rdg=dma(2, 4), rdu=dma(2, 4), ry=dma(2), ract=dma(4), rdmo=dma(4), rxp=dma(1), zfar=dma(5),
        rxt=dma(2 * nb), rot=dma(2 * nb), rat_in=dma(2, 2 * nb), rgl=dma(2 * nb),
        zgu=dma(2, nz), zdn=dma(nz), zat=dma(2, nz), zgl=dma(nz),
        fgu=dma(2, nb), fdn=dma(nb), fat=dma(2, nb), fgl=dma(1),
    )


INPUTS = ("ids", "tok", "cot", "ga", "gf", "cos_h", "sin_h", "wq_h", "wk_h", "wv_h", "wo_h", "wg_h", "wu_h", "wd_h")
OUTPUTS = ("out_h", "gin_h", "oat_h", "ogu_h", "odn_h", "ogl_h")


def layer_kernel(plan_names, tok, d, f, n, nb, *refs):
    r = types.SimpleNamespace(**dict(zip(INPUTS + OUTPUTS + plan_names, refs)))
    nz, pairs = n // 2, d // 128
    fs, dh, blk = f // nb, d // 2, d // nz
    b, s = lax.axis_index("batch"), lax.axis_index("seq")
    z, c = s // 2, lax.rem(s, 2)
    by, bx = b // 2, lax.rem(b, 2)
    e = 2 * b + c
    sib = (b, s + 1 - 2 * c)
    gain_a, gain_f = r.ga[...].reshape(1, d), r.gf[...].reshape(1, d)
    pending, used = [], [0]

    def remote(src, dst, ssem, rsem, dev):
        return pltpu.make_async_remote_copy(
            src_ref=src, dst_ref=dst, send_sem=ssem, recv_sem=rsem, device_id=dev, device_id_type=MESH
        )

    def send_lazy(make):
        at = used[0]
        used[0] += 1
        pending.append((make, at))
        cond, src, dst, rsem, dev = make()

        @pl.when(cond)
        def _():
            remote(src, dst, r.ssem.at[at], rsem, dev).start()

    def send(cond, src, dst, rsem, dev):
        send_lazy(lambda: (cond, src, dst, rsem, dev))

    def plane_send_lazy(make, to_b, to_c):
        def here():
            return (b == to_b) & (c == to_c)

        send_lazy(lambda: (jnp.logical_not(here()), *make(), (to_b, 2 * z + to_c)))

        @pl.when(here())
        def _():
            pltpu.make_async_copy(*make()).start()

    def plane_send(src, dst, rsem, to_b, to_c):
        plane_send_lazy(lambda: (src, dst, rsem), to_b, to_c)

    def arrived(dst, rsem):
        remote(dst, dst, r.ssem.at[0], rsem, sib).wait_recv()

    loads = {}
    for i, name in enumerate(("wk", "wv", "wq", "cos", "sin", "wo", "wg", "wu", "wd")):
        loads[name] = pltpu.make_async_copy(getattr(r, name + "_h"), getattr(r, name), r.wsem.at[i])
        loads[name].start()

    r.x_all[s] = r.tok[0]
    r.id_all[s] = jnp.broadcast_to(r.ids[...], (8, tok))

    bar = pltpu.get_barrier_semaphore()
    for zz in range(nz):
        for cc in range(2):
            @pl.when(2 * zz + cc != s)
            def _(zz=zz, cc=cc):
                pl.semaphore_signal(bar, inc=1, device_id=(b, 2 * zz + cc), device_id_type=MESH)
    for bb in range(nb):
        for cc in range(2):
            @pl.when(bb != b)
            def _(bb=bb, cc=cc):
                pl.semaphore_signal(bar, inc=1, device_id=(bb, 2 * z + cc), device_id_type=MESH)
    pl.semaphore_wait(bar, n - 1 + 2 * (nb - 1))

    always = s >= 0
    half = tok // 2

    def rows_of(ref, t, ch):
        return ref.at[t, pl.ds(ch * half, half)]

    right, left = (b, s + 2), (b, s - 2)
    for zz in range(nz):
        for cc in range(2):
            send(2 * zz + cc != s, r.id_all.at[s], r.id_all.at[s], r.rid.at[s], (b, 2 * zz + cc))
    for ch in range(2):
        mine = rows_of(r.x_all, s, ch)
        send(z + 1 < nz, mine, mine, r.rx.at[ch, s], right)
        send(always, mine, mine, r.rx.at[ch, s], sib)

    lane = lax.broadcasted_iota(jnp.int32, (tok, 128), 1)
    first = lane < 64
    half_mask = (jnp.where(first, 1.0, 0.0).astype(BF16), jnp.where(first, 0.0, 1.0).astype(BF16))

    def turn(u):
        low = lax.rem(lax.broadcasted_iota(jnp.int32, u.shape, 1), 64) < 32
        return jnp.where(low, pltpu.roll(u, 96, 1), pltpu.roll(u, 32, 1))

    def twice(u):
        return jnp.concatenate([u, u], axis=1)

    def stack(u):
        return jnp.concatenate([u * half_mask[0], u * half_mask[1]], axis=0)

    def unstack(u):
        return jnp.where(first, u[:tok], u[tok:])

    own = pl.ds(pl.multiple_of(c * tok, tok), tok)

    loads["wq"].wait()
    loads["cos"].wait()
    loads["sin"].wait()

    u = mm(r.tok[0], r.wq[...])
    co, si = r.cos[z, own, :], r.sin[z, own, :]
    for p in range(pairs):
        part = u[:, p * 128:(p + 1) * 128]
        r.q_all[s, :, p * 128:(p + 1) * 128] = ((part * co + turn(part) * si) * 0.125).astype(BF16)
    send(always, r.q_all.at[s], r.q_all.at[s], r.rq.at[s], sib)
    for dz in range(1, nz):
        send(z - dz >= 0, r.q_all.at[s], r.q_all.at[s], r.rq.at[s], (b, s - 2 * dz))

    def transpose_into(dst, value):
        for p in range(d // 128):
            dst[p * 128:(p + 1) * 128, :] = value[:, p * 128:(p + 1) * 128].T.astype(BF16)

    tokens = pl.ds(pl.multiple_of(e * tok, tok), tok)
    ex, ey = 2 * bx + c, 2 * by + c
    x_tokens, y_tokens = (pl.ds(pl.multiple_of(i * tok, tok), tok) for i in (ex, ey))
    transpose_into(r.xT, r.tok[0].astype(F32))
    for bb in range(nb):
        plane_send(r.xT, r.xT_b.at[:, tokens], r.rxt.at[e], bb, 1)
    r.idcol[...] = jnp.broadcast_to(r.ids[...].astype(F32), (128, tok)).T

    def ids_of(block):
        return jnp.concatenate(
            [r.id_all[2 * block, 0:1, :], r.id_all[2 * block + 1, 0:1, :]], axis=1
        ).astype(F32)

    def set_bias(block, local_is_query):
        shape = (tok, 2 * tok)
        mine = s * tok + lax.broadcasted_iota(jnp.int32, shape, 0)
        theirs = block * (2 * tok) + lax.broadcasted_iota(jnp.int32, shape, 1)
        my_id = twice(r.idcol[...])
        their_id = jnp.broadcast_to(ids_of(block), shape)
        causal = (theirs <= mine) if local_is_query else (mine <= theirs)
        allowed = (my_id == their_id) & causal & ((my_id != 0.0) | (mine == theirs))
        bias = jnp.where(allowed, 0.0, MASKED)
        r.bias[...] = jnp.concatenate([bias, bias], axis=0)

    r.m[...] = jnp.full(r.m.shape, MASKED, F32)
    r.l[...] = jnp.zeros(r.l.shape, F32)
    r.acc[...] = jnp.zeros(r.acc.shape, F32)
    loads["wk"].wait()
    loads["wv"].wait()

    def forward_step(j, _):
        kb = z - j
        mine, other = 2 * kb + c, 2 * kb + 1 - c

        @pl.when(j > 0)
        def _():
            for ch in range(2):
                got = rows_of(r.x_all, mine, ch)
                arrived(got, r.rx.at[ch, mine])

                @pl.when(z + 1 < nz)
                def _():
                    remote(got, got, r.fsem.at[ch, mine], r.rx.at[ch, mine], right).start()

                remote(got, got, r.bsem.at[ch, mine], r.rx.at[ch, mine], sib).start()

            arrived(r.id_all.at[mine], r.rid.at[mine])

        for ch in range(2):
            arrived(rows_of(r.x_all, other, ch), r.rx.at[ch, other])
        arrived(r.id_all.at[other], r.rid.at[other])
        set_bias(kb, True)

        xb = r.x_all[pl.ds(2 * kb, 2)].reshape(2 * tok, d)
        u = mm(xb, r.wk[...])
        co, si = r.cos[kb], r.sin[kb]
        for p in range(pairs):
            part = u[:, p * 128:(p + 1) * 128]
            r.k_all[kb, :, p * 128:(p + 1) * 128] = (part * co + turn(part) * si).astype(BF16)
        r.v_all[kb] = mm(xb, r.wv[...]).astype(BF16)

        def pair(p, _):
            lanes = pl.ds(pl.multiple_of(p * 128, 128), 128)
            qp, kp, vp = r.q_all[s, :, lanes], r.k_all[kb, :, lanes], r.v_all[kb, :, lanes]
            sc = mm_nt(stack(qp), kp) + r.bias[...]
            m_old = r.m[p]
            m_new = jnp.maximum(m_old, jnp.max(sc, axis=1, keepdims=True))
            alpha = jnp.exp(m_old - m_new)
            ex = jnp.exp(sc - twice(m_new))
            r.m[p] = m_new
            r.l[p] = r.l[p] * alpha + jnp.sum(ex, axis=1, keepdims=True)
            r.acc[:, lanes] = r.acc[:, lanes] * unstack(alpha) + unstack(mm(ex.astype(BF16), vp))
            return 0

        lax.fori_loop(0, pairs, pair, 0, unroll=True)
        return 0

    lax.fori_loop(0, z + 1, forward_step, 0)

    def finish(p, _):
        lanes = pl.ds(pl.multiple_of(p * 128, 128), 128)
        r.acc[:, lanes] = r.acc[:, lanes] / unstack(r.l[p])
        r.m[p] = r.m[p] + jnp.log(r.l[p])
        return 0

    lax.fori_loop(0, pairs, finish, 0, unroll=True)
    r.olow[...] = r.acc[...].astype(BF16)

    loads["wo"].wait()
    r1 = r.tok[0].astype(F32) + mm(r.olow[...], r.wo[...])
    ri1 = lax.rsqrt(jnp.mean(r1 * r1, axis=1, keepdims=True) + EPSILON)
    r.ri1[...] = jnp.broadcast_to(ri1, (tok, 128))
    n1 = r1 * ri1
    r.n1[...] = n1
    h1 = n1 * gain_a
    r.h1[...] = h1
    r.hb[...] = h1.astype(BF16)
    transpose_into(r.hT, h1)
    for i in range(2):
        plane_send(r.hT, r.hT_b.at[:, x_tokens], r.rh.at[ex], 2 * by + i, 0)
    transpose_into(r.oT, r.acc[...])
    loads["wg"].wait()
    loads["wu"].wait()

    for i in range(f // 512):
        at = slice(i * 512, (i + 1) * 512)
        g = mm(r.hb[...], r.wg[:, at])
        u = mm(r.hb[...], r.wu[:, at])
        r.g32[:, at] = g
        r.u32[:, at] = u
        a = g / (1.0 + jnp.exp(-g)) * u
        r.act[:, at] = a.astype(BF16)
        for k in range(4):
            r.actT[2 * i + k // 2, k % 2] = a[:, k * 128:(k + 1) * 128].T.astype(BF16)
    for i in range(2):
        plane_send(r.actT.at[:, i], r.act_b.at[:, :, y_tokens], r.ract.at[ey], 2 * i + bx, 1)
    loads["wd"].wait()
    r2 = r.h1[...] + mm(r.act[...], r.wd[...])
    ri2 = lax.rsqrt(jnp.mean(r2 * r2, axis=1, keepdims=True) + EPSILON)
    n2 = r2 * ri2
    r.out_v[...] = n2 * gain_f
    out_copy = pltpu.make_async_copy(r.out_v, r.out_h, r.osem.at[0])
    out_copy.start()
    ct = r.cot[0].astype(F32)
    gain_ffn = jnp.sum(ct * n2, axis=0, keepdims=True)
    t2 = ct * gain_f
    dr2 = ri2 * (t2 - n2 * jnp.mean(n2 * t2, axis=1, keepdims=True))
    r.dr[...] = dr2
    r.dmo[...] = dr2.astype(BF16)
    for i in range(2):
        plane_send(r.dmo, r.dmo_b.at[y_tokens, :], r.rdmo.at[ey], 2 * i + bx, 1)

    for unit in range(2):
        for i in range(2):
            at = pl.ds(pl.multiple_of((2 * i + (by if unit else 1 - by)) * fs, fs), fs)
            da = mm_nt(r.dmo[...], r.wd[at, :])
            g, u = r.g32[:, at], r.u32[:, at]
            sg = 1.0 / (1.0 + jnp.exp(-g))
            r.dg[:, at] = (da * u * (sg * (1.0 + g * (1.0 - sg)))).astype(BF16)
            plane_send(r.dg.at[:, at], r.dgu_b.at[0, unit, x_tokens, :], r.rdg.at[unit, ex], 2 * by + i, 0)
            r.du[:, at] = (da * (g * sg)).astype(BF16)
        for i in range(2):
            at = pl.ds(pl.multiple_of((2 * i + (by if unit else 1 - by)) * fs, fs), fs)
            plane_send(r.du.at[:, at], r.dgu_b.at[1, unit, x_tokens, :], r.rdu.at[unit, ex], 2 * by + i, 0)
    dh1 = r.dr[...] + mm_nt(r.dg[...], r.wg[...]) + mm_nt(r.du[...], r.wu[...])
    n1 = r.n1[...]
    gain_attn = jnp.sum(dh1 * n1, axis=0, keepdims=True)
    t1 = dh1 * gain_a
    dr1 = r.ri1[:, 0:1] * (t1 - n1 * jnp.mean(n1 * t1, axis=1, keepdims=True))
    r.dr[...] = dr1
    r.dattn[...] = dr1.astype(BF16)
    r.gl[...] = jnp.concatenate([gain_attn, gain_ffn, jnp.zeros((6, d), F32)], axis=0)
    plane_send(r.gl, r.gl_b.at[e], r.rgl.at[e], 0, 0)
    r.do_all[s] = mm_nt(r.dattn[...], r.wo[...]).astype(BF16)
    for ch in range(2):
        mine = rows_of(r.do_all, s, ch)
        send(z > 0, mine, mine, r.rdo.at[ch, s], left)
        send(always, mine, mine, r.rdo.at[ch, s], sib)

    stats = jnp.zeros((tok, 128), F32)
    for p in range(pairs):
        prod = r.do_all[s, :, p * 128:(p + 1) * 128].astype(F32) * r.acc[:, p * 128:(p + 1) * 128]
        for h in range(2):
            head = 2 * p + h
            part = jnp.sum(jnp.where(first == (h == 0), prod, 0.0), axis=1, keepdims=True)
            part = jnp.broadcast_to(part, (tok, 128))
            r.delta[p, h * tok:(h + 1) * tok] = part
            stats = jnp.where(lane == head, r.m[p, h * tok:(h + 1) * tok], stats)
            stats = jnp.where(lane == 16 + head, part, stats)
    r.st_all[s] = stats.T[0:32, :]
    send(z > 0, r.st_all.at[s], r.st_all.at[s], r.rst.at[s], left)
    send(always, r.st_all.at[s], r.st_all.at[s], r.rst.at[s], sib)

    def each_source(dst_of, rsem, count):
        for i in range(count):
            arrived(dst_of(i), rsem.at[i])

    gate_up_sem = (r.rdg, r.rdu)

    def pair_sum(k, unit, out):
        @pl.when(c == 0)
        def _():
            if k == 0 and unit == 0:
                each_source(lambda i: r.hT_b.at[:, pl.ds(i * tok, tok)], r.rh, 4)
            each_source(lambda i: r.dgu_b.at[k, unit, pl.ds(i * tok, tok), :], gate_up_sem[k].at[unit], 4)
            out[k] = mm(r.hT_b[...], r.dgu_b[k, unit]).astype(BF16)

    def cross_y(k):
        send_lazy(lambda: (c == 0, r.pyu.at[k], r.ryu.at[k], r.ry.at[k], (2 * (1 - by) + bx, s)))

    pair_sum(0, 0, r.pyu)
    cross_y(0)

    r.acc[...] = jnp.zeros(r.acc.shape, F32)

    def query_step(kb, _):
        set_bias(kb, True)

        def pair(p, _):
            lanes = pl.ds(pl.multiple_of(p * 128, 128), 128)
            qp, kp, vp = r.q_all[s, :, lanes], r.k_all[kb, :, lanes], r.v_all[kb, :, lanes]
            dop = r.do_all[s, :, lanes]
            pf = jnp.exp(mm_nt(stack(qp), kp) + r.bias[...] - twice(r.m[p]))
            dp = mm_nt(stack(dop), vp)
            ds = (pf * (dp - twice(r.delta[p]))).astype(BF16)
            r.acc[:, lanes] += unstack(mm(ds, kp))
            return 0

        lax.fori_loop(0, pairs, pair, 0, unroll=True)
        return 0

    lax.fori_loop(0, z + 1, query_step, 0)

    def turn_back(src, dst, factor):
        co, si = r.cos[z, own, :], r.sin[z, own, :]
        for p in range(pairs):
            g = src[:, p * 128:(p + 1) * 128] * factor
            dst[:, p * 128:(p + 1) * 128] = (g * co - turn(g) * si).astype(BF16)

    turn_back(r.acc, r.dq, 0.125)

    def columns(i):
        return pl.ds(pl.multiple_of(i * dh, dh), dh)

    pair_sum(1, 0, r.pyu)

    @pl.when(c == 1)
    def _():
        each_source(lambda i: r.act_b.at[:, :, pl.ds(i * tok, tok)], r.ract, 4)
        each_source(lambda i: r.dmo_b.at[pl.ds(i * tok, tok), :], r.rdmo, 4)
        whole = r.act_b[...].reshape(n * tok, 4 * tok)
        r.pxd[...] = mm(whole, r.dmo_b[:, columns(1 - bx)]).astype(BF16).reshape(n, tok, dh)

    send(c == 1, r.pxd, r.rxd, r.rxp.at[0], (2 * by + 1 - bx, s))

    r.acc[...] = jnp.zeros(r.acc.shape, F32)
    r.acc2[...] = jnp.zeros(r.acc2.shape, F32)

    def key_step(j):
        qb = z + j
        mine, other = 2 * qb + c, 2 * qb + 1 - c

        @pl.when(j > 0)
        def _():
            arrived(r.id_all.at[mine], r.rid.at[mine])
            arrived(r.id_all.at[other], r.rid.at[other])
            arrived(r.q_all.at[mine], r.rq.at[mine])
            remote(r.q_all.at[mine], r.q_all.at[mine], r.bsem.at[2, mine], r.rq.at[mine], sib).start()
            blocks = [(rows_of(r.do_all, mine, ch), r.rdo.at[ch, mine]) for ch in range(2)]
            blocks.append((r.st_all.at[mine], r.rst.at[mine]))
            for i, (got, sem) in enumerate(blocks):
                arrived(got, sem)

                @pl.when(z > 0)
                def _():
                    remote(got, got, r.fsem.at[2 + i, mine], sem, left).start()

                remote(got, got, r.bsem.at[3 + i, mine], sem, sib).start()

        arrived(r.q_all.at[other], r.rq.at[other])
        for ch in range(2):
            arrived(rows_of(r.do_all, other, ch), r.rdo.at[ch, other])
        arrived(r.st_all.at[other], r.rst.at[other])
        set_bias(qb, False)

        def pair(p, _):
            lanes = pl.ds(pl.multiple_of(p * 128, 128), 128)
            kp, vp = r.k_all[z, own, lanes], r.v_all[z, own, lanes]
            qp = r.q_all[pl.ds(2 * qb, 2), :, lanes].reshape(2 * tok, 128)
            dop = r.do_all[pl.ds(2 * qb, 2), :, lanes].reshape(2 * tok, 128)

            def row(base):
                return jnp.concatenate(
                    [
                        jnp.broadcast_to(
                            jnp.concatenate(
                                [r.st_all[2 * qb + i, pl.ds(base + 2 * p + h, 1), :] for i in range(2)], axis=1
                            ),
                            (tok, 2 * tok),
                        )
                        for h in range(2)
                    ],
                    axis=0,
                )

            pf = jnp.exp(mm_nt(stack(kp), qp) + r.bias[...] - row(0))
            dp = mm_nt(stack(vp), dop)
            ds = (pf * (dp - row(16))).astype(BF16)
            r.acc2[:, lanes] += unstack(mm(pf.astype(BF16), dop))
            r.acc[:, lanes] += unstack(mm(ds, qp))
            return 0

        lax.fori_loop(0, pairs, pair, 0, unroll=True)

    def attn_send(k, pair):
        for i, value in enumerate(pair):
            for h in range(2):
                plane_send_lazy(
                    lambda value=value, h=h: (
                        value.at[:, pl.ds(h * dh, dh)], r.at_b.at[k, tokens, :], r.rat_in.at[k, e]
                    ),
                    2 * i + h,
                    1,
                )

    def keys_done():
        turn_back(r.acc, r.dk, 1.0)
        r.dv[...] = r.acc2[...].astype(BF16)
        attn_send(1, (r.dk, r.dv))
        r.gin_v[...] = (
            r.dr[...] + mm_nt(r.dq[...], r.wq[...]) + mm_nt(r.dk[...], r.wk[...]) + mm_nt(r.dv[...], r.wv[...])
        )
        pltpu.make_async_copy(r.gin_v, r.gin_h, r.osem.at[1]).start()

    end = (z == 0) | (z == nz - 1)

    def share(src_of, dst_of, far_of, to_c):
        send_lazy(
            lambda: ((c == to_c) & end, src_of(nz - 1 - z), *far_of(), (b, 2 * jnp.where(z == 0, 1, nz - 2) + to_c))
        )
        for zz in range(nz):
            def make(zz=zz):
                distance = jnp.abs(z - zz)
                here = (distance == 1) | ((distance == 2) & end)
                return ((c == to_c) & here, src_of(zz), *dst_of(), (b, 2 * zz + to_c))

            send_lazy(make)

    def pass_on(own_of, dst_of, far_of, to_c):
        target = jnp.where(z == 1, nz - 1, 0)

        @pl.when((c == to_c) & jnp.logical_not(end))
        def _():
            far, sem = far_of()
            arrived(far, sem)
            far[...] = (own_of(target)[...].astype(F32) + far[...].astype(F32)).astype(BF16)

        send_lazy(lambda: ((c == to_c) & jnp.logical_not(end), far_of()[0], *dst_of(), (b, 2 * target + to_c)))

    gate_up = [
        (
            lambda zz, k=k: r.pgu.at[k, pl.ds(pl.multiple_of(zz * blk, blk), blk), :],
            lambda k=k: (r.rgu.at[k, z], r.zgu.at[k, z]),
            lambda k=k: (r.ugu.at[k], r.zfar.at[k]),
            0,
        )
        for k in range(2)
    ]
    down = (
        lambda zz: r.pdn.at[pl.ds(2 * zz, 2)],
        lambda: (r.rdn.at[z], r.zdn.at[z]),
        lambda: (r.udn, r.zfar.at[2]),
        1,
    )
    attn = [
        (
            lambda zz, k=k: r.pat.at[k, pl.ds(pl.multiple_of(zz * blk, blk), blk), :],
            lambda k=k: (r.rat.at[k, z], r.zat.at[k, z]),
            lambda k=k: (r.uat.at[k], r.zfar.at[3 + k]),
            1,
        )
        for k in range(2)
    ]

    def plane_gate_up(k):
        @pl.when(c == 0)
        def _():
            arrived(r.ryu.at[k], r.ry.at[k])
            if k == 0:
                remote(r.pyu.at[1], r.ryu.at[1], r.usem.at[0], r.ry.at[1], (2 * (1 - by) + bx, s)).start()
            r.pgu[k] = (r.pgu[k].astype(F32) + r.ryu[k].astype(F32)).astype(BF16)

        share(*gate_up[k])

    def first_sums():
        pair_sum(0, 1, r.pgu)
        pair_sum(1, 1, r.pgu)

        @pl.when(c == 1)
        def _():
            whole = r.act_b[...].reshape(n * tok, 4 * tok)
            own = mm(whole, r.dmo_b[:, columns(bx)]).reshape(n, tok, dh)
            arrived(r.rxd, r.rxp.at[0])
            r.pdn[...] = (own + r.rxd[...].astype(F32)).astype(BF16)

        share(*down)
        plane_gate_up(0)
        for bb in (2, 3):
            plane_send_lazy(lambda: (r.oT, r.oT_b.at[:, tokens], r.rot.at[e]), bb, 1)
        attn_send(0, (r.dq, r.dattn))

    def second_sums():
        plane_gate_up(1)

    last = nz - z
    first_at, second_at = jnp.minimum(2, last), last

    def key_loop(j, _):
        pl.when(j == first_at)(first_sums)
        pl.when(j == second_at)(second_sums)

        @pl.when(j < last)
        def _():
            key_step(j)

        pl.when(j == last - 1)(keys_done)
        return 0

    lax.fori_loop(0, last + 1, key_loop, 0)

    def attn_sum(k):
        @pl.when(c == 1)
        def _():
            if k == 0:
                each_source(lambda i: r.xT_b.at[:, pl.ds(i * tok, tok)], r.rxt, 2 * nb)
            each_source(lambda i: r.at_b.at[k, pl.ds(i * tok, tok), :], r.rat_in.at[k], 2 * nb)
            if k == 0:
                @pl.when(b >= 2)
                def _():
                    each_source(lambda i: r.oT_b.at[:, pl.ds(i * tok, tok)], r.rot, 2 * nb)
                    r.pat[k] = mm(r.oT_b[...], r.at_b[k]).astype(BF16)

                @pl.when(b < 2)
                def _():
                    r.pat[k] = mm(r.xT_b[...], r.at_b[k]).astype(BF16)
            else:
                r.pat[k] = mm(r.xT_b[...], r.at_b[k]).astype(BF16)

        share(*attn[k])

    def totals(total_of, own, recv_of, rsem_of):
        for is_end, slots in ((True, (1, 2)), (False, (0, nz - 1, nz - 1 - z))):
            @pl.when(end == is_end)
            def _(slots=slots):
                total = own().astype(F32)
                for at in slots:
                    arrived(recv_of(at), rsem_of(at))
                    total = total + recv_of(at)[...].astype(F32)
                total_of()[...] = total.astype(BF16)

    def spread(src_of, dst, rsem, from_c):
        for bb in range(nb):
            for cc in range(2):
                here = (b == bb) & (s == 2 * z + cc)
                send(
                    (c == from_c) & jnp.logical_not(here), src_of(cc), dst, rsem, (bb, 2 * z + cc)
                )

                @pl.when((c == from_c) & here)
                def _(cc=cc):
                    pltpu.make_async_copy(src_of(cc), dst, rsem).start()

    attn_sum(0)
    pass_on(*gate_up[0])
    pass_on(*gate_up[1])
    pass_on(*down)
    attn_sum(1)
    pass_on(*attn[0])

    adds = (b == 0) & (c == 0)

    @pl.when(adds)
    def _():
        total = None
        for i in range(2 * nb):
            arrived(r.gl_b.at[i], r.rgl.at[i])
            total = r.gl_b[i] if total is None else total + r.gl_b[i]
        r.gz[z] = total

    for zz in range(nz):
        send(adds & (z != zz), r.gz.at[z], r.gz.at[z], r.zgl.at[z], (0, 2 * zz))

    @pl.when(adds)
    def _():
        total = r.gz[z]
        for dz in range(1, nz):
            at = lax.rem(z + dz, nz)
            arrived(r.gz.at[at], r.zgl.at[at])
            total = total + r.gz[at]
        r.gsum[...] = total

    for bb in range(nb):
        for cc in range(2):
            here = (bb == 0) and (cc == 0)
            if not here:
                send(adds, r.gsum, r.ogl_h, r.fgl.at[0], (bb, 2 * z + cc))

    @pl.when(adds)
    def _():
        pltpu.make_async_copy(r.gsum, r.ogl_h, r.fgl.at[0]).start()

    rows = pl.ds(pl.multiple_of(z * blk, blk), blk)

    for k in range(2):
        @pl.when(c == 0)
        def _(k=k):
            totals(
                lambda: r.sgu.at[k], lambda: r.pgu[k, rows, :], lambda at: r.rgu.at[k, at], lambda at: r.zgu.at[k, at]
            )

        spread(
            lambda cc: r.sgu.at[k, pl.ds(cc * (blk // 2), blk // 2), :], r.ogu_h.at[b, k], r.fgu.at[k, b], 0
        )

    @pl.when(c == 1)
    def _():
        totals(lambda: r.sdn, lambda: r.pdn[pl.ds(2 * z, 2)], lambda at: r.rdn.at[at], lambda at: r.zdn.at[at])

    spread(lambda cc: r.sdn.at[cc], r.odn_h.at[b], r.fdn.at[b], 1)

    pass_on(*attn[1])
    for k in range(2):
        @pl.when(c == 1)
        def _(k=k):
            totals(
                lambda: r.sat.at[k], lambda: r.pat[k, rows, :], lambda at: r.rat.at[k, at], lambda at: r.zat.at[k, at]
            )

        spread(
            lambda cc: r.sat.at[k, pl.ds(cc * (blk // 2), blk // 2), :], r.oat_h.at[b, k], r.fat.at[k, b], 1
        )

    for bb in range(nb):
        arrived(r.ogu_h.at[bb, 0], r.fgu.at[0, bb])
        arrived(r.ogu_h.at[bb, 1], r.fgu.at[1, bb])
        arrived(r.odn_h.at[bb], r.fdn.at[bb])
        arrived(r.oat_h.at[bb, 0], r.fat.at[0, bb])
        arrived(r.oat_h.at[bb, 1], r.fat.at[1, bb])
    arrived(r.ogl_h, r.fgl.at[0])
    out_copy.wait()
    pltpu.make_async_copy(r.gin_v, r.gin_h, r.osem.at[1]).wait()
    assert used[0] <= r.ssem.shape[0], used
    @pl.when(c == 0)
    def _():
        remote(r.pyu.at[1], r.ryu.at[1], r.usem.at[0], r.ry.at[1], (2 * (1 - by) + bx, s)).wait_send()

    for make, at in pending:
        cond, src, dst, rsem, dev = make()

        @pl.when(cond)
        def _():
            remote(src, dst, r.ssem.at[at], rsem, dev).wait_send()

    def sent_on(t, _):
        @pl.when((lax.rem(t, 2) == c) & (t < s))
        def _():
            for ch in range(2):
                got = rows_of(r.x_all, t, ch)
                remote(got, got, r.bsem.at[ch, t], r.rx.at[ch, t], sib).wait_send()

                @pl.when(z + 1 < nz)
                def _():
                    remote(got, got, r.fsem.at[ch, t], r.rx.at[ch, t], right).wait_send()

        @pl.when((lax.rem(t, 2) == c) & (t > s))
        def _():
            remote(r.q_all.at[t], r.q_all.at[t], r.bsem.at[2, t], r.rq.at[t], sib).wait_send()
            blocks = [(rows_of(r.do_all, t, ch), r.rdo.at[ch, t]) for ch in range(2)]
            blocks.append((r.st_all.at[t], r.rst.at[t]))
            for i, (got, sem) in enumerate(blocks):
                remote(got, got, r.bsem.at[3 + i, t], sem, sib).wait_send()

                @pl.when(z > 0)
                def _():
                    remote(got, got, r.fsem.at[2 + i, t], sem, left).wait_send()
        return 0

    lax.fori_loop(0, n, sent_on, 0)


def unpack_kernel(
    n, nb, out_in, gin_in, oat_h, ogu_h, odn_h, ogl_h,
    out, gin, gq_h, gk_h, gv_h, go_h, gg_h, gu_h, gd_h, g1, g2,
    oat, ogu, odn, ogl, gq, gk, gv, go, gg, gu, gd, out_v, gin_v, isem, osem,
):
    s = lax.axis_index("seq")
    fs = ogu.shape[3]
    tok, dh = odn.shape[1], odn.shape[2]
    copy = pltpu.make_async_copy
    loads = [copy(a, b, isem.at[i]) for i, (a, b) in enumerate(
        ((ogu_h, ogu), (oat_h, oat), (odn_h, odn), (ogl_h, ogl), (out_in, out_v), (gin_in, gin_v)))]
    stores = [copy(a, b, osem.at[i]) for i, (a, b) in enumerate(
        ((gg, gg_h), (gu, gu_h), (gq, gq_h), (gk, gk_h), (gv, gv_h), (go, go_h), (gd, gd_h),
         (out_v, out.at[0]), (gin_v, gin.at[0])))]
    for load in loads:
        load.start()
    loads[0].wait()
    columns = [slice(i * fs, (i + 1) * fs) for i in (2 * (bb % 2) + bb // 2 for bb in range(nb))]
    for bb in range(nb):
        gg[:, columns[bb]] = ogu[bb, 0].astype(F32)
    stores[0].start()
    for bb in range(nb):
        gu[:, columns[bb]] = ogu[bb, 1].astype(F32)
    stores[1].start()
    loads[1].wait()
    for m, (ref, k, bb) in enumerate(((gq, 0, 0), (gk, 1, 0), (gv, 1, 2), (go, 0, 2))):
        ref[:, :dh] = oat[bb, k].astype(F32)
        ref[:, dh:] = oat[bb + 1, k].astype(F32)
        stores[2 + m].start()
    loads[2].wait()
    for bb in range(nb):
        gd[(bb // 2) * tok:(bb // 2 + 1) * tok, (bb % 2) * dh:(bb % 2 + 1) * dh] = odn[bb].astype(F32)
    stores[6].start()
    for i in (4, 5):
        loads[i].wait()
        stores[3 + i].start()
    loads[3].wait()
    d = ogl.shape[1]
    own = d // n
    gains = pltpu.roll(ogl[...], lax.rem(d - s * own, d), 1)
    g1[...] = gains[0:1, :own]
    g2[...] = gains[1:2, :own]
    for store in stores:
        store.wait()


def rope_constants(length, head_dim):
    half = head_dim // 2
    inverse = np.exp(-2.0 * math.log(THETA) / head_dim * np.arange(half)).astype(np.float32)
    angle = np.arange(length, dtype=np.float32)[:, None] * inverse
    cos, sin = np.cos(angle.astype(np.float64)), np.sin(angle.astype(np.float64))
    return (
        np.concatenate([cos, cos, cos, cos], 1).astype(np.float32),
        np.concatenate([-sin, sin, -sin, sin], 1).astype(np.float32),
    )


def fused_local(n, nb, tokens, doc_ids, w_query, w_key, w_value, w_out, w_gate, w_up, w_down, gain_attn, gain_ffn, cotangent):
    _, tok, d = tokens.shape
    f = w_gate.shape[1]
    nz = n // 2
    cos, sin = rope_constants(n * tok, d // HEADS)
    cos = jnp.asarray(cos.reshape(nz, 2 * tok, 128))
    sin = jnp.asarray(sin.reshape(nz, 2 * tok, 128))
    plan = scratch_plan(tok, d, f, n, nb)
    vmem, anywhere = pl.BlockSpec(memory_space=pltpu.VMEM), pl.BlockSpec(memory_space=pl.ANY)
    shape = jax.ShapeDtypeStruct
    parts = pl.pallas_call(
        functools.partial(layer_kernel, tuple(plan), tok, d, f, n, nb),
        out_shape=(
            shape((tok, d), F32), shape((tok, d), F32), shape((nb, 2, d // n, d // 2), BF16),
            shape((nb, 2, d // n, f // nb), BF16), shape((nb, tok, d // 2), BF16), shape((8, d), F32),
        ),
        in_specs=[vmem] * 5 + [anywhere] * 9,
        out_specs=[anywhere] * 6,
        scratch_shapes=list(plan.values()),
        compiler_params=pltpu.CompilerParams(
            collective_id=0, has_side_effects=True, vmem_limit_bytes=62 * 2**20
        ),
        name="layer",
    )(
        doc_ids, tokens, cotangent, gain_attn, gain_ffn, cos, sin,
        w_query, w_key, w_value, w_out, w_gate, w_up, w_down,
    )
    own = d // n
    grads = [shape((own, d), F32)] * 4 + [shape((own, f), F32)] * 2 + [shape((f // n, d), F32)]
    results = pl.pallas_call(
        functools.partial(unpack_kernel, n, nb),
        out_shape=(shape((1, tok, d), F32), shape((1, tok, d), F32), *grads, shape((1, own), F32), shape((1, own), F32)),
        in_specs=[pl.BlockSpec(memory_space=pltpu.HBM)] * 6,
        out_specs=[anywhere] * 9 + [vmem] * 2,
        scratch_shapes=[pltpu.VMEM(parts[i].shape, parts[i].dtype) for i in (2, 3, 4, 5)]
        + [pltpu.VMEM(g.shape, g.dtype) for g in grads]
        + [pltpu.VMEM((tok, d), F32)] * 2
        + [pltpu.SemaphoreType.DMA((6,)), pltpu.SemaphoreType.DMA((9,))],
        compiler_params=pltpu.CompilerParams(vmem_limit_bytes=62 * 2**20),
        name="unpack",
    )(*parts)
    return results[:9] + (results[9].reshape(own), results[10].reshape(own))


def fits(shapes, n, nb):
    (_, tok, d), f = shapes[0], shapes[6][1]
    return (
        nb == 4 and n == 8 and n * tok <= 1024 and tok == 128 and shapes[0][0] == 1
        and d == HEADS * 64 and d % 256 == 0 and d % (16 * n) == 0 and f == 2 * tok * n and f % 512 == 0
    )


def solution(mesh):
    nb, n = mesh.shape["batch"], mesh.shape["seq"]

    def either(*args):
        shapes = [a.shape for a in args]
        if fits(shapes, n, nb):
            return fused_local(n, nb, *args)
        return local(*args)

    return jax.shard_map(
        either,
        mesh=mesh,
        in_specs=(
            P("batch", "seq", None),
            P("batch", "seq"),
            P(),
            P(),
            P(),
            P(),
            P(),
            P(),
            P(),
            P(),
            P(),
            P("batch", "seq", None),
        ),
        out_specs=(
            P("batch", "seq", None),
            P("batch", "seq", None),
            P("seq", None),
            P("seq", None),
            P("seq", None),
            P("seq", None),
            P("seq", None),
            P("seq", None),
            P("seq", None),
            P("seq"),
            P("seq"),
        ),
        check_vma=False,
    )
```

```python
import functools
import math
import types

import jax
import jax.numpy as jnp
import numpy as np
from jax import lax
from jax.experimental import pallas as pl
from jax.experimental.pallas import tpu as pltpu
from jax.sharding import PartitionSpec as P

HEADS = 12
NSEG = 8


EPSILON = 1e-06
THETA = 10000.0
MASKED = -1e30


def root_mean_square_norm(values, gain):
    return values * lax.rsqrt(jnp.mean(values * values, -1, keepdims=True) + EPSILON) * gain


def swiglu(gate, up_part):
    return jax.nn.silu(gate) * up_part


def rope_tables(positions, head_dim):
    half_dim = head_dim // 2
    inverse = jnp.exp(-2.0 * math.log(THETA) / head_dim * jnp.arange(half_dim, dtype=jnp.float32))
    angle = positions.astype(jnp.float32)[..., None] * inverse
    return (
        jnp.concatenate([jnp.cos(angle), jnp.cos(angle)], -1),
        jnp.concatenate([jnp.sin(angle), jnp.sin(angle)], -1),
    )


def rotate(values, cosine, sine):
    half_dim = values.shape[-1] // 2
    turned = jnp.concatenate([-values[..., half_dim:], values[..., :half_dim]], -1)
    return values * cosine + turned * sine


def rotate_back(grads, cosine, sine):
    half_dim = grads.shape[-1] // 2
    turned = grads * sine
    return grads * cosine + jnp.concatenate([turned[..., half_dim:], -turned[..., :half_dim]], -1)


def block_size(total_rows):
    return max((d for d in range(1, min(total_rows, 2048) + 1) if total_rows % d == 0))


def doc_begin(segment_begins, where_at):
    earlier = segment_begins[:, None, :] <= where_at[:, :, None]
    return jnp.max(jnp.where(earlier, segment_begins[:, None, :], 0), -1)


def outer_sum(remaining_tokens, right):
    return lax.dot_general(
        remaining_tokens, right, (((0,), (0,)), ((), ())), preferred_element_type=jnp.float32
    )


def back_product(grads, weight_matrix):
    return lax.dot_general(
        grads, weight_matrix, (((1,), (1,)), ((), ())), preferred_element_type=jnp.float32
    )


def masked_scores(queries, key_block, key_at, query_at, query_begin):
    batch_rows, block_rows, model_width = key_block.shape
    head_count = queries.shape[2]
    head_dim = model_width // head_count
    key_heads = key_block.reshape(batch_rows, block_rows, head_count, head_dim)
    scores = jnp.einsum(
        "bqhd,bkhd->bhqk", queries, key_heads, preferred_element_type=jnp.float32
    ) * (1.0 / math.sqrt(head_dim))
    key_pos = key_at[None, None, :]
    query_pos = query_at[:, :, None]
    begin_pos = query_begin[:, :, None]
    allowed = (
        (key_pos <= query_pos) & (key_pos >= begin_pos) & ((begin_pos > 0) | (key_pos == query_pos))
    )
    return (scores, allowed[:, None], key_heads)


def grad_terms(
    queries, grad_heads, lse, delta, query_at, query_begin, key_block, value_block, key_at
):
    scores, allowed, key_heads = masked_scores(queries, key_block, key_at, query_at, query_begin)
    value_heads = value_block.reshape(key_heads.shape)
    probs = jnp.where(allowed, jnp.exp(scores - lse[..., None]), 0.0)
    dprob = jnp.einsum(
        "bqhd,bkhd->bhqk", grad_heads, value_heads, preferred_element_type=jnp.float32
    )
    dscore = (probs * (dprob - delta[..., None])).astype(jnp.bfloat16)
    return (probs.astype(jnp.bfloat16), dscore, key_heads, value_heads)


def over_rows(update, carried, arrays, first_row):
    total_rows = arrays[0].shape[1]
    block_rows = block_size(total_rows)

    def over_step(block_index, state):
        offset = block_index * block_rows
        blocks = tuple((lax.dynamic_slice_in_dim(item, offset, block_rows, 1) for item in arrays))
        key_at = first_row + offset + jnp.arange(block_rows, dtype=jnp.int32)
        return update(state, blocks, key_at)

    return lax.fori_loop(0, total_rows // block_rows, over_step, carried)


def local(
    tokens,
    doc_ids,
    w_query,
    w_key,
    w_value,
    w_out,
    w_gate,
    w_up,
    w_down,
    gain_attn,
    gain_ffn,
    cotangent,
):
    batch_rows, local_len, model_width = tokens.shape
    head_count = HEADS
    head_dim = model_width // head_count
    shape_heads = (batch_rows, local_len, head_count, head_dim)
    scale = 1.0 / math.sqrt(head_dim)
    labels = jnp.arange(NSEG, dtype=jnp.int32)
    member = (doc_ids[:, :, None] == labels).astype(jnp.int32)
    totals = lax.psum(jnp.sum(member, 1), "seq")
    segment_begins = jnp.cumsum(totals, 1) - totals
    local_at = lax.axis_index("seq") * local_len + jnp.arange(local_len, dtype=jnp.int32)
    query_at = jnp.broadcast_to(local_at, (batch_rows, local_len))
    query_begin = doc_begin(segment_begins, query_at)
    cosine, sine = rope_tables(query_at - query_begin, head_dim)
    cosine = cosine[:, :, None, :]
    sine = sine[:, :, None, :]
    flat_tokens = tokens.reshape(batch_rows * local_len, model_width)
    queries = rotate(
        jnp.dot(flat_tokens, w_query, preferred_element_type=jnp.float32).reshape(shape_heads),
        cosine,
        sine,
    ).astype(jnp.bfloat16)
    key_send = (
        rotate(
            jnp.dot(flat_tokens, w_key, preferred_element_type=jnp.float32).reshape(shape_heads),
            cosine,
            sine,
        )
        .astype(jnp.bfloat16)
        .reshape(batch_rows, local_len, model_width)
    )
    value_send = (
        jnp.dot(flat_tokens, w_value, preferred_element_type=jnp.float32)
        .astype(jnp.bfloat16)
        .reshape(batch_rows, local_len, model_width)
    )

    def stats_step(state, blocks, key_at):
        run_max, run_sum = state
        scores, allowed, key_heads = masked_scores(
            queries, blocks[0], key_at, query_at, query_begin
        )
        scores = jnp.where(allowed, scores, MASKED)
        new_max = jnp.maximum(run_max, jnp.max(scores, -1))
        weights = jnp.where(allowed, jnp.exp(scores - new_max[..., None]), 0.0)
        return (new_max, run_sum * jnp.exp(run_max - new_max) + jnp.sum(weights, -1))

    stats_init = (
        jnp.full((batch_rows, head_count, local_len), MASKED, jnp.float32),
        jnp.zeros((batch_rows, head_count, local_len), jnp.float32),
    )
    zero_heads = jnp.zeros(shape_heads, jnp.float32)
    run_max, run_sum = over_rows(
        stats_step, stats_init, (lax.all_gather(key_send, "seq", axis=1, tiled=True),), jnp.int32(0)
    )
    lse = run_max + jnp.log(run_sum)

    def output_step(state, blocks, key_at):
        scores, allowed, key_heads = masked_scores(
            queries, blocks[0], key_at, query_at, query_begin
        )
        value_heads = blocks[1].reshape(key_heads.shape)
        probs = jnp.where(allowed, jnp.exp(scores - lse[..., None]), 0.0).astype(jnp.bfloat16)
        return state + jnp.einsum(
            "bhqk,bkhd->bqhd", probs, value_heads, preferred_element_type=jnp.float32
        )

    attended = over_rows(
        output_step,
        zero_heads,
        (
            lax.all_gather(key_send, "seq", axis=1, tiled=True),
            lax.all_gather(value_send, "seq", axis=1, tiled=True),
        ),
        jnp.int32(0),
    )
    attended_low = attended.astype(jnp.bfloat16).reshape(batch_rows * local_len, model_width)
    first_sum = flat_tokens.astype(jnp.float32) + jnp.dot(
        attended_low, w_out, preferred_element_type=jnp.float32
    )
    hidden, norm_first_back = jax.vjp(root_mean_square_norm, first_sum, gain_attn)
    hidden_low = hidden.astype(jnp.bfloat16)
    gate = jnp.dot(hidden_low, w_gate, preferred_element_type=jnp.float32)
    up_part = jnp.dot(hidden_low, w_up, preferred_element_type=jnp.float32)
    active, swiglu_back = jax.vjp(swiglu, gate, up_part)
    active_low = active.astype(jnp.bfloat16)
    second_sum = hidden + jnp.dot(active_low, w_down, preferred_element_type=jnp.float32)
    output, norm_second_back = jax.vjp(root_mean_square_norm, second_sum, gain_ffn)
    second_grad, grad_gain_ffn = norm_second_back(
        cotangent.reshape(batch_rows * local_len, model_width).astype(jnp.float32)
    )
    branch_grad = second_grad.astype(jnp.bfloat16)
    grad_down = outer_sum(active_low, branch_grad)
    gate_grad, up_grad = swiglu_back(back_product(branch_grad, w_down))
    gate_low = gate_grad.astype(jnp.bfloat16)
    up_low = up_grad.astype(jnp.bfloat16)
    grad_gate = outer_sum(hidden_low, gate_low)
    grad_up = outer_sum(hidden_low, up_low)
    hidden_grad = second_grad + back_product(gate_low, w_gate) + back_product(up_low, w_up)
    first_grad, grad_gain_attn = norm_first_back(hidden_grad)
    attn_grad = first_grad.astype(jnp.bfloat16)
    grad_out = outer_sum(attended_low, attn_grad)
    grad_heads = back_product(attn_grad, w_out).astype(jnp.bfloat16).reshape(shape_heads)
    delta = jnp.swapaxes(jnp.sum(grad_heads.astype(jnp.float32) * attended, -1), 1, 2)

    def query_step(state, blocks, key_at):
        probs_low, dscore, key_heads, value_heads = grad_terms(
            queries, grad_heads, lse, delta, query_at, query_begin, blocks[0], blocks[1], key_at
        )
        return (
            state
            + jnp.einsum("bhqk,bkhd->bqhd", dscore, key_heads, preferred_element_type=jnp.float32)
            * scale
        )

    all_keys, all_values = (
        lax.all_gather(key_send, "seq", axis=1, tiled=True),
        lax.all_gather(value_send, "seq", axis=1, tiled=True),
    )
    query_grad = over_rows(query_step, zero_heads, (all_keys, all_values), 0)
    first_row = jnp.int32(0)
    span_rows = local_len * lax.axis_size("seq")
    block_rows = block_size(span_rows)
    empty = jnp.zeros((batch_rows, span_rows, head_count, head_dim), jnp.float32)

    def key_step(block_index, state):
        offset = block_index * block_rows
        key_block = lax.dynamic_slice_in_dim(all_keys, offset, block_rows, 1)
        value_block = lax.dynamic_slice_in_dim(all_values, offset, block_rows, 1)
        key_at = first_row + offset + jnp.arange(block_rows, dtype=jnp.int32)
        probs_low, dscore, key_heads, value_heads = grad_terms(
            queries, grad_heads, lse, delta, query_at, query_begin, key_block, value_block, key_at
        )
        key_part = (
            jnp.einsum("bhqk,bqhd->bkhd", dscore, queries, preferred_element_type=jnp.float32)
            * scale
        )
        value_part = jnp.einsum(
            "bhqk,bqhd->bkhd", probs_low, grad_heads, preferred_element_type=jnp.float32
        )
        return (
            lax.dynamic_update_slice_in_dim(state[0], key_part, offset, 1),
            lax.dynamic_update_slice_in_dim(state[1], value_part, offset, 1),
        )

    key_all, value_all = lax.fori_loop(0, span_rows // block_rows, key_step, (empty, empty))
    joined = jnp.concatenate(
        [
            key_all.reshape(batch_rows, span_rows, model_width),
            value_all.reshape(batch_rows, span_rows, model_width),
        ],
        -1,
    )
    summed_keys = jnp.swapaxes(
        lax.psum_scatter(jnp.swapaxes(joined, 0, 1), "seq", scatter_dimension=0, tiled=True), 0, 1
    )
    key_grad = summed_keys[..., :model_width].reshape(shape_heads)
    value_grad = summed_keys[..., model_width:]
    flat_len = batch_rows * local_len
    query_low = (
        rotate_back(query_grad, cosine, sine).astype(jnp.bfloat16).reshape(flat_len, model_width)
    )
    key_low = (
        rotate_back(key_grad, cosine, sine).astype(jnp.bfloat16).reshape(flat_len, model_width)
    )
    value_low = value_grad.astype(jnp.bfloat16).reshape(flat_len, model_width)
    grad_input = (
        first_grad
        + back_product(query_low, w_query)
        + back_product(key_low, w_key)
        + back_product(value_low, w_value)
    )
    grad_query = outer_sum(flat_tokens, query_low)
    grad_key = outer_sum(flat_tokens, key_low)
    value_weight_gradient = outer_sum(flat_tokens, value_low)
    shares = (
        lax.psum_scatter(grad_query, "seq", scatter_dimension=0, tiled=True),
        lax.psum_scatter(grad_key, "seq", scatter_dimension=0, tiled=True),
        lax.psum_scatter(value_weight_gradient, "seq", scatter_dimension=0, tiled=True),
        lax.psum_scatter(grad_out, "seq", scatter_dimension=0, tiled=True),
        lax.psum_scatter(grad_gate, "seq", scatter_dimension=0, tiled=True),
        lax.psum_scatter(grad_up, "seq", scatter_dimension=0, tiled=True),
        lax.psum_scatter(grad_down, "seq", scatter_dimension=0, tiled=True),
        lax.psum_scatter(grad_gain_attn, "seq", scatter_dimension=0, tiled=True),
        lax.psum_scatter(grad_gain_ffn, "seq", scatter_dimension=0, tiled=True),
    )
    results = (
        lax.psum(shares[0].astype(jnp.bfloat16), "batch").astype(jnp.float32),
        lax.psum(shares[1].astype(jnp.bfloat16), "batch").astype(jnp.float32),
        lax.psum(shares[2].astype(jnp.bfloat16), "batch").astype(jnp.float32),
        lax.psum(shares[3].astype(jnp.bfloat16), "batch").astype(jnp.float32),
        lax.psum(shares[4].astype(jnp.bfloat16), "batch").astype(jnp.float32),
        lax.psum(shares[5].astype(jnp.bfloat16), "batch").astype(jnp.float32),
        lax.psum(shares[6].astype(jnp.bfloat16), "batch").astype(jnp.float32),
        lax.psum(shares[7].astype(jnp.bfloat16), "batch").astype(jnp.float32),
        lax.psum(shares[8].astype(jnp.bfloat16), "batch").astype(jnp.float32),
    )
    output_rows = output.reshape(batch_rows, local_len, model_width)
    input_rows = grad_input.reshape(batch_rows, local_len, model_width)
    return (
        output_rows,
        input_rows,
        results[0],
        results[1],
        results[2],
        results[3],
        results[4],
        results[5],
        results[6],
        results[7],
        results[8],
    )


MESH = pl.DeviceIdType.MESH
F32 = jnp.float32
BF16 = jnp.bfloat16


def mm(a, b):
    return lax.dot_general(a, b, (((1,), (0,)), ((), ())), preferred_element_type=F32)


def mm_nt(a, b):
    return lax.dot_general(a, b, (((1,), (1,)), ((), ())), preferred_element_type=F32)


def scratch_plan(tok, d, f, n, nb):
    nz, plane, heads = n // 2, 2 * nb * tok, HEADS
    vm = pltpu.VMEM
    dma = lambda *shape: pltpu.SemaphoreType.DMA(shape)
    return dict(
        wq=vm((d, d), BF16), wk=vm((d, d), BF16), wv=vm((d, d), BF16), wo=vm((d, d), BF16),
        wg=vm((d, f), BF16), wu=vm((d, f), BF16), wd=vm((f, d), BF16),
        cos=vm((nz, 2 * tok, 128), F32), sin=vm((nz, 2 * tok, 128), F32),
        x_all=vm((n, tok, d), BF16), q_all=vm((n, tok, d), BF16), do_all=vm((n, tok, d), BF16),
        k_all=vm((nz, 2 * tok, d), BF16), v_all=vm((nz, 2 * tok, d), BF16),
        st_all=vm((n, 32, tok), F32), id_all=vm((n, 8, tok), jnp.int32),
        idcol=vm((tok, 128), F32), bias=vm((2 * tok, 2 * tok), F32),
        m=vm((heads // 2, 2 * tok, 128), F32), l=vm((heads // 2, 2 * tok, 128), F32),
        delta=vm((heads // 2, 2 * tok, 128), F32),
        acc=vm((tok, d), F32), acc2=vm((tok, d), F32),
        olow=vm((tok, d), BF16), hb=vm((tok, d), BF16), h1=vm((tok, d), F32), n1=vm((tok, d), F32),
        ri1=vm((tok, 128), F32), dr=vm((tok, d), F32),
        act=vm((tok, f), BF16),
        dg=vm((tok, f), BF16), du=vm((tok, f), BF16), dmo=vm((tok, d), BF16), dattn=vm((tok, d), BF16),
        dq=vm((tok, d), BF16), dk=vm((tok, d), BF16), dv=vm((tok, d), BF16),
        hT=vm((d, tok), BF16), xT=vm((d, tok), BF16), oT=vm((d, tok), BF16),
        gl=vm((8, d), F32), out_v=vm((tok, d), F32), gin_v=vm((tok, d), F32),
        hT_b=vm((d, plane), BF16), dmo_b=vm((plane, d), BF16),
        wgT=vm((f // nb, d), BF16), wuT=vm((f // nb, d), BF16), tmpT=vm((128, d), BF16),
        act_x=vm((f // nb, plane), BF16), da_x=vm((f // nb, plane), BF16),
        fa=vm((f // nb, plane), F32), fb=vm((f // nb, plane), F32), dgu=vm((2, f // nb, plane), BF16),
        xT_b=vm((d, plane), BF16), o2=vm((d, 2 * tok), BF16), da2=vm((2 * tok, d), BF16), at_b=vm((2, plane, d // 2), BF16), gl_b=vm((2 * nb, 8, d), F32),
        pgu=vm((2, d, f // nb), BF16), pdn=vm((n, f // (nb * n), d), BF16),
        pat=vm((2, d, d // 2), BF16), pout=vm((d, d), BF16),
        ugu=vm((2, 2, d // nz, f // nb), BF16), udn=vm((2, 2, f // (nb * n), d), BF16),
        uat=vm((2, 2, d // nz, d // 2), BF16),
        uout=vm((2, d // nz, d), BF16), rout=vm((nz, d // nz, d), BF16), sout=vm((2, d // n, d), BF16),
        rso=vm((nb, 2, d // (2 * n), d // 2), BF16), fso=vm((2, d // (2 * n), d // 2), BF16),
        rgu=vm((2, nz, d // nz, f // nb), BF16), rdn=vm((nz, 2, f // (nb * n), d), BF16), rat=vm((2, nz, d // nz, d // 2), BF16),
        sgu=vm((2, d // nz, f // nb), BF16), sdn=vm((2, f // (nb * n), d), BF16), sat=vm((2, d // nz, d // 2), BF16),
        gz=vm((nz, 8, d), F32), gsum=vm((8, d), F32),
        wsem=dma(9), osem=dma(2), ssem=dma(230), fsem=dma(5, n), bsem=dma(6, n),
        rx=dma(2, n), rq=dma(n), rdo=dma(2, n), rst=dma(n), rid=dma(n),
        rh=dma(2 * nb), rdmo=dma(2 * nb), rax=dma(1), rda=dma(1), zfar=dma(6, 2),
        rxt=dma(2 * nb), ro2=dma(2), rda2=dma(2), zout=dma(nz), rrso=dma(nb), fout=dma(nb), rat_in=dma(2, 2 * nb), rgl=dma(2 * nb),
        zgu=dma(2, nz), zdn=dma(nz), zat=dma(2, nz), zgl=dma(nz),
        fgu=dma(2, nb), fdn=dma(nb), fat=dma(2, nb), fgl=dma(1),
    )


INPUTS = ("ids", "tok", "cot", "ga", "gf", "cos_h", "sin_h", "wq_h", "wk_h", "wv_h", "wo_h", "wg_h", "wu_h", "wd_h")
OUTPUTS = ("out_h", "gin_h", "oat_h", "ogu_h", "odn_h", "oout_h", "ogl_h")


def layer_kernel(plan_names, tok, d, f, n, nb, *refs):
    r = types.SimpleNamespace(**dict(zip(INPUTS + OUTPUTS + plan_names, refs)))
    nz, pairs = n // 2, d // 128
    fs, dh, blk = f // nb, d // 2, d // nz
    b, s = lax.axis_index("batch"), lax.axis_index("seq")
    z, c = s // 2, lax.rem(s, 2)
    by, bx = b // 2, lax.rem(b, 2)
    e = 2 * b + c
    sib = (b, s + 1 - 2 * c)
    gain_a, gain_f = r.ga[...].reshape(1, d), r.gf[...].reshape(1, d)
    pending, used = [], [0]

    def remote(src, dst, ssem, rsem, dev):
        return pltpu.make_async_remote_copy(
            src_ref=src, dst_ref=dst, send_sem=ssem, recv_sem=rsem, device_id=dev, device_id_type=MESH
        )

    def send_lazy(make):
        at = used[0]
        used[0] += 1
        pending.append((make, at))
        cond, src, dst, rsem, dev = make()

        @pl.when(cond)
        def _():
            remote(src, dst, r.ssem.at[at], rsem, dev).start()

    def send(cond, src, dst, rsem, dev):
        send_lazy(lambda: (cond, src, dst, rsem, dev))

    def plane_send_lazy(make, to_b, to_c, also=None):
        def here():
            return (b == to_b) & (c == to_c)

        def wanted(cond):
            return cond if also is None else cond & also()

        send_lazy(lambda: (wanted(jnp.logical_not(here())), *make(), (to_b, 2 * z + to_c)))

        @pl.when(wanted(here()))
        def _():
            pltpu.make_async_copy(*make()).start()

    def plane_send(src, dst, rsem, to_b, to_c):
        plane_send_lazy(lambda: (src, dst, rsem), to_b, to_c)

    def arrived(dst, rsem):
        remote(dst, dst, r.ssem.at[0], rsem, sib).wait_recv()

    loads = {}
    for i, name in enumerate(("wk", "wv", "wq", "cos", "sin", "wo", "wg", "wu", "wd")):
        loads[name] = pltpu.make_async_copy(getattr(r, name + "_h"), getattr(r, name), r.wsem.at[i])
        loads[name].start()

    r.x_all[s] = r.tok[0]
    r.id_all[s] = jnp.broadcast_to(r.ids[...], (8, tok))

    bar = pltpu.get_barrier_semaphore()
    for zz in range(nz):
        for cc in range(2):
            @pl.when(2 * zz + cc != s)
            def _(zz=zz, cc=cc):
                pl.semaphore_signal(bar, inc=1, device_id=(b, 2 * zz + cc), device_id_type=MESH)
    for bb in range(nb):
        for cc in range(2):
            @pl.when(bb != b)
            def _(bb=bb, cc=cc):
                pl.semaphore_signal(bar, inc=1, device_id=(bb, 2 * z + cc), device_id_type=MESH)
    pl.semaphore_wait(bar, n - 1 + 2 * (nb - 1))

    always = s >= 0
    half = tok // 2

    def rows_of(ref, t, ch):
        return ref.at[t, pl.ds(ch * half, half)]

    right, left = (b, s + 2), (b, s - 2)
    for zz in range(nz):
        for cc in range(2):
            send(2 * zz + cc != s, r.id_all.at[s], r.id_all.at[s], r.rid.at[s], (b, 2 * zz + cc))
    for ch in range(2):
        mine = rows_of(r.x_all, s, ch)
        send(z + 1 < nz, mine, mine, r.rx.at[ch, s], right)
        send(always, mine, mine, r.rx.at[ch, s], sib)

    lane = lax.broadcasted_iota(jnp.int32, (tok, 128), 1)
    first = lane < 64
    half_mask = (jnp.where(first, 1.0, 0.0).astype(BF16), jnp.where(first, 0.0, 1.0).astype(BF16))

    def turn(u):
        low = lax.rem(lax.broadcasted_iota(jnp.int32, u.shape, 1), 64) < 32
        return jnp.where(low, pltpu.roll(u, 96, 1), pltpu.roll(u, 32, 1))

    def twice(u):
        return jnp.concatenate([u, u], axis=1)

    def stack(u):
        return jnp.concatenate([u * half_mask[0], u * half_mask[1]], axis=0)

    def unstack(u):
        return jnp.where(first, u[:tok], u[tok:])

    own = pl.ds(pl.multiple_of(c * tok, tok), tok)

    loads["wq"].wait()
    loads["cos"].wait()
    loads["sin"].wait()

    u = mm(r.tok[0], r.wq[...])
    co, si = r.cos[z, own, :], r.sin[z, own, :]
    for p in range(pairs):
        part = u[:, p * 128:(p + 1) * 128]
        r.q_all[s, :, p * 128:(p + 1) * 128] = ((part * co + turn(part) * si) * 0.125).astype(BF16)
    send(always, r.q_all.at[s], r.q_all.at[s], r.rq.at[s], sib)
    for dz in range(1, nz):
        send(z - dz >= 0, r.q_all.at[s], r.q_all.at[s], r.rq.at[s], (b, s - 2 * dz))

    def transpose_into(dst, value):
        for p in range(d // 128):
            dst[p * 128:(p + 1) * 128, :] = value[:, p * 128:(p + 1) * 128].T.astype(BF16)

    tokens = pl.ds(pl.multiple_of(e * tok, tok), tok)
    transpose_into(r.xT, r.tok[0].astype(F32))
    for bb in range(nb):
        plane_send(r.xT, r.xT_b.at[:, tokens], r.rxt.at[e], bb, 1)
    r.idcol[...] = jnp.broadcast_to(r.ids[...].astype(F32), (128, tok)).T

    def ids_of(block):
        return jnp.concatenate(
            [r.id_all[2 * block, 0:1, :], r.id_all[2 * block + 1, 0:1, :]], axis=1
        ).astype(F32)

    def set_bias(block, local_is_query):
        shape = (tok, 2 * tok)
        mine = s * tok + lax.broadcasted_iota(jnp.int32, shape, 0)
        theirs = block * (2 * tok) + lax.broadcasted_iota(jnp.int32, shape, 1)
        my_id = twice(r.idcol[...])
        their_id = jnp.broadcast_to(ids_of(block), shape)
        causal = (theirs <= mine) if local_is_query else (mine <= theirs)
        allowed = (my_id == their_id) & causal & ((my_id != 0.0) | (mine == theirs))
        bias = jnp.where(allowed, 0.0, MASKED)
        r.bias[...] = jnp.concatenate([bias, bias], axis=0)

    units = fs // n

    def quarter_weights():
        for src, dst in ((r.wg, r.wgT), (r.wu, r.wuT)):
            for t in range(n):
                tile = src[:, pl.ds(pl.multiple_of((2 * t + by) * 128, 128), 128)].astype(F32)
                for p in range(pairs):
                    r.tmpT[:, p * 128:(p + 1) * 128] = tile[p * 128:(p + 1) * 128].T.astype(BF16)
                dst[t * units:(t + 1) * units, :] = r.tmpT[pl.ds(pl.multiple_of(bx * units, units), units), :]

    r.m[...] = jnp.full(r.m.shape, MASKED, F32)
    r.l[...] = jnp.zeros(r.l.shape, F32)
    r.acc[...] = jnp.zeros(r.acc.shape, F32)
    loads["wk"].wait()
    loads["wv"].wait()

    def forward_step(j, _):
        kb = z - j
        mine, other = 2 * kb + c, 2 * kb + 1 - c

        @pl.when(j > 0)
        def _():
            for ch in range(2):
                got = rows_of(r.x_all, mine, ch)
                arrived(got, r.rx.at[ch, mine])

                @pl.when(z + 1 < nz)
                def _():
                    remote(got, got, r.fsem.at[ch, mine], r.rx.at[ch, mine], right).start()

                remote(got, got, r.bsem.at[ch, mine], r.rx.at[ch, mine], sib).start()

            arrived(r.id_all.at[mine], r.rid.at[mine])

        for ch in range(2):
            arrived(rows_of(r.x_all, other, ch), r.rx.at[ch, other])
        arrived(r.id_all.at[other], r.rid.at[other])
        set_bias(kb, True)

        xb = r.x_all[pl.ds(2 * kb, 2)].reshape(2 * tok, d)
        u = mm(xb, r.wk[...])
        co, si = r.cos[kb], r.sin[kb]
        for p in range(pairs):
            part = u[:, p * 128:(p + 1) * 128]
            r.k_all[kb, :, p * 128:(p + 1) * 128] = (part * co + turn(part) * si).astype(BF16)
        r.v_all[kb] = mm(xb, r.wv[...]).astype(BF16)

        def pair(p, _):
            lanes = pl.ds(pl.multiple_of(p * 128, 128), 128)
            qp, kp, vp = r.q_all[s, :, lanes], r.k_all[kb, :, lanes], r.v_all[kb, :, lanes]
            sc = mm_nt(stack(qp), kp) + r.bias[...]
            m_old = r.m[p]
            m_new = jnp.maximum(m_old, jnp.max(sc, axis=1, keepdims=True))
            alpha = jnp.exp(m_old - m_new)
            ex = jnp.exp(sc - twice(m_new))
            r.m[p] = m_new
            r.l[p] = r.l[p] * alpha + jnp.sum(ex, axis=1, keepdims=True)
            r.acc[:, lanes] = r.acc[:, lanes] * unstack(alpha) + unstack(mm(ex.astype(BF16), vp))
            return 0

        lax.fori_loop(0, pairs, pair, 0, unroll=True)

        @pl.when((j == 0) & (c == 0))
        def _():
            loads["wg"].wait()
            loads["wu"].wait()
            quarter_weights()

        return 0

    lax.fori_loop(0, z + 1, forward_step, 0)

    def finish(p, _):
        lanes = pl.ds(pl.multiple_of(p * 128, 128), 128)
        r.acc[:, lanes] = r.acc[:, lanes] / unstack(r.l[p])
        r.m[p] = r.m[p] + jnp.log(r.l[p])
        return 0

    lax.fori_loop(0, pairs, finish, 0, unroll=True)
    r.olow[...] = r.acc[...].astype(BF16)

    loads["wo"].wait()
    r1 = r.tok[0].astype(F32) + mm(r.olow[...], r.wo[...])
    ri1 = lax.rsqrt(jnp.mean(r1 * r1, axis=1, keepdims=True) + EPSILON)
    r.ri1[...] = jnp.broadcast_to(ri1, (tok, 128))
    n1 = r1 * ri1
    r.n1[...] = n1
    h1 = n1 * gain_a
    r.h1[...] = h1
    r.hb[...] = h1.astype(BF16)
    transpose_into(r.hT, h1)
    for bb in range(nb):
        plane_send(r.hT, r.hT_b.at[:, tokens], r.rh.at[e], bb, 0)
    transpose_into(r.oT, r.acc[...])

    @pl.when(c == 1)
    def _():
        loads["wg"].wait()
        loads["wu"].wait()

    def gate_at(i):
        return (slice((i // 2) * tok, (i // 2 + 1) * tok), slice((i % 2) * 512, (i % 2 + 1) * 512))

    def up_at(i):
        return gate_at(i + f // 512)

    for i in range(f // 512):
        at = slice(i * 512, (i + 1) * 512)
        g = mm(r.hb[...], r.wg[:, at])
        u = mm(r.hb[...], r.wu[:, at])
        r.fa[gate_at(i)] = g
        r.fa[up_at(i)] = u
        a = g / (1.0 + jnp.exp(-g)) * u
        r.act[:, at] = a.astype(BF16)
    loads["wd"].wait()
    r2 = r.h1[...] + mm(r.act[...], r.wd[...])
    ri2 = lax.rsqrt(jnp.mean(r2 * r2, axis=1, keepdims=True) + EPSILON)
    n2 = r2 * ri2
    r.out_v[...] = n2 * gain_f
    out_copy = pltpu.make_async_copy(r.out_v, r.out_h, r.osem.at[0])
    out_copy.start()
    ct = r.cot[0].astype(F32)
    gain_ffn = jnp.sum(ct * n2, axis=0, keepdims=True)
    t2 = ct * gain_f
    dr2 = ri2 * (t2 - n2 * jnp.mean(n2 * t2, axis=1, keepdims=True))
    r.dr[...] = dr2
    r.dmo[...] = dr2.astype(BF16)
    for bb in range(nb):
        plane_send(r.dmo, r.dmo_b.at[tokens, :], r.rdmo.at[e], bb, 1)

    for i in range(f // 512):
        at = slice(i * 512, (i + 1) * 512)
        da = mm_nt(r.dmo[...], r.wd[at, :])
        g, u = r.fa[gate_at(i)], r.fa[up_at(i)]
        sg = 1.0 / (1.0 + jnp.exp(-g))
        r.dg[:, at] = (da * u * (sg * (1.0 + g * (1.0 - sg)))).astype(BF16)
        r.du[:, at] = (da * (g * sg)).astype(BF16)
    dh1 = r.dr[...] + mm_nt(r.dg[...], r.wg[...]) + mm_nt(r.du[...], r.wu[...])
    n1 = r.n1[...]
    gain_attn = jnp.sum(dh1 * n1, axis=0, keepdims=True)
    t1 = dh1 * gain_a
    dr1 = r.ri1[:, 0:1] * (t1 - n1 * jnp.mean(n1 * t1, axis=1, keepdims=True))
    r.dr[...] = dr1
    r.dattn[...] = dr1.astype(BF16)
    r.gl[...] = jnp.concatenate([gain_attn, gain_ffn, jnp.zeros((6, d), F32)], axis=0)
    plane_send(r.gl, r.gl_b.at[e], r.rgl.at[e], 0, 0)
    plane_send_lazy(lambda: (r.oT, r.o2.at[:, own], r.ro2.at[c]), b, 1)
    plane_send_lazy(lambda: (r.dattn, r.da2.at[own, :], r.rda2.at[c]), b, 1)

    r.do_all[s] = mm_nt(r.dattn[...], r.wo[...]).astype(BF16)
    for ch in range(2):
        mine = rows_of(r.do_all, s, ch)
        send(z > 0, mine, mine, r.rdo.at[ch, s], left)
        send(always, mine, mine, r.rdo.at[ch, s], sib)

    stats = jnp.zeros((tok, 128), F32)
    for p in range(pairs):
        prod = r.do_all[s, :, p * 128:(p + 1) * 128].astype(F32) * r.acc[:, p * 128:(p + 1) * 128]
        for h in range(2):
            head = 2 * p + h
            part = jnp.sum(jnp.where(first == (h == 0), prod, 0.0), axis=1, keepdims=True)
            part = jnp.broadcast_to(part, (tok, 128))
            r.delta[p, h * tok:(h + 1) * tok] = part
            stats = jnp.where(lane == head, r.m[p, h * tok:(h + 1) * tok], stats)
            stats = jnp.where(lane == 16 + head, part, stats)
    r.st_all[s] = stats.T[0:32, :]
    send(z > 0, r.st_all.at[s], r.st_all.at[s], r.rst.at[s], left)
    send(always, r.st_all.at[s], r.st_all.at[s], r.rst.at[s], sib)

    def each_source(dst_of, rsem, count):
        for i in range(count):
            arrived(dst_of(i), rsem.at[i])

    end = (z == 0) | (z == nz - 1)

    def on(to_c, some):
        return (c == to_c) & (b < 2) if some else c == to_c

    def share(src_of, dst_of, far_of, to_c, some=False):
        near = lambda: jnp.where(z < nz // 2, 0, nz - 1)
        for i in range(2):
            send_lazy(
                lambda i=i: (
                    on(to_c, some) & end, src_of(jnp.abs(nz - 1 - i - z)), *far_of(i),
                    (b, 2 * jnp.where(z == 0, 1, nz - 2) + to_c),
                )
            )
        send_lazy(
            lambda: (on(to_c, some) & end, src_of(jnp.where(z == 0, 1, nz - 2)), *dst_of(),
                     (b, 2 * jnp.where(z == 0, 1, nz - 2) + to_c))
        )
        send_lazy(
            lambda: (on(to_c, some) & jnp.logical_not(end), src_of(near()), *dst_of(), (b, 2 * near() + to_c))
        )

    def pass_on(own_of, dst_of, far_of, to_c, some=False):
        def here():
            return on(to_c, some) & jnp.logical_not(end)

        for i in range(2):
            def target(i=i):
                return nz - 1 - z if i else jnp.where(z == 1, nz - 1, 0)

            @pl.when(here())
            def _(i=i, target=target):
                far, sem = far_of(i)
                arrived(far, sem)
                far[...] = (own_of(target())[...].astype(F32) + far[...].astype(F32)).astype(BF16)

            send_lazy(lambda i=i, target=target: (here(), far_of(i)[0], *dst_of(), (b, 2 * target() + to_c)))

    gate_up = [
        (
            lambda zz, k=k: r.pgu.at[k, pl.ds(pl.multiple_of(zz * blk, blk), blk), :],
            lambda k=k: (r.rgu.at[k, z], r.zgu.at[k, z]),
            lambda i, k=k: (r.ugu.at[k, i], r.zfar.at[k, i]),
            0,
        )
        for k in range(2)
    ]
    down = (
        lambda zz: r.pdn.at[pl.ds(2 * zz, 2)],
        lambda: (r.rdn.at[z], r.zdn.at[z]),
        lambda i: (r.udn.at[i], r.zfar.at[2, i]),
        1,
    )
    outp = (
        lambda zz: r.pout.at[pl.ds(pl.multiple_of(zz * blk, blk), blk), :],
        lambda: (r.rout.at[z], r.zout.at[z]),
        lambda i: (r.uout.at[i], r.zfar.at[5, i]),
        1,
    )
    attn = [
        (
            lambda zz, k=k: r.pat.at[k, pl.ds(pl.multiple_of(zz * blk, blk), blk), :],
            lambda k=k: (r.rat.at[k, z], r.zat.at[k, z]),
            lambda i, k=k: (r.uat.at[k, i], r.zfar.at[3 + k, i]),
            1,
            k == 0,
        )
        for k in range(2)
    ]

    def hidden_again():
        @pl.when(c == 0)
        def _():
            each_source(lambda i: r.hT_b.at[:, pl.ds(i * tok, tok)], r.rh, 2 * nb)
            for i in range(2 * nb * tok // 512):
                at = slice(i * 512, (i + 1) * 512)
                g = mm(r.wgT[...], r.hT_b[:, at])
                u = mm(r.wuT[...], r.hT_b[:, at])
                sg = 1.0 / (1.0 + jnp.exp(-g))
                r.act_x[:, at] = (g * sg * u).astype(BF16)
                r.fa[:, at] = u * (sg * (1.0 + g * (1.0 - sg)))
                r.fb[:, at] = g * sg

        send_lazy(lambda: (c == 0, r.act_x, r.act_x, r.rax.at[0], sib))

    def hidden_sums():
        @pl.when(c == 1)
        def _():
            each_source(lambda i: r.dmo_b.at[pl.ds(i * tok, tok), :], r.rdmo, 2 * nb)
            rows_d = jnp.concatenate(
                [r.wd[pl.ds(pl.multiple_of(t * nb * units + b * units, units), units), :] for t in range(n)], axis=0
            )
            r.da_x[...] = mm_nt(rows_d, r.dmo_b[...]).astype(BF16)

        send_lazy(lambda: (c == 1, r.da_x, r.da_x, r.rda.at[0], sib))

        @pl.when(c == 1)
        def _():
            arrived(r.act_x, r.rax.at[0])
            r.pdn[...] = mm(r.act_x[...], r.dmo_b[...]).astype(BF16).reshape(n, units, d)

        share(*down)
        for k in range(2):
            @pl.when(c == 0)
            def _(k=k):
                if k == 0:
                    arrived(r.da_x, r.rda.at[0])
                r.dgu[k] = (r.da_x[...].astype(F32) * (r.fb if k else r.fa)[...]).astype(BF16)
                r.pgu[k] = mm_nt(r.hT_b[...], r.dgu[k]).astype(BF16)

            share(*gate_up[k])
        pass_on(*outp)

    @pl.when(c == 1)
    def _():
        for i in range(2):
            arrived(r.o2.at[:, pl.ds(i * tok, tok)], r.ro2.at[i])
            arrived(r.da2.at[pl.ds(i * tok, tok), :], r.rda2.at[i])
        r.pout[...] = mm(r.o2[...], r.da2[...]).astype(BF16)

    share(*outp)

    r.acc[...] = jnp.zeros(r.acc.shape, F32)

    def query_step(kb, _):
        set_bias(kb, True)

        def pair(p, _):
            lanes = pl.ds(pl.multiple_of(p * 128, 128), 128)
            qp, kp, vp = r.q_all[s, :, lanes], r.k_all[kb, :, lanes], r.v_all[kb, :, lanes]
            dop = r.do_all[s, :, lanes]
            pf = jnp.exp(mm_nt(stack(qp), kp) + r.bias[...] - twice(r.m[p]))
            dp = mm_nt(stack(dop), vp)
            ds = (pf * (dp - twice(r.delta[p]))).astype(BF16)
            r.acc[:, lanes] += unstack(mm(ds, kp))
            return 0

        lax.fori_loop(0, pairs, pair, 0, unroll=True)
        return 0

    lax.fori_loop(0, z + 1, query_step, 0)

    def turn_back(src, dst, factor):
        co, si = r.cos[z, own, :], r.sin[z, own, :]
        for p in range(pairs):
            g = src[:, p * 128:(p + 1) * 128] * factor
            dst[:, p * 128:(p + 1) * 128] = (g * co - turn(g) * si).astype(BF16)

    turn_back(r.acc, r.dq, 0.125)

    def attn_send(k, pair, also=None):
        for i, value in enumerate(pair):
            for h in range(2):
                plane_send_lazy(
                    lambda value=value, h=h: (
                        value.at[:, pl.ds(h * dh, dh)], r.at_b.at[k, tokens, :], r.rat_in.at[k, e]
                    ),
                    2 * i + h,
                    1,
                    also,
                )

    attn_send(0, (r.dq,))
    hidden_again()

    r.acc[...] = jnp.zeros(r.acc.shape, F32)
    r.acc2[...] = jnp.zeros(r.acc2.shape, F32)

    def key_step(j):
        qb = z + j
        mine, other = 2 * qb + c, 2 * qb + 1 - c

        @pl.when(j > 0)
        def _():
            arrived(r.id_all.at[mine], r.rid.at[mine])
            arrived(r.id_all.at[other], r.rid.at[other])
            arrived(r.q_all.at[mine], r.rq.at[mine])
            remote(r.q_all.at[mine], r.q_all.at[mine], r.bsem.at[2, mine], r.rq.at[mine], sib).start()
            blocks = [(rows_of(r.do_all, mine, ch), r.rdo.at[ch, mine]) for ch in range(2)]
            blocks.append((r.st_all.at[mine], r.rst.at[mine]))
            for i, (got, sem) in enumerate(blocks):
                arrived(got, sem)

                @pl.when(z > 0)
                def _():
                    remote(got, got, r.fsem.at[2 + i, mine], sem, left).start()

                remote(got, got, r.bsem.at[3 + i, mine], sem, sib).start()

        arrived(r.q_all.at[other], r.rq.at[other])
        for ch in range(2):
            arrived(rows_of(r.do_all, other, ch), r.rdo.at[ch, other])
        arrived(r.st_all.at[other], r.rst.at[other])
        set_bias(qb, False)

        def pair(p, _):
            lanes = pl.ds(pl.multiple_of(p * 128, 128), 128)
            kp, vp = r.k_all[z, own, lanes], r.v_all[z, own, lanes]
            qp = r.q_all[pl.ds(2 * qb, 2), :, lanes].reshape(2 * tok, 128)
            dop = r.do_all[pl.ds(2 * qb, 2), :, lanes].reshape(2 * tok, 128)

            def row(base):
                return jnp.concatenate(
                    [
                        jnp.broadcast_to(
                            jnp.concatenate(
                                [r.st_all[2 * qb + i, pl.ds(base + 2 * p + h, 1), :] for i in range(2)], axis=1
                            ),
                            (tok, 2 * tok),
                        )
                        for h in range(2)
                    ],
                    axis=0,
                )

            pf = jnp.exp(mm_nt(stack(kp), qp) + r.bias[...] - row(0))
            dp = mm_nt(stack(vp), dop)
            ds = (pf * (dp - row(16))).astype(BF16)
            r.acc2[:, lanes] += unstack(mm(pf.astype(BF16), dop))
            r.acc[:, lanes] += unstack(mm(ds, qp))
            return 0

        lax.fori_loop(0, pairs, pair, 0, unroll=True)

    def keys_done():
        turn_back(r.acc, r.dk, 1.0)
        r.dv[...] = r.acc2[...].astype(BF16)
        attn_send(1, (r.dk, r.dv))
    last = nz - z
    sums_at = jnp.where(z == 0, 2, last)

    def key_loop(j, _):
        pl.when(j == sums_at)(hidden_sums)

        @pl.when(j < last)
        def _():
            key_step(j)

        pl.when(j == last - 1)(keys_done)
        return 0

    lax.fori_loop(0, last + 1, key_loop, 0)
    r.gin_v[...] = (
        r.dr[...] + mm_nt(r.dq[...], r.wq[...]) + mm_nt(r.dk[...], r.wk[...]) + mm_nt(r.dv[...], r.wv[...])
    )
    pltpu.make_async_copy(r.gin_v, r.gin_h, r.osem.at[1]).start()


    @pl.when(c == 1)
    def _():
        each_source(lambda i: r.xT_b.at[:, pl.ds(i * tok, tok)], r.rxt, 2 * nb)

    def attn_sum(k):
        @pl.when(on(1, k == 0))
        def _():
            each_source(lambda i: r.at_b.at[k, pl.ds(i * tok, tok), :], r.rat_in.at[k], 2 * nb)
            r.pat[k] = mm(r.xT_b[...], r.at_b[k]).astype(BF16)

        share(*attn[k])

    def totals(total_of, own, recv_of, rsem_of):
        def add(slots):
            total = own().astype(F32)
            for at in slots:
                arrived(recv_of(at), rsem_of(at))
                total = total + recv_of(at)[...].astype(F32)
            total_of()[...] = total.astype(BF16).reshape(total_of().shape)

        pl.when(end)(lambda: add((1, 2)))
        pl.when(jnp.logical_not(end))(lambda: add((jnp.where(z == 1, 0, nz - 1), nz - 1 - z)))

    def spread(src_of, dst_of, from_c, some=False):
        for bb in range(nb):
            for cc in range(2):
                def here(bb=bb, cc=cc):
                    return (b == bb) & (c == cc)

                send_lazy(
                    lambda bb=bb, cc=cc, here=here: (
                        on(from_c, some) & jnp.logical_not(here()), src_of(cc), *dst_of(), (bb, 2 * z + cc)
                    )
                )

                @pl.when(on(from_c, some) & here())
                def _(cc=cc):
                    pltpu.make_async_copy(src_of(cc), *dst_of()).start()

    rows = pl.ds(pl.multiple_of(z * blk, blk), blk)
    quarter = blk // 4

    def out_total():
        @pl.when(c == 1)
        def _():
            total = None
            for bb in range(nb):
                arrived(r.rso.at[bb], r.rrso.at[bb])
                part = r.rso[bb].astype(F32)
                total = part if total is None else total + part
            r.fso[...] = total.astype(BF16)

        spread(lambda cc: r.fso.at[cc], lambda: (r.oout_h.at[b], r.fout.at[b]), 1)

    def gate_up_total(k):
        @pl.when(c == 0)
        def _():
            totals(
                lambda: r.sgu.at[k], lambda: r.pgu[k, rows, :], lambda at: r.rgu.at[k, at], lambda at: r.zgu.at[k, at]
            )

        spread(
            lambda cc: r.sgu.at[k, pl.ds(cc * (blk // 2), blk // 2), :], lambda: (r.ogu_h.at[b, k], r.fgu.at[k, b]), 0
        )

    attn_sum(0)
    @pl.when(c == 1)
    def _():
        totals(lambda: r.sout, lambda: r.pout[rows, :], lambda at: r.rout.at[at], lambda at: r.zout.at[at])

    for bb in range(nb):
        at = (slice(None), pl.ds((bb // 2) * quarter, quarter), pl.ds((bb % 2) * dh, dh))
        send((c == 1) & (b != bb), r.sout.at[at], r.rso.at[b], r.rrso.at[b], (bb, s))

        @pl.when((c == 1) & (b == bb))
        def _(at=at):
            pltpu.make_async_copy(r.sout.at[at], r.rso.at[b], r.rrso.at[b]).start()

    pass_on(*gate_up[0])
    gate_up_total(0)
    pass_on(*gate_up[1])
    gate_up_total(1)
    pass_on(*down)
    attn_sum(1)
    pass_on(*attn[0])
    out_total()

    adds = (b == 0) & (c == 0)

    @pl.when(adds)
    def _():
        total = None
        for i in range(2 * nb):
            arrived(r.gl_b.at[i], r.rgl.at[i])
            total = r.gl_b[i] if total is None else total + r.gl_b[i]
        r.gz[z] = total

    for zz in range(nz):
        send(adds & (z != zz), r.gz.at[z], r.gz.at[z], r.zgl.at[z], (0, 2 * zz))

    @pl.when(adds)
    def _():
        total = r.gz[z]
        for dz in range(1, nz):
            at = lax.rem(z + dz, nz)
            arrived(r.gz.at[at], r.zgl.at[at])
            total = total + r.gz[at]
        r.gsum[...] = total

    for bb in range(nb):
        for cc in range(2):
            here = (bb == 0) and (cc == 0)
            if not here:
                send(adds, r.gsum, r.ogl_h, r.fgl.at[0], (bb, 2 * z + cc))

    @pl.when(adds)
    def _():
        pltpu.make_async_copy(r.gsum, r.ogl_h, r.fgl.at[0]).start()

    @pl.when(c == 1)
    def _():
        totals(lambda: r.sdn, lambda: r.pdn[pl.ds(2 * z, 2)], lambda at: r.rdn.at[at], lambda at: r.zdn.at[at])

    spread(lambda cc: r.sdn.at[cc], lambda: (r.odn_h.at[b], r.fdn.at[b]), 1)
    pass_on(*attn[1])
    for k in range(2):
        @pl.when(on(1, k == 0))
        def _(k=k):
            totals(
                lambda: r.sat.at[k], lambda: r.pat[k, rows, :], lambda at: r.rat.at[k, at], lambda at: r.zat.at[k, at]
            )

        spread(
            lambda cc: r.sat.at[k, pl.ds(cc * (blk // 2), blk // 2), :], lambda: (r.oat_h.at[b, k], r.fat.at[k, b]), 1,
            k == 0,
        )

    for bb in range(nb):
        arrived(r.ogu_h.at[bb, 0], r.fgu.at[0, bb])
        arrived(r.ogu_h.at[bb, 1], r.fgu.at[1, bb])
        arrived(r.odn_h.at[bb], r.fdn.at[bb])
        if bb < 2:
            arrived(r.oat_h.at[bb, 0], r.fat.at[0, bb])
        arrived(r.oout_h.at[bb], r.fout.at[bb])
        arrived(r.oat_h.at[bb, 1], r.fat.at[1, bb])
    arrived(r.ogl_h, r.fgl.at[0])
    out_copy.wait()
    pltpu.make_async_copy(r.gin_v, r.gin_h, r.osem.at[1]).wait()
    assert used[0] <= r.ssem.shape[0], used
    for make, at in pending:
        cond, src, dst, rsem, dev = make()

        @pl.when(cond)
        def _():
            remote(src, dst, r.ssem.at[at], rsem, dev).wait_send()

    def sent_on(t, _):
        @pl.when((lax.rem(t, 2) == c) & (t < s))
        def _():
            for ch in range(2):
                got = rows_of(r.x_all, t, ch)
                remote(got, got, r.bsem.at[ch, t], r.rx.at[ch, t], sib).wait_send()

                @pl.when(z + 1 < nz)
                def _():
                    remote(got, got, r.fsem.at[ch, t], r.rx.at[ch, t], right).wait_send()

        @pl.when((lax.rem(t, 2) == c) & (t > s))
        def _():
            remote(r.q_all.at[t], r.q_all.at[t], r.bsem.at[2, t], r.rq.at[t], sib).wait_send()
            blocks = [(rows_of(r.do_all, t, ch), r.rdo.at[ch, t]) for ch in range(2)]
            blocks.append((r.st_all.at[t], r.rst.at[t]))
            for i, (got, sem) in enumerate(blocks):
                remote(got, got, r.bsem.at[3 + i, t], sem, sib).wait_send()

                @pl.when(z > 0)
                def _():
                    remote(got, got, r.fsem.at[2 + i, t], sem, left).wait_send()
        return 0

    lax.fori_loop(0, n, sent_on, 0)


def unpack_kernel(
    n, nb, out_in, gin_in, oat_h, ogu_h, odn_h, oout_h, ogl_h,
    out, gin, gq_h, gk_h, gv_h, go_h, gg_h, gu_h, gd_h, g1, g2,
    oat, ogu, odn, oout, ogl, gq, gk, gv, go, gg, gu, gd, out_v, gin_v, isem, osem,
):
    s = lax.axis_index("seq")
    fs = ogu.shape[3]
    units, dh = odn.shape[1], odn.shape[2] // 2
    copy = pltpu.make_async_copy
    loads = [copy(a, b, isem.at[i]) for i, (a, b) in enumerate(
        ((ogu_h, ogu), (oat_h, oat), (odn_h, odn), (ogl_h, ogl), (out_in, out_v), (gin_in, gin_v), (oout_h, oout)))]
    stores = [copy(a, b, osem.at[i]) for i, (a, b) in enumerate(
        ((gg, gg_h), (gu, gu_h), (gq, gq_h), (gk, gk_h), (gv, gv_h), (go, go_h), (gd, gd_h),
         (out_v, out.at[0]), (gin_v, gin.at[0])))]
    for load in loads:
        load.start()
    loads[0].wait()
    low = lax.broadcasted_iota(jnp.int32, (ogu.shape[2], 128), 1) < 64

    def interleave(k, dst):
        for t in range(n):
            for y in range(2):
                at = slice((t // 2) * 128, (t // 2 + 1) * 128)
                one, two = ogu[2 * y, k, :, at].astype(F32), ogu[2 * y + 1, k, :, at].astype(F32)
                if t % 2:
                    one = pltpu.roll(one, 64, 1)
                else:
                    two = pltpu.roll(two, 64, 1)
                dst[:, (2 * t + y) * 128:(2 * t + y + 1) * 128] = jnp.where(low, one, two)

    interleave(0, gg)
    stores[0].start()
    interleave(1, gu)
    stores[1].start()
    loads[1].wait()
    for m, (ref, k, bb) in enumerate(((gq, 0, 0), (gk, 1, 0), (gv, 1, 2))):
        ref[:, :dh] = oat[bb, k].astype(F32)
        ref[:, dh:] = oat[bb + 1, k].astype(F32)
        stores[2 + m].start()
    loads[6].wait()
    part = oout.shape[1]
    for bb in range(nb):
        go[(bb // 2) * part:(bb // 2 + 1) * part, (bb % 2) * dh:(bb % 2 + 1) * dh] = oout[bb].astype(F32)
    stores[5].start()
    loads[2].wait()
    for bb in range(nb):
        gd[bb * units:(bb + 1) * units, :] = odn[bb].astype(F32)
    stores[6].start()
    for i in (4, 5):
        loads[i].wait()
        stores[3 + i].start()
    loads[3].wait()
    d = ogl.shape[1]
    own = d // n
    gains = pltpu.roll(ogl[...], lax.rem(d - s * own, d), 1)
    g1[...] = gains[0:1, :own]
    g2[...] = gains[1:2, :own]
    for store in stores:
        store.wait()


def rope_constants(length, head_dim):
    half = head_dim // 2
    inverse = np.exp(-2.0 * math.log(THETA) / head_dim * np.arange(half)).astype(np.float32)
    angle = np.arange(length, dtype=np.float32)[:, None] * inverse
    cos, sin = np.cos(angle.astype(np.float64)), np.sin(angle.astype(np.float64))
    return (
        np.concatenate([cos, cos, cos, cos], 1).astype(np.float32),
        np.concatenate([-sin, sin, -sin, sin], 1).astype(np.float32),
    )


def fused_local(n, nb, tokens, doc_ids, w_query, w_key, w_value, w_out, w_gate, w_up, w_down, gain_attn, gain_ffn, cotangent):
    _, tok, d = tokens.shape
    f = w_gate.shape[1]
    nz = n // 2
    cos, sin = rope_constants(n * tok, d // HEADS)
    cos = jnp.asarray(cos.reshape(nz, 2 * tok, 128))
    sin = jnp.asarray(sin.reshape(nz, 2 * tok, 128))
    plan = scratch_plan(tok, d, f, n, nb)
    vmem, anywhere = pl.BlockSpec(memory_space=pltpu.VMEM), pl.BlockSpec(memory_space=pl.ANY)
    shape = jax.ShapeDtypeStruct
    parts = pl.pallas_call(
        functools.partial(layer_kernel, tuple(plan), tok, d, f, n, nb),
        out_shape=(
            shape((tok, d), F32), shape((tok, d), F32), shape((nb, 2, d // n, d // 2), BF16),
            shape((nb, 2, d // n, f // nb), BF16), shape((nb, f // (nb * n), d), BF16), shape((nb, d // (2 * n), d // 2), BF16), shape((8, d), F32),
        ),
        in_specs=[vmem] * 5 + [anywhere] * 9,
        out_specs=[anywhere] * 7,
        scratch_shapes=list(plan.values()),
        compiler_params=pltpu.CompilerParams(
            collective_id=0, has_side_effects=True, vmem_limit_bytes=62 * 2**20
        ),
        name="layer",
    )(
        doc_ids, tokens, cotangent, gain_attn, gain_ffn, cos, sin,
        w_query, w_key, w_value, w_out, w_gate, w_up, w_down,
    )
    own = d // n
    grads = [shape((own, d), F32)] * 4 + [shape((own, f), F32)] * 2 + [shape((f // n, d), F32)]
    results = pl.pallas_call(
        functools.partial(unpack_kernel, n, nb),
        out_shape=(shape((1, tok, d), F32), shape((1, tok, d), F32), *grads, shape((1, own), F32), shape((1, own), F32)),
        in_specs=[pl.BlockSpec(memory_space=pltpu.HBM)] * 7,
        out_specs=[anywhere] * 9 + [vmem] * 2,
        scratch_shapes=[pltpu.VMEM(parts[i].shape, parts[i].dtype) for i in (2, 3, 4, 5, 6)]
        + [pltpu.VMEM(g.shape, g.dtype) for g in grads]
        + [pltpu.VMEM((tok, d), F32)] * 2
        + [pltpu.SemaphoreType.DMA((7,)), pltpu.SemaphoreType.DMA((9,))],
        compiler_params=pltpu.CompilerParams(vmem_limit_bytes=62 * 2**20),
        name="unpack",
    )(*parts)
    return results[:9] + (results[9].reshape(own), results[10].reshape(own))


def fits(shapes, n, nb):
    (_, tok, d), f = shapes[0], shapes[6][1]
    return (
        nb == 4 and n == 8 and n * tok <= 1024 and tok == 128 and shapes[0][0] == 1
        and d == HEADS * 64 and d % 256 == 0 and d % (32 * n) == 0 and f == 2 * tok * n and f % 512 == 0
    )


def solution(mesh):
    nb, n = mesh.shape["batch"], mesh.shape["seq"]

    def either(*args):
        shapes = [a.shape for a in args]
        if fits(shapes, n, nb):
            return fused_local(n, nb, *args)
        return local(*args)

    return jax.shard_map(
        either,
        mesh=mesh,
        in_specs=(
            P("batch", "seq", None),
            P("batch", "seq"),
            P(),
            P(),
            P(),
            P(),
            P(),
            P(),
            P(),
            P(),
            P(),
            P("batch", "seq", None),
        ),
        out_specs=(
            P("batch", "seq", None),
            P("batch", "seq", None),
            P("seq", None),
            P("seq", None),
            P("seq", None),
            P("seq", None),
            P("seq", None),
            P("seq", None),
            P("seq", None),
            P("seq"),
            P("seq"),
        ),
        check_vma=False,
    )
```

```python
import functools
import math
import types

import jax
import jax.numpy as jnp
import numpy as np
from jax import lax
from jax.experimental import pallas as pl
from jax.experimental.pallas import tpu as pltpu
from jax.sharding import PartitionSpec as P

HEADS = 12
NSEG = 8


EPSILON = 1e-06
THETA = 10000.0
MASKED = -1e30


def root_mean_square_norm(values, gain):
    return values * lax.rsqrt(jnp.mean(values * values, -1, keepdims=True) + EPSILON) * gain


def swiglu(gate, up_part):
    return jax.nn.silu(gate) * up_part


def rope_tables(positions, head_dim):
    half_dim = head_dim // 2
    inverse = jnp.exp(-2.0 * math.log(THETA) / head_dim * jnp.arange(half_dim, dtype=jnp.float32))
    angle = positions.astype(jnp.float32)[..., None] * inverse
    return (
        jnp.concatenate([jnp.cos(angle), jnp.cos(angle)], -1),
        jnp.concatenate([jnp.sin(angle), jnp.sin(angle)], -1),
    )


def rotate(values, cosine, sine):
    half_dim = values.shape[-1] // 2
    turned = jnp.concatenate([-values[..., half_dim:], values[..., :half_dim]], -1)
    return values * cosine + turned * sine


def rotate_back(grads, cosine, sine):
    half_dim = grads.shape[-1] // 2
    turned = grads * sine
    return grads * cosine + jnp.concatenate([turned[..., half_dim:], -turned[..., :half_dim]], -1)


def block_size(total_rows):
    return max((d for d in range(1, min(total_rows, 2048) + 1) if total_rows % d == 0))


def doc_begin(segment_begins, where_at):
    earlier = segment_begins[:, None, :] <= where_at[:, :, None]
    return jnp.max(jnp.where(earlier, segment_begins[:, None, :], 0), -1)


def outer_sum(remaining_tokens, right):
    return lax.dot_general(
        remaining_tokens, right, (((0,), (0,)), ((), ())), preferred_element_type=jnp.float32
    )


def back_product(grads, weight_matrix):
    return lax.dot_general(
        grads, weight_matrix, (((1,), (1,)), ((), ())), preferred_element_type=jnp.float32
    )


def masked_scores(queries, key_block, key_at, query_at, query_begin):
    batch_rows, block_rows, model_width = key_block.shape
    head_count = queries.shape[2]
    head_dim = model_width // head_count
    key_heads = key_block.reshape(batch_rows, block_rows, head_count, head_dim)
    scores = jnp.einsum(
        "bqhd,bkhd->bhqk", queries, key_heads, preferred_element_type=jnp.float32
    ) * (1.0 / math.sqrt(head_dim))
    key_pos = key_at[None, None, :]
    query_pos = query_at[:, :, None]
    begin_pos = query_begin[:, :, None]
    allowed = (
        (key_pos <= query_pos) & (key_pos >= begin_pos) & ((begin_pos > 0) | (key_pos == query_pos))
    )
    return (scores, allowed[:, None], key_heads)


def grad_terms(
    queries, grad_heads, lse, delta, query_at, query_begin, key_block, value_block, key_at
):
    scores, allowed, key_heads = masked_scores(queries, key_block, key_at, query_at, query_begin)
    value_heads = value_block.reshape(key_heads.shape)
    probs = jnp.where(allowed, jnp.exp(scores - lse[..., None]), 0.0)
    dprob = jnp.einsum(
        "bqhd,bkhd->bhqk", grad_heads, value_heads, preferred_element_type=jnp.float32
    )
    dscore = (probs * (dprob - delta[..., None])).astype(jnp.bfloat16)
    return (probs.astype(jnp.bfloat16), dscore, key_heads, value_heads)


def over_rows(update, carried, arrays, first_row):
    total_rows = arrays[0].shape[1]
    block_rows = block_size(total_rows)

    def over_step(block_index, state):
        offset = block_index * block_rows
        blocks = tuple((lax.dynamic_slice_in_dim(item, offset, block_rows, 1) for item in arrays))
        key_at = first_row + offset + jnp.arange(block_rows, dtype=jnp.int32)
        return update(state, blocks, key_at)

    return lax.fori_loop(0, total_rows // block_rows, over_step, carried)


def local(
    tokens,
    doc_ids,
    w_query,
    w_key,
    w_value,
    w_out,
    w_gate,
    w_up,
    w_down,
    gain_attn,
    gain_ffn,
    cotangent,
):
    batch_rows, local_len, model_width = tokens.shape
    head_count = HEADS
    head_dim = model_width // head_count
    shape_heads = (batch_rows, local_len, head_count, head_dim)
    scale = 1.0 / math.sqrt(head_dim)
    labels = jnp.arange(NSEG, dtype=jnp.int32)
    member = (doc_ids[:, :, None] == labels).astype(jnp.int32)
    totals = lax.psum(jnp.sum(member, 1), "seq")
    segment_begins = jnp.cumsum(totals, 1) - totals
    local_at = lax.axis_index("seq") * local_len + jnp.arange(local_len, dtype=jnp.int32)
    query_at = jnp.broadcast_to(local_at, (batch_rows, local_len))
    query_begin = doc_begin(segment_begins, query_at)
    cosine, sine = rope_tables(query_at - query_begin, head_dim)
    cosine = cosine[:, :, None, :]
    sine = sine[:, :, None, :]
    flat_tokens = tokens.reshape(batch_rows * local_len, model_width)
    queries = rotate(
        jnp.dot(flat_tokens, w_query, preferred_element_type=jnp.float32).reshape(shape_heads),
        cosine,
        sine,
    ).astype(jnp.bfloat16)
    key_send = (
        rotate(
            jnp.dot(flat_tokens, w_key, preferred_element_type=jnp.float32).reshape(shape_heads),
            cosine,
            sine,
        )
        .astype(jnp.bfloat16)
        .reshape(batch_rows, local_len, model_width)
    )
    value_send = (
        jnp.dot(flat_tokens, w_value, preferred_element_type=jnp.float32)
        .astype(jnp.bfloat16)
        .reshape(batch_rows, local_len, model_width)
    )

    def stats_step(state, blocks, key_at):
        run_max, run_sum = state
        scores, allowed, key_heads = masked_scores(
            queries, blocks[0], key_at, query_at, query_begin
        )
        scores = jnp.where(allowed, scores, MASKED)
        new_max = jnp.maximum(run_max, jnp.max(scores, -1))
        weights = jnp.where(allowed, jnp.exp(scores - new_max[..., None]), 0.0)
        return (new_max, run_sum * jnp.exp(run_max - new_max) + jnp.sum(weights, -1))

    stats_init = (
        jnp.full((batch_rows, head_count, local_len), MASKED, jnp.float32),
        jnp.zeros((batch_rows, head_count, local_len), jnp.float32),
    )
    zero_heads = jnp.zeros(shape_heads, jnp.float32)
    run_max, run_sum = over_rows(
        stats_step, stats_init, (lax.all_gather(key_send, "seq", axis=1, tiled=True),), jnp.int32(0)
    )
    lse = run_max + jnp.log(run_sum)

    def output_step(state, blocks, key_at):
        scores, allowed, key_heads = masked_scores(
            queries, blocks[0], key_at, query_at, query_begin
        )
        value_heads = blocks[1].reshape(key_heads.shape)
        probs = jnp.where(allowed, jnp.exp(scores - lse[..., None]), 0.0).astype(jnp.bfloat16)
        return state + jnp.einsum(
            "bhqk,bkhd->bqhd", probs, value_heads, preferred_element_type=jnp.float32
        )

    attended = over_rows(
        output_step,
        zero_heads,
        (
            lax.all_gather(key_send, "seq", axis=1, tiled=True),
            lax.all_gather(value_send, "seq", axis=1, tiled=True),
        ),
        jnp.int32(0),
    )
    attended_low = attended.astype(jnp.bfloat16).reshape(batch_rows * local_len, model_width)
    first_sum = flat_tokens.astype(jnp.float32) + jnp.dot(
        attended_low, w_out, preferred_element_type=jnp.float32
    )
    hidden, norm_first_back = jax.vjp(root_mean_square_norm, first_sum, gain_attn)
    hidden_low = hidden.astype(jnp.bfloat16)
    gate = jnp.dot(hidden_low, w_gate, preferred_element_type=jnp.float32)
    up_part = jnp.dot(hidden_low, w_up, preferred_element_type=jnp.float32)
    active, swiglu_back = jax.vjp(swiglu, gate, up_part)
    active_low = active.astype(jnp.bfloat16)
    second_sum = hidden + jnp.dot(active_low, w_down, preferred_element_type=jnp.float32)
    output, norm_second_back = jax.vjp(root_mean_square_norm, second_sum, gain_ffn)
    second_grad, grad_gain_ffn = norm_second_back(
        cotangent.reshape(batch_rows * local_len, model_width).astype(jnp.float32)
    )
    branch_grad = second_grad.astype(jnp.bfloat16)
    grad_down = outer_sum(active_low, branch_grad)
    gate_grad, up_grad = swiglu_back(back_product(branch_grad, w_down))
    gate_low = gate_grad.astype(jnp.bfloat16)
    up_low = up_grad.astype(jnp.bfloat16)
    grad_gate = outer_sum(hidden_low, gate_low)
    grad_up = outer_sum(hidden_low, up_low)
    hidden_grad = second_grad + back_product(gate_low, w_gate) + back_product(up_low, w_up)
    first_grad, grad_gain_attn = norm_first_back(hidden_grad)
    attn_grad = first_grad.astype(jnp.bfloat16)
    grad_out = outer_sum(attended_low, attn_grad)
    grad_heads = back_product(attn_grad, w_out).astype(jnp.bfloat16).reshape(shape_heads)
    delta = jnp.swapaxes(jnp.sum(grad_heads.astype(jnp.float32) * attended, -1), 1, 2)

    def query_step(state, blocks, key_at):
        probs_low, dscore, key_heads, value_heads = grad_terms(
            queries, grad_heads, lse, delta, query_at, query_begin, blocks[0], blocks[1], key_at
        )
        return (
            state
            + jnp.einsum("bhqk,bkhd->bqhd", dscore, key_heads, preferred_element_type=jnp.float32)
            * scale
        )

    all_keys, all_values = (
        lax.all_gather(key_send, "seq", axis=1, tiled=True),
        lax.all_gather(value_send, "seq", axis=1, tiled=True),
    )
    query_grad = over_rows(query_step, zero_heads, (all_keys, all_values), 0)
    first_row = jnp.int32(0)
    span_rows = local_len * lax.axis_size("seq")
    block_rows = block_size(span_rows)
    empty = jnp.zeros((batch_rows, span_rows, head_count, head_dim), jnp.float32)

    def key_step(block_index, state):
        offset = block_index * block_rows
        key_block = lax.dynamic_slice_in_dim(all_keys, offset, block_rows, 1)
        value_block = lax.dynamic_slice_in_dim(all_values, offset, block_rows, 1)
        key_at = first_row + offset + jnp.arange(block_rows, dtype=jnp.int32)
        probs_low, dscore, key_heads, value_heads = grad_terms(
            queries, grad_heads, lse, delta, query_at, query_begin, key_block, value_block, key_at
        )
        key_part = (
            jnp.einsum("bhqk,bqhd->bkhd", dscore, queries, preferred_element_type=jnp.float32)
            * scale
        )
        value_part = jnp.einsum(
            "bhqk,bqhd->bkhd", probs_low, grad_heads, preferred_element_type=jnp.float32
        )
        return (
            lax.dynamic_update_slice_in_dim(state[0], key_part, offset, 1),
            lax.dynamic_update_slice_in_dim(state[1], value_part, offset, 1),
        )

    key_all, value_all = lax.fori_loop(0, span_rows // block_rows, key_step, (empty, empty))
    joined = jnp.concatenate(
        [
            key_all.reshape(batch_rows, span_rows, model_width),
            value_all.reshape(batch_rows, span_rows, model_width),
        ],
        -1,
    )
    summed_keys = jnp.swapaxes(
        lax.psum_scatter(jnp.swapaxes(joined, 0, 1), "seq", scatter_dimension=0, tiled=True), 0, 1
    )
    key_grad = summed_keys[..., :model_width].reshape(shape_heads)
    value_grad = summed_keys[..., model_width:]
    flat_len = batch_rows * local_len
    query_low = (
        rotate_back(query_grad, cosine, sine).astype(jnp.bfloat16).reshape(flat_len, model_width)
    )
    key_low = (
        rotate_back(key_grad, cosine, sine).astype(jnp.bfloat16).reshape(flat_len, model_width)
    )
    value_low = value_grad.astype(jnp.bfloat16).reshape(flat_len, model_width)
    grad_input = (
        first_grad
        + back_product(query_low, w_query)
        + back_product(key_low, w_key)
        + back_product(value_low, w_value)
    )
    grad_query = outer_sum(flat_tokens, query_low)
    grad_key = outer_sum(flat_tokens, key_low)
    value_weight_gradient = outer_sum(flat_tokens, value_low)
    shares = (
        lax.psum_scatter(grad_query, "seq", scatter_dimension=0, tiled=True),
        lax.psum_scatter(grad_key, "seq", scatter_dimension=0, tiled=True),
        lax.psum_scatter(value_weight_gradient, "seq", scatter_dimension=0, tiled=True),
        lax.psum_scatter(grad_out, "seq", scatter_dimension=0, tiled=True),
        lax.psum_scatter(grad_gate, "seq", scatter_dimension=0, tiled=True),
        lax.psum_scatter(grad_up, "seq", scatter_dimension=0, tiled=True),
        lax.psum_scatter(grad_down, "seq", scatter_dimension=0, tiled=True),
        lax.psum_scatter(grad_gain_attn, "seq", scatter_dimension=0, tiled=True),
        lax.psum_scatter(grad_gain_ffn, "seq", scatter_dimension=0, tiled=True),
    )
    results = (
        lax.psum(shares[0].astype(jnp.bfloat16), "batch").astype(jnp.float32),
        lax.psum(shares[1].astype(jnp.bfloat16), "batch").astype(jnp.float32),
        lax.psum(shares[2].astype(jnp.bfloat16), "batch").astype(jnp.float32),
        lax.psum(shares[3].astype(jnp.bfloat16), "batch").astype(jnp.float32),
        lax.psum(shares[4].astype(jnp.bfloat16), "batch").astype(jnp.float32),
        lax.psum(shares[5].astype(jnp.bfloat16), "batch").astype(jnp.float32),
        lax.psum(shares[6].astype(jnp.bfloat16), "batch").astype(jnp.float32),
        lax.psum(shares[7].astype(jnp.bfloat16), "batch").astype(jnp.float32),
        lax.psum(shares[8].astype(jnp.bfloat16), "batch").astype(jnp.float32),
    )
    output_rows = output.reshape(batch_rows, local_len, model_width)
    input_rows = grad_input.reshape(batch_rows, local_len, model_width)
    return (
        output_rows,
        input_rows,
        results[0],
        results[1],
        results[2],
        results[3],
        results[4],
        results[5],
        results[6],
        results[7],
        results[8],
    )


MESH = pl.DeviceIdType.MESH
F32 = jnp.float32
BF16 = jnp.bfloat16


def mm(a, b):
    return lax.dot_general(a, b, (((1,), (0,)), ((), ())), preferred_element_type=F32)


def mm_nt(a, b):
    return lax.dot_general(a, b, (((1,), (1,)), ((), ())), preferred_element_type=F32)


def scratch_plan(tok, d, f, n, nb):
    nz, plane, heads = n // 2, 2 * nb * tok, HEADS
    vm = pltpu.VMEM
    dma = lambda *shape: pltpu.SemaphoreType.DMA(shape)
    return dict(
        wq=vm((d, d), BF16), wk=vm((d, d), BF16), wv=vm((d, d), BF16), wo=vm((d, d), BF16),
        wg=vm((d, f), BF16), wu=vm((d, f), BF16), wd=vm((f, d), BF16),
        cos=vm((nz, 2 * tok, 128), F32), sin=vm((nz, 2 * tok, 128), F32),
        x_all=vm((n, tok, d), BF16), q_all=vm((n, tok, d), BF16), do_all=vm((n, tok, d), BF16),
        k_all=vm((nz, 2 * tok, d), BF16), v_all=vm((nz, 2 * tok, d), BF16),
        st_all=vm((n, 32, tok), F32), id_all=vm((n, 8, tok), jnp.int32),
        idcol=vm((tok, 128), F32), bias=vm((2 * tok, 2 * tok), F32),
        m=vm((heads // 2, 2 * tok, 128), F32), l=vm((heads // 2, 2 * tok, 128), F32),
        delta=vm((heads // 2, 2 * tok, 128), F32),
        acc=vm((tok, d), F32), acc2=vm((tok, d), F32),
        olow=vm((tok, d), BF16), hb=vm((tok, d), BF16), h1=vm((tok, d), F32), n1=vm((tok, d), F32),
        ri1=vm((tok, 128), F32), dr=vm((tok, d), F32),
        act=vm((tok, f), BF16),
        dg=vm((tok, f), BF16), du=vm((tok, f), BF16), dmo=vm((tok, d), BF16), dattn=vm((tok, d), BF16),
        dq=vm((tok, d), BF16), dk=vm((tok, d), BF16), dv=vm((tok, d), BF16),
        hT=vm((d, tok), BF16), xT=vm((d, tok), BF16), oT=vm((d, tok), BF16),
        gl=vm((8, d), F32), out_v=vm((tok, d), F32), gin_v=vm((tok, d), F32),
        hT_b=vm((d, plane), BF16), dmo_b=vm((plane, d), BF16),
        wgT=vm((f // nb, d), BF16), wuT=vm((f // nb, d), BF16), tmpT=vm((128, d), BF16),
        act_x=vm((f // nb, plane), BF16), da_x=vm((f // nb, plane), BF16),
        fa=vm((f // nb, plane), F32), fb=vm((f // nb, plane), F32), dgu=vm((2, f // nb, plane), BF16),
        xT_b=vm((d, plane), BF16), o2=vm((d, 2 * tok), BF16), da2=vm((2 * tok, d), BF16), at_b=vm((2, plane, d // 2), BF16), gl_b=vm((2 * nb, 8, d), F32),
        pgu=vm((2, d, f // nb), BF16), pdn=vm((n, f // (nb * n), d), BF16),
        pat=vm((d, d // 2), BF16), pq=vm((n, d // (2 * n), d // 2), BF16), pout=vm((d, d), BF16),
        ugu=vm((2, 2, d // nz, f // nb), BF16), udn=vm((2, 2, f // (nb * n), d), BF16),
        uat=vm((2, d // nz, d // 2), BF16), uq=vm((2, 2, d // (2 * n), d // 2), BF16),
        uout=vm((2, d // nz, d), BF16), rout=vm((nz, d // nz, d), BF16), sout=vm((2, d // n, d), BF16),
        rso=vm((nb, 2, d // (2 * n), d // 2), BF16), fso=vm((2, d // (2 * n), d // 2), BF16),
        rgu=vm((2, nz, d // nz, f // nb), BF16), rdn=vm((nz, 2, f // (nb * n), d), BF16), rat=vm((nz, d // nz, d // 2), BF16), rqz=vm((nz, 2, d // (2 * n), d // 2), BF16),
        sgu=vm((2, d // nz, f // nb), BF16), sdn=vm((2, f // (nb * n), d), BF16), sat=vm((d // nz, d // 2), BF16), sq=vm((2, d // (2 * n), d // 2), BF16),
        gz=vm((nz, 8, d), F32), gsum=vm((8, d), F32),
        wsem=dma(9), osem=dma(2), ssem=dma(230), fsem=dma(5, n), bsem=dma(6, n),
        rx=dma(2, n), rq=dma(n), rdo=dma(2, n), rst=dma(n), rid=dma(n),
        rh=dma(2 * nb), rdmo=dma(2 * nb), rax=dma(1), rda=dma(1), zfar=dma(6, 2),
        rxt=dma(2 * nb), ro2=dma(2), rda2=dma(2), zout=dma(nz), rrso=dma(nb), fout=dma(nb), rat_in=dma(2, 2 * nb), rgl=dma(2 * nb),
        zgu=dma(2, nz), zdn=dma(nz), zat=dma(nz), zq=dma(nz), zgl=dma(nz),
        fgu=dma(2, nb), fdn=dma(nb), fat=dma(nb), fq=dma(nb), fgl=dma(1),
    )


INPUTS = ("ids", "tok", "cot", "ga", "gf", "cos_h", "sin_h", "wq_h", "wk_h", "wv_h", "wo_h", "wg_h", "wu_h", "wd_h")
OUTPUTS = ("out_h", "gin_h", "oat_h", "ogu_h", "odn_h", "oout_h", "oq_h", "ogl_h")


def layer_kernel(plan_names, tok, d, f, n, nb, *refs):
    r = types.SimpleNamespace(**dict(zip(INPUTS + OUTPUTS + plan_names, refs)))
    nz, pairs = n // 2, d // 128
    fs, dh, blk = f // nb, d // 2, d // nz
    b, s = lax.axis_index("batch"), lax.axis_index("seq")
    z, c = s // 2, lax.rem(s, 2)
    by, bx = b // 2, lax.rem(b, 2)
    e = 2 * b + c
    sib = (b, s + 1 - 2 * c)
    gain_a, gain_f = r.ga[...].reshape(1, d), r.gf[...].reshape(1, d)
    pending, used = [], [0]

    def remote(src, dst, ssem, rsem, dev):
        return pltpu.make_async_remote_copy(
            src_ref=src, dst_ref=dst, send_sem=ssem, recv_sem=rsem, device_id=dev, device_id_type=MESH
        )

    def send_lazy(make):
        at = used[0]
        used[0] += 1
        pending.append((make, at))
        cond, src, dst, rsem, dev = make()

        @pl.when(cond)
        def _():
            remote(src, dst, r.ssem.at[at], rsem, dev).start()

    def send(cond, src, dst, rsem, dev):
        send_lazy(lambda: (cond, src, dst, rsem, dev))

    def plane_send_lazy(make, to_b, to_c, also=None):
        def here():
            return (b == to_b) & (c == to_c)

        def wanted(cond):
            return cond if also is None else cond & also()

        send_lazy(lambda: (wanted(jnp.logical_not(here())), *make(), (to_b, 2 * z + to_c)))

        @pl.when(wanted(here()))
        def _():
            pltpu.make_async_copy(*make()).start()

    def plane_send(src, dst, rsem, to_b, to_c):
        plane_send_lazy(lambda: (src, dst, rsem), to_b, to_c)

    def arrived(dst, rsem):
        remote(dst, dst, r.ssem.at[0], rsem, sib).wait_recv()

    loads = {}
    for i, name in enumerate(("wk", "wv", "wq", "cos", "sin", "wo", "wg", "wu", "wd")):
        loads[name] = pltpu.make_async_copy(getattr(r, name + "_h"), getattr(r, name), r.wsem.at[i])
        loads[name].start()

    r.x_all[s] = r.tok[0]
    r.id_all[s] = jnp.broadcast_to(r.ids[...], (8, tok))

    bar = pltpu.get_barrier_semaphore()
    for zz in range(nz):
        for cc in range(2):
            @pl.when(2 * zz + cc != s)
            def _(zz=zz, cc=cc):
                pl.semaphore_signal(bar, inc=1, device_id=(b, 2 * zz + cc), device_id_type=MESH)
    for bb in range(nb):
        for cc in range(2):
            @pl.when(bb != b)
            def _(bb=bb, cc=cc):
                pl.semaphore_signal(bar, inc=1, device_id=(bb, 2 * z + cc), device_id_type=MESH)
    pl.semaphore_wait(bar, n - 1 + 2 * (nb - 1))

    always = s >= 0
    half = tok // 2

    def rows_of(ref, t, ch):
        return ref.at[t, pl.ds(ch * half, half)]

    right, left = (b, s + 2), (b, s - 2)
    send(always, r.id_all.at[s], r.id_all.at[s], r.rid.at[s], sib)
    for ch in range(2):
        mine = rows_of(r.x_all, s, ch)
        send(z + 1 < nz, mine, mine, r.rx.at[ch, s], right)
        send(always, mine, mine, r.rx.at[ch, s], sib)
    for zz in range(nz):
        for cc in range(2):
            send(z != zz, r.id_all.at[s], r.id_all.at[s], r.rid.at[s], (b, 2 * zz + cc))

    lane = lax.broadcasted_iota(jnp.int32, (tok, 128), 1)
    first = lane < 64
    half_mask = (jnp.where(first, 1.0, 0.0).astype(BF16), jnp.where(first, 0.0, 1.0).astype(BF16))

    def turn(u):
        low = lax.rem(lax.broadcasted_iota(jnp.int32, u.shape, 1), 64) < 32
        return jnp.where(low, pltpu.roll(u, 96, 1), pltpu.roll(u, 32, 1))

    def twice(u):
        return jnp.concatenate([u, u], axis=1)

    def stack(u):
        return jnp.concatenate([u * half_mask[0], u * half_mask[1]], axis=0)

    def unstack(u):
        return jnp.where(first, u[:tok], u[tok:])

    own = pl.ds(pl.multiple_of(c * tok, tok), tok)

    loads["wq"].wait()
    loads["cos"].wait()
    loads["sin"].wait()

    u = mm(r.tok[0], r.wq[...])
    co, si = r.cos[z, own, :], r.sin[z, own, :]
    for p in range(pairs):
        part = u[:, p * 128:(p + 1) * 128]
        r.q_all[s, :, p * 128:(p + 1) * 128] = ((part * co + turn(part) * si) * 0.125).astype(BF16)
    send(always, r.q_all.at[s], r.q_all.at[s], r.rq.at[s], sib)
    for dz in range(1, nz):
        send(z - dz >= 0, r.q_all.at[s], r.q_all.at[s], r.rq.at[s], (b, s - 2 * dz))

    def transpose_into(dst, value):
        for p in range(d // 128):
            dst[p * 128:(p + 1) * 128, :] = value[:, p * 128:(p + 1) * 128].T.astype(BF16)

    tokens = pl.ds(pl.multiple_of(e * tok, tok), tok)
    side, across = 2 * by + 1 - bx, 2 * (1 - by) + bx

    def relay(slot_of, rsem, to_c):
        for source, target in ((lambda: 2 * side, across), (lambda: 2 * across + 1, side)):
            @pl.when(c == to_c)
            def _(source=source):
                arrived(slot_of(source()), rsem.at[source()])

            send_lazy(
                lambda source=source, target=target: (
                    c == to_c, slot_of(source()), slot_of(source()), rsem.at[source()], (target, s)
                )
            )

    def hT_slot(i):
        return r.hT_b.at[:, pl.ds(pl.multiple_of(i * tok, tok), tok)]

    def dmo_slot(i):
        return r.dmo_b.at[pl.ds(pl.multiple_of(i * tok, tok), tok), :]
    transpose_into(r.xT, r.tok[0].astype(F32))
    for bb in range(nb):
        plane_send(r.xT, r.xT_b.at[:, tokens], r.rxt.at[e], bb, 1)
    r.idcol[...] = jnp.broadcast_to(r.ids[...].astype(F32), (128, tok)).T

    def ids_of(block):
        return jnp.concatenate(
            [r.id_all[2 * block, 0:1, :], r.id_all[2 * block + 1, 0:1, :]], axis=1
        ).astype(F32)

    def set_bias(block, local_is_query):
        shape = (tok, 2 * tok)
        mine = s * tok + lax.broadcasted_iota(jnp.int32, shape, 0)
        theirs = block * (2 * tok) + lax.broadcasted_iota(jnp.int32, shape, 1)
        my_id = twice(r.idcol[...])
        their_id = jnp.broadcast_to(ids_of(block), shape)
        causal = (theirs <= mine) if local_is_query else (mine <= theirs)
        allowed = (my_id == their_id) & causal & ((my_id != 0.0) | (mine == theirs))
        bias = jnp.where(allowed, 0.0, MASKED)
        r.bias[...] = jnp.concatenate([bias, bias], axis=0)

    units = fs // n

    def quarter_weights():
        for src, dst in ((r.wg, r.wgT), (r.wu, r.wuT)):
            for t in range(n):
                tile = src[:, pl.ds(pl.multiple_of((2 * t + by) * 128, 128), 128)].astype(F32)
                for p in range(pairs):
                    r.tmpT[:, p * 128:(p + 1) * 128] = tile[p * 128:(p + 1) * 128].T.astype(BF16)
                dst[t * units:(t + 1) * units, :] = r.tmpT[pl.ds(pl.multiple_of(bx * units, units), units), :]

    r.m[...] = jnp.full(r.m.shape, MASKED, F32)
    r.l[...] = jnp.zeros(r.l.shape, F32)
    r.acc[...] = jnp.zeros(r.acc.shape, F32)
    loads["wk"].wait()
    loads["wv"].wait()

    def forward_step(j, _):
        kb = z - j
        mine, other = 2 * kb + c, 2 * kb + 1 - c

        @pl.when(j > 0)
        def _():
            for ch in range(2):
                got = rows_of(r.x_all, mine, ch)
                arrived(got, r.rx.at[ch, mine])

                @pl.when(z + 1 < nz)
                def _():
                    remote(got, got, r.fsem.at[ch, mine], r.rx.at[ch, mine], right).start()

                remote(got, got, r.bsem.at[ch, mine], r.rx.at[ch, mine], sib).start()

            arrived(r.id_all.at[mine], r.rid.at[mine])

        for ch in range(2):
            arrived(rows_of(r.x_all, other, ch), r.rx.at[ch, other])
        arrived(r.id_all.at[other], r.rid.at[other])
        set_bias(kb, True)

        xb = r.x_all[pl.ds(2 * kb, 2)].reshape(2 * tok, d)
        u = mm(xb, r.wk[...])
        co, si = r.cos[kb], r.sin[kb]
        for p in range(pairs):
            part = u[:, p * 128:(p + 1) * 128]
            r.k_all[kb, :, p * 128:(p + 1) * 128] = (part * co + turn(part) * si).astype(BF16)
        r.v_all[kb] = mm(xb, r.wv[...]).astype(BF16)

        def pair(p, _):
            lanes = pl.ds(pl.multiple_of(p * 128, 128), 128)
            qp, kp, vp = r.q_all[s, :, lanes], r.k_all[kb, :, lanes], r.v_all[kb, :, lanes]
            sc = mm_nt(stack(qp), kp) + r.bias[...]
            m_old = r.m[p]
            m_new = jnp.maximum(m_old, jnp.max(sc, axis=1, keepdims=True))
            alpha = jnp.exp(m_old - m_new)
            ex = jnp.exp(sc - twice(m_new))
            r.m[p] = m_new
            r.l[p] = r.l[p] * alpha + jnp.sum(ex, axis=1, keepdims=True)
            r.acc[:, lanes] = r.acc[:, lanes] * unstack(alpha) + unstack(mm(ex.astype(BF16), vp))
            return 0

        lax.fori_loop(0, pairs, pair, 0, unroll=True)

        @pl.when((j == 0) & (c == 0))
        def _():
            loads["wg"].wait()
            loads["wu"].wait()
            quarter_weights()

        return 0

    lax.fori_loop(0, z + 1, forward_step, 0)

    def finish(p, _):
        lanes = pl.ds(pl.multiple_of(p * 128, 128), 128)
        r.acc[:, lanes] = r.acc[:, lanes] / unstack(r.l[p])
        r.m[p] = r.m[p] + jnp.log(r.l[p])
        return 0

    lax.fori_loop(0, pairs, finish, 0, unroll=True)
    r.olow[...] = r.acc[...].astype(BF16)

    loads["wo"].wait()
    r1 = r.tok[0].astype(F32) + mm(r.olow[...], r.wo[...])
    ri1 = lax.rsqrt(jnp.mean(r1 * r1, axis=1, keepdims=True) + EPSILON)
    r.ri1[...] = jnp.broadcast_to(ri1, (tok, 128))
    n1 = r1 * ri1
    r.n1[...] = n1
    h1 = n1 * gain_a
    r.h1[...] = h1
    r.hb[...] = h1.astype(BF16)
    transpose_into(r.hT, h1)
    for to_b in (b, side, across):
        plane_send(r.hT, r.hT_b.at[:, tokens], r.rh.at[e], to_b, 0)
    transpose_into(r.oT, r.acc[...])

    @pl.when(c == 1)
    def _():
        loads["wg"].wait()
        loads["wu"].wait()

    def gate_at(i):
        return (slice((i // 2) * tok, (i // 2 + 1) * tok), slice((i % 2) * 512, (i % 2 + 1) * 512))

    def up_at(i):
        return gate_at(i + f // 512)

    for i in range(f // 512):
        at = slice(i * 512, (i + 1) * 512)
        g = mm(r.hb[...], r.wg[:, at])
        u = mm(r.hb[...], r.wu[:, at])
        r.fa[gate_at(i)] = g
        r.fa[up_at(i)] = u
        a = g / (1.0 + jnp.exp(-g)) * u
        r.act[:, at] = a.astype(BF16)
    loads["wd"].wait()
    r2 = r.h1[...] + mm(r.act[...], r.wd[...])
    ri2 = lax.rsqrt(jnp.mean(r2 * r2, axis=1, keepdims=True) + EPSILON)
    n2 = r2 * ri2
    r.out_v[...] = n2 * gain_f
    out_copy = pltpu.make_async_copy(r.out_v, r.out_h, r.osem.at[0])
    out_copy.start()
    ct = r.cot[0].astype(F32)
    gain_ffn = jnp.sum(ct * n2, axis=0, keepdims=True)
    t2 = ct * gain_f
    dr2 = ri2 * (t2 - n2 * jnp.mean(n2 * t2, axis=1, keepdims=True))
    r.dr[...] = dr2
    r.dmo[...] = dr2.astype(BF16)
    for to_b in (b, side, across):
        plane_send(r.dmo, r.dmo_b.at[tokens, :], r.rdmo.at[e], to_b, 1)

    for i in range(f // 512):
        at = slice(i * 512, (i + 1) * 512)
        da = mm_nt(r.dmo[...], r.wd[at, :])
        g, u = r.fa[gate_at(i)], r.fa[up_at(i)]
        sg = 1.0 / (1.0 + jnp.exp(-g))
        r.dg[:, at] = (da * u * (sg * (1.0 + g * (1.0 - sg)))).astype(BF16)
        r.du[:, at] = (da * (g * sg)).astype(BF16)
    dh1 = r.dr[...] + mm_nt(r.dg[...], r.wg[...]) + mm_nt(r.du[...], r.wu[...])
    n1 = r.n1[...]
    gain_attn = jnp.sum(dh1 * n1, axis=0, keepdims=True)
    t1 = dh1 * gain_a
    dr1 = r.ri1[:, 0:1] * (t1 - n1 * jnp.mean(n1 * t1, axis=1, keepdims=True))
    r.dr[...] = dr1
    r.dattn[...] = dr1.astype(BF16)
    r.gl[...] = jnp.concatenate([gain_attn, gain_ffn, jnp.zeros((6, d), F32)], axis=0)
    plane_send(r.gl, r.gl_b.at[e], r.rgl.at[e], 0, 0)
    plane_send_lazy(lambda: (r.oT, r.o2.at[:, own], r.ro2.at[c]), b, 1)
    plane_send_lazy(lambda: (r.dattn, r.da2.at[own, :], r.rda2.at[c]), b, 1)

    r.do_all[s] = mm_nt(r.dattn[...], r.wo[...]).astype(BF16)
    for ch in range(2):
        mine = rows_of(r.do_all, s, ch)
        send(z > 0, mine, mine, r.rdo.at[ch, s], left)
        send(always, mine, mine, r.rdo.at[ch, s], sib)

    stats = jnp.zeros((tok, 128), F32)
    for p in range(pairs):
        prod = r.do_all[s, :, p * 128:(p + 1) * 128].astype(F32) * r.acc[:, p * 128:(p + 1) * 128]
        for h in range(2):
            head = 2 * p + h
            part = jnp.sum(jnp.where(first == (h == 0), prod, 0.0), axis=1, keepdims=True)
            part = jnp.broadcast_to(part, (tok, 128))
            r.delta[p, h * tok:(h + 1) * tok] = part
            stats = jnp.where(lane == head, r.m[p, h * tok:(h + 1) * tok], stats)
            stats = jnp.where(lane == 16 + head, part, stats)
    r.st_all[s] = stats.T[0:32, :]
    send(z > 0, r.st_all.at[s], r.st_all.at[s], r.rst.at[s], left)
    send(always, r.st_all.at[s], r.st_all.at[s], r.rst.at[s], sib)

    def each_source(dst_of, rsem, count):
        for i in range(count):
            arrived(dst_of(i), rsem.at[i])

    end = (z == 0) | (z == nz - 1)

    def on(to_c, some):
        return c == to_c

    def share(src_of, dst_of, far_of, to_c, some=False):
        near = lambda: jnp.where(z < nz // 2, 0, nz - 1)
        for i in range(2):
            send_lazy(
                lambda i=i: (
                    on(to_c, some) & end, src_of(jnp.abs(nz - 1 - i - z)), *far_of(i),
                    (b, 2 * jnp.where(z == 0, 1, nz - 2) + to_c),
                )
            )
        send_lazy(
            lambda: (on(to_c, some) & end, src_of(jnp.where(z == 0, 1, nz - 2)), *dst_of(),
                     (b, 2 * jnp.where(z == 0, 1, nz - 2) + to_c))
        )
        send_lazy(
            lambda: (on(to_c, some) & jnp.logical_not(end), src_of(near()), *dst_of(), (b, 2 * near() + to_c))
        )

    def pass_on(own_of, dst_of, far_of, to_c, some=False):
        def here():
            return on(to_c, some) & jnp.logical_not(end)

        for i in range(2):
            def target(i=i):
                return nz - 1 - z if i else jnp.where(z == 1, nz - 1, 0)

            @pl.when(here())
            def _(i=i, target=target):
                far, sem = far_of(i)
                arrived(far, sem)
                far[...] = (own_of(target())[...].astype(F32) + far[...].astype(F32)).astype(BF16)

            send_lazy(lambda i=i, target=target: (here(), far_of(i)[0], *dst_of(), (b, 2 * target() + to_c)))

    gate_up = [
        (
            lambda zz, k=k: r.pgu.at[k, pl.ds(pl.multiple_of(zz * blk, blk), blk), :],
            lambda k=k: (r.rgu.at[k, z], r.zgu.at[k, z]),
            lambda i, k=k: (r.ugu.at[k, i], r.zfar.at[k, i]),
            0,
        )
        for k in range(2)
    ]
    down = (
        lambda zz: r.pdn.at[pl.ds(2 * zz, 2)],
        lambda: (r.rdn.at[z], r.zdn.at[z]),
        lambda i: (r.udn.at[i], r.zfar.at[2, i]),
        1,
    )
    outp = (
        lambda zz: r.pout.at[pl.ds(pl.multiple_of(zz * blk, blk), blk), :],
        lambda: (r.rout.at[z], r.zout.at[z]),
        lambda i: (r.uout.at[i], r.zfar.at[5, i]),
        1,
    )
    early = (
        lambda zz: r.pq.at[pl.ds(2 * zz, 2)],
        lambda: (r.rqz.at[z], r.zq.at[z]),
        lambda i: (r.uq.at[i], r.zfar.at[3, i]),
        1,
    )
    late = (
        lambda zz: r.pat.at[pl.ds(pl.multiple_of(zz * blk, blk), blk), :],
        lambda: (r.rat.at[z], r.zat.at[z]),
        lambda i: (r.uat.at[i], r.zfar.at[4, i]),
        1,
    )

    def hidden_again():
        @pl.when(c == 0)
        def _():
            for i in range(2 * nb):
                @pl.when((i != 2 * side) & (i != 2 * across + 1))
                def _(i=i):
                    arrived(hT_slot(i), r.rh.at[i])

            for i in range(2 * nb * tok // 512):
                at = slice(i * 512, (i + 1) * 512)
                g = mm(r.wgT[...], r.hT_b[:, at])
                u = mm(r.wuT[...], r.hT_b[:, at])
                sg = 1.0 / (1.0 + jnp.exp(-g))
                r.act_x[:, at] = (g * sg * u).astype(BF16)
                r.fa[:, at] = u * (sg * (1.0 + g * (1.0 - sg)))
                r.fb[:, at] = g * sg

        send_lazy(lambda: (c == 0, r.act_x, r.act_x, r.rax.at[0], sib))

    def hidden_sums():
        @pl.when(c == 1)
        def _():
            for i in range(2 * nb):
                @pl.when((i != 2 * side) & (i != 2 * across + 1))
                def _(i=i):
                    arrived(dmo_slot(i), r.rdmo.at[i])

            rows_d = jnp.concatenate(
                [r.wd[pl.ds(pl.multiple_of(t * nb * units + b * units, units), units), :] for t in range(n)], axis=0
            )
            r.da_x[...] = mm_nt(rows_d, r.dmo_b[...]).astype(BF16)

        send_lazy(lambda: (c == 1, r.da_x, r.da_x, r.rda.at[0], sib))

        @pl.when(c == 1)
        def _():
            arrived(r.act_x, r.rax.at[0])
            r.pdn[...] = mm(r.act_x[...], r.dmo_b[...]).astype(BF16).reshape(n, units, d)

        share(*down)
        for k in range(2):
            @pl.when(c == 0)
            def _(k=k):
                if k == 0:
                    arrived(r.da_x, r.rda.at[0])
                r.dgu[k] = (r.da_x[...].astype(F32) * (r.fb if k else r.fa)[...]).astype(BF16)
                r.pgu[k] = mm_nt(r.hT_b[...], r.dgu[k]).astype(BF16)

            share(*gate_up[k])
        pass_on(*outp)

    @pl.when(c == 1)
    def _():
        for i in range(2):
            arrived(r.o2.at[:, pl.ds(i * tok, tok)], r.ro2.at[i])
            arrived(r.da2.at[pl.ds(i * tok, tok), :], r.rda2.at[i])
        r.pout[...] = mm(r.o2[...], r.da2[...]).astype(BF16)

    share(*outp)

    relay(hT_slot, r.rh, 0)

    r.acc[...] = jnp.zeros(r.acc.shape, F32)

    def query_step(kb, _):
        @pl.when(kb == jnp.maximum(z - 1, 0))
        def _():
            relay(dmo_slot, r.rdmo, 1)

        set_bias(kb, True)

        def pair(p, _):
            lanes = pl.ds(pl.multiple_of(p * 128, 128), 128)
            qp, kp, vp = r.q_all[s, :, lanes], r.k_all[kb, :, lanes], r.v_all[kb, :, lanes]
            dop = r.do_all[s, :, lanes]
            pf = jnp.exp(mm_nt(stack(qp), kp) + r.bias[...] - twice(r.m[p]))
            dp = mm_nt(stack(dop), vp)
            ds = (pf * (dp - twice(r.delta[p]))).astype(BF16)
            r.acc[:, lanes] += unstack(mm(ds, kp))
            return 0

        lax.fori_loop(0, pairs, pair, 0, unroll=True)
        return 0

    lax.fori_loop(0, z + 1, query_step, 0)

    def turn_back(src, dst, factor):
        co, si = r.cos[z, own, :], r.sin[z, own, :]
        for p in range(pairs):
            g = src[:, p * 128:(p + 1) * 128] * factor
            dst[:, p * 128:(p + 1) * 128] = (g * co - turn(g) * si).astype(BF16)

    turn_back(r.acc, r.dq, 0.125)

    def half_send(k, value, h, bb):
        plane_send_lazy(
            lambda: (value.at[:, pl.ds(h * dh, dh)], r.at_b.at[k, tokens, :], r.rat_in.at[k, e]), bb, 1
        )

    for bb in range(nb):
        half_send(0, r.dq, bb % 2, bb)
    hidden_again()

    r.acc[...] = jnp.zeros(r.acc.shape, F32)
    r.acc2[...] = jnp.zeros(r.acc2.shape, F32)

    def key_step(j):
        qb = z + j
        mine, other = 2 * qb + c, 2 * qb + 1 - c

        @pl.when(j > 0)
        def _():
            arrived(r.id_all.at[mine], r.rid.at[mine])
            arrived(r.id_all.at[other], r.rid.at[other])
            arrived(r.q_all.at[mine], r.rq.at[mine])
            remote(r.q_all.at[mine], r.q_all.at[mine], r.bsem.at[2, mine], r.rq.at[mine], sib).start()
            blocks = [(rows_of(r.do_all, mine, ch), r.rdo.at[ch, mine]) for ch in range(2)]
            blocks.append((r.st_all.at[mine], r.rst.at[mine]))
            for i, (got, sem) in enumerate(blocks):
                arrived(got, sem)

                @pl.when(z > 0)
                def _():
                    remote(got, got, r.fsem.at[2 + i, mine], sem, left).start()

                remote(got, got, r.bsem.at[3 + i, mine], sem, sib).start()

        arrived(r.q_all.at[other], r.rq.at[other])
        for ch in range(2):
            arrived(rows_of(r.do_all, other, ch), r.rdo.at[ch, other])
        arrived(r.st_all.at[other], r.rst.at[other])
        set_bias(qb, False)

        def pair(p, _):
            lanes = pl.ds(pl.multiple_of(p * 128, 128), 128)
            kp, vp = r.k_all[z, own, lanes], r.v_all[z, own, lanes]
            qp = r.q_all[pl.ds(2 * qb, 2), :, lanes].reshape(2 * tok, 128)
            dop = r.do_all[pl.ds(2 * qb, 2), :, lanes].reshape(2 * tok, 128)

            def row(base):
                return jnp.concatenate(
                    [
                        jnp.broadcast_to(
                            jnp.concatenate(
                                [r.st_all[2 * qb + i, pl.ds(base + 2 * p + h, 1), :] for i in range(2)], axis=1
                            ),
                            (tok, 2 * tok),
                        )
                        for h in range(2)
                    ],
                    axis=0,
                )

            pf = jnp.exp(mm_nt(stack(kp), qp) + r.bias[...] - row(0))
            dp = mm_nt(stack(vp), dop)
            ds = (pf * (dp - row(16))).astype(BF16)
            r.acc2[:, lanes] += unstack(mm(pf.astype(BF16), dop))
            r.acc[:, lanes] += unstack(mm(ds, qp))
            return 0

        lax.fori_loop(0, pairs, pair, 0, unroll=True)

    def keys_done():
        turn_back(r.acc, r.dk, 1.0)
        r.dv[...] = r.acc2[...].astype(BF16)
        for bb in range(nb):
            half_send(1, r.dv if bb >= 2 else r.dk, bb % 2, bb)
    last = nz - z
    sums_at = jnp.where(z == 0, 2, jnp.where(z == nz - 1, 0, last))

    def key_loop(j, _):
        pl.when(j == sums_at)(hidden_sums)

        @pl.when(j < last)
        def _():
            key_step(j)

        pl.when(j == last - 1)(keys_done)
        return 0

    lax.fori_loop(0, last + 1, key_loop, 0)
    r.gin_v[...] = (
        r.dr[...] + mm_nt(r.dq[...], r.wq[...]) + mm_nt(r.dk[...], r.wk[...]) + mm_nt(r.dv[...], r.wv[...])
    )
    pltpu.make_async_copy(r.gin_v, r.gin_h, r.osem.at[1]).start()


    @pl.when(c == 1)
    def _():
        each_source(lambda i: r.xT_b.at[:, pl.ds(i * tok, tok)], r.rxt, 2 * nb)

    def attn_sum(k):
        @pl.when(c == 1)
        def _():
            each_source(lambda i: r.at_b.at[k, pl.ds(i * tok, tok), :], r.rat_in.at[k], 2 * nb)
            if k:
                r.pat[...] = mm(r.xT_b[...], r.at_b[k]).astype(BF16)
            else:
                part = d // (2 * n)
                some = jnp.concatenate(
                    [r.xT_b[pl.ds(pl.multiple_of((2 * t + by) * part, part), part), :] for t in range(n)], axis=0
                )
                r.pq[...] = mm(some, r.at_b[k]).astype(BF16).reshape(n, part, dh)

        share(*(late if k else early))

    def totals(total_of, own, recv_of, rsem_of):
        def add(slots):
            total = own().astype(F32)
            for at in slots:
                arrived(recv_of(at), rsem_of(at))
                total = total + recv_of(at)[...].astype(F32)
            total_of()[...] = total.astype(BF16).reshape(total_of().shape)

        pl.when(end)(lambda: add((1, 2)))
        pl.when(jnp.logical_not(end))(lambda: add((jnp.where(z == 1, 0, nz - 1), nz - 1 - z)))

    def spread(src_of, dst_of, from_c, some=False):
        for bb in range(nb):
            for cc in range(2):
                def here(bb=bb, cc=cc):
                    return (b == bb) & (c == cc)

                send_lazy(
                    lambda bb=bb, cc=cc, here=here: (
                        on(from_c, some) & jnp.logical_not(here()), src_of(cc), *dst_of(), (bb, 2 * z + cc)
                    )
                )

                @pl.when(on(from_c, some) & here())
                def _(cc=cc):
                    pltpu.make_async_copy(src_of(cc), *dst_of()).start()

    rows = pl.ds(pl.multiple_of(z * blk, blk), blk)
    quarter = blk // 4

    def out_total():
        @pl.when(c == 1)
        def _():
            total = None
            for bb in range(nb):
                arrived(r.rso.at[bb], r.rrso.at[bb])
                part = r.rso[bb].astype(F32)
                total = part if total is None else total + part
            r.fso[...] = total.astype(BF16)

        spread(lambda cc: r.fso.at[cc], lambda: (r.oout_h.at[b], r.fout.at[b]), 1)

    def gate_up_total(k):
        @pl.when(c == 0)
        def _():
            totals(
                lambda: r.sgu.at[k], lambda: r.pgu[k, rows, :], lambda at: r.rgu.at[k, at], lambda at: r.zgu.at[k, at]
            )

        spread(
            lambda cc: r.sgu.at[k, pl.ds(cc * (blk // 2), blk // 2), :], lambda: (r.ogu_h.at[b, k], r.fgu.at[k, b]), 0
        )

    attn_sum(0)
    @pl.when(c == 1)
    def _():
        totals(lambda: r.sout, lambda: r.pout[rows, :], lambda at: r.rout.at[at], lambda at: r.zout.at[at])

    for bb in range(nb):
        at = (slice(None), pl.ds((bb // 2) * quarter, quarter), pl.ds((bb % 2) * dh, dh))
        send((c == 1) & (b != bb), r.sout.at[at], r.rso.at[b], r.rrso.at[b], (bb, s))

        @pl.when((c == 1) & (b == bb))
        def _(at=at):
            pltpu.make_async_copy(r.sout.at[at], r.rso.at[b], r.rrso.at[b]).start()

    pass_on(*gate_up[0])
    gate_up_total(0)
    pass_on(*gate_up[1])
    gate_up_total(1)
    pass_on(*down)
    attn_sum(1)
    pass_on(*early)
    out_total()

    adds = (b == 0) & (c == 0)

    @pl.when(adds)
    def _():
        total = None
        for i in range(2 * nb):
            arrived(r.gl_b.at[i], r.rgl.at[i])
            total = r.gl_b[i] if total is None else total + r.gl_b[i]
        r.gz[z] = total

    for zz in range(nz):
        send(adds & (z != zz), r.gz.at[z], r.gz.at[z], r.zgl.at[z], (0, 2 * zz))

    @pl.when(adds)
    def _():
        total = r.gz[z]
        for dz in range(1, nz):
            at = lax.rem(z + dz, nz)
            arrived(r.gz.at[at], r.zgl.at[at])
            total = total + r.gz[at]
        r.gsum[...] = total

    for bb in range(nb):
        for cc in range(2):
            here = (bb == 0) and (cc == 0)
            if not here:
                send(adds, r.gsum, r.ogl_h, r.fgl.at[0], (bb, 2 * z + cc))

    @pl.when(adds)
    def _():
        pltpu.make_async_copy(r.gsum, r.ogl_h, r.fgl.at[0]).start()

    @pl.when(c == 1)
    def _():
        totals(lambda: r.sdn, lambda: r.pdn[pl.ds(2 * z, 2)], lambda at: r.rdn.at[at], lambda at: r.zdn.at[at])

    spread(lambda cc: r.sdn.at[cc], lambda: (r.odn_h.at[b], r.fdn.at[b]), 1)
    pass_on(*late)

    @pl.when(c == 1)
    def _():
        totals(lambda: r.sq, lambda: r.pq[pl.ds(2 * z, 2)], lambda at: r.rqz.at[at], lambda at: r.zq.at[at])

    spread(lambda cc: r.sq.at[cc], lambda: (r.oq_h.at[b], r.fq.at[b]), 1)

    @pl.when(c == 1)
    def _():
        totals(lambda: r.sat, lambda: r.pat[rows, :], lambda at: r.rat.at[at], lambda at: r.zat.at[at])

    spread(
        lambda cc: r.sat.at[pl.ds(cc * (blk // 2), blk // 2), :], lambda: (r.oat_h.at[b], r.fat.at[b]), 1
    )

    for bb in range(nb):
        arrived(r.ogu_h.at[bb, 0], r.fgu.at[0, bb])
        arrived(r.ogu_h.at[bb, 1], r.fgu.at[1, bb])
        arrived(r.odn_h.at[bb], r.fdn.at[bb])
        arrived(r.oq_h.at[bb], r.fq.at[bb])
        arrived(r.oout_h.at[bb], r.fout.at[bb])
        arrived(r.oat_h.at[bb], r.fat.at[bb])
    arrived(r.ogl_h, r.fgl.at[0])
    out_copy.wait()
    pltpu.make_async_copy(r.gin_v, r.gin_h, r.osem.at[1]).wait()
    assert used[0] <= r.ssem.shape[0], used
    for make, at in pending:
        cond, src, dst, rsem, dev = make()

        @pl.when(cond)
        def _():
            remote(src, dst, r.ssem.at[at], rsem, dev).wait_send()

    def sent_on(t, _):
        @pl.when((lax.rem(t, 2) == c) & (t < s))
        def _():
            for ch in range(2):
                got = rows_of(r.x_all, t, ch)
                remote(got, got, r.bsem.at[ch, t], r.rx.at[ch, t], sib).wait_send()

                @pl.when(z + 1 < nz)
                def _():
                    remote(got, got, r.fsem.at[ch, t], r.rx.at[ch, t], right).wait_send()

        @pl.when((lax.rem(t, 2) == c) & (t > s))
        def _():
            remote(r.q_all.at[t], r.q_all.at[t], r.bsem.at[2, t], r.rq.at[t], sib).wait_send()
            blocks = [(rows_of(r.do_all, t, ch), r.rdo.at[ch, t]) for ch in range(2)]
            blocks.append((r.st_all.at[t], r.rst.at[t]))
            for i, (got, sem) in enumerate(blocks):
                remote(got, got, r.bsem.at[3 + i, t], sem, sib).wait_send()

                @pl.when(z > 0)
                def _():
                    remote(got, got, r.fsem.at[2 + i, t], sem, left).wait_send()
        return 0

    lax.fori_loop(0, n, sent_on, 0)


def unpack_kernel(
    n, nb, out_in, gin_in, oat_h, ogu_h, odn_h, oout_h, oq_h, ogl_h,
    out, gin, gq_h, gk_h, gv_h, go_h, gg_h, gu_h, gd_h, g1, g2,
    oat, ogu, odn, oout, oq, ogl, gq, gk, gv, go, gg, gu, gd, out_v, gin_v, isem, osem,
):
    s = lax.axis_index("seq")
    fs = ogu.shape[3]
    units, dh = odn.shape[1], odn.shape[2] // 2
    copy = pltpu.make_async_copy
    loads = [copy(a, b, isem.at[i]) for i, (a, b) in enumerate(
        ((ogu_h, ogu), (oat_h, oat), (odn_h, odn), (ogl_h, ogl), (out_in, out_v), (gin_in, gin_v), (oout_h, oout), (oq_h, oq)))]
    stores = [copy(a, b, osem.at[i]) for i, (a, b) in enumerate(
        ((gg, gg_h), (gu, gu_h), (gq, gq_h), (gk, gk_h), (gv, gv_h), (go, go_h), (gd, gd_h),
         (out_v, out.at[0]), (gin_v, gin.at[0])))]
    for load in loads:
        load.start()
    loads[0].wait()
    low = lax.broadcasted_iota(jnp.int32, (ogu.shape[2], 128), 1) < 64

    def interleave(k, dst):
        for t in range(n):
            for y in range(2):
                at = slice((t // 2) * 128, (t // 2 + 1) * 128)
                one, two = ogu[2 * y, k, :, at].astype(F32), ogu[2 * y + 1, k, :, at].astype(F32)
                if t % 2:
                    one = pltpu.roll(one, 64, 1)
                else:
                    two = pltpu.roll(two, 64, 1)
                dst[:, (2 * t + y) * 128:(2 * t + y + 1) * 128] = jnp.where(low, one, two)

    interleave(0, gg)
    stores[0].start()
    interleave(1, gu)
    stores[1].start()
    loads[1].wait()
    for m, (ref, bb) in enumerate(((gk, 0), (gv, 2))):
        ref[:, :dh] = oat[bb].astype(F32)
        ref[:, dh:] = oat[bb + 1].astype(F32)
        stores[3 + m].start()
    loads[6].wait()
    loads[7].wait()
    part = oout.shape[1]
    for m, (src, dst) in enumerate(((oq, gq), (oout, go))):
        for bb in range(nb):
            dst[(bb // 2) * part:(bb // 2 + 1) * part, (bb % 2) * dh:(bb % 2 + 1) * dh] = src[bb].astype(F32)
        stores[5 if m else 2].start()
    loads[2].wait()
    for bb in range(nb):
        gd[bb * units:(bb + 1) * units, :] = odn[bb].astype(F32)
    stores[6].start()
    for i in (4, 5):
        loads[i].wait()
        stores[3 + i].start()
    loads[3].wait()
    d = ogl.shape[1]
    own = d // n
    gains = pltpu.roll(ogl[...], lax.rem(d - s * own, d), 1)
    g1[...] = gains[0:1, :own]
    g2[...] = gains[1:2, :own]
    for store in stores:
        store.wait()


def rope_constants(length, head_dim):
    half = head_dim // 2
    inverse = np.exp(-2.0 * math.log(THETA) / head_dim * np.arange(half)).astype(np.float32)
    angle = np.arange(length, dtype=np.float32)[:, None] * inverse
    cos, sin = np.cos(angle.astype(np.float64)), np.sin(angle.astype(np.float64))
    return (
        np.concatenate([cos, cos, cos, cos], 1).astype(np.float32),
        np.concatenate([-sin, sin, -sin, sin], 1).astype(np.float32),
    )


def fused_local(n, nb, tokens, doc_ids, w_query, w_key, w_value, w_out, w_gate, w_up, w_down, gain_attn, gain_ffn, cotangent):
    _, tok, d = tokens.shape
    f = w_gate.shape[1]
    nz = n // 2
    cos, sin = rope_constants(n * tok, d // HEADS)
    cos = jnp.asarray(cos.reshape(nz, 2 * tok, 128))
    sin = jnp.asarray(sin.reshape(nz, 2 * tok, 128))
    plan = scratch_plan(tok, d, f, n, nb)
    vmem, anywhere = pl.BlockSpec(memory_space=pltpu.VMEM), pl.BlockSpec(memory_space=pl.ANY)
    shape = jax.ShapeDtypeStruct
    parts = pl.pallas_call(
        functools.partial(layer_kernel, tuple(plan), tok, d, f, n, nb),
        out_shape=(
            shape((tok, d), F32), shape((tok, d), F32), shape((nb, d // n, d // 2), BF16),
            shape((nb, 2, d // n, f // nb), BF16), shape((nb, f // (nb * n), d), BF16), shape((nb, d // (2 * n), d // 2), BF16),
            shape((nb, d // (2 * n), d // 2), BF16), shape((8, d), F32),
        ),
        in_specs=[vmem] * 5 + [anywhere] * 9,
        out_specs=[anywhere] * 8,
        scratch_shapes=list(plan.values()),
        compiler_params=pltpu.CompilerParams(
            collective_id=0, has_side_effects=True, vmem_limit_bytes=62 * 2**20
        ),
        name="layer",
    )(
        doc_ids, tokens, cotangent, gain_attn, gain_ffn, cos, sin,
        w_query, w_key, w_value, w_out, w_gate, w_up, w_down,
    )
    own = d // n
    grads = [shape((own, d), F32)] * 4 + [shape((own, f), F32)] * 2 + [shape((f // n, d), F32)]
    results = pl.pallas_call(
        functools.partial(unpack_kernel, n, nb),
        out_shape=(shape((1, tok, d), F32), shape((1, tok, d), F32), *grads, shape((1, own), F32), shape((1, own), F32)),
        in_specs=[pl.BlockSpec(memory_space=pltpu.HBM)] * 8,
        out_specs=[anywhere] * 9 + [vmem] * 2,
        scratch_shapes=[pltpu.VMEM(parts[i].shape, parts[i].dtype) for i in (2, 3, 4, 5, 6, 7)]
        + [pltpu.VMEM(g.shape, g.dtype) for g in grads]
        + [pltpu.VMEM((tok, d), F32)] * 2
        + [pltpu.SemaphoreType.DMA((8,)), pltpu.SemaphoreType.DMA((9,))],
        compiler_params=pltpu.CompilerParams(vmem_limit_bytes=62 * 2**20),
        name="unpack",
    )(*parts)
    return results[:9] + (results[9].reshape(own), results[10].reshape(own))


def fits(shapes, n, nb):
    (_, tok, d), f = shapes[0], shapes[6][1]
    return (
        nb == 4 and n == 8 and n * tok <= 1024 and tok == 128 and shapes[0][0] == 1
        and d == HEADS * 64 and d % 256 == 0 and d % (32 * n) == 0 and f == 2 * tok * n and f % 512 == 0
    )


def solution(mesh):
    nb, n = mesh.shape["batch"], mesh.shape["seq"]

    def either(*args):
        shapes = [a.shape for a in args]
        if fits(shapes, n, nb):
            return fused_local(n, nb, *args)
        return local(*args)

    return jax.shard_map(
        either,
        mesh=mesh,
        in_specs=(
            P("batch", "seq", None),
            P("batch", "seq"),
            P(),
            P(),
            P(),
            P(),
            P(),
            P(),
            P(),
            P(),
            P(),
            P("batch", "seq", None),
        ),
        out_specs=(
            P("batch", "seq", None),
            P("batch", "seq", None),
            P("seq", None),
            P("seq", None),
            P("seq", None),
            P("seq", None),
            P("seq", None),
            P("seq", None),
            P("seq", None),
            P("seq"),
            P("seq"),
        ),
        check_vma=False,
    )
```

```python
import functools
import math
import types

import jax
import jax.numpy as jnp
import numpy as np
from jax import lax
from jax.experimental import pallas as pl
from jax.experimental.pallas import tpu as pltpu
from jax.sharding import PartitionSpec as P

HEADS = 12
NSEG = 8


EPSILON = 1e-06
THETA = 10000.0
MASKED = -1e30


def root_mean_square_norm(values, gain):
    return values * lax.rsqrt(jnp.mean(values * values, -1, keepdims=True) + EPSILON) * gain


def swiglu(gate, up_part):
    return jax.nn.silu(gate) * up_part


def rope_tables(positions, head_dim):
    half_dim = head_dim // 2
    inverse = jnp.exp(-2.0 * math.log(THETA) / head_dim * jnp.arange(half_dim, dtype=jnp.float32))
    angle = positions.astype(jnp.float32)[..., None] * inverse
    return (
        jnp.concatenate([jnp.cos(angle), jnp.cos(angle)], -1),
        jnp.concatenate([jnp.sin(angle), jnp.sin(angle)], -1),
    )


def rotate(values, cosine, sine):
    half_dim = values.shape[-1] // 2
    turned = jnp.concatenate([-values[..., half_dim:], values[..., :half_dim]], -1)
    return values * cosine + turned * sine


def rotate_back(grads, cosine, sine):
    half_dim = grads.shape[-1] // 2
    turned = grads * sine
    return grads * cosine + jnp.concatenate([turned[..., half_dim:], -turned[..., :half_dim]], -1)


def block_size(total_rows):
    return max((d for d in range(1, min(total_rows, 2048) + 1) if total_rows % d == 0))


def doc_begin(segment_begins, where_at):
    earlier = segment_begins[:, None, :] <= where_at[:, :, None]
    return jnp.max(jnp.where(earlier, segment_begins[:, None, :], 0), -1)


def outer_sum(remaining_tokens, right):
    return lax.dot_general(
        remaining_tokens, right, (((0,), (0,)), ((), ())), preferred_element_type=jnp.float32
    )


def back_product(grads, weight_matrix):
    return lax.dot_general(
        grads, weight_matrix, (((1,), (1,)), ((), ())), preferred_element_type=jnp.float32
    )


def masked_scores(queries, key_block, key_at, query_at, query_begin):
    batch_rows, block_rows, model_width = key_block.shape
    head_count = queries.shape[2]
    head_dim = model_width // head_count
    key_heads = key_block.reshape(batch_rows, block_rows, head_count, head_dim)
    scores = jnp.einsum(
        "bqhd,bkhd->bhqk", queries, key_heads, preferred_element_type=jnp.float32
    ) * (1.0 / math.sqrt(head_dim))
    key_pos = key_at[None, None, :]
    query_pos = query_at[:, :, None]
    begin_pos = query_begin[:, :, None]
    allowed = (
        (key_pos <= query_pos) & (key_pos >= begin_pos) & ((begin_pos > 0) | (key_pos == query_pos))
    )
    return (scores, allowed[:, None], key_heads)


def grad_terms(
    queries, grad_heads, lse, delta, query_at, query_begin, key_block, value_block, key_at
):
    scores, allowed, key_heads = masked_scores(queries, key_block, key_at, query_at, query_begin)
    value_heads = value_block.reshape(key_heads.shape)
    probs = jnp.where(allowed, jnp.exp(scores - lse[..., None]), 0.0)
    dprob = jnp.einsum(
        "bqhd,bkhd->bhqk", grad_heads, value_heads, preferred_element_type=jnp.float32
    )
    dscore = (probs * (dprob - delta[..., None])).astype(jnp.bfloat16)
    return (probs.astype(jnp.bfloat16), dscore, key_heads, value_heads)


def over_rows(update, carried, arrays, first_row):
    total_rows = arrays[0].shape[1]
    block_rows = block_size(total_rows)

    def over_step(block_index, state):
        offset = block_index * block_rows
        blocks = tuple((lax.dynamic_slice_in_dim(item, offset, block_rows, 1) for item in arrays))
        key_at = first_row + offset + jnp.arange(block_rows, dtype=jnp.int32)
        return update(state, blocks, key_at)

    return lax.fori_loop(0, total_rows // block_rows, over_step, carried)


def local(
    tokens,
    doc_ids,
    w_query,
    w_key,
    w_value,
    w_out,
    w_gate,
    w_up,
    w_down,
    gain_attn,
    gain_ffn,
    cotangent,
):
    batch_rows, local_len, model_width = tokens.shape
    head_count = HEADS
    head_dim = model_width // head_count
    shape_heads = (batch_rows, local_len, head_count, head_dim)
    scale = 1.0 / math.sqrt(head_dim)
    labels = jnp.arange(NSEG, dtype=jnp.int32)
    member = (doc_ids[:, :, None] == labels).astype(jnp.int32)
    totals = lax.psum(jnp.sum(member, 1), "seq")
    segment_begins = jnp.cumsum(totals, 1) - totals
    local_at = lax.axis_index("seq") * local_len + jnp.arange(local_len, dtype=jnp.int32)
    query_at = jnp.broadcast_to(local_at, (batch_rows, local_len))
    query_begin = doc_begin(segment_begins, query_at)
    cosine, sine = rope_tables(query_at - query_begin, head_dim)
    cosine = cosine[:, :, None, :]
    sine = sine[:, :, None, :]
    flat_tokens = tokens.reshape(batch_rows * local_len, model_width)
    queries = rotate(
        jnp.dot(flat_tokens, w_query, preferred_element_type=jnp.float32).reshape(shape_heads),
        cosine,
        sine,
    ).astype(jnp.bfloat16)
    key_send = (
        rotate(
            jnp.dot(flat_tokens, w_key, preferred_element_type=jnp.float32).reshape(shape_heads),
            cosine,
            sine,
        )
        .astype(jnp.bfloat16)
        .reshape(batch_rows, local_len, model_width)
    )
    value_send = (
        jnp.dot(flat_tokens, w_value, preferred_element_type=jnp.float32)
        .astype(jnp.bfloat16)
        .reshape(batch_rows, local_len, model_width)
    )

    def stats_step(state, blocks, key_at):
        run_max, run_sum = state
        scores, allowed, key_heads = masked_scores(
            queries, blocks[0], key_at, query_at, query_begin
        )
        scores = jnp.where(allowed, scores, MASKED)
        new_max = jnp.maximum(run_max, jnp.max(scores, -1))
        weights = jnp.where(allowed, jnp.exp(scores - new_max[..., None]), 0.0)
        return (new_max, run_sum * jnp.exp(run_max - new_max) + jnp.sum(weights, -1))

    stats_init = (
        jnp.full((batch_rows, head_count, local_len), MASKED, jnp.float32),
        jnp.zeros((batch_rows, head_count, local_len), jnp.float32),
    )
    zero_heads = jnp.zeros(shape_heads, jnp.float32)
    run_max, run_sum = over_rows(
        stats_step, stats_init, (lax.all_gather(key_send, "seq", axis=1, tiled=True),), jnp.int32(0)
    )
    lse = run_max + jnp.log(run_sum)

    def output_step(state, blocks, key_at):
        scores, allowed, key_heads = masked_scores(
            queries, blocks[0], key_at, query_at, query_begin
        )
        value_heads = blocks[1].reshape(key_heads.shape)
        probs = jnp.where(allowed, jnp.exp(scores - lse[..., None]), 0.0).astype(jnp.bfloat16)
        return state + jnp.einsum(
            "bhqk,bkhd->bqhd", probs, value_heads, preferred_element_type=jnp.float32
        )

    attended = over_rows(
        output_step,
        zero_heads,
        (
            lax.all_gather(key_send, "seq", axis=1, tiled=True),
            lax.all_gather(value_send, "seq", axis=1, tiled=True),
        ),
        jnp.int32(0),
    )
    attended_low = attended.astype(jnp.bfloat16).reshape(batch_rows * local_len, model_width)
    first_sum = flat_tokens.astype(jnp.float32) + jnp.dot(
        attended_low, w_out, preferred_element_type=jnp.float32
    )
    hidden, norm_first_back = jax.vjp(root_mean_square_norm, first_sum, gain_attn)
    hidden_low = hidden.astype(jnp.bfloat16)
    gate = jnp.dot(hidden_low, w_gate, preferred_element_type=jnp.float32)
    up_part = jnp.dot(hidden_low, w_up, preferred_element_type=jnp.float32)
    active, swiglu_back = jax.vjp(swiglu, gate, up_part)
    active_low = active.astype(jnp.bfloat16)
    second_sum = hidden + jnp.dot(active_low, w_down, preferred_element_type=jnp.float32)
    output, norm_second_back = jax.vjp(root_mean_square_norm, second_sum, gain_ffn)
    second_grad, grad_gain_ffn = norm_second_back(
        cotangent.reshape(batch_rows * local_len, model_width).astype(jnp.float32)
    )
    branch_grad = second_grad.astype(jnp.bfloat16)
    grad_down = outer_sum(active_low, branch_grad)
    gate_grad, up_grad = swiglu_back(back_product(branch_grad, w_down))
    gate_low = gate_grad.astype(jnp.bfloat16)
    up_low = up_grad.astype(jnp.bfloat16)
    grad_gate = outer_sum(hidden_low, gate_low)
    grad_up = outer_sum(hidden_low, up_low)
    hidden_grad = second_grad + back_product(gate_low, w_gate) + back_product(up_low, w_up)
    first_grad, grad_gain_attn = norm_first_back(hidden_grad)
    attn_grad = first_grad.astype(jnp.bfloat16)
    grad_out = outer_sum(attended_low, attn_grad)
    grad_heads = back_product(attn_grad, w_out).astype(jnp.bfloat16).reshape(shape_heads)
    delta = jnp.swapaxes(jnp.sum(grad_heads.astype(jnp.float32) * attended, -1), 1, 2)

    def query_step(state, blocks, key_at):
        probs_low, dscore, key_heads, value_heads = grad_terms(
            queries, grad_heads, lse, delta, query_at, query_begin, blocks[0], blocks[1], key_at
        )
        return (
            state
            + jnp.einsum("bhqk,bkhd->bqhd", dscore, key_heads, preferred_element_type=jnp.float32)
            * scale
        )

    all_keys, all_values = (
        lax.all_gather(key_send, "seq", axis=1, tiled=True),
        lax.all_gather(value_send, "seq", axis=1, tiled=True),
    )
    query_grad = over_rows(query_step, zero_heads, (all_keys, all_values), 0)
    first_row = jnp.int32(0)
    span_rows = local_len * lax.axis_size("seq")
    block_rows = block_size(span_rows)
    empty = jnp.zeros((batch_rows, span_rows, head_count, head_dim), jnp.float32)

    def key_step(block_index, state):
        offset = block_index * block_rows
        key_block = lax.dynamic_slice_in_dim(all_keys, offset, block_rows, 1)
        value_block = lax.dynamic_slice_in_dim(all_values, offset, block_rows, 1)
        key_at = first_row + offset + jnp.arange(block_rows, dtype=jnp.int32)
        probs_low, dscore, key_heads, value_heads = grad_terms(
            queries, grad_heads, lse, delta, query_at, query_begin, key_block, value_block, key_at
        )
        key_part = (
            jnp.einsum("bhqk,bqhd->bkhd", dscore, queries, preferred_element_type=jnp.float32)
            * scale
        )
        value_part = jnp.einsum(
            "bhqk,bqhd->bkhd", probs_low, grad_heads, preferred_element_type=jnp.float32
        )
        return (
            lax.dynamic_update_slice_in_dim(state[0], key_part, offset, 1),
            lax.dynamic_update_slice_in_dim(state[1], value_part, offset, 1),
        )

    key_all, value_all = lax.fori_loop(0, span_rows // block_rows, key_step, (empty, empty))
    joined = jnp.concatenate(
        [
            key_all.reshape(batch_rows, span_rows, model_width),
            value_all.reshape(batch_rows, span_rows, model_width),
        ],
        -1,
    )
    summed_keys = jnp.swapaxes(
        lax.psum_scatter(jnp.swapaxes(joined, 0, 1), "seq", scatter_dimension=0, tiled=True), 0, 1
    )
    key_grad = summed_keys[..., :model_width].reshape(shape_heads)
    value_grad = summed_keys[..., model_width:]
    flat_len = batch_rows * local_len
    query_low = (
        rotate_back(query_grad, cosine, sine).astype(jnp.bfloat16).reshape(flat_len, model_width)
    )
    key_low = (
        rotate_back(key_grad, cosine, sine).astype(jnp.bfloat16).reshape(flat_len, model_width)
    )
    value_low = value_grad.astype(jnp.bfloat16).reshape(flat_len, model_width)
    grad_input = (
        first_grad
        + back_product(query_low, w_query)
        + back_product(key_low, w_key)
        + back_product(value_low, w_value)
    )
    grad_query = outer_sum(flat_tokens, query_low)
    grad_key = outer_sum(flat_tokens, key_low)
    value_weight_gradient = outer_sum(flat_tokens, value_low)
    shares = (
        lax.psum_scatter(grad_query, "seq", scatter_dimension=0, tiled=True),
        lax.psum_scatter(grad_key, "seq", scatter_dimension=0, tiled=True),
        lax.psum_scatter(value_weight_gradient, "seq", scatter_dimension=0, tiled=True),
        lax.psum_scatter(grad_out, "seq", scatter_dimension=0, tiled=True),
        lax.psum_scatter(grad_gate, "seq", scatter_dimension=0, tiled=True),
        lax.psum_scatter(grad_up, "seq", scatter_dimension=0, tiled=True),
        lax.psum_scatter(grad_down, "seq", scatter_dimension=0, tiled=True),
        lax.psum_scatter(grad_gain_attn, "seq", scatter_dimension=0, tiled=True),
        lax.psum_scatter(grad_gain_ffn, "seq", scatter_dimension=0, tiled=True),
    )
    results = (
        lax.psum(shares[0].astype(jnp.bfloat16), "batch").astype(jnp.float32),
        lax.psum(shares[1].astype(jnp.bfloat16), "batch").astype(jnp.float32),
        lax.psum(shares[2].astype(jnp.bfloat16), "batch").astype(jnp.float32),
        lax.psum(shares[3].astype(jnp.bfloat16), "batch").astype(jnp.float32),
        lax.psum(shares[4].astype(jnp.bfloat16), "batch").astype(jnp.float32),
        lax.psum(shares[5].astype(jnp.bfloat16), "batch").astype(jnp.float32),
        lax.psum(shares[6].astype(jnp.bfloat16), "batch").astype(jnp.float32),
        lax.psum(shares[7].astype(jnp.bfloat16), "batch").astype(jnp.float32),
        lax.psum(shares[8].astype(jnp.bfloat16), "batch").astype(jnp.float32),
    )
    output_rows = output.reshape(batch_rows, local_len, model_width)
    input_rows = grad_input.reshape(batch_rows, local_len, model_width)
    return (
        output_rows,
        input_rows,
        results[0],
        results[1],
        results[2],
        results[3],
        results[4],
        results[5],
        results[6],
        results[7],
        results[8],
    )


MESH = pl.DeviceIdType.MESH
F32 = jnp.float32
BF16 = jnp.bfloat16


def mm(a, b):
    return lax.dot_general(a, b, (((1,), (0,)), ((), ())), preferred_element_type=F32)


def mm_nt(a, b):
    return lax.dot_general(a, b, (((1,), (1,)), ((), ())), preferred_element_type=F32)


def scratch_plan(tok, d, f, n, nb):
    nz, plane, heads = n // 2, 2 * nb * tok, HEADS
    vm = pltpu.VMEM
    dma = lambda *shape: pltpu.SemaphoreType.DMA(shape)
    return dict(
        wq=vm((d, d), BF16), wk=vm((d, d), BF16), wv=vm((d, d), BF16), wo=vm((d, d), BF16),
        wg=vm((d, f), BF16), wu=vm((d, f), BF16), wd=vm((f, d), BF16),
        cos=vm((nz, 2 * tok, 128), F32), sin=vm((nz, 2 * tok, 128), F32),
        ids=vm((1, tok), jnp.int32), cot=vm((tok, d), BF16), ga=vm((d,), F32), gf=vm((d,), F32),
        x_all=vm((n, tok, d), BF16), q_all=vm((n, tok, d), BF16), do_all=vm((n, tok, d), BF16),
        k_all=vm((nz, 2 * tok, d), BF16), v_all=vm((nz, 2 * tok, d), BF16),
        st_all=vm((n, 32, tok), F32), id_all=vm((n, 8, tok), jnp.int32),
        idcol=vm((tok, 128), F32), bias=vm((2 * tok, 2 * tok), F32),
        m=vm((heads // 2, 2 * tok, 128), F32), l=vm((heads // 2, 2 * tok, 128), F32),
        delta=vm((heads // 2, 2 * tok, 128), F32),
        acc=vm((tok, d), F32), acc2=vm((tok, d), F32),
        olow=vm((tok, d), BF16), hb=vm((tok, d), BF16), h1=vm((tok, d), F32), n1=vm((tok, d), F32),
        ri1=vm((tok, 128), F32), dr=vm((tok, d), F32),
        act=vm((tok, f), BF16),
        dg=vm((tok, f), BF16), du=vm((tok, f), BF16), dmo=vm((tok, d), BF16), dattn=vm((tok, d), BF16),
        dq=vm((tok, d), BF16), dk=vm((tok, d), BF16), dv=vm((tok, d), BF16),
        hT=vm((d, tok), BF16), xT=vm((d, tok), BF16), oT=vm((d, tok), BF16),
        gl=vm((8, d), F32), out_v=vm((tok, d), F32), gin_v=vm((tok, d), F32),
        hT_b=vm((d, plane), BF16), dmo_b=vm((plane, d), BF16),
        wgT=vm((f // nb, d), BF16), wuT=vm((f // nb, d), BF16), tmpT=vm((128, d), BF16),
        act_x=vm((f // nb, plane), BF16), da_x=vm((f // nb, plane), BF16),
        fa=vm((f // nb, plane), F32), fb=vm((f // nb, plane), F32), dgu=vm((2, f // nb, plane), BF16),
        xT_b=vm((d, plane), BF16), o2=vm((d, 2 * tok), BF16), da2=vm((2 * tok, d), BF16), at_b=vm((2, plane, d // 2), BF16), gl_b=vm((2 * nb, 8, d), F32),
        pgu=vm((2, d, f // nb), BF16), pdn=vm((n, f // (nb * n), d), BF16),
        pat=vm((d, d // 2), BF16), pq=vm((n, d // (2 * n), d // 2), BF16), pout=vm((d, d), BF16),
        ugu=vm((2, 2, d // nz, f // nb), BF16), udn=vm((2, 2, f // (nb * n), d), BF16),
        uat=vm((2, d // nz, d // 2), BF16), uq=vm((2, 2, d // (2 * n), d // 2), BF16),
        uout=vm((2, d // nz, d), BF16), rout=vm((nz, d // nz, d), BF16), sout=vm((2, d // n, d), BF16),
        rso=vm((nb, 2, d // (2 * n), d // 2), BF16), fso=vm((2, d // (2 * n), d // 2), BF16),
        rgu=vm((2, nz, d // nz, f // nb), BF16), rdn=vm((nz, 2, f // (nb * n), d), BF16), rat=vm((nz, d // nz, d // 2), BF16), rqz=vm((nz, 2, d // (2 * n), d // 2), BF16),
        sgu=vm((2, d // nz, f // nb), BF16), sdn=vm((2, f // (nb * n), d), BF16), sat=vm((d // nz, d // 2), BF16), sq=vm((2, d // (2 * n), d // 2), BF16),
        gz=vm((nz, 8, d), F32), gsum=vm((8, d), F32),
        wsem=dma(14), osem=dma(2), ssem=dma(230), fsem=dma(5, n), bsem=dma(6, n),
        rx=dma(2, n), rq=dma(n), rdo=dma(2, n), rst=dma(n), rid=dma(n),
        rh=dma(2 * nb), rdmo=dma(2 * nb), rax=dma(1), rda=dma(1), zfar=dma(6, 2),
        rxt=dma(2 * nb), ro2=dma(2), rda2=dma(2), zout=dma(nz), rrso=dma(nb), fout=dma(nb), rat_in=dma(2, 2 * nb), rgl=dma(2 * nb),
        zgu=dma(2, nz), zdn=dma(nz), zat=dma(nz), zq=dma(nz), zgl=dma(nz),
        fgu=dma(2, nb), fdn=dma(nb), fat=dma(nb), fq=dma(nb), fgl=dma(1),
    )


INPUTS = ("ids_h", "tok_h", "cot_h", "ga_h", "gf_h", "cos_h", "sin_h", "wq_h", "wk_h", "wv_h", "wo_h", "wg_h", "wu_h", "wd_h")
OUTPUTS = ("out_h", "gin_h", "oat_h", "ogu_h", "odn_h", "oout_h", "oq_h", "ogl_h")


def layer_kernel(plan_names, tok, d, f, n, nb, *refs):
    r = types.SimpleNamespace(**dict(zip(INPUTS + OUTPUTS + plan_names, refs)))
    nz, pairs = n // 2, d // 128
    fs, dh, blk = f // nb, d // 2, d // nz
    b, s = lax.axis_index("batch"), lax.axis_index("seq")
    z, c = s // 2, lax.rem(s, 2)
    by, bx = b // 2, lax.rem(b, 2)
    e = 2 * b + c
    sib = (b, s + 1 - 2 * c)
    pending, used = [], [0]

    def remote(src, dst, ssem, rsem, dev):
        return pltpu.make_async_remote_copy(
            src_ref=src, dst_ref=dst, send_sem=ssem, recv_sem=rsem, device_id=dev, device_id_type=MESH
        )

    def send_lazy(make):
        at = used[0]
        used[0] += 1
        pending.append((make, at))
        cond, src, dst, rsem, dev = make()

        @pl.when(cond)
        def _():
            remote(src, dst, r.ssem.at[at], rsem, dev).start()

    def send(cond, src, dst, rsem, dev):
        send_lazy(lambda: (cond, src, dst, rsem, dev))

    def plane_send_lazy(make, to_b, to_c, also=None):
        def here():
            return (b == to_b) & (c == to_c)

        def wanted(cond):
            return cond if also is None else cond & also()

        send_lazy(lambda: (wanted(jnp.logical_not(here())), *make(), (to_b, 2 * z + to_c)))

        @pl.when(wanted(here()))
        def _():
            pltpu.make_async_copy(*make()).start()

    def plane_send(src, dst, rsem, to_b, to_c):
        plane_send_lazy(lambda: (src, dst, rsem), to_b, to_c)

    def arrived(dst, rsem):
        remote(dst, dst, r.ssem.at[0], rsem, sib).wait_recv()

    loads = {}
    for i, (name, src, dst) in enumerate(
        (
            ("tok", r.tok_h.at[0], r.x_all.at[s]), ("ids", r.ids_h, r.ids), ("ga", r.ga_h, r.ga), ("gf", r.gf_h, r.gf),
            ("cot", r.cot_h.at[0], r.cot),
        )
    ):
        loads[name] = pltpu.make_async_copy(src, dst, r.wsem.at[9 + i])
    loads["tok"].start()
    loads["ids"].start()
    bar = pltpu.get_barrier_semaphore()
    for zz in range(nz):
        for cc in range(2):
            @pl.when(2 * zz + cc != s)
            def _(zz=zz, cc=cc):
                pl.semaphore_signal(bar, inc=1, device_id=(b, 2 * zz + cc), device_id_type=MESH)
    for bb in range(nb):
        for cc in range(2):
            @pl.when(bb != b)
            def _(bb=bb, cc=cc):
                pl.semaphore_signal(bar, inc=1, device_id=(bb, 2 * z + cc), device_id_type=MESH)
    for i, name in enumerate(("wk", "wv", "wq", "cos", "sin", "wo", "wg", "wu", "wd")):
        loads[name] = pltpu.make_async_copy(getattr(r, name + "_h"), getattr(r, name), r.wsem.at[i])
        loads[name].start()
    for name in ("ga", "gf", "cot"):
        loads[name].start()
    loads["ids"].wait()
    r.id_all[s] = jnp.broadcast_to(r.ids[...], (8, tok))
    loads["tok"].wait()
    pl.semaphore_wait(bar, n - 1 + 2 * (nb - 1))

    always = s >= 0
    half = tok // 2

    def rows_of(ref, t, ch):
        return ref.at[t, pl.ds(ch * half, half)]

    right, left = (b, s + 2), (b, s - 2)
    send(always, r.id_all.at[s], r.id_all.at[s], r.rid.at[s], sib)
    for ch in range(2):
        mine = rows_of(r.x_all, s, ch)
        send(z + 1 < nz, mine, mine, r.rx.at[ch, s], right)
        send(always, mine, mine, r.rx.at[ch, s], sib)
    for zz in range(nz):
        for cc in range(2):
            send(z != zz, r.id_all.at[s], r.id_all.at[s], r.rid.at[s], (b, 2 * zz + cc))

    lane = lax.broadcasted_iota(jnp.int32, (tok, 128), 1)
    first = lane < 64
    half_mask = (jnp.where(first, 1.0, 0.0).astype(BF16), jnp.where(first, 0.0, 1.0).astype(BF16))

    def turn(u):
        low = lax.rem(lax.broadcasted_iota(jnp.int32, u.shape, 1), 64) < 32
        return jnp.where(low, pltpu.roll(u, 96, 1), pltpu.roll(u, 32, 1))

    def twice(u):
        return jnp.concatenate([u, u], axis=1)

    def stack(u):
        return jnp.concatenate([u * half_mask[0], u * half_mask[1]], axis=0)

    def unstack(u):
        return jnp.where(first, u[:tok], u[tok:])

    own = pl.ds(pl.multiple_of(c * tok, tok), tok)

    loads["wq"].wait()
    loads["cos"].wait()
    loads["sin"].wait()

    u = mm(r.x_all[s], r.wq[...])
    co, si = r.cos[z, own, :], r.sin[z, own, :]
    for p in range(pairs):
        part = u[:, p * 128:(p + 1) * 128]
        r.q_all[s, :, p * 128:(p + 1) * 128] = ((part * co + turn(part) * si) * 0.125).astype(BF16)
    send(always, r.q_all.at[s], r.q_all.at[s], r.rq.at[s], sib)
    for dz in range(1, nz):
        send(z - dz >= 0, r.q_all.at[s], r.q_all.at[s], r.rq.at[s], (b, s - 2 * dz))

    def transpose_into(dst, value):
        for p in range(d // 128):
            dst[p * 128:(p + 1) * 128, :] = value[:, p * 128:(p + 1) * 128].T.astype(BF16)

    tokens = pl.ds(pl.multiple_of(e * tok, tok), tok)
    side, across = 2 * by + 1 - bx, 2 * (1 - by) + bx

    def relay(slot_of, rsem, to_c):
        for source, target in ((lambda: 2 * side, across), (lambda: 2 * across + 1, side)):
            @pl.when(c == to_c)
            def _(source=source):
                arrived(slot_of(source()), rsem.at[source()])

            send_lazy(
                lambda source=source, target=target: (
                    c == to_c, slot_of(source()), slot_of(source()), rsem.at[source()], (target, s)
                )
            )

    def hT_slot(i):
        return r.hT_b.at[:, pl.ds(pl.multiple_of(i * tok, tok), tok)]

    def dmo_slot(i):
        return r.dmo_b.at[pl.ds(pl.multiple_of(i * tok, tok), tok), :]
    transpose_into(r.xT, r.x_all[s].astype(F32))
    for bb in range(nb):
        plane_send(r.xT, r.xT_b.at[:, tokens], r.rxt.at[e], bb, 1)
    r.idcol[...] = jnp.broadcast_to(r.ids[...].astype(F32), (128, tok)).T

    def ids_of(block):
        return jnp.concatenate(
            [r.id_all[2 * block, 0:1, :], r.id_all[2 * block + 1, 0:1, :]], axis=1
        ).astype(F32)

    def set_bias(block, local_is_query):
        shape = (tok, 2 * tok)
        mine = s * tok + lax.broadcasted_iota(jnp.int32, shape, 0)
        theirs = block * (2 * tok) + lax.broadcasted_iota(jnp.int32, shape, 1)
        my_id = twice(r.idcol[...])
        their_id = jnp.broadcast_to(ids_of(block), shape)
        causal = (theirs <= mine) if local_is_query else (mine <= theirs)
        allowed = (my_id == their_id) & causal & ((my_id != 0.0) | (mine == theirs))
        bias = jnp.where(allowed, 0.0, MASKED)
        r.bias[...] = jnp.concatenate([bias, bias], axis=0)

    units = fs // n

    def quarter_weights():
        for src, dst in ((r.wg, r.wgT), (r.wu, r.wuT)):
            for t in range(n):
                tile = src[:, pl.ds(pl.multiple_of((2 * t + by) * 128, 128), 128)].astype(F32)
                for p in range(pairs):
                    r.tmpT[:, p * 128:(p + 1) * 128] = tile[p * 128:(p + 1) * 128].T.astype(BF16)
                dst[t * units:(t + 1) * units, :] = r.tmpT[pl.ds(pl.multiple_of(bx * units, units), units), :]

    r.m[...] = jnp.full(r.m.shape, MASKED, F32)
    r.l[...] = jnp.zeros(r.l.shape, F32)
    r.acc[...] = jnp.zeros(r.acc.shape, F32)
    loads["wk"].wait()
    loads["wv"].wait()

    def forward_step(j, _):
        kb = z - j
        mine, other = 2 * kb + c, 2 * kb + 1 - c

        @pl.when(j > 0)
        def _():
            for ch in range(2):
                got = rows_of(r.x_all, mine, ch)
                arrived(got, r.rx.at[ch, mine])

                @pl.when(z + 1 < nz)
                def _():
                    remote(got, got, r.fsem.at[ch, mine], r.rx.at[ch, mine], right).start()

                remote(got, got, r.bsem.at[ch, mine], r.rx.at[ch, mine], sib).start()

            arrived(r.id_all.at[mine], r.rid.at[mine])

        for ch in range(2):
            arrived(rows_of(r.x_all, other, ch), r.rx.at[ch, other])
        arrived(r.id_all.at[other], r.rid.at[other])
        set_bias(kb, True)

        xb = r.x_all[pl.ds(2 * kb, 2)].reshape(2 * tok, d)
        u = mm(xb, r.wk[...])
        co, si = r.cos[kb], r.sin[kb]
        for p in range(pairs):
            part = u[:, p * 128:(p + 1) * 128]
            r.k_all[kb, :, p * 128:(p + 1) * 128] = (part * co + turn(part) * si).astype(BF16)
        r.v_all[kb] = mm(xb, r.wv[...]).astype(BF16)

        def pair(p, _):
            lanes = pl.ds(pl.multiple_of(p * 128, 128), 128)
            qp, kp, vp = r.q_all[s, :, lanes], r.k_all[kb, :, lanes], r.v_all[kb, :, lanes]
            sc = mm_nt(stack(qp), kp) + r.bias[...]
            m_old = r.m[p]
            m_new = jnp.maximum(m_old, jnp.max(sc, axis=1, keepdims=True))
            alpha = jnp.exp(m_old - m_new)
            ex = jnp.exp(sc - twice(m_new))
            r.m[p] = m_new
            r.l[p] = r.l[p] * alpha + jnp.sum(ex, axis=1, keepdims=True)
            r.acc[:, lanes] = r.acc[:, lanes] * unstack(alpha) + unstack(mm(ex.astype(BF16), vp))
            return 0

        lax.fori_loop(0, pairs, pair, 0, unroll=True)

        @pl.when((j == 0) & (c == 0))
        def _():
            loads["wg"].wait()
            loads["wu"].wait()
            quarter_weights()

        return 0

    lax.fori_loop(0, z + 1, forward_step, 0)

    def finish(p, _):
        lanes = pl.ds(pl.multiple_of(p * 128, 128), 128)
        r.acc[:, lanes] = r.acc[:, lanes] / unstack(r.l[p])
        r.m[p] = r.m[p] + jnp.log(r.l[p])
        return 0

    lax.fori_loop(0, pairs, finish, 0, unroll=True)
    r.olow[...] = r.acc[...].astype(BF16)

    loads["wo"].wait()
    loads["ga"].wait()
    loads["gf"].wait()
    loads["cot"].wait()
    gain_a, gain_f = r.ga[...].reshape(1, d), r.gf[...].reshape(1, d)
    r1 = r.x_all[s].astype(F32) + mm(r.olow[...], r.wo[...])
    ri1 = lax.rsqrt(jnp.mean(r1 * r1, axis=1, keepdims=True) + EPSILON)
    r.ri1[...] = jnp.broadcast_to(ri1, (tok, 128))
    n1 = r1 * ri1
    r.n1[...] = n1
    h1 = n1 * gain_a
    r.h1[...] = h1
    r.hb[...] = h1.astype(BF16)
    transpose_into(r.hT, h1)
    for to_b in (b, side, across):
        plane_send(r.hT, r.hT_b.at[:, tokens], r.rh.at[e], to_b, 0)
    transpose_into(r.oT, r.acc[...])

    @pl.when(c == 1)
    def _():
        loads["wg"].wait()
        loads["wu"].wait()

    def gate_at(i):
        return (slice((i // 2) * tok, (i // 2 + 1) * tok), slice((i % 2) * 512, (i % 2 + 1) * 512))

    def up_at(i):
        return gate_at(i + f // 512)

    for i in range(f // 512):
        at = slice(i * 512, (i + 1) * 512)
        g = mm(r.hb[...], r.wg[:, at])
        u = mm(r.hb[...], r.wu[:, at])
        r.fa[gate_at(i)] = g
        r.fa[up_at(i)] = u
        a = g / (1.0 + jnp.exp(-g)) * u
        r.act[:, at] = a.astype(BF16)
    loads["wd"].wait()
    r2 = r.h1[...] + mm(r.act[...], r.wd[...])
    ri2 = lax.rsqrt(jnp.mean(r2 * r2, axis=1, keepdims=True) + EPSILON)
    n2 = r2 * ri2
    r.out_v[...] = n2 * gain_f
    out_copy = pltpu.make_async_copy(r.out_v, r.out_h, r.osem.at[0])
    out_copy.start()
    ct = r.cot[...].astype(F32)
    gain_ffn = jnp.sum(ct * n2, axis=0, keepdims=True)
    t2 = ct * gain_f
    dr2 = ri2 * (t2 - n2 * jnp.mean(n2 * t2, axis=1, keepdims=True))
    r.dr[...] = dr2
    r.dmo[...] = dr2.astype(BF16)
    for to_b in (b, side, across):
        plane_send(r.dmo, r.dmo_b.at[tokens, :], r.rdmo.at[e], to_b, 1)

    for i in range(f // 512):
        at = slice(i * 512, (i + 1) * 512)
        da = mm_nt(r.dmo[...], r.wd[at, :])
        g, u = r.fa[gate_at(i)], r.fa[up_at(i)]
        sg = 1.0 / (1.0 + jnp.exp(-g))
        r.dg[:, at] = (da * u * (sg * (1.0 + g * (1.0 - sg)))).astype(BF16)
        r.du[:, at] = (da * (g * sg)).astype(BF16)
    dh1 = r.dr[...] + mm_nt(r.dg[...], r.wg[...]) + mm_nt(r.du[...], r.wu[...])
    n1 = r.n1[...]
    gain_attn = jnp.sum(dh1 * n1, axis=0, keepdims=True)
    t1 = dh1 * gain_a
    dr1 = r.ri1[:, 0:1] * (t1 - n1 * jnp.mean(n1 * t1, axis=1, keepdims=True))
    r.dr[...] = dr1
    r.dattn[...] = dr1.astype(BF16)
    r.gl[...] = jnp.concatenate([gain_attn, gain_ffn, jnp.zeros((6, d), F32)], axis=0)
    plane_send(r.gl, r.gl_b.at[e], r.rgl.at[e], 0, 0)
    plane_send_lazy(lambda: (r.oT, r.o2.at[:, own], r.ro2.at[c]), b, 1)
    plane_send_lazy(lambda: (r.dattn, r.da2.at[own, :], r.rda2.at[c]), b, 1)

    r.do_all[s] = mm_nt(r.dattn[...], r.wo[...]).astype(BF16)
    for ch in range(2):
        mine = rows_of(r.do_all, s, ch)
        send(z > 0, mine, mine, r.rdo.at[ch, s], left)
        send(always, mine, mine, r.rdo.at[ch, s], sib)

    stats = jnp.zeros((tok, 128), F32)
    for p in range(pairs):
        prod = r.do_all[s, :, p * 128:(p + 1) * 128].astype(F32) * r.acc[:, p * 128:(p + 1) * 128]
        for h in range(2):
            head = 2 * p + h
            part = jnp.sum(jnp.where(first == (h == 0), prod, 0.0), axis=1, keepdims=True)
            part = jnp.broadcast_to(part, (tok, 128))
            r.delta[p, h * tok:(h + 1) * tok] = part
            stats = jnp.where(lane == head, r.m[p, h * tok:(h + 1) * tok], stats)
            stats = jnp.where(lane == 16 + head, part, stats)
    r.st_all[s] = stats.T[0:32, :]
    send(z > 0, r.st_all.at[s], r.st_all.at[s], r.rst.at[s], left)
    send(always, r.st_all.at[s], r.st_all.at[s], r.rst.at[s], sib)

    def each_source(dst_of, rsem, count):
        for i in range(count):
            arrived(dst_of(i), rsem.at[i])

    end = (z == 0) | (z == nz - 1)

    def on(to_c, some):
        return c == to_c

    def share(src_of, dst_of, far_of, to_c, some=False):
        near = lambda: jnp.where(z < nz // 2, 0, nz - 1)
        for i in range(2):
            send_lazy(
                lambda i=i: (
                    on(to_c, some) & end, src_of(jnp.abs(nz - 1 - i - z)), *far_of(i),
                    (b, 2 * jnp.where(z == 0, 1, nz - 2) + to_c),
                )
            )
        send_lazy(
            lambda: (on(to_c, some) & jnp.logical_not(end), src_of(near()), *dst_of(), (b, 2 * near() + to_c))
        )

    def share_near(src_of, dst_of, far_of, to_c, some=False):
        send_lazy(
            lambda: (on(to_c, some) & end, src_of(jnp.where(z == 0, 1, nz - 2)), *dst_of(),
                     (b, 2 * jnp.where(z == 0, 1, nz - 2) + to_c))
        )

    def pass_on(own_of, dst_of, far_of, to_c, some=False):
        def here():
            return on(to_c, some) & jnp.logical_not(end)

        for i in range(2):
            def target(i=i):
                return nz - 1 - z if i else jnp.where(z == 1, nz - 1, 0)

            @pl.when(here())
            def _(i=i, target=target):
                far, sem = far_of(i)
                arrived(far, sem)
                far[...] = (own_of(target())[...].astype(F32) + far[...].astype(F32)).astype(BF16)

            send_lazy(lambda i=i, target=target: (here(), far_of(i)[0], *dst_of(), (b, 2 * target() + to_c)))

    gate_up = [
        (
            lambda zz, k=k: r.pgu.at[k, pl.ds(pl.multiple_of(zz * blk, blk), blk), :],
            lambda k=k: (r.rgu.at[k, z], r.zgu.at[k, z]),
            lambda i, k=k: (r.ugu.at[k, i], r.zfar.at[k, i]),
            0,
        )
        for k in range(2)
    ]
    down = (
        lambda zz: r.pdn.at[pl.ds(2 * zz, 2)],
        lambda: (r.rdn.at[z], r.zdn.at[z]),
        lambda i: (r.udn.at[i], r.zfar.at[2, i]),
        1,
    )
    outp = (
        lambda zz: r.pout.at[pl.ds(pl.multiple_of(zz * blk, blk), blk), :],
        lambda: (r.rout.at[z], r.zout.at[z]),
        lambda i: (r.uout.at[i], r.zfar.at[5, i]),
        1,
    )
    early = (
        lambda zz: r.pq.at[pl.ds(2 * zz, 2)],
        lambda: (r.rqz.at[z], r.zq.at[z]),
        lambda i: (r.uq.at[i], r.zfar.at[3, i]),
        1,
    )
    late = (
        lambda zz: r.pat.at[pl.ds(pl.multiple_of(zz * blk, blk), blk), :],
        lambda: (r.rat.at[z], r.zat.at[z]),
        lambda i: (r.uat.at[i], r.zfar.at[4, i]),
        1,
    )

    def hidden_again():
        @pl.when(c == 0)
        def _():
            for i in range(2 * nb):
                @pl.when((i != 2 * side) & (i != 2 * across + 1))
                def _(i=i):
                    arrived(hT_slot(i), r.rh.at[i])

            for i in range(2 * nb * tok // 512):
                at = slice(i * 512, (i + 1) * 512)
                g = mm(r.wgT[...], r.hT_b[:, at])
                u = mm(r.wuT[...], r.hT_b[:, at])
                sg = 1.0 / (1.0 + jnp.exp(-g))
                r.act_x[:, at] = (g * sg * u).astype(BF16)
                r.fa[:, at] = u * (sg * (1.0 + g * (1.0 - sg)))
                r.fb[:, at] = g * sg

        send_lazy(lambda: (c == 0, r.act_x, r.act_x, r.rax.at[0], sib))

    def hidden_sums():
        @pl.when(c == 1)
        def _():
            for i in range(2 * nb):
                @pl.when((i != 2 * side) & (i != 2 * across + 1))
                def _(i=i):
                    arrived(dmo_slot(i), r.rdmo.at[i])

            rows_d = jnp.concatenate(
                [r.wd[pl.ds(pl.multiple_of(t * nb * units + b * units, units), units), :] for t in range(n)], axis=0
            )
            r.da_x[...] = mm_nt(rows_d, r.dmo_b[...]).astype(BF16)

        send_lazy(lambda: (c == 1, r.da_x, r.da_x, r.rda.at[0], sib))

        @pl.when(c == 1)
        def _():
            arrived(r.act_x, r.rax.at[0])
            r.pdn[...] = mm(r.act_x[...], r.dmo_b[...]).astype(BF16).reshape(n, units, d)

        share(*down)
        share_near(*down)
        for k in range(2):
            @pl.when(c == 0)
            def _(k=k):
                if k == 0:
                    arrived(r.da_x, r.rda.at[0])
                r.dgu[k] = (r.da_x[...].astype(F32) * (r.fb if k else r.fa)[...]).astype(BF16)
                r.pgu[k] = mm_nt(r.hT_b[...], r.dgu[k]).astype(BF16)

            share(*gate_up[k])
            share_near(*gate_up[k])
        pass_on(*outp)

    @pl.when(c == 1)
    def _():
        for i in range(2):
            arrived(r.o2.at[:, pl.ds(i * tok, tok)], r.ro2.at[i])
            arrived(r.da2.at[pl.ds(i * tok, tok), :], r.rda2.at[i])
        r.pout[...] = mm(r.o2[...], r.da2[...]).astype(BF16)

    share(*outp)
    share_near(*outp)

    relay(hT_slot, r.rh, 0)

    r.acc[...] = jnp.zeros(r.acc.shape, F32)

    def query_step(kb, _):
        @pl.when(kb == jnp.maximum(z - 1, 0))
        def _():
            relay(dmo_slot, r.rdmo, 1)

        set_bias(kb, True)

        def pair(p, _):
            lanes = pl.ds(pl.multiple_of(p * 128, 128), 128)
            qp, kp, vp = r.q_all[s, :, lanes], r.k_all[kb, :, lanes], r.v_all[kb, :, lanes]
            dop = r.do_all[s, :, lanes]
            pf = jnp.exp(mm_nt(stack(qp), kp) + r.bias[...] - twice(r.m[p]))
            dp = mm_nt(stack(dop), vp)
            ds = (pf * (dp - twice(r.delta[p]))).astype(BF16)
            r.acc[:, lanes] += unstack(mm(ds, kp))
            return 0

        lax.fori_loop(0, pairs, pair, 0, unroll=True)
        return 0

    lax.fori_loop(0, z + 1, query_step, 0)

    def turn_back(src, dst, factor):
        co, si = r.cos[z, own, :], r.sin[z, own, :]
        for p in range(pairs):
            g = src[:, p * 128:(p + 1) * 128] * factor
            dst[:, p * 128:(p + 1) * 128] = (g * co - turn(g) * si).astype(BF16)

    turn_back(r.acc, r.dq, 0.125)

    def half_send(k, value, h, bb):
        plane_send_lazy(
            lambda: (value.at[:, pl.ds(h * dh, dh)], r.at_b.at[k, tokens, :], r.rat_in.at[k, e]), bb, 1
        )

    for bb in range(nb):
        half_send(0, r.dq, bb % 2, bb)
    hidden_again()

    r.acc[...] = jnp.zeros(r.acc.shape, F32)
    r.acc2[...] = jnp.zeros(r.acc2.shape, F32)

    def key_step(j):
        qb = z + j
        mine, other = 2 * qb + c, 2 * qb + 1 - c

        @pl.when(j > 0)
        def _():
            arrived(r.id_all.at[mine], r.rid.at[mine])
            arrived(r.id_all.at[other], r.rid.at[other])
            arrived(r.q_all.at[mine], r.rq.at[mine])
            remote(r.q_all.at[mine], r.q_all.at[mine], r.bsem.at[2, mine], r.rq.at[mine], sib).start()
            blocks = [(rows_of(r.do_all, mine, ch), r.rdo.at[ch, mine]) for ch in range(2)]
            blocks.append((r.st_all.at[mine], r.rst.at[mine]))
            for i, (got, sem) in enumerate(blocks):
                arrived(got, sem)

                @pl.when(z > 0)
                def _():
                    remote(got, got, r.fsem.at[2 + i, mine], sem, left).start()

                remote(got, got, r.bsem.at[3 + i, mine], sem, sib).start()

        arrived(r.q_all.at[other], r.rq.at[other])
        for ch in range(2):
            arrived(rows_of(r.do_all, other, ch), r.rdo.at[ch, other])
        arrived(r.st_all.at[other], r.rst.at[other])
        set_bias(qb, False)

        def pair(p, _):
            lanes = pl.ds(pl.multiple_of(p * 128, 128), 128)
            kp, vp = r.k_all[z, own, lanes], r.v_all[z, own, lanes]
            qp = r.q_all[pl.ds(2 * qb, 2), :, lanes].reshape(2 * tok, 128)
            dop = r.do_all[pl.ds(2 * qb, 2), :, lanes].reshape(2 * tok, 128)

            def row(base):
                return jnp.concatenate(
                    [
                        jnp.broadcast_to(
                            jnp.concatenate(
                                [r.st_all[2 * qb + i, pl.ds(base + 2 * p + h, 1), :] for i in range(2)], axis=1
                            ),
                            (tok, 2 * tok),
                        )
                        for h in range(2)
                    ],
                    axis=0,
                )

            pf = jnp.exp(mm_nt(stack(kp), qp) + r.bias[...] - row(0))
            dp = mm_nt(stack(vp), dop)
            ds = (pf * (dp - row(16))).astype(BF16)
            r.acc2[:, lanes] += unstack(mm(pf.astype(BF16), dop))
            r.acc[:, lanes] += unstack(mm(ds, qp))
            return 0

        lax.fori_loop(0, pairs, pair, 0, unroll=True)

    def keys_done():
        turn_back(r.acc, r.dk, 1.0)
        r.dv[...] = r.acc2[...].astype(BF16)
        for bb in range(nb):
            half_send(1, r.dv if bb >= 2 else r.dk, bb % 2, bb)
    last = nz - z
    sums_at = jnp.where(z == 0, 2, jnp.where(z == nz - 1, 0, last))

    def key_loop(j, _):
        pl.when(j == sums_at)(hidden_sums)

        @pl.when(j < last)
        def _():
            key_step(j)

        pl.when(j == last - 1)(keys_done)
        return 0

    lax.fori_loop(0, last + 1, key_loop, 0)
    r.gin_v[...] = (
        r.dr[...] + mm_nt(r.dq[...], r.wq[...]) + mm_nt(r.dk[...], r.wk[...]) + mm_nt(r.dv[...], r.wv[...])
    )
    pltpu.make_async_copy(r.gin_v, r.gin_h, r.osem.at[1]).start()


    @pl.when(c == 1)
    def _():
        each_source(lambda i: r.xT_b.at[:, pl.ds(i * tok, tok)], r.rxt, 2 * nb)

    def attn_sum(k):
        @pl.when(c == 1)
        def _():
            each_source(lambda i: r.at_b.at[k, pl.ds(i * tok, tok), :], r.rat_in.at[k], 2 * nb)
            if k:
                r.pat[...] = mm(r.xT_b[...], r.at_b[k]).astype(BF16)
            else:
                part = d // (2 * n)
                some = jnp.concatenate(
                    [r.xT_b[pl.ds(pl.multiple_of((2 * t + by) * part, part), part), :] for t in range(n)], axis=0
                )
                r.pq[...] = mm(some, r.at_b[k]).astype(BF16).reshape(n, part, dh)

        share(*(late if k else early))

    def totals(total_of, own, recv_of, rsem_of):
        def add(slots):
            total = own().astype(F32)
            for at in slots:
                arrived(recv_of(at), rsem_of(at))
                total = total + recv_of(at)[...].astype(F32)
            total_of()[...] = total.astype(BF16).reshape(total_of().shape)

        pl.when(end)(lambda: add((1, 2)))
        pl.when(jnp.logical_not(end))(lambda: add((jnp.where(z == 1, 0, nz - 1), nz - 1 - z)))

    def spread(src_of, dst_of, from_c, some=False):
        for bb in range(nb):
            for cc in range(2):
                def here(bb=bb, cc=cc):
                    return (b == bb) & (c == cc)

                send_lazy(
                    lambda bb=bb, cc=cc, here=here: (
                        on(from_c, some) & jnp.logical_not(here()), src_of(cc), *dst_of(), (bb, 2 * z + cc)
                    )
                )

                @pl.when(on(from_c, some) & here())
                def _(cc=cc):
                    pltpu.make_async_copy(src_of(cc), *dst_of()).start()

    rows = pl.ds(pl.multiple_of(z * blk, blk), blk)
    quarter = blk // 4

    def out_total():
        @pl.when(c == 1)
        def _():
            total = None
            for bb in range(nb):
                arrived(r.rso.at[bb], r.rrso.at[bb])
                part = r.rso[bb].astype(F32)
                total = part if total is None else total + part
            r.fso[...] = total.astype(BF16)

        spread(lambda cc: r.fso.at[cc], lambda: (r.oout_h.at[b], r.fout.at[b]), 1)

    def gate_up_total(k):
        @pl.when(c == 0)
        def _():
            totals(
                lambda: r.sgu.at[k], lambda: r.pgu[k, rows, :], lambda at: r.rgu.at[k, at], lambda at: r.zgu.at[k, at]
            )

        spread(
            lambda cc: r.sgu.at[k, pl.ds(cc * (blk // 2), blk // 2), :], lambda: (r.ogu_h.at[b, k], r.fgu.at[k, b]), 0
        )

    attn_sum(0)
    @pl.when(c == 1)
    def _():
        totals(lambda: r.sout, lambda: r.pout[rows, :], lambda at: r.rout.at[at], lambda at: r.zout.at[at])

    for bb in range(nb):
        at = (slice(None), pl.ds((bb // 2) * quarter, quarter), pl.ds((bb % 2) * dh, dh))
        send((c == 1) & (b != bb), r.sout.at[at], r.rso.at[b], r.rrso.at[b], (bb, s))

        @pl.when((c == 1) & (b == bb))
        def _(at=at):
            pltpu.make_async_copy(r.sout.at[at], r.rso.at[b], r.rrso.at[b]).start()

    pass_on(*gate_up[0])
    gate_up_total(0)
    pass_on(*gate_up[1])
    gate_up_total(1)
    pass_on(*down)
    attn_sum(1)
    for part in (early, late):
        share_near(*part)
    pass_on(*early)
    out_total()

    adds = (b == 0) & (c == 0)

    @pl.when(adds)
    def _():
        total = None
        for i in range(2 * nb):
            arrived(r.gl_b.at[i], r.rgl.at[i])
            total = r.gl_b[i] if total is None else total + r.gl_b[i]
        r.gz[z] = total

    for zz in range(nz):
        send(adds & (z != zz), r.gz.at[z], r.gz.at[z], r.zgl.at[z], (0, 2 * zz))

    @pl.when(adds)
    def _():
        total = r.gz[z]
        for dz in range(1, nz):
            at = lax.rem(z + dz, nz)
            arrived(r.gz.at[at], r.zgl.at[at])
            total = total + r.gz[at]
        r.gsum[...] = total

    for bb in range(nb):
        for cc in range(2):
            here = (bb == 0) and (cc == 0)
            if not here:
                send(adds, r.gsum, r.ogl_h, r.fgl.at[0], (bb, 2 * z + cc))

    @pl.when(adds)
    def _():
        pltpu.make_async_copy(r.gsum, r.ogl_h, r.fgl.at[0]).start()

    @pl.when(c == 1)
    def _():
        totals(lambda: r.sdn, lambda: r.pdn[pl.ds(2 * z, 2)], lambda at: r.rdn.at[at], lambda at: r.zdn.at[at])

    spread(lambda cc: r.sdn.at[cc], lambda: (r.odn_h.at[b], r.fdn.at[b]), 1)
    pass_on(*late)

    @pl.when(c == 1)
    def _():
        totals(lambda: r.sq, lambda: r.pq[pl.ds(2 * z, 2)], lambda at: r.rqz.at[at], lambda at: r.zq.at[at])

    spread(lambda cc: r.sq.at[cc], lambda: (r.oq_h.at[b], r.fq.at[b]), 1)

    @pl.when(c == 1)
    def _():
        totals(lambda: r.sat, lambda: r.pat[rows, :], lambda at: r.rat.at[at], lambda at: r.zat.at[at])

    spread(
        lambda cc: r.sat.at[pl.ds(cc * (blk // 2), blk // 2), :], lambda: (r.oat_h.at[b], r.fat.at[b]), 1
    )

    for bb in range(nb):
        arrived(r.ogu_h.at[bb, 0], r.fgu.at[0, bb])
        arrived(r.ogu_h.at[bb, 1], r.fgu.at[1, bb])
        arrived(r.odn_h.at[bb], r.fdn.at[bb])
        arrived(r.oq_h.at[bb], r.fq.at[bb])
        arrived(r.oout_h.at[bb], r.fout.at[bb])
        arrived(r.oat_h.at[bb], r.fat.at[bb])
    arrived(r.ogl_h, r.fgl.at[0])
    out_copy.wait()
    pltpu.make_async_copy(r.gin_v, r.gin_h, r.osem.at[1]).wait()
    assert used[0] <= r.ssem.shape[0], used
    for make, at in pending:
        cond, src, dst, rsem, dev = make()

        @pl.when(cond)
        def _():
            remote(src, dst, r.ssem.at[at], rsem, dev).wait_send()

    def sent_on(t, _):
        @pl.when((lax.rem(t, 2) == c) & (t < s))
        def _():
            for ch in range(2):
                got = rows_of(r.x_all, t, ch)
                remote(got, got, r.bsem.at[ch, t], r.rx.at[ch, t], sib).wait_send()

                @pl.when(z + 1 < nz)
                def _():
                    remote(got, got, r.fsem.at[ch, t], r.rx.at[ch, t], right).wait_send()

        @pl.when((lax.rem(t, 2) == c) & (t > s))
        def _():
            remote(r.q_all.at[t], r.q_all.at[t], r.bsem.at[2, t], r.rq.at[t], sib).wait_send()
            blocks = [(rows_of(r.do_all, t, ch), r.rdo.at[ch, t]) for ch in range(2)]
            blocks.append((r.st_all.at[t], r.rst.at[t]))
            for i, (got, sem) in enumerate(blocks):
                remote(got, got, r.bsem.at[3 + i, t], sem, sib).wait_send()

                @pl.when(z > 0)
                def _():
                    remote(got, got, r.fsem.at[2 + i, t], sem, left).wait_send()
        return 0

    lax.fori_loop(0, n, sent_on, 0)


def unpack_kernel(
    n, nb, out_in, gin_in, oat_h, ogu_h, odn_h, oout_h, oq_h, ogl_h,
    out, gin, gq_h, gk_h, gv_h, go_h, gg_h, gu_h, gd_h, g1, g2,
    oat, ogu, odn, oout, oq, ogl, gq, gk, gv, go, gg, gu, gd, out_v, gin_v, isem, osem,
):
    s = lax.axis_index("seq")
    fs = ogu.shape[3]
    units, dh = odn.shape[1], odn.shape[2] // 2
    copy = pltpu.make_async_copy
    loads = [copy(a, b, isem.at[i]) for i, (a, b) in enumerate(
        ((ogu_h, ogu), (oat_h, oat), (odn_h, odn), (ogl_h, ogl), (out_in, out_v), (gin_in, gin_v), (oout_h, oout), (oq_h, oq)))]
    stores = [copy(a, b, osem.at[i]) for i, (a, b) in enumerate(
        ((gg, gg_h), (gu, gu_h), (gq, gq_h), (gk, gk_h), (gv, gv_h), (go, go_h), (gd, gd_h),
         (out_v, out.at[0]), (gin_v, gin.at[0])))]
    for load in loads:
        load.start()
    loads[0].wait()
    low = lax.broadcasted_iota(jnp.int32, (ogu.shape[2], 128), 1) < 64

    def interleave(k, dst):
        for t in range(n):
            for y in range(2):
                at = slice((t // 2) * 128, (t // 2 + 1) * 128)
                one, two = ogu[2 * y, k, :, at].astype(F32), ogu[2 * y + 1, k, :, at].astype(F32)
                if t % 2:
                    one = pltpu.roll(one, 64, 1)
                else:
                    two = pltpu.roll(two, 64, 1)
                dst[:, (2 * t + y) * 128:(2 * t + y + 1) * 128] = jnp.where(low, one, two)

    interleave(0, gg)
    stores[0].start()
    interleave(1, gu)
    stores[1].start()
    loads[1].wait()
    for m, (ref, bb) in enumerate(((gk, 0), (gv, 2))):
        ref[:, :dh] = oat[bb].astype(F32)
        ref[:, dh:] = oat[bb + 1].astype(F32)
        stores[3 + m].start()
    loads[6].wait()
    loads[7].wait()
    part = oout.shape[1]
    for m, (src, dst) in enumerate(((oq, gq), (oout, go))):
        for bb in range(nb):
            dst[(bb // 2) * part:(bb // 2 + 1) * part, (bb % 2) * dh:(bb % 2 + 1) * dh] = src[bb].astype(F32)
        stores[5 if m else 2].start()
    loads[2].wait()
    for bb in range(nb):
        gd[bb * units:(bb + 1) * units, :] = odn[bb].astype(F32)
    stores[6].start()
    for i in (4, 5):
        loads[i].wait()
        stores[3 + i].start()
    loads[3].wait()
    d = ogl.shape[1]
    own = d // n
    gains = pltpu.roll(ogl[...], lax.rem(d - s * own, d), 1)
    g1[...] = gains[0:1, :own]
    g2[...] = gains[1:2, :own]
    for store in stores:
        store.wait()


def rope_constants(length, head_dim):
    half = head_dim // 2
    inverse = np.exp(-2.0 * math.log(THETA) / head_dim * np.arange(half)).astype(np.float32)
    angle = np.arange(length, dtype=np.float32)[:, None] * inverse
    cos, sin = np.cos(angle.astype(np.float64)), np.sin(angle.astype(np.float64))
    return (
        np.concatenate([cos, cos, cos, cos], 1).astype(np.float32),
        np.concatenate([-sin, sin, -sin, sin], 1).astype(np.float32),
    )


def fused_local(n, nb, tokens, doc_ids, w_query, w_key, w_value, w_out, w_gate, w_up, w_down, gain_attn, gain_ffn, cotangent):
    _, tok, d = tokens.shape
    f = w_gate.shape[1]
    nz = n // 2
    cos, sin = rope_constants(n * tok, d // HEADS)
    cos = jnp.asarray(cos.reshape(nz, 2 * tok, 128))
    sin = jnp.asarray(sin.reshape(nz, 2 * tok, 128))
    plan = scratch_plan(tok, d, f, n, nb)
    vmem, anywhere = pl.BlockSpec(memory_space=pltpu.VMEM), pl.BlockSpec(memory_space=pl.ANY)
    shape = jax.ShapeDtypeStruct
    parts = pl.pallas_call(
        functools.partial(layer_kernel, tuple(plan), tok, d, f, n, nb),
        out_shape=(
            shape((tok, d), F32), shape((tok, d), F32), shape((nb, d // n, d // 2), BF16),
            shape((nb, 2, d // n, f // nb), BF16), shape((nb, f // (nb * n), d), BF16), shape((nb, d // (2 * n), d // 2), BF16),
            shape((nb, d // (2 * n), d // 2), BF16), shape((8, d), F32),
        ),
        in_specs=[anywhere] * 14,
        out_specs=[anywhere] * 8,
        scratch_shapes=list(plan.values()),
        compiler_params=pltpu.CompilerParams(
            collective_id=0, has_side_effects=True, vmem_limit_bytes=62 * 2**20
        ),
        name="layer",
    )(
        doc_ids, tokens, cotangent, gain_attn, gain_ffn, cos, sin,
        w_query, w_key, w_value, w_out, w_gate, w_up, w_down,
    )
    own = d // n
    grads = [shape((own, d), F32)] * 4 + [shape((own, f), F32)] * 2 + [shape((f // n, d), F32)]
    results = pl.pallas_call(
        functools.partial(unpack_kernel, n, nb),
        out_shape=(shape((1, tok, d), F32), shape((1, tok, d), F32), *grads, shape((1, own), F32), shape((1, own), F32)),
        in_specs=[pl.BlockSpec(memory_space=pltpu.HBM)] * 8,
        out_specs=[anywhere] * 9 + [vmem] * 2,
        scratch_shapes=[pltpu.VMEM(parts[i].shape, parts[i].dtype) for i in (2, 3, 4, 5, 6, 7)]
        + [pltpu.VMEM(g.shape, g.dtype) for g in grads]
        + [pltpu.VMEM((tok, d), F32)] * 2
        + [pltpu.SemaphoreType.DMA((8,)), pltpu.SemaphoreType.DMA((9,))],
        compiler_params=pltpu.CompilerParams(vmem_limit_bytes=62 * 2**20),
        name="unpack",
    )(*parts)
    return results[:9] + (results[9].reshape(own), results[10].reshape(own))


def fits(shapes, n, nb):
    (_, tok, d), f = shapes[0], shapes[6][1]
    return (
        nb == 4 and n == 8 and n * tok <= 1024 and tok == 128 and shapes[0][0] == 1
        and d == HEADS * 64 and d % 256 == 0 and d % (32 * n) == 0 and f == 2 * tok * n and f % 512 == 0
    )


def solution(mesh):
    nb, n = mesh.shape["batch"], mesh.shape["seq"]

    def either(*args):
        shapes = [a.shape for a in args]
        if fits(shapes, n, nb):
            return fused_local(n, nb, *args)
        return local(*args)

    return jax.shard_map(
        either,
        mesh=mesh,
        in_specs=(
            P("batch", "seq", None),
            P("batch", "seq"),
            P(),
            P(),
            P(),
            P(),
            P(),
            P(),
            P(),
            P(),
            P(),
            P("batch", "seq", None),
        ),
        out_specs=(
            P("batch", "seq", None),
            P("batch", "seq", None),
            P("seq", None),
            P("seq", None),
            P("seq", None),
            P("seq", None),
            P("seq", None),
            P("seq", None),
            P("seq", None),
            P("seq"),
            P("seq"),
        ),
        check_vma=False,
    )
```

```python
import functools
import math
import types

import jax
import jax.numpy as jnp
import numpy as np
from jax import lax
from jax.experimental import pallas as pl
from jax.experimental.pallas import tpu as pltpu
from jax.sharding import PartitionSpec as P

HEADS = 12
NSEG = 8


EPSILON = 1e-06
THETA = 10000.0
MASKED = -1e30


def root_mean_square_norm(values, gain):
    return values * lax.rsqrt(jnp.mean(values * values, -1, keepdims=True) + EPSILON) * gain


def swiglu(gate, up_part):
    return jax.nn.silu(gate) * up_part


def rope_tables(positions, head_dim):
    half_dim = head_dim // 2
    inverse = jnp.exp(-2.0 * math.log(THETA) / head_dim * jnp.arange(half_dim, dtype=jnp.float32))
    angle = positions.astype(jnp.float32)[..., None] * inverse
    return (
        jnp.concatenate([jnp.cos(angle), jnp.cos(angle)], -1),
        jnp.concatenate([jnp.sin(angle), jnp.sin(angle)], -1),
    )


def rotate(values, cosine, sine):
    half_dim = values.shape[-1] // 2
    turned = jnp.concatenate([-values[..., half_dim:], values[..., :half_dim]], -1)
    return values * cosine + turned * sine


def rotate_back(grads, cosine, sine):
    half_dim = grads.shape[-1] // 2
    turned = grads * sine
    return grads * cosine + jnp.concatenate([turned[..., half_dim:], -turned[..., :half_dim]], -1)


def block_size(total_rows):
    return max((d for d in range(1, min(total_rows, 2048) + 1) if total_rows % d == 0))


def doc_begin(segment_begins, where_at):
    earlier = segment_begins[:, None, :] <= where_at[:, :, None]
    return jnp.max(jnp.where(earlier, segment_begins[:, None, :], 0), -1)


def outer_sum(remaining_tokens, right):
    return lax.dot_general(
        remaining_tokens, right, (((0,), (0,)), ((), ())), preferred_element_type=jnp.float32
    )


def back_product(grads, weight_matrix):
    return lax.dot_general(
        grads, weight_matrix, (((1,), (1,)), ((), ())), preferred_element_type=jnp.float32
    )


def masked_scores(queries, key_block, key_at, query_at, query_begin):
    batch_rows, block_rows, model_width = key_block.shape
    head_count = queries.shape[2]
    head_dim = model_width // head_count
    key_heads = key_block.reshape(batch_rows, block_rows, head_count, head_dim)
    scores = jnp.einsum(
        "bqhd,bkhd->bhqk", queries, key_heads, preferred_element_type=jnp.float32
    ) * (1.0 / math.sqrt(head_dim))
    key_pos = key_at[None, None, :]
    query_pos = query_at[:, :, None]
    begin_pos = query_begin[:, :, None]
    allowed = (
        (key_pos <= query_pos) & (key_pos >= begin_pos) & ((begin_pos > 0) | (key_pos == query_pos))
    )
    return (scores, allowed[:, None], key_heads)


def grad_terms(
    queries, grad_heads, lse, delta, query_at, query_begin, key_block, value_block, key_at
):
    scores, allowed, key_heads = masked_scores(queries, key_block, key_at, query_at, query_begin)
    value_heads = value_block.reshape(key_heads.shape)
    probs = jnp.where(allowed, jnp.exp(scores - lse[..., None]), 0.0)
    dprob = jnp.einsum(
        "bqhd,bkhd->bhqk", grad_heads, value_heads, preferred_element_type=jnp.float32
    )
    dscore = (probs * (dprob - delta[..., None])).astype(jnp.bfloat16)
    return (probs.astype(jnp.bfloat16), dscore, key_heads, value_heads)


def over_rows(update, carried, arrays, first_row):
    total_rows = arrays[0].shape[1]
    block_rows = block_size(total_rows)

    def over_step(block_index, state):
        offset = block_index * block_rows
        blocks = tuple((lax.dynamic_slice_in_dim(item, offset, block_rows, 1) for item in arrays))
        key_at = first_row + offset + jnp.arange(block_rows, dtype=jnp.int32)
        return update(state, blocks, key_at)

    return lax.fori_loop(0, total_rows // block_rows, over_step, carried)


def local(
    tokens,
    doc_ids,
    w_query,
    w_key,
    w_value,
    w_out,
    w_gate,
    w_up,
    w_down,
    gain_attn,
    gain_ffn,
    cotangent,
):
    batch_rows, local_len, model_width = tokens.shape
    head_count = HEADS
    head_dim = model_width // head_count
    shape_heads = (batch_rows, local_len, head_count, head_dim)
    scale = 1.0 / math.sqrt(head_dim)
    labels = jnp.arange(NSEG, dtype=jnp.int32)
    member = (doc_ids[:, :, None] == labels).astype(jnp.int32)
    totals = lax.psum(jnp.sum(member, 1), "seq")
    segment_begins = jnp.cumsum(totals, 1) - totals
    local_at = lax.axis_index("seq") * local_len + jnp.arange(local_len, dtype=jnp.int32)
    query_at = jnp.broadcast_to(local_at, (batch_rows, local_len))
    query_begin = doc_begin(segment_begins, query_at)
    cosine, sine = rope_tables(query_at - query_begin, head_dim)
    cosine = cosine[:, :, None, :]
    sine = sine[:, :, None, :]
    flat_tokens = tokens.reshape(batch_rows * local_len, model_width)
    queries = rotate(
        jnp.dot(flat_tokens, w_query, preferred_element_type=jnp.float32).reshape(shape_heads),
        cosine,
        sine,
    ).astype(jnp.bfloat16)
    key_send = (
        rotate(
            jnp.dot(flat_tokens, w_key, preferred_element_type=jnp.float32).reshape(shape_heads),
            cosine,
            sine,
        )
        .astype(jnp.bfloat16)
        .reshape(batch_rows, local_len, model_width)
    )
    value_send = (
        jnp.dot(flat_tokens, w_value, preferred_element_type=jnp.float32)
        .astype(jnp.bfloat16)
        .reshape(batch_rows, local_len, model_width)
    )

    def stats_step(state, blocks, key_at):
        run_max, run_sum = state
        scores, allowed, key_heads = masked_scores(
            queries, blocks[0], key_at, query_at, query_begin
        )
        scores = jnp.where(allowed, scores, MASKED)
        new_max = jnp.maximum(run_max, jnp.max(scores, -1))
        weights = jnp.where(allowed, jnp.exp(scores - new_max[..., None]), 0.0)
        return (new_max, run_sum * jnp.exp(run_max - new_max) + jnp.sum(weights, -1))

    stats_init = (
        jnp.full((batch_rows, head_count, local_len), MASKED, jnp.float32),
        jnp.zeros((batch_rows, head_count, local_len), jnp.float32),
    )
    zero_heads = jnp.zeros(shape_heads, jnp.float32)
    run_max, run_sum = over_rows(
        stats_step, stats_init, (lax.all_gather(key_send, "seq", axis=1, tiled=True),), jnp.int32(0)
    )
    lse = run_max + jnp.log(run_sum)

    def output_step(state, blocks, key_at):
        scores, allowed, key_heads = masked_scores(
            queries, blocks[0], key_at, query_at, query_begin
        )
        value_heads = blocks[1].reshape(key_heads.shape)
        probs = jnp.where(allowed, jnp.exp(scores - lse[..., None]), 0.0).astype(jnp.bfloat16)
        return state + jnp.einsum(
            "bhqk,bkhd->bqhd", probs, value_heads, preferred_element_type=jnp.float32
        )

    attended = over_rows(
        output_step,
        zero_heads,
        (
            lax.all_gather(key_send, "seq", axis=1, tiled=True),
            lax.all_gather(value_send, "seq", axis=1, tiled=True),
        ),
        jnp.int32(0),
    )
    attended_low = attended.astype(jnp.bfloat16).reshape(batch_rows * local_len, model_width)
    first_sum = flat_tokens.astype(jnp.float32) + jnp.dot(
        attended_low, w_out, preferred_element_type=jnp.float32
    )
    hidden, norm_first_back = jax.vjp(root_mean_square_norm, first_sum, gain_attn)
    hidden_low = hidden.astype(jnp.bfloat16)
    gate = jnp.dot(hidden_low, w_gate, preferred_element_type=jnp.float32)
    up_part = jnp.dot(hidden_low, w_up, preferred_element_type=jnp.float32)
    active, swiglu_back = jax.vjp(swiglu, gate, up_part)
    active_low = active.astype(jnp.bfloat16)
    second_sum = hidden + jnp.dot(active_low, w_down, preferred_element_type=jnp.float32)
    output, norm_second_back = jax.vjp(root_mean_square_norm, second_sum, gain_ffn)
    second_grad, grad_gain_ffn = norm_second_back(
        cotangent.reshape(batch_rows * local_len, model_width).astype(jnp.float32)
    )
    branch_grad = second_grad.astype(jnp.bfloat16)
    grad_down = outer_sum(active_low, branch_grad)
    gate_grad, up_grad = swiglu_back(back_product(branch_grad, w_down))
    gate_low = gate_grad.astype(jnp.bfloat16)
    up_low = up_grad.astype(jnp.bfloat16)
    grad_gate = outer_sum(hidden_low, gate_low)
    grad_up = outer_sum(hidden_low, up_low)
    hidden_grad = second_grad + back_product(gate_low, w_gate) + back_product(up_low, w_up)
    first_grad, grad_gain_attn = norm_first_back(hidden_grad)
    attn_grad = first_grad.astype(jnp.bfloat16)
    grad_out = outer_sum(attended_low, attn_grad)
    grad_heads = back_product(attn_grad, w_out).astype(jnp.bfloat16).reshape(shape_heads)
    delta = jnp.swapaxes(jnp.sum(grad_heads.astype(jnp.float32) * attended, -1), 1, 2)

    def query_step(state, blocks, key_at):
        probs_low, dscore, key_heads, value_heads = grad_terms(
            queries, grad_heads, lse, delta, query_at, query_begin, blocks[0], blocks[1], key_at
        )
        return (
            state
            + jnp.einsum("bhqk,bkhd->bqhd", dscore, key_heads, preferred_element_type=jnp.float32)
            * scale
        )

    all_keys, all_values = (
        lax.all_gather(key_send, "seq", axis=1, tiled=True),
        lax.all_gather(value_send, "seq", axis=1, tiled=True),
    )
    query_grad = over_rows(query_step, zero_heads, (all_keys, all_values), 0)
    first_row = jnp.int32(0)
    span_rows = local_len * lax.axis_size("seq")
    block_rows = block_size(span_rows)
    empty = jnp.zeros((batch_rows, span_rows, head_count, head_dim), jnp.float32)

    def key_step(block_index, state):
        offset = block_index * block_rows
        key_block = lax.dynamic_slice_in_dim(all_keys, offset, block_rows, 1)
        value_block = lax.dynamic_slice_in_dim(all_values, offset, block_rows, 1)
        key_at = first_row + offset + jnp.arange(block_rows, dtype=jnp.int32)
        probs_low, dscore, key_heads, value_heads = grad_terms(
            queries, grad_heads, lse, delta, query_at, query_begin, key_block, value_block, key_at
        )
        key_part = (
            jnp.einsum("bhqk,bqhd->bkhd", dscore, queries, preferred_element_type=jnp.float32)
            * scale
        )
        value_part = jnp.einsum(
            "bhqk,bqhd->bkhd", probs_low, grad_heads, preferred_element_type=jnp.float32
        )
        return (
            lax.dynamic_update_slice_in_dim(state[0], key_part, offset, 1),
            lax.dynamic_update_slice_in_dim(state[1], value_part, offset, 1),
        )

    key_all, value_all = lax.fori_loop(0, span_rows // block_rows, key_step, (empty, empty))
    joined = jnp.concatenate(
        [
            key_all.reshape(batch_rows, span_rows, model_width),
            value_all.reshape(batch_rows, span_rows, model_width),
        ],
        -1,
    )
    summed_keys = jnp.swapaxes(
        lax.psum_scatter(jnp.swapaxes(joined, 0, 1), "seq", scatter_dimension=0, tiled=True), 0, 1
    )
    key_grad = summed_keys[..., :model_width].reshape(shape_heads)
    value_grad = summed_keys[..., model_width:]
    flat_len = batch_rows * local_len
    query_low = (
        rotate_back(query_grad, cosine, sine).astype(jnp.bfloat16).reshape(flat_len, model_width)
    )
    key_low = (
        rotate_back(key_grad, cosine, sine).astype(jnp.bfloat16).reshape(flat_len, model_width)
    )
    value_low = value_grad.astype(jnp.bfloat16).reshape(flat_len, model_width)
    grad_input = (
        first_grad
        + back_product(query_low, w_query)
        + back_product(key_low, w_key)
        + back_product(value_low, w_value)
    )
    grad_query = outer_sum(flat_tokens, query_low)
    grad_key = outer_sum(flat_tokens, key_low)
    value_weight_gradient = outer_sum(flat_tokens, value_low)
    shares = (
        lax.psum_scatter(grad_query, "seq", scatter_dimension=0, tiled=True),
        lax.psum_scatter(grad_key, "seq", scatter_dimension=0, tiled=True),
        lax.psum_scatter(value_weight_gradient, "seq", scatter_dimension=0, tiled=True),
        lax.psum_scatter(grad_out, "seq", scatter_dimension=0, tiled=True),
        lax.psum_scatter(grad_gate, "seq", scatter_dimension=0, tiled=True),
        lax.psum_scatter(grad_up, "seq", scatter_dimension=0, tiled=True),
        lax.psum_scatter(grad_down, "seq", scatter_dimension=0, tiled=True),
        lax.psum_scatter(grad_gain_attn, "seq", scatter_dimension=0, tiled=True),
        lax.psum_scatter(grad_gain_ffn, "seq", scatter_dimension=0, tiled=True),
    )
    results = (
        lax.psum(shares[0].astype(jnp.bfloat16), "batch").astype(jnp.float32),
        lax.psum(shares[1].astype(jnp.bfloat16), "batch").astype(jnp.float32),
        lax.psum(shares[2].astype(jnp.bfloat16), "batch").astype(jnp.float32),
        lax.psum(shares[3].astype(jnp.bfloat16), "batch").astype(jnp.float32),
        lax.psum(shares[4].astype(jnp.bfloat16), "batch").astype(jnp.float32),
        lax.psum(shares[5].astype(jnp.bfloat16), "batch").astype(jnp.float32),
        lax.psum(shares[6].astype(jnp.bfloat16), "batch").astype(jnp.float32),
        lax.psum(shares[7].astype(jnp.bfloat16), "batch").astype(jnp.float32),
        lax.psum(shares[8].astype(jnp.bfloat16), "batch").astype(jnp.float32),
    )
    output_rows = output.reshape(batch_rows, local_len, model_width)
    input_rows = grad_input.reshape(batch_rows, local_len, model_width)
    return (
        output_rows,
        input_rows,
        results[0],
        results[1],
        results[2],
        results[3],
        results[4],
        results[5],
        results[6],
        results[7],
        results[8],
    )


MESH = pl.DeviceIdType.MESH
F32 = jnp.float32
BF16 = jnp.bfloat16


def mm(a, b):
    return lax.dot_general(a, b, (((1,), (0,)), ((), ())), preferred_element_type=F32)


def mm_nt(a, b):
    return lax.dot_general(a, b, (((1,), (1,)), ((), ())), preferred_element_type=F32)


def scratch_plan(tok, d, f, n, nb):
    nz, plane, heads = n // 2, 2 * nb * tok, HEADS
    vm = pltpu.VMEM
    dma = lambda *shape: pltpu.SemaphoreType.DMA(shape)
    return dict(
        wq=vm((d, d), BF16), wk=vm((d, d), BF16), wv=vm((d, d), BF16), wo=vm((d, d), BF16),
        wg=vm((d, f), BF16), wu=vm((d, f), BF16), wd=vm((f, d), BF16),
        cos=vm((nz, 2 * tok, 128), F32), sin=vm((nz, 2 * tok, 128), F32),
        ids=vm((1, tok), jnp.int32), cot=vm((tok, d), BF16), ga=vm((d,), F32), gf=vm((d,), F32),
        x_all=vm((n, tok, d), BF16), q_all=vm((n, tok, d), BF16), do_all=vm((n, tok, d), BF16),
        k_all=vm((nz, 2 * tok, d), BF16), v_all=vm((nz, 2 * tok, d), BF16),
        st_all=vm((n, 32, tok), F32), id_all=vm((n, 8, tok), jnp.int32),
        idcol=vm((tok, 128), F32), bias=vm((2 * tok, 2 * tok), F32),
        m=vm((heads // 2, 2 * tok, 128), F32), l=vm((heads // 2, 2 * tok, 128), F32),
        delta=vm((heads // 2, 2 * tok, 128), F32),
        acc=vm((tok, d), F32), acc2=vm((tok, d), F32),
        olow=vm((tok, d), BF16), hb=vm((tok, d), BF16), h1=vm((tok, d), F32), n1=vm((tok, d), F32),
        ri1=vm((tok, 128), F32), dr=vm((tok, d), F32),
        act=vm((tok, f), BF16),
        dg=vm((tok, f), BF16), du=vm((tok, f), BF16), dmo=vm((tok, d), BF16), dattn=vm((tok, d), BF16),
        dq=vm((tok, d), BF16), dk=vm((tok, d), BF16), dv=vm((tok, d), BF16),
        hT=vm((d, tok), BF16), xT=vm((d, tok), BF16), oT=vm((d, tok), BF16),
        gl=vm((8, d), F32), out_v=vm((tok, d), F32), gin_v=vm((tok, d), F32),
        hT_b=vm((d, plane), BF16), dmo_b=vm((plane, d), BF16),
        wgT=vm((f // nb, d), BF16), wuT=vm((f // nb, d), BF16), tmpT=vm((128, d), BF16),
        act_x=vm((f // nb, plane), BF16), da_x=vm((f // nb, plane), BF16),
        fa=vm((f // nb, plane), F32), fb=vm((f // nb, plane), F32), dgu=vm((2, f // nb, plane), BF16),
        xT_b=vm((d, plane), BF16), o2=vm((d, 2 * tok), BF16), da2=vm((2 * tok, d), BF16), at_b=vm((2, plane, d // 2), BF16), gl_b=vm((2 * nb, 8, d), F32),
        pgu=vm((2, d, f // nb), BF16), pdn=vm((n, f // (nb * n), d), BF16),
        pat=vm((d, d // 2), BF16), pq=vm((n, d // (2 * n), d // 2), BF16), pout=vm((d, d), BF16),
        ugu=vm((2, 2, d // nz, f // nb), BF16), udn=vm((2, 2, f // (nb * n), d), BF16),
        uat=vm((2, d // nz, d // 2), BF16), uq=vm((2, 2, d // (2 * n), d // 2), BF16),
        uout=vm((2, d // nz, d), BF16), rout=vm((nz, d // nz, d), BF16), sout=vm((2, d // n, d), BF16),
        rso=vm((nb, 2, d // (2 * n), d // 2), BF16), fso=vm((2, d // (2 * n), d // 2), BF16),
        rgu=vm((2, nz, d // nz, f // nb), BF16), rdn=vm((nz, 2, f // (nb * n), d), BF16), rat=vm((nz, d // nz, d // 2), BF16), rqz=vm((nz, 2, d // (2 * n), d // 2), BF16),
        sgu=vm((2, d // nz, f // nb), BF16), sdn=vm((2, f // (nb * n), d), BF16), sat=vm((d // nz, d // 2), BF16), sq=vm((2, d // (2 * n), d // 2), BF16),
        gz=vm((nz, 8, d), F32), gsum=vm((8, d), F32),
        wsem=dma(14), osem=dma(2), ssem=dma(230), fsem=dma(5, n), bsem=dma(6, n),
        rx=dma(2, n), rq=dma(n), rdo=dma(2, n), rst=dma(n), rid=dma(n),
        rh=dma(2 * nb), rdmo=dma(2 * nb), rax=dma(1), rda=dma(1), zfar=dma(7, 2),
        rxt=dma(2 * nb), ro2=dma(2), rda2=dma(2), zout=dma(nz), rrso=dma(nb), fout=dma(nb), rat_in=dma(2, 2 * nb), rgl=dma(2 * nb),
        zgu=dma(3, nz), zdn=dma(nz), zat=dma(nz), zq=dma(nz), zgl=dma(nz),
        fgu=dma(3, nb), fdn=dma(nb), fat=dma(nb), fq=dma(nb), fgl=dma(1),
    )


INPUTS = ("ids_h", "tok_h", "cot_h", "ga_h", "gf_h", "cos_h", "sin_h", "wq_h", "wk_h", "wv_h", "wo_h", "wg_h", "wu_h", "wd_h")
OUTPUTS = ("out_h", "gin_h", "oat_h", "ogu_h", "odn_h", "oout_h", "oq_h", "ogl_h")


def layer_kernel(plan_names, tok, d, f, n, nb, *refs):
    r = types.SimpleNamespace(**dict(zip(INPUTS + OUTPUTS + plan_names, refs)))
    nz, pairs = n // 2, d // 128
    fs, dh, blk = f // nb, d // 2, d // nz
    b, s = lax.axis_index("batch"), lax.axis_index("seq")
    z, c = s // 2, lax.rem(s, 2)
    by, bx = b // 2, lax.rem(b, 2)
    e = 2 * b + c
    sib = (b, s + 1 - 2 * c)
    pending, used = [], [0]

    def remote(src, dst, ssem, rsem, dev):
        return pltpu.make_async_remote_copy(
            src_ref=src, dst_ref=dst, send_sem=ssem, recv_sem=rsem, device_id=dev, device_id_type=MESH
        )

    def send_lazy(make):
        at = used[0]
        used[0] += 1
        pending.append((make, at))
        cond, src, dst, rsem, dev = make()

        @pl.when(cond)
        def _():
            remote(src, dst, r.ssem.at[at], rsem, dev).start()

    def send(cond, src, dst, rsem, dev):
        send_lazy(lambda: (cond, src, dst, rsem, dev))

    def plane_send_lazy(make, to_b, to_c, also=None):
        def here():
            return (b == to_b) & (c == to_c)

        def wanted(cond):
            return cond if also is None else cond & also()

        send_lazy(lambda: (wanted(jnp.logical_not(here())), *make(), (to_b, 2 * z + to_c)))

        @pl.when(wanted(here()))
        def _():
            pltpu.make_async_copy(*make()).start()

    def plane_send(src, dst, rsem, to_b, to_c):
        plane_send_lazy(lambda: (src, dst, rsem), to_b, to_c)

    def arrived(dst, rsem):
        remote(dst, dst, r.ssem.at[0], rsem, sib).wait_recv()

    loads = {}
    for i, (name, src, dst) in enumerate(
        (
            ("tok", r.tok_h.at[0], r.x_all.at[s]), ("ids", r.ids_h, r.ids), ("ga", r.ga_h, r.ga), ("gf", r.gf_h, r.gf),
            ("cot", r.cot_h.at[0], r.cot),
        )
    ):
        loads[name] = pltpu.make_async_copy(src, dst, r.wsem.at[9 + i])
    loads["tok"].start()
    loads["ids"].start()
    bar = pltpu.get_barrier_semaphore()
    for zz in range(nz):
        for cc in range(2):
            @pl.when(2 * zz + cc != s)
            def _(zz=zz, cc=cc):
                pl.semaphore_signal(bar, inc=1, device_id=(b, 2 * zz + cc), device_id_type=MESH)
    for bb in range(nb):
        for cc in range(2):
            @pl.when(bb != b)
            def _(bb=bb, cc=cc):
                pl.semaphore_signal(bar, inc=1, device_id=(bb, 2 * z + cc), device_id_type=MESH)
    for i, name in enumerate(("wk", "wv", "wq", "cos", "sin", "wo", "wg", "wu", "wd")):
        loads[name] = pltpu.make_async_copy(getattr(r, name + "_h"), getattr(r, name), r.wsem.at[i])
        loads[name].start()
    for name in ("ga", "gf", "cot"):
        loads[name].start()
    loads["ids"].wait()
    r.id_all[s] = jnp.broadcast_to(r.ids[...], (8, tok))
    loads["tok"].wait()
    pl.semaphore_wait(bar, n - 1 + 2 * (nb - 1))

    always = s >= 0
    half = tok // 2

    def rows_of(ref, t, ch):
        return ref.at[t, pl.ds(ch * half, half)]

    right, left = (b, s + 2), (b, s - 2)
    send(always, r.id_all.at[s], r.id_all.at[s], r.rid.at[s], sib)
    for ch in range(2):
        mine = rows_of(r.x_all, s, ch)
        send(z + 1 < nz, mine, mine, r.rx.at[ch, s], right)
        send(always, mine, mine, r.rx.at[ch, s], sib)
    for zz in range(nz):
        for cc in range(2):
            send(z != zz, r.id_all.at[s], r.id_all.at[s], r.rid.at[s], (b, 2 * zz + cc))

    lane = lax.broadcasted_iota(jnp.int32, (tok, 128), 1)
    first = lane < 64
    half_mask = (jnp.where(first, 1.0, 0.0).astype(BF16), jnp.where(first, 0.0, 1.0).astype(BF16))

    def turn(u):
        low = lax.rem(lax.broadcasted_iota(jnp.int32, u.shape, 1), 64) < 32
        return jnp.where(low, pltpu.roll(u, 96, 1), pltpu.roll(u, 32, 1))

    def twice(u):
        return jnp.concatenate([u, u], axis=1)

    def stack(u):
        return jnp.concatenate([u * half_mask[0], u * half_mask[1]], axis=0)

    def unstack(u):
        return jnp.where(first, u[:tok], u[tok:])

    own = pl.ds(pl.multiple_of(c * tok, tok), tok)

    loads["wq"].wait()
    loads["cos"].wait()
    loads["sin"].wait()

    u = mm(r.x_all[s], r.wq[...])
    co, si = r.cos[z, own, :], r.sin[z, own, :]
    for p in range(pairs):
        part = u[:, p * 128:(p + 1) * 128]
        r.q_all[s, :, p * 128:(p + 1) * 128] = ((part * co + turn(part) * si) * 0.125).astype(BF16)
    send(always, r.q_all.at[s], r.q_all.at[s], r.rq.at[s], sib)
    for dz in range(1, nz):
        send(z - dz >= 0, r.q_all.at[s], r.q_all.at[s], r.rq.at[s], (b, s - 2 * dz))

    def transpose_into(dst, value):
        for p in range(d // 128):
            dst[p * 128:(p + 1) * 128, :] = value[:, p * 128:(p + 1) * 128].T.astype(BF16)

    tokens = pl.ds(pl.multiple_of(e * tok, tok), tok)
    side, across = 2 * by + 1 - bx, 2 * (1 - by) + bx

    def relay(slot_of, rsem, to_c):
        for source, target in ((lambda: 2 * side, across), (lambda: 2 * across + 1, side)):
            @pl.when(c == to_c)
            def _(source=source):
                arrived(slot_of(source()), rsem.at[source()])

            send_lazy(
                lambda source=source, target=target: (
                    c == to_c, slot_of(source()), slot_of(source()), rsem.at[source()], (target, s)
                )
            )

    def hT_slot(i):
        return r.hT_b.at[:, pl.ds(pl.multiple_of(i * tok, tok), tok)]

    def dmo_slot(i):
        return r.dmo_b.at[pl.ds(pl.multiple_of(i * tok, tok), tok), :]
    transpose_into(r.xT, r.x_all[s].astype(F32))
    for bb in range(nb):
        plane_send(r.xT, r.xT_b.at[:, tokens], r.rxt.at[e], bb, 1)
    r.idcol[...] = jnp.broadcast_to(r.ids[...].astype(F32), (128, tok)).T

    def ids_of(block):
        return jnp.concatenate(
            [r.id_all[2 * block, 0:1, :], r.id_all[2 * block + 1, 0:1, :]], axis=1
        ).astype(F32)

    def set_bias(block, local_is_query):
        shape = (tok, 2 * tok)
        mine = s * tok + lax.broadcasted_iota(jnp.int32, shape, 0)
        theirs = block * (2 * tok) + lax.broadcasted_iota(jnp.int32, shape, 1)
        my_id = twice(r.idcol[...])
        their_id = jnp.broadcast_to(ids_of(block), shape)
        causal = (theirs <= mine) if local_is_query else (mine <= theirs)
        allowed = (my_id == their_id) & causal & ((my_id != 0.0) | (mine == theirs))
        bias = jnp.where(allowed, 0.0, MASKED)
        r.bias[...] = jnp.concatenate([bias, bias], axis=0)

    units = fs // n

    def quarter_weights():
        for src, dst in ((r.wg, r.wgT), (r.wu, r.wuT)):
            for t in range(n):
                tile = src[:, pl.ds(pl.multiple_of((2 * t + by) * 128, 128), 128)].astype(F32)
                for p in range(pairs):
                    r.tmpT[:, p * 128:(p + 1) * 128] = tile[p * 128:(p + 1) * 128].T.astype(BF16)
                dst[t * units:(t + 1) * units, :] = r.tmpT[pl.ds(pl.multiple_of(bx * units, units), units), :]

    r.m[...] = jnp.full(r.m.shape, MASKED, F32)
    r.l[...] = jnp.zeros(r.l.shape, F32)
    r.acc[...] = jnp.zeros(r.acc.shape, F32)
    loads["wk"].wait()
    loads["wv"].wait()

    def forward_step(j, _):
        kb = z - j
        mine, other = 2 * kb + c, 2 * kb + 1 - c

        @pl.when(j > 0)
        def _():
            for ch in range(2):
                got = rows_of(r.x_all, mine, ch)
                arrived(got, r.rx.at[ch, mine])

                @pl.when(z + 1 < nz)
                def _():
                    remote(got, got, r.fsem.at[ch, mine], r.rx.at[ch, mine], right).start()

                remote(got, got, r.bsem.at[ch, mine], r.rx.at[ch, mine], sib).start()

            arrived(r.id_all.at[mine], r.rid.at[mine])

        for ch in range(2):
            arrived(rows_of(r.x_all, other, ch), r.rx.at[ch, other])
        arrived(r.id_all.at[other], r.rid.at[other])
        set_bias(kb, True)

        xb = r.x_all[pl.ds(2 * kb, 2)].reshape(2 * tok, d)
        u = mm(xb, r.wk[...])
        co, si = r.cos[kb], r.sin[kb]
        for p in range(pairs):
            part = u[:, p * 128:(p + 1) * 128]
            r.k_all[kb, :, p * 128:(p + 1) * 128] = (part * co + turn(part) * si).astype(BF16)
        r.v_all[kb] = mm(xb, r.wv[...]).astype(BF16)

        def pair(p, _):
            lanes = pl.ds(pl.multiple_of(p * 128, 128), 128)
            qp, kp, vp = r.q_all[s, :, lanes], r.k_all[kb, :, lanes], r.v_all[kb, :, lanes]
            sc = mm_nt(stack(qp), kp) + r.bias[...]
            m_old = r.m[p]
            m_new = jnp.maximum(m_old, jnp.max(sc, axis=1, keepdims=True))
            alpha = jnp.exp(m_old - m_new)
            ex = jnp.exp(sc - twice(m_new))
            r.m[p] = m_new
            r.l[p] = r.l[p] * alpha + jnp.sum(ex, axis=1, keepdims=True)
            r.acc[:, lanes] = r.acc[:, lanes] * unstack(alpha) + unstack(mm(ex.astype(BF16), vp))
            return 0

        lax.fori_loop(0, pairs, pair, 0, unroll=True)

        @pl.when((j == 0) & (c == 0))
        def _():
            loads["wg"].wait()
            loads["wu"].wait()
            quarter_weights()

        return 0

    lax.fori_loop(0, z + 1, forward_step, 0)

    def finish(p, _):
        lanes = pl.ds(pl.multiple_of(p * 128, 128), 128)
        r.acc[:, lanes] = r.acc[:, lanes] / unstack(r.l[p])
        r.m[p] = r.m[p] + jnp.log(r.l[p])
        return 0

    lax.fori_loop(0, pairs, finish, 0, unroll=True)
    r.olow[...] = r.acc[...].astype(BF16)

    loads["wo"].wait()
    loads["ga"].wait()
    loads["gf"].wait()
    loads["cot"].wait()
    gain_a, gain_f = r.ga[...].reshape(1, d), r.gf[...].reshape(1, d)
    r1 = r.x_all[s].astype(F32) + mm(r.olow[...], r.wo[...])
    ri1 = lax.rsqrt(jnp.mean(r1 * r1, axis=1, keepdims=True) + EPSILON)
    r.ri1[...] = jnp.broadcast_to(ri1, (tok, 128))
    n1 = r1 * ri1
    r.n1[...] = n1
    h1 = n1 * gain_a
    r.h1[...] = h1
    r.hb[...] = h1.astype(BF16)
    transpose_into(r.hT, h1)
    for to_b in (b, side, across):
        plane_send(r.hT, r.hT_b.at[:, tokens], r.rh.at[e], to_b, 0)

    @pl.when(c == 1)
    def _():
        loads["wg"].wait()
        loads["wu"].wait()

    def gate_at(i):
        return (slice((i // 2) * tok, (i // 2 + 1) * tok), slice((i % 2) * 512, (i % 2 + 1) * 512))

    def up_at(i):
        return gate_at(i + f // 512)

    for i in range(f // 512):
        at = slice(i * 512, (i + 1) * 512)
        g = mm(r.hb[...], r.wg[:, at])
        u = mm(r.hb[...], r.wu[:, at])
        r.fa[gate_at(i)] = g
        r.fa[up_at(i)] = u
        a = g / (1.0 + jnp.exp(-g)) * u
        r.act[:, at] = a.astype(BF16)
    loads["wd"].wait()
    r2 = r.h1[...] + mm(r.act[...], r.wd[...])
    ri2 = lax.rsqrt(jnp.mean(r2 * r2, axis=1, keepdims=True) + EPSILON)
    n2 = r2 * ri2
    ct = r.cot[...].astype(F32)
    t2 = ct * gain_f
    dr2 = ri2 * (t2 - n2 * jnp.mean(n2 * t2, axis=1, keepdims=True))
    r.dr[...] = dr2
    r.dmo[...] = dr2.astype(BF16)
    for to_b in (b, side, across):
        plane_send(r.dmo, r.dmo_b.at[tokens, :], r.rdmo.at[e], to_b, 1)

    r.out_v[...] = n2 * gain_f
    out_copy = pltpu.make_async_copy(r.out_v, r.out_h, r.osem.at[0])
    out_copy.start()
    gain_ffn = jnp.sum(ct * n2, axis=0, keepdims=True)
    transpose_into(r.oT, r.acc[...])

    for i in range(f // 512):
        at = slice(i * 512, (i + 1) * 512)
        da = mm_nt(r.dmo[...], r.wd[at, :])
        g, u = r.fa[gate_at(i)], r.fa[up_at(i)]
        sg = 1.0 / (1.0 + jnp.exp(-g))
        r.dg[:, at] = (da * u * (sg * (1.0 + g * (1.0 - sg)))).astype(BF16)
        r.du[:, at] = (da * (g * sg)).astype(BF16)
    dh1 = r.dr[...] + mm_nt(r.dg[...], r.wg[...]) + mm_nt(r.du[...], r.wu[...])
    n1 = r.n1[...]
    gain_attn = jnp.sum(dh1 * n1, axis=0, keepdims=True)
    t1 = dh1 * gain_a
    dr1 = r.ri1[:, 0:1] * (t1 - n1 * jnp.mean(n1 * t1, axis=1, keepdims=True))
    r.dr[...] = dr1
    r.dattn[...] = dr1.astype(BF16)
    r.gl[...] = jnp.concatenate([gain_attn, gain_ffn, jnp.zeros((6, d), F32)], axis=0)
    plane_send(r.gl, r.gl_b.at[e], r.rgl.at[e], 0, 0)
    plane_send_lazy(lambda: (r.oT, r.o2.at[:, own], r.ro2.at[c]), b, 1)
    plane_send_lazy(lambda: (r.dattn, r.da2.at[own, :], r.rda2.at[c]), b, 1)

    r.do_all[s] = mm_nt(r.dattn[...], r.wo[...]).astype(BF16)
    for ch in range(2):
        mine = rows_of(r.do_all, s, ch)
        send(z > 0, mine, mine, r.rdo.at[ch, s], left)
        send(always, mine, mine, r.rdo.at[ch, s], sib)

    stats = jnp.zeros((tok, 128), F32)
    for p in range(pairs):
        prod = r.do_all[s, :, p * 128:(p + 1) * 128].astype(F32) * r.acc[:, p * 128:(p + 1) * 128]
        for h in range(2):
            head = 2 * p + h
            part = jnp.sum(jnp.where(first == (h == 0), prod, 0.0), axis=1, keepdims=True)
            part = jnp.broadcast_to(part, (tok, 128))
            r.delta[p, h * tok:(h + 1) * tok] = part
            stats = jnp.where(lane == head, r.m[p, h * tok:(h + 1) * tok], stats)
            stats = jnp.where(lane == 16 + head, part, stats)
    r.st_all[s] = stats.T[0:32, :]
    send(z > 0, r.st_all.at[s], r.st_all.at[s], r.rst.at[s], left)
    send(always, r.st_all.at[s], r.st_all.at[s], r.rst.at[s], sib)

    def each_source(dst_of, rsem, count):
        for i in range(count):
            arrived(dst_of(i), rsem.at[i])

    end = (z == 0) | (z == nz - 1)

    def on(to_c, some):
        return c == to_c

    def share(src_of, dst_of, far_of, to_c, some=False):
        near = lambda: jnp.where(z < nz // 2, 0, nz - 1)
        for i in range(2):
            send_lazy(
                lambda i=i: (
                    on(to_c, some) & end, src_of(jnp.abs(nz - 1 - i - z)), *far_of(i),
                    (b, 2 * jnp.where(z == 0, 1, nz - 2) + to_c),
                )
            )
        send_lazy(
            lambda: (on(to_c, some) & jnp.logical_not(end), src_of(near()), *dst_of(), (b, 2 * near() + to_c))
        )

    def share_near(src_of, dst_of, far_of, to_c, some=False):
        send_lazy(
            lambda: (on(to_c, some) & end, src_of(jnp.where(z == 0, 1, nz - 2)), *dst_of(),
                     (b, 2 * jnp.where(z == 0, 1, nz - 2) + to_c))
        )

    def pass_on(own_of, dst_of, far_of, to_c, some=False):
        def here():
            return on(to_c, some) & jnp.logical_not(end)

        for i in range(2):
            def target(i=i):
                return nz - 1 - z if i else jnp.where(z == 1, nz - 1, 0)

            @pl.when(here())
            def _(i=i, target=target):
                far, sem = far_of(i)
                arrived(far, sem)
                far[...] = (own_of(target())[...].astype(F32) + far[...].astype(F32)).astype(BF16)

            send_lazy(lambda i=i, target=target: (here(), far_of(i)[0], *dst_of(), (b, 2 * target() + to_c)))

    pieces = ((0, pl.ds(fs * 0 // 4, fs * 4 // 4)), (1, pl.ds(fs * 0 // 4, fs * 2 // 4)), (1, pl.ds(fs * 2 // 4, fs * 2 // 4)))
    gate_up = [
        (
            lambda zz, k=k, at=at: r.pgu.at[k, pl.ds(pl.multiple_of(zz * blk, blk), blk), at],
            lambda p=p, k=k, at=at: (r.rgu.at[k, z, :, at], r.zgu.at[p, z]),
            lambda i, p=p, k=k, at=at: (r.ugu.at[k, i, :, at], r.zfar.at[p, i]),
            0,
        )
        for p, (k, at) in enumerate(pieces)
    ]
    down = (
        lambda zz: r.pdn.at[pl.ds(2 * zz, 2)],
        lambda: (r.rdn.at[z], r.zdn.at[z]),
        lambda i: (r.udn.at[i], r.zfar.at[3, i]),
        1,
    )
    outp = (
        lambda zz: r.pout.at[pl.ds(pl.multiple_of(zz * blk, blk), blk), :],
        lambda: (r.rout.at[z], r.zout.at[z]),
        lambda i: (r.uout.at[i], r.zfar.at[4, i]),
        1,
    )
    early = (
        lambda zz: r.pq.at[pl.ds(2 * zz, 2)],
        lambda: (r.rqz.at[z], r.zq.at[z]),
        lambda i: (r.uq.at[i], r.zfar.at[5, i]),
        1,
    )
    late = (
        lambda zz: r.pat.at[pl.ds(pl.multiple_of(zz * blk, blk), blk), :],
        lambda: (r.rat.at[z], r.zat.at[z]),
        lambda i: (r.uat.at[i], r.zfar.at[6, i]),
        1,
    )

    def hidden_again():
        @pl.when(c == 0)
        def _():
            for i in range(2 * nb):
                @pl.when((i != 2 * side) & (i != 2 * across + 1))
                def _(i=i):
                    arrived(hT_slot(i), r.rh.at[i])

            for i in range(2 * nb * tok // 512):
                at = slice(i * 512, (i + 1) * 512)
                g = mm(r.wgT[...], r.hT_b[:, at])
                u = mm(r.wuT[...], r.hT_b[:, at])
                sg = 1.0 / (1.0 + jnp.exp(-g))
                r.act_x[:, at] = (g * sg * u).astype(BF16)
                r.fa[:, at] = u * (sg * (1.0 + g * (1.0 - sg)))
                r.fb[:, at] = g * sg

        send_lazy(lambda: (c == 0, r.act_x, r.act_x, r.rax.at[0], sib))

    def hidden_sums():
        @pl.when(c == 1)
        def _():
            for i in range(2 * nb):
                @pl.when((i != 2 * side) & (i != 2 * across + 1))
                def _(i=i):
                    arrived(dmo_slot(i), r.rdmo.at[i])

            rows_d = jnp.concatenate(
                [r.wd[pl.ds(pl.multiple_of(t * nb * units + b * units, units), units), :] for t in range(n)], axis=0
            )
            r.da_x[...] = mm_nt(rows_d, r.dmo_b[...]).astype(BF16)

        send_lazy(lambda: (c == 1, r.da_x, r.da_x, r.rda.at[0], sib))

        @pl.when(c == 1)
        def _():
            arrived(r.act_x, r.rax.at[0])
            r.pdn[...] = mm(r.act_x[...], r.dmo_b[...]).astype(BF16).reshape(n, units, d)

        share(*down)
        share_near(*down)
        for k in range(2):
            @pl.when(c == 0)
            def _(k=k):
                if k == 0:
                    arrived(r.da_x, r.rda.at[0])
                r.dgu[k] = (r.da_x[...].astype(F32) * (r.fb if k else r.fa)[...]).astype(BF16)
                r.pgu[k] = mm_nt(r.hT_b[...], r.dgu[k]).astype(BF16)

            for p, (of, _) in enumerate(pieces):
                if of == k:
                    share(*gate_up[p])
                    share_near(*gate_up[p])
        pass_on(*outp)

    @pl.when(c == 1)
    def _():
        for i in range(2):
            arrived(r.o2.at[:, pl.ds(i * tok, tok)], r.ro2.at[i])
            arrived(r.da2.at[pl.ds(i * tok, tok), :], r.rda2.at[i])
        r.pout[...] = mm(r.o2[...], r.da2[...]).astype(BF16)

    share(*outp)
    share_near(*outp)

    relay(hT_slot, r.rh, 0)

    r.acc[...] = jnp.zeros(r.acc.shape, F32)

    def query_step(kb, _):
        @pl.when(kb == jnp.maximum(z - 1, 0))
        def _():
            relay(dmo_slot, r.rdmo, 1)

        set_bias(kb, True)

        def pair(p, _):
            lanes = pl.ds(pl.multiple_of(p * 128, 128), 128)
            qp, kp, vp = r.q_all[s, :, lanes], r.k_all[kb, :, lanes], r.v_all[kb, :, lanes]
            dop = r.do_all[s, :, lanes]
            pf = jnp.exp(mm_nt(stack(qp), kp) + r.bias[...] - twice(r.m[p]))
            dp = mm_nt(stack(dop), vp)
            ds = (pf * (dp - twice(r.delta[p]))).astype(BF16)
            r.acc[:, lanes] += unstack(mm(ds, kp))
            return 0

        lax.fori_loop(0, pairs, pair, 0, unroll=True)
        return 0

    lax.fori_loop(0, z + 1, query_step, 0)

    def turn_back(src, dst, factor):
        co, si = r.cos[z, own, :], r.sin[z, own, :]
        for p in range(pairs):
            g = src[:, p * 128:(p + 1) * 128] * factor
            dst[:, p * 128:(p + 1) * 128] = (g * co - turn(g) * si).astype(BF16)

    turn_back(r.acc, r.dq, 0.125)

    def half_send(k, value, h, bb):
        plane_send_lazy(
            lambda: (value.at[:, pl.ds(h * dh, dh)], r.at_b.at[k, tokens, :], r.rat_in.at[k, e]), bb, 1
        )

    for bb in range(nb):
        half_send(0, r.dq, bb % 2, bb)
    hidden_again()

    r.acc[...] = jnp.zeros(r.acc.shape, F32)
    r.acc2[...] = jnp.zeros(r.acc2.shape, F32)

    def key_step(j):
        qb = z + j
        mine, other = 2 * qb + c, 2 * qb + 1 - c

        @pl.when(j > 0)
        def _():
            arrived(r.id_all.at[mine], r.rid.at[mine])
            arrived(r.id_all.at[other], r.rid.at[other])
            arrived(r.q_all.at[mine], r.rq.at[mine])
            remote(r.q_all.at[mine], r.q_all.at[mine], r.bsem.at[2, mine], r.rq.at[mine], sib).start()
            blocks = [(rows_of(r.do_all, mine, ch), r.rdo.at[ch, mine]) for ch in range(2)]
            blocks.append((r.st_all.at[mine], r.rst.at[mine]))
            for i, (got, sem) in enumerate(blocks):
                arrived(got, sem)

                @pl.when(z > 0)
                def _():
                    remote(got, got, r.fsem.at[2 + i, mine], sem, left).start()

                remote(got, got, r.bsem.at[3 + i, mine], sem, sib).start()

        arrived(r.q_all.at[other], r.rq.at[other])
        for ch in range(2):
            arrived(rows_of(r.do_all, other, ch), r.rdo.at[ch, other])
        arrived(r.st_all.at[other], r.rst.at[other])
        set_bias(qb, False)

        def pair(p, _):
            lanes = pl.ds(pl.multiple_of(p * 128, 128), 128)
            kp, vp = r.k_all[z, own, lanes], r.v_all[z, own, lanes]
            qp = r.q_all[pl.ds(2 * qb, 2), :, lanes].reshape(2 * tok, 128)
            dop = r.do_all[pl.ds(2 * qb, 2), :, lanes].reshape(2 * tok, 128)

            def row(base):
                return jnp.concatenate(
                    [
                        jnp.broadcast_to(
                            jnp.concatenate(
                                [r.st_all[2 * qb + i, pl.ds(base + 2 * p + h, 1), :] for i in range(2)], axis=1
                            ),
                            (tok, 2 * tok),
                        )
                        for h in range(2)
                    ],
                    axis=0,
                )

            pf = jnp.exp(mm_nt(stack(kp), qp) + r.bias[...] - row(0))
            dp = mm_nt(stack(vp), dop)
            ds = (pf * (dp - row(16))).astype(BF16)
            r.acc2[:, lanes] += unstack(mm(pf.astype(BF16), dop))
            r.acc[:, lanes] += unstack(mm(ds, qp))
            return 0

        lax.fori_loop(0, pairs, pair, 0, unroll=True)

    def keys_done():
        turn_back(r.acc, r.dk, 1.0)
        r.dv[...] = r.acc2[...].astype(BF16)
        for bb in range(nb):
            half_send(1, r.dv if bb >= 2 else r.dk, bb % 2, bb)
    last = nz - z
    sums_at = jnp.where(z == 0, 2, jnp.where(z == nz - 1, 0, last))

    def key_loop(j, _):
        pl.when(j == sums_at)(hidden_sums)

        @pl.when(j < last)
        def _():
            key_step(j)

        pl.when(j == last - 1)(keys_done)
        return 0

    lax.fori_loop(0, last + 1, key_loop, 0)
    r.gin_v[...] = (
        r.dr[...] + mm_nt(r.dq[...], r.wq[...]) + mm_nt(r.dk[...], r.wk[...]) + mm_nt(r.dv[...], r.wv[...])
    )
    pltpu.make_async_copy(r.gin_v, r.gin_h, r.osem.at[1]).start()


    @pl.when(c == 1)
    def _():
        each_source(lambda i: r.xT_b.at[:, pl.ds(i * tok, tok)], r.rxt, 2 * nb)

    def attn_sum(k):
        @pl.when(c == 1)
        def _():
            each_source(lambda i: r.at_b.at[k, pl.ds(i * tok, tok), :], r.rat_in.at[k], 2 * nb)
            if k:
                r.pat[...] = mm(r.xT_b[...], r.at_b[k]).astype(BF16)
            else:
                part = d // (2 * n)
                some = jnp.concatenate(
                    [r.xT_b[pl.ds(pl.multiple_of((2 * t + by) * part, part), part), :] for t in range(n)], axis=0
                )
                r.pq[...] = mm(some, r.at_b[k]).astype(BF16).reshape(n, part, dh)

        share(*(late if k else early))

    def totals(total_of, own, recv_of, rsem_of):
        def add(slots):
            total = own().astype(F32)
            for at in slots:
                arrived(recv_of(at), rsem_of(at))
                total = total + recv_of(at)[...].astype(F32)
            total_of()[...] = total.astype(BF16).reshape(total_of().shape)

        pl.when(end)(lambda: add((1, 2)))
        pl.when(jnp.logical_not(end))(lambda: add((jnp.where(z == 1, 0, nz - 1), nz - 1 - z)))

    def spread(src_of, dst_of, from_c, some=False):
        for bb in range(nb):
            for cc in range(2):
                def here(bb=bb, cc=cc):
                    return (b == bb) & (c == cc)

                send_lazy(
                    lambda bb=bb, cc=cc, here=here: (
                        on(from_c, some) & jnp.logical_not(here()), src_of(cc), *dst_of(), (bb, 2 * z + cc)
                    )
                )

                @pl.when(on(from_c, some) & here())
                def _(cc=cc):
                    pltpu.make_async_copy(src_of(cc), *dst_of()).start()

    rows = pl.ds(pl.multiple_of(z * blk, blk), blk)
    quarter = blk // 4

    def out_total():
        @pl.when(c == 1)
        def _():
            total = None
            for bb in range(nb):
                arrived(r.rso.at[bb], r.rrso.at[bb])
                part = r.rso[bb].astype(F32)
                total = part if total is None else total + part
            r.fso[...] = total.astype(BF16)

        spread(lambda cc: r.fso.at[cc], lambda: (r.oout_h.at[b], r.fout.at[b]), 1)

    def gate_up_total(p):
        k, cols = pieces[p]

        @pl.when(c == 0)
        def _():
            totals(
                lambda: r.sgu.at[k, :, cols], lambda: r.pgu[k, rows, cols], lambda at: r.rgu.at[k, at, :, cols],
                lambda at: r.zgu.at[p, at],
            )

        spread(
            lambda cc: r.sgu.at[k, pl.ds(cc * (blk // 2), blk // 2), cols],
            lambda: (r.ogu_h.at[b, k, :, cols], r.fgu.at[p, b]),
            0,
        )

    attn_sum(0)
    @pl.when(c == 1)
    def _():
        totals(lambda: r.sout, lambda: r.pout[rows, :], lambda at: r.rout.at[at], lambda at: r.zout.at[at])

    for bb in range(nb):
        at = (slice(None), pl.ds((bb // 2) * quarter, quarter), pl.ds((bb % 2) * dh, dh))
        send((c == 1) & (b != bb), r.sout.at[at], r.rso.at[b], r.rrso.at[b], (bb, s))

        @pl.when((c == 1) & (b == bb))
        def _(at=at):
            pltpu.make_async_copy(r.sout.at[at], r.rso.at[b], r.rrso.at[b]).start()

    pass_on(*gate_up[0])
    gate_up_total(0)
    for part in gate_up[1:]:
        pass_on(*part)
    for p in range(1, len(pieces)):
        gate_up_total(p)
    pass_on(*down)
    attn_sum(1)
    for part in (early, late):
        share_near(*part)
    pass_on(*early)
    out_total()

    adds = (b == 0) & (c == 0)

    @pl.when(adds)
    def _():
        total = None
        for i in range(2 * nb):
            arrived(r.gl_b.at[i], r.rgl.at[i])
            total = r.gl_b[i] if total is None else total + r.gl_b[i]
        r.gz[z] = total

    for zz in range(nz):
        send(adds & (z != zz), r.gz.at[z], r.gz.at[z], r.zgl.at[z], (0, 2 * zz))

    @pl.when(adds)
    def _():
        total = r.gz[z]
        for dz in range(1, nz):
            at = lax.rem(z + dz, nz)
            arrived(r.gz.at[at], r.zgl.at[at])
            total = total + r.gz[at]
        r.gsum[...] = total

    for bb in range(nb):
        for cc in range(2):
            here = (bb == 0) and (cc == 0)
            if not here:
                send(adds, r.gsum, r.ogl_h, r.fgl.at[0], (bb, 2 * z + cc))

    @pl.when(adds)
    def _():
        pltpu.make_async_copy(r.gsum, r.ogl_h, r.fgl.at[0]).start()

    @pl.when(c == 1)
    def _():
        totals(lambda: r.sdn, lambda: r.pdn[pl.ds(2 * z, 2)], lambda at: r.rdn.at[at], lambda at: r.zdn.at[at])

    spread(lambda cc: r.sdn.at[cc], lambda: (r.odn_h.at[b], r.fdn.at[b]), 1)
    pass_on(*late)

    @pl.when(c == 1)
    def _():
        totals(lambda: r.sq, lambda: r.pq[pl.ds(2 * z, 2)], lambda at: r.rqz.at[at], lambda at: r.zq.at[at])

    spread(lambda cc: r.sq.at[cc], lambda: (r.oq_h.at[b], r.fq.at[b]), 1)

    @pl.when(c == 1)
    def _():
        totals(lambda: r.sat, lambda: r.pat[rows, :], lambda at: r.rat.at[at], lambda at: r.zat.at[at])

    spread(
        lambda cc: r.sat.at[pl.ds(cc * (blk // 2), blk // 2), :], lambda: (r.oat_h.at[b], r.fat.at[b]), 1
    )

    for bb in range(nb):
        for p, (k, at) in enumerate(pieces):
            arrived(r.ogu_h.at[bb, k, :, at], r.fgu.at[p, bb])
        arrived(r.odn_h.at[bb], r.fdn.at[bb])
        arrived(r.oq_h.at[bb], r.fq.at[bb])
        arrived(r.oout_h.at[bb], r.fout.at[bb])
        arrived(r.oat_h.at[bb], r.fat.at[bb])
    arrived(r.ogl_h, r.fgl.at[0])
    out_copy.wait()
    pltpu.make_async_copy(r.gin_v, r.gin_h, r.osem.at[1]).wait()
    assert used[0] <= r.ssem.shape[0], used
    for make, at in pending:
        cond, src, dst, rsem, dev = make()

        @pl.when(cond)
        def _():
            remote(src, dst, r.ssem.at[at], rsem, dev).wait_send()

    def sent_on(t, _):
        @pl.when((lax.rem(t, 2) == c) & (t < s))
        def _():
            for ch in range(2):
                got = rows_of(r.x_all, t, ch)
                remote(got, got, r.bsem.at[ch, t], r.rx.at[ch, t], sib).wait_send()

                @pl.when(z + 1 < nz)
                def _():
                    remote(got, got, r.fsem.at[ch, t], r.rx.at[ch, t], right).wait_send()

        @pl.when((lax.rem(t, 2) == c) & (t > s))
        def _():
            remote(r.q_all.at[t], r.q_all.at[t], r.bsem.at[2, t], r.rq.at[t], sib).wait_send()
            blocks = [(rows_of(r.do_all, t, ch), r.rdo.at[ch, t]) for ch in range(2)]
            blocks.append((r.st_all.at[t], r.rst.at[t]))
            for i, (got, sem) in enumerate(blocks):
                remote(got, got, r.bsem.at[3 + i, t], sem, sib).wait_send()

                @pl.when(z > 0)
                def _():
                    remote(got, got, r.fsem.at[2 + i, t], sem, left).wait_send()
        return 0

    lax.fori_loop(0, n, sent_on, 0)


def unpack_kernel(
    n, nb, out_in, gin_in, oat_h, ogu_h, odn_h, oout_h, oq_h, ogl_h,
    out, gin, gq_h, gk_h, gv_h, go_h, gg_h, gu_h, gd_h, g1_h, g2_h,
    oat, ogu, odn, oout, oq, ogl, gq, gk, gv, go, gg, gu, gd, out_v, gin_v, g1, g2, isem, osem,
):
    s = lax.axis_index("seq")
    fs = ogu.shape[3]
    units, dh = odn.shape[1], odn.shape[2] // 2
    copy = pltpu.make_async_copy
    loads = [copy(a, b, isem.at[i]) for i, (a, b) in enumerate(
        ((ogu_h, ogu), (oat_h, oat), (odn_h, odn), (ogl_h, ogl), (out_in, out_v), (gin_in, gin_v), (oout_h, oout), (oq_h, oq)))]
    stores = [copy(a, b, osem.at[i]) for i, (a, b) in enumerate(
        ((gg, gg_h), (gu, gu_h), (gq, gq_h), (gk, gk_h), (gv, gv_h), (go, go_h), (gd, gd_h),
         (out_v, out.at[0]), (gin_v, gin.at[0]), (g1, g1_h), (g2, g2_h)))]
    for load in loads:
        load.start()
    loads[0].wait()
    low = lax.broadcasted_iota(jnp.int32, (ogu.shape[2], 128), 1) < 64

    def interleave(k, dst):
        for t in range(n):
            for y in range(2):
                at = slice((t // 2) * 128, (t // 2 + 1) * 128)
                one, two = ogu[2 * y, k, :, at].astype(F32), ogu[2 * y + 1, k, :, at].astype(F32)
                if t % 2:
                    one = pltpu.roll(one, 64, 1)
                else:
                    two = pltpu.roll(two, 64, 1)
                dst[:, (2 * t + y) * 128:(2 * t + y + 1) * 128] = jnp.where(low, one, two)

    interleave(0, gg)
    stores[0].start()
    interleave(1, gu)
    stores[1].start()
    loads[1].wait()
    for m, (ref, bb) in enumerate(((gk, 0), (gv, 2))):
        ref[:, :dh] = oat[bb].astype(F32)
        ref[:, dh:] = oat[bb + 1].astype(F32)
        stores[3 + m].start()
    loads[6].wait()
    loads[7].wait()
    part = oout.shape[1]
    for m, (src, dst) in enumerate(((oq, gq), (oout, go))):
        for bb in range(nb):
            dst[(bb // 2) * part:(bb // 2 + 1) * part, (bb % 2) * dh:(bb % 2 + 1) * dh] = src[bb].astype(F32)
        stores[5 if m else 2].start()
    loads[2].wait()
    for bb in range(nb):
        gd[bb * units:(bb + 1) * units, :] = odn[bb].astype(F32)
    stores[6].start()
    for i in (4, 5):
        loads[i].wait()
        stores[3 + i].start()
    loads[3].wait()
    d = ogl.shape[1]
    own = d // n
    gains = pltpu.roll(ogl[...], lax.rem(d - s * own, d), 1)
    g1[...] = gains[0:1, :own]
    g2[...] = gains[1:2, :own]
    stores[9].start()
    stores[10].start()
    for store in stores:
        store.wait()


def rope_constants(length, head_dim):
    half = head_dim // 2
    inverse = np.exp(-2.0 * math.log(THETA) / head_dim * np.arange(half)).astype(np.float32)
    angle = np.arange(length, dtype=np.float32)[:, None] * inverse
    cos, sin = np.cos(angle.astype(np.float64)), np.sin(angle.astype(np.float64))
    return (
        np.concatenate([cos, cos, cos, cos], 1).astype(np.float32),
        np.concatenate([-sin, sin, -sin, sin], 1).astype(np.float32),
    )


def fused_local(n, nb, tokens, doc_ids, w_query, w_key, w_value, w_out, w_gate, w_up, w_down, gain_attn, gain_ffn, cotangent):
    _, tok, d = tokens.shape
    f = w_gate.shape[1]
    nz = n // 2
    cos, sin = rope_constants(n * tok, d // HEADS)
    cos = jnp.asarray(cos.reshape(nz, 2 * tok, 128))
    sin = jnp.asarray(sin.reshape(nz, 2 * tok, 128))
    plan = scratch_plan(tok, d, f, n, nb)
    vmem, anywhere = pl.BlockSpec(memory_space=pltpu.VMEM), pl.BlockSpec(memory_space=pl.ANY)
    shape = jax.ShapeDtypeStruct
    parts = pl.pallas_call(
        functools.partial(layer_kernel, tuple(plan), tok, d, f, n, nb),
        out_shape=(
            shape((tok, d), F32), shape((tok, d), F32), shape((nb, d // n, d // 2), BF16),
            shape((nb, 2, d // n, f // nb), BF16), shape((nb, f // (nb * n), d), BF16), shape((nb, d // (2 * n), d // 2), BF16),
            shape((nb, d // (2 * n), d // 2), BF16), shape((8, d), F32),
        ),
        in_specs=[anywhere] * 14,
        out_specs=[anywhere] * 8,
        scratch_shapes=list(plan.values()),
        compiler_params=pltpu.CompilerParams(
            collective_id=0, has_side_effects=True, vmem_limit_bytes=62 * 2**20
        ),
        name="layer",
    )(
        doc_ids, tokens, cotangent, gain_attn, gain_ffn, cos, sin,
        w_query, w_key, w_value, w_out, w_gate, w_up, w_down,
    )
    own = d // n
    grads = [shape((own, d), F32)] * 4 + [shape((own, f), F32)] * 2 + [shape((f // n, d), F32)]
    results = pl.pallas_call(
        functools.partial(unpack_kernel, n, nb),
        out_shape=(shape((1, tok, d), F32), shape((1, tok, d), F32), *grads, shape((1, own), F32), shape((1, own), F32)),
        in_specs=[pl.BlockSpec(memory_space=pltpu.HBM)] * 8,
        out_specs=[anywhere] * 11,
        scratch_shapes=[pltpu.VMEM(parts[i].shape, parts[i].dtype) for i in (2, 3, 4, 5, 6, 7)]
        + [pltpu.VMEM(g.shape, g.dtype) for g in grads]
        + [pltpu.VMEM((tok, d), F32)] * 2
        + [pltpu.VMEM((1, own), F32)] * 2
        + [pltpu.SemaphoreType.DMA((8,)), pltpu.SemaphoreType.DMA((11,))],
        compiler_params=pltpu.CompilerParams(vmem_limit_bytes=62 * 2**20),
        name="unpack",
    )(*parts)
    return results[:9] + (results[9].reshape(own), results[10].reshape(own))


def fits(shapes, n, nb):
    (_, tok, d), f = shapes[0], shapes[6][1]
    return (
        nb == 4 and n == 8 and n * tok <= 1024 and tok == 128 and shapes[0][0] == 1
        and d == HEADS * 64 and d % 256 == 0 and d % (32 * n) == 0 and f == 2 * tok * n and f % 512 == 0
    )


def solution(mesh):
    nb, n = mesh.shape["batch"], mesh.shape["seq"]

    def either(*args):
        shapes = [a.shape for a in args]
        if fits(shapes, n, nb):
            return fused_local(n, nb, *args)
        return local(*args)

    return jax.shard_map(
        either,
        mesh=mesh,
        in_specs=(
            P("batch", "seq", None),
            P("batch", "seq"),
            P(),
            P(),
            P(),
            P(),
            P(),
            P(),
            P(),
            P(),
            P(),
            P("batch", "seq", None),
        ),
        out_specs=(
            P("batch", "seq", None),
            P("batch", "seq", None),
            P("seq", None),
            P("seq", None),
            P("seq", None),
            P("seq", None),
            P("seq", None),
            P("seq", None),
            P("seq", None),
            P("seq"),
            P("seq"),
        ),
        check_vma=False,
    )
```

```python
import functools
import math
import types

import jax
import jax.numpy as jnp
import numpy as np
from jax import lax
from jax.experimental import pallas as pl
from jax.experimental.pallas import tpu as pltpu
from jax.sharding import PartitionSpec as P

HEADS = 12
NSEG = 8


EPSILON = 1e-06
THETA = 10000.0
MASKED = -1e30


def root_mean_square_norm(values, gain):
    return values * lax.rsqrt(jnp.mean(values * values, -1, keepdims=True) + EPSILON) * gain


def swiglu(gate, up_part):
    return jax.nn.silu(gate) * up_part


def rope_tables(positions, head_dim):
    half_dim = head_dim // 2
    inverse = jnp.exp(-2.0 * math.log(THETA) / head_dim * jnp.arange(half_dim, dtype=jnp.float32))
    angle = positions.astype(jnp.float32)[..., None] * inverse
    return (
        jnp.concatenate([jnp.cos(angle), jnp.cos(angle)], -1),
        jnp.concatenate([jnp.sin(angle), jnp.sin(angle)], -1),
    )


def rotate(values, cosine, sine):
    half_dim = values.shape[-1] // 2
    turned = jnp.concatenate([-values[..., half_dim:], values[..., :half_dim]], -1)
    return values * cosine + turned * sine


def rotate_back(grads, cosine, sine):
    half_dim = grads.shape[-1] // 2
    turned = grads * sine
    return grads * cosine + jnp.concatenate([turned[..., half_dim:], -turned[..., :half_dim]], -1)


def block_size(total_rows):
    return max((d for d in range(1, min(total_rows, 2048) + 1) if total_rows % d == 0))


def doc_begin(segment_begins, where_at):
    earlier = segment_begins[:, None, :] <= where_at[:, :, None]
    return jnp.max(jnp.where(earlier, segment_begins[:, None, :], 0), -1)


def outer_sum(remaining_tokens, right):
    return lax.dot_general(
        remaining_tokens, right, (((0,), (0,)), ((), ())), preferred_element_type=jnp.float32
    )


def back_product(grads, weight_matrix):
    return lax.dot_general(
        grads, weight_matrix, (((1,), (1,)), ((), ())), preferred_element_type=jnp.float32
    )


def masked_scores(queries, key_block, key_at, query_at, query_begin):
    batch_rows, block_rows, model_width = key_block.shape
    head_count = queries.shape[2]
    head_dim = model_width // head_count
    key_heads = key_block.reshape(batch_rows, block_rows, head_count, head_dim)
    scores = jnp.einsum(
        "bqhd,bkhd->bhqk", queries, key_heads, preferred_element_type=jnp.float32
    ) * (1.0 / math.sqrt(head_dim))
    key_pos = key_at[None, None, :]
    query_pos = query_at[:, :, None]
    begin_pos = query_begin[:, :, None]
    allowed = (
        (key_pos <= query_pos) & (key_pos >= begin_pos) & ((begin_pos > 0) | (key_pos == query_pos))
    )
    return (scores, allowed[:, None], key_heads)


def grad_terms(
    queries, grad_heads, lse, delta, query_at, query_begin, key_block, value_block, key_at
):
    scores, allowed, key_heads = masked_scores(queries, key_block, key_at, query_at, query_begin)
    value_heads = value_block.reshape(key_heads.shape)
    probs = jnp.where(allowed, jnp.exp(scores - lse[..., None]), 0.0)
    dprob = jnp.einsum(
        "bqhd,bkhd->bhqk", grad_heads, value_heads, preferred_element_type=jnp.float32
    )
    dscore = (probs * (dprob - delta[..., None])).astype(jnp.bfloat16)
    return (probs.astype(jnp.bfloat16), dscore, key_heads, value_heads)


def over_rows(update, carried, arrays, first_row):
    total_rows = arrays[0].shape[1]
    block_rows = block_size(total_rows)

    def over_step(block_index, state):
        offset = block_index * block_rows
        blocks = tuple((lax.dynamic_slice_in_dim(item, offset, block_rows, 1) for item in arrays))
        key_at = first_row + offset + jnp.arange(block_rows, dtype=jnp.int32)
        return update(state, blocks, key_at)

    return lax.fori_loop(0, total_rows // block_rows, over_step, carried)


def local(
    tokens,
    doc_ids,
    w_query,
    w_key,
    w_value,
    w_out,
    w_gate,
    w_up,
    w_down,
    gain_attn,
    gain_ffn,
    cotangent,
):
    batch_rows, local_len, model_width = tokens.shape
    head_count = HEADS
    head_dim = model_width // head_count
    shape_heads = (batch_rows, local_len, head_count, head_dim)
    scale = 1.0 / math.sqrt(head_dim)
    labels = jnp.arange(NSEG, dtype=jnp.int32)
    member = (doc_ids[:, :, None] == labels).astype(jnp.int32)
    totals = lax.psum(jnp.sum(member, 1), "seq")
    segment_begins = jnp.cumsum(totals, 1) - totals
    local_at = lax.axis_index("seq") * local_len + jnp.arange(local_len, dtype=jnp.int32)
    query_at = jnp.broadcast_to(local_at, (batch_rows, local_len))
    query_begin = doc_begin(segment_begins, query_at)
    cosine, sine = rope_tables(query_at - query_begin, head_dim)
    cosine = cosine[:, :, None, :]
    sine = sine[:, :, None, :]
    flat_tokens = tokens.reshape(batch_rows * local_len, model_width)
    queries = rotate(
        jnp.dot(flat_tokens, w_query, preferred_element_type=jnp.float32).reshape(shape_heads),
        cosine,
        sine,
    ).astype(jnp.bfloat16)
    key_send = (
        rotate(
            jnp.dot(flat_tokens, w_key, preferred_element_type=jnp.float32).reshape(shape_heads),
            cosine,
            sine,
        )
        .astype(jnp.bfloat16)
        .reshape(batch_rows, local_len, model_width)
    )
    value_send = (
        jnp.dot(flat_tokens, w_value, preferred_element_type=jnp.float32)
        .astype(jnp.bfloat16)
        .reshape(batch_rows, local_len, model_width)
    )

    def stats_step(state, blocks, key_at):
        run_max, run_sum = state
        scores, allowed, key_heads = masked_scores(
            queries, blocks[0], key_at, query_at, query_begin
        )
        scores = jnp.where(allowed, scores, MASKED)
        new_max = jnp.maximum(run_max, jnp.max(scores, -1))
        weights = jnp.where(allowed, jnp.exp(scores - new_max[..., None]), 0.0)
        return (new_max, run_sum * jnp.exp(run_max - new_max) + jnp.sum(weights, -1))

    stats_init = (
        jnp.full((batch_rows, head_count, local_len), MASKED, jnp.float32),
        jnp.zeros((batch_rows, head_count, local_len), jnp.float32),
    )
    zero_heads = jnp.zeros(shape_heads, jnp.float32)
    run_max, run_sum = over_rows(
        stats_step, stats_init, (lax.all_gather(key_send, "seq", axis=1, tiled=True),), jnp.int32(0)
    )
    lse = run_max + jnp.log(run_sum)

    def output_step(state, blocks, key_at):
        scores, allowed, key_heads = masked_scores(
            queries, blocks[0], key_at, query_at, query_begin
        )
        value_heads = blocks[1].reshape(key_heads.shape)
        probs = jnp.where(allowed, jnp.exp(scores - lse[..., None]), 0.0).astype(jnp.bfloat16)
        return state + jnp.einsum(
            "bhqk,bkhd->bqhd", probs, value_heads, preferred_element_type=jnp.float32
        )

    attended = over_rows(
        output_step,
        zero_heads,
        (
            lax.all_gather(key_send, "seq", axis=1, tiled=True),
            lax.all_gather(value_send, "seq", axis=1, tiled=True),
        ),
        jnp.int32(0),
    )
    attended_low = attended.astype(jnp.bfloat16).reshape(batch_rows * local_len, model_width)
    first_sum = flat_tokens.astype(jnp.float32) + jnp.dot(
        attended_low, w_out, preferred_element_type=jnp.float32
    )
    hidden, norm_first_back = jax.vjp(root_mean_square_norm, first_sum, gain_attn)
    hidden_low = hidden.astype(jnp.bfloat16)
    gate = jnp.dot(hidden_low, w_gate, preferred_element_type=jnp.float32)
    up_part = jnp.dot(hidden_low, w_up, preferred_element_type=jnp.float32)
    active, swiglu_back = jax.vjp(swiglu, gate, up_part)
    active_low = active.astype(jnp.bfloat16)
    second_sum = hidden + jnp.dot(active_low, w_down, preferred_element_type=jnp.float32)
    output, norm_second_back = jax.vjp(root_mean_square_norm, second_sum, gain_ffn)
    second_grad, grad_gain_ffn = norm_second_back(
        cotangent.reshape(batch_rows * local_len, model_width).astype(jnp.float32)
    )
    branch_grad = second_grad.astype(jnp.bfloat16)
    grad_down = outer_sum(active_low, branch_grad)
    gate_grad, up_grad = swiglu_back(back_product(branch_grad, w_down))
    gate_low = gate_grad.astype(jnp.bfloat16)
    up_low = up_grad.astype(jnp.bfloat16)
    grad_gate = outer_sum(hidden_low, gate_low)
    grad_up = outer_sum(hidden_low, up_low)
    hidden_grad = second_grad + back_product(gate_low, w_gate) + back_product(up_low, w_up)
    first_grad, grad_gain_attn = norm_first_back(hidden_grad)
    attn_grad = first_grad.astype(jnp.bfloat16)
    grad_out = outer_sum(attended_low, attn_grad)
    grad_heads = back_product(attn_grad, w_out).astype(jnp.bfloat16).reshape(shape_heads)
    delta = jnp.swapaxes(jnp.sum(grad_heads.astype(jnp.float32) * attended, -1), 1, 2)

    def query_step(state, blocks, key_at):
        probs_low, dscore, key_heads, value_heads = grad_terms(
            queries, grad_heads, lse, delta, query_at, query_begin, blocks[0], blocks[1], key_at
        )
        return (
            state
            + jnp.einsum("bhqk,bkhd->bqhd", dscore, key_heads, preferred_element_type=jnp.float32)
            * scale
        )

    all_keys, all_values = (
        lax.all_gather(key_send, "seq", axis=1, tiled=True),
        lax.all_gather(value_send, "seq", axis=1, tiled=True),
    )
    query_grad = over_rows(query_step, zero_heads, (all_keys, all_values), 0)
    first_row = jnp.int32(0)
    span_rows = local_len * lax.axis_size("seq")
    block_rows = block_size(span_rows)
    empty = jnp.zeros((batch_rows, span_rows, head_count, head_dim), jnp.float32)

    def key_step(block_index, state):
        offset = block_index * block_rows
        key_block = lax.dynamic_slice_in_dim(all_keys, offset, block_rows, 1)
        value_block = lax.dynamic_slice_in_dim(all_values, offset, block_rows, 1)
        key_at = first_row + offset + jnp.arange(block_rows, dtype=jnp.int32)
        probs_low, dscore, key_heads, value_heads = grad_terms(
            queries, grad_heads, lse, delta, query_at, query_begin, key_block, value_block, key_at
        )
        key_part = (
            jnp.einsum("bhqk,bqhd->bkhd", dscore, queries, preferred_element_type=jnp.float32)
            * scale
        )
        value_part = jnp.einsum(
            "bhqk,bqhd->bkhd", probs_low, grad_heads, preferred_element_type=jnp.float32
        )
        return (
            lax.dynamic_update_slice_in_dim(state[0], key_part, offset, 1),
            lax.dynamic_update_slice_in_dim(state[1], value_part, offset, 1),
        )

    key_all, value_all = lax.fori_loop(0, span_rows // block_rows, key_step, (empty, empty))
    joined = jnp.concatenate(
        [
            key_all.reshape(batch_rows, span_rows, model_width),
            value_all.reshape(batch_rows, span_rows, model_width),
        ],
        -1,
    )
    summed_keys = jnp.swapaxes(
        lax.psum_scatter(jnp.swapaxes(joined, 0, 1), "seq", scatter_dimension=0, tiled=True), 0, 1
    )
    key_grad = summed_keys[..., :model_width].reshape(shape_heads)
    value_grad = summed_keys[..., model_width:]
    flat_len = batch_rows * local_len
    query_low = (
        rotate_back(query_grad, cosine, sine).astype(jnp.bfloat16).reshape(flat_len, model_width)
    )
    key_low = (
        rotate_back(key_grad, cosine, sine).astype(jnp.bfloat16).reshape(flat_len, model_width)
    )
    value_low = value_grad.astype(jnp.bfloat16).reshape(flat_len, model_width)
    grad_input = (
        first_grad
        + back_product(query_low, w_query)
        + back_product(key_low, w_key)
        + back_product(value_low, w_value)
    )
    grad_query = outer_sum(flat_tokens, query_low)
    grad_key = outer_sum(flat_tokens, key_low)
    value_weight_gradient = outer_sum(flat_tokens, value_low)
    shares = (
        lax.psum_scatter(grad_query, "seq", scatter_dimension=0, tiled=True),
        lax.psum_scatter(grad_key, "seq", scatter_dimension=0, tiled=True),
        lax.psum_scatter(value_weight_gradient, "seq", scatter_dimension=0, tiled=True),
        lax.psum_scatter(grad_out, "seq", scatter_dimension=0, tiled=True),
        lax.psum_scatter(grad_gate, "seq", scatter_dimension=0, tiled=True),
        lax.psum_scatter(grad_up, "seq", scatter_dimension=0, tiled=True),
        lax.psum_scatter(grad_down, "seq", scatter_dimension=0, tiled=True),
        lax.psum_scatter(grad_gain_attn, "seq", scatter_dimension=0, tiled=True),
        lax.psum_scatter(grad_gain_ffn, "seq", scatter_dimension=0, tiled=True),
    )
    results = (
        lax.psum(shares[0].astype(jnp.bfloat16), "batch").astype(jnp.float32),
        lax.psum(shares[1].astype(jnp.bfloat16), "batch").astype(jnp.float32),
        lax.psum(shares[2].astype(jnp.bfloat16), "batch").astype(jnp.float32),
        lax.psum(shares[3].astype(jnp.bfloat16), "batch").astype(jnp.float32),
        lax.psum(shares[4].astype(jnp.bfloat16), "batch").astype(jnp.float32),
        lax.psum(shares[5].astype(jnp.bfloat16), "batch").astype(jnp.float32),
        lax.psum(shares[6].astype(jnp.bfloat16), "batch").astype(jnp.float32),
        lax.psum(shares[7].astype(jnp.bfloat16), "batch").astype(jnp.float32),
        lax.psum(shares[8].astype(jnp.bfloat16), "batch").astype(jnp.float32),
    )
    output_rows = output.reshape(batch_rows, local_len, model_width)
    input_rows = grad_input.reshape(batch_rows, local_len, model_width)
    return (
        output_rows,
        input_rows,
        results[0],
        results[1],
        results[2],
        results[3],
        results[4],
        results[5],
        results[6],
        results[7],
        results[8],
    )


MESH = pl.DeviceIdType.MESH
F32 = jnp.float32
BF16 = jnp.bfloat16


def mm(a, b):
    return lax.dot_general(a, b, (((1,), (0,)), ((), ())), preferred_element_type=F32)


def mm_nt(a, b):
    return lax.dot_general(a, b, (((1,), (1,)), ((), ())), preferred_element_type=F32)


def scratch_plan(tok, d, f, n, nb):
    nz, plane, heads = n // 2, 2 * nb * tok, HEADS
    vm = pltpu.VMEM
    dma = lambda *shape: pltpu.SemaphoreType.DMA(shape)
    return dict(
        wq=vm((d, d), BF16), wk=vm((d, d), BF16), wv=vm((d, d), BF16), wo=vm((d, d), BF16),
        wg=vm((d, f), BF16), wu=vm((d, f), BF16), wd=vm((f, d), BF16),
        cos=vm((nz, 2 * tok, 128), F32), sin=vm((nz, 2 * tok, 128), F32),
        ids=vm((1, tok), jnp.int32), cot=vm((tok, d), BF16), ga=vm((d,), F32), gf=vm((d,), F32),
        x_all=vm((n, tok, d), BF16), q_all=vm((n, tok, d), BF16), do_all=vm((n, tok, d), BF16),
        k_all=vm((nz, 2 * tok, d), BF16), v_all=vm((nz, 2 * tok, d), BF16),
        st_all=vm((n, 32, tok), F32), id_all=vm((n, 8, tok), jnp.int32),
        idcol=vm((tok, 128), F32), bias=vm((2 * tok, 2 * tok), F32),
        m=vm((heads // 2, 2 * tok, 128), F32), l=vm((heads // 2, 2 * tok, 128), F32),
        delta=vm((heads // 2, 2 * tok, 128), F32),
        acc=vm((tok, d), F32), acc2=vm((tok, d), F32),
        olow=vm((tok, d), BF16), hb=vm((tok, d), BF16), h1=vm((tok, d), F32), n1=vm((tok, d), F32),
        ri1=vm((tok, 128), F32), dr=vm((tok, d), F32),
        act=vm((tok, f), BF16),
        dg=vm((tok, f), BF16), du=vm((tok, f), BF16), dmo=vm((tok, d), BF16), dattn=vm((tok, d), BF16),
        dq=vm((tok, d), BF16), dk=vm((tok, d), BF16), dv=vm((tok, d), BF16),
        hT=vm((d, tok), BF16), xT=vm((d, tok), BF16), oT=vm((d, tok), BF16),
        gl=vm((8, d), F32), out_v=vm((tok, d), F32), gin_v=vm((tok, d), F32),
        hT_b=vm((d, plane), BF16), dmo_b=vm((plane, d), BF16),
        wgT=vm((f // nb, d), BF16), wuT=vm((f // nb, d), BF16), tmpT=vm((128, d), BF16),
        act_x=vm((f // nb, plane), BF16), da_x=vm((f // nb, plane), BF16),
        fa=vm((f // nb, plane), F32), fb=vm((f // nb, plane), F32), dgu=vm((2, f // nb, plane), BF16),
        xT_b=vm((d, plane), BF16), o2=vm((d, 2 * tok), BF16), da2=vm((2 * tok, d), BF16), at_b=vm((2, plane, d // 2), BF16), gl_b=vm((2 * nb, 8, d), F32),
        pgu=vm((2, d, f // nb), BF16), pdn=vm((n, f // (nb * n), d), BF16),
        pat=vm((d, d // 2), BF16), pq=vm((n, d // (2 * n), d // 2), BF16), pout=vm((d, d), BF16),
        ugu=vm((2, 2, d // nz, f // nb), BF16), udn=vm((2, 2, f // (nb * n), d), BF16),
        uat=vm((2, d // nz, d // 2), BF16), uq=vm((2, 2, d // (2 * n), d // 2), BF16),
        uout=vm((2, d // nz, d), BF16), rout=vm((nz, d // nz, d), BF16), sout=vm((2, d // n, d), BF16),
        rso=vm((nb, 2, d // (2 * n), d // 2), BF16), fso=vm((2, d // (2 * n), d // 2), BF16),
        rgu=vm((2, nz, d // nz, f // nb), BF16), rdn=vm((nz, 2, f // (nb * n), d), BF16), rat=vm((nz, d // nz, d // 2), BF16), rqz=vm((nz, 2, d // (2 * n), d // 2), BF16),
        sgu=vm((2, d // nz, f // nb), BF16), sdn=vm((2, f // (nb * n), d), BF16), sat=vm((d // nz, d // 2), BF16), sq=vm((2, d // (2 * n), d // 2), BF16),
        gz=vm((nz, 8, d), F32), gsum=vm((8, d), F32),
        wsem=dma(14), osem=dma(2), ssem=dma(230), fsem=dma(5, n), bsem=dma(6, n),
        rx=dma(2, n), rq=dma(n), rdo=dma(2, n), rst=dma(n), rid=dma(n),
        rh=dma(2 * nb), rdmo=dma(2 * nb), rax=dma(1), rda=dma(1), zfar=dma(7, 2),
        rxt=dma(2 * nb), ro2=dma(2), rda2=dma(2), zout=dma(nz), rrso=dma(nb), fout=dma(nb), rat_in=dma(2, 2 * nb), rgl=dma(2 * nb),
        zgu=dma(3, nz), zdn=dma(nz), zat=dma(nz), zq=dma(nz), zgl=dma(nz),
        fgu=dma(3, nb), fdn=dma(nb), fat=dma(nb), fq=dma(nb), fgl=dma(1),
    )


INPUTS = ("ids_h", "tok_h", "cot_h", "ga_h", "gf_h", "cos_h", "sin_h", "wq_h", "wk_h", "wv_h", "wo_h", "wg_h", "wu_h", "wd_h")
OUTPUTS = ("out_h", "gin_h", "oat_h", "ogu_h", "odn_h", "oout_h", "oq_h", "ogl_h")


def layer_kernel(plan_names, tok, d, f, n, nb, *refs):
    r = types.SimpleNamespace(**dict(zip(INPUTS + OUTPUTS + plan_names, refs)))
    nz, pairs = n // 2, d // 128
    fs, dh, blk = f // nb, d // 2, d // nz
    b, s = lax.axis_index("batch"), lax.axis_index("seq")
    z, c = s // 2, lax.rem(s, 2)
    by, bx = b // 2, lax.rem(b, 2)
    e = 2 * b + c
    sib = (b, s + 1 - 2 * c)
    pending, used = [], [0]

    def remote(src, dst, ssem, rsem, dev):
        return pltpu.make_async_remote_copy(
            src_ref=src, dst_ref=dst, send_sem=ssem, recv_sem=rsem, device_id=dev, device_id_type=MESH
        )

    def send_lazy(make):
        at = used[0]
        used[0] += 1
        pending.append((make, at))
        cond, src, dst, rsem, dev = make()

        @pl.when(cond)
        def _():
            remote(src, dst, r.ssem.at[at], rsem, dev).start()

    def send(cond, src, dst, rsem, dev):
        send_lazy(lambda: (cond, src, dst, rsem, dev))

    def plane_send_lazy(make, to_b, to_c, also=None):
        def here():
            return (b == to_b) & (c == to_c)

        def wanted(cond):
            return cond if also is None else cond & also()

        send_lazy(lambda: (wanted(jnp.logical_not(here())), *make(), (to_b, 2 * z + to_c)))

        @pl.when(wanted(here()))
        def _():
            pltpu.make_async_copy(*make()).start()

    def plane_send(src, dst, rsem, to_b, to_c):
        plane_send_lazy(lambda: (src, dst, rsem), to_b, to_c)

    def arrived(dst, rsem):
        remote(dst, dst, r.ssem.at[0], rsem, sib).wait_recv()

    loads = {}
    for i, (name, src, dst) in enumerate(
        (
            ("tok", r.tok_h.at[0], r.x_all.at[s]), ("ids", r.ids_h, r.ids), ("ga", r.ga_h, r.ga), ("gf", r.gf_h, r.gf),
            ("cot", r.cot_h.at[0], r.cot),
        )
    ):
        loads[name] = pltpu.make_async_copy(src, dst, r.wsem.at[9 + i])
    loads["tok"].start()
    loads["ids"].start()
    bar = pltpu.get_barrier_semaphore()
    for zz in range(nz):
        for cc in range(2):
            @pl.when(2 * zz + cc != s)
            def _(zz=zz, cc=cc):
                pl.semaphore_signal(bar, inc=1, device_id=(b, 2 * zz + cc), device_id_type=MESH)
    for bb in range(nb):
        for cc in range(2):
            @pl.when(bb != b)
            def _(bb=bb, cc=cc):
                pl.semaphore_signal(bar, inc=1, device_id=(bb, 2 * z + cc), device_id_type=MESH)
    for i, name in enumerate(("wk", "wv", "wq", "cos", "sin", "wo", "wg", "wu", "wd")):
        loads[name] = pltpu.make_async_copy(getattr(r, name + "_h"), getattr(r, name), r.wsem.at[i])
        loads[name].start()
    for name in ("ga", "gf", "cot"):
        loads[name].start()
    loads["ids"].wait()
    r.id_all[s] = jnp.broadcast_to(r.ids[...], (8, tok))
    loads["tok"].wait()
    pl.semaphore_wait(bar, n - 1 + 2 * (nb - 1))

    always = s >= 0
    half = tok // 2

    def rows_of(ref, t, ch):
        return ref.at[t, pl.ds(ch * half, half)]

    right, left = (b, s + 2), (b, s - 2)
    send(always, r.id_all.at[s], r.id_all.at[s], r.rid.at[s], sib)
    for ch in range(2):
        mine = rows_of(r.x_all, s, ch)
        send(z + 1 < nz, mine, mine, r.rx.at[ch, s], right)
        send(always, mine, mine, r.rx.at[ch, s], sib)
    for zz in range(nz):
        for cc in range(2):
            send(z != zz, r.id_all.at[s], r.id_all.at[s], r.rid.at[s], (b, 2 * zz + cc))

    lane = lax.broadcasted_iota(jnp.int32, (tok, 128), 1)
    first = lane < 64
    half_mask = (jnp.where(first, 1.0, 0.0).astype(BF16), jnp.where(first, 0.0, 1.0).astype(BF16))

    def turn(u):
        low = lax.rem(lax.broadcasted_iota(jnp.int32, u.shape, 1), 64) < 32
        return jnp.where(low, pltpu.roll(u, 96, 1), pltpu.roll(u, 32, 1))

    def twice(u):
        return jnp.concatenate([u, u], axis=1)

    def stack(u):
        return jnp.concatenate([u * half_mask[0], u * half_mask[1]], axis=0)

    def unstack(u):
        return jnp.where(first, u[:tok], u[tok:])

    own = pl.ds(pl.multiple_of(c * tok, tok), tok)

    loads["wq"].wait()
    loads["cos"].wait()
    loads["sin"].wait()

    u = mm(r.x_all[s], r.wq[...])
    co, si = r.cos[z, own, :], r.sin[z, own, :]
    for p in range(pairs):
        part = u[:, p * 128:(p + 1) * 128]
        r.q_all[s, :, p * 128:(p + 1) * 128] = ((part * co + turn(part) * si) * 0.125).astype(BF16)
    send(always, r.q_all.at[s], r.q_all.at[s], r.rq.at[s], sib)
    for dz in range(1, nz):
        send(z - dz >= 0, r.q_all.at[s], r.q_all.at[s], r.rq.at[s], (b, s - 2 * dz))

    def transpose_into(dst, value):
        for p in range(d // 128):
            dst[p * 128:(p + 1) * 128, :] = value[:, p * 128:(p + 1) * 128].T.astype(BF16)

    tokens = pl.ds(pl.multiple_of(e * tok, tok), tok)
    side, across = 2 * by + 1 - bx, 2 * (1 - by) + bx

    def relay(slot_of, rsem, to_c):
        for source, target in ((lambda: 2 * side, across), (lambda: 2 * across + 1, side)):
            @pl.when(c == to_c)
            def _(source=source):
                arrived(slot_of(source()), rsem.at[source()])

            send_lazy(
                lambda source=source, target=target: (
                    c == to_c, slot_of(source()), slot_of(source()), rsem.at[source()], (target, s)
                )
            )

    def hT_slot(i):
        return r.hT_b.at[:, pl.ds(pl.multiple_of(i * tok, tok), tok)]

    def dmo_slot(i):
        return r.dmo_b.at[pl.ds(pl.multiple_of(i * tok, tok), tok), :]
    transpose_into(r.xT, r.x_all[s].astype(F32))
    for bb in range(nb):
        plane_send(r.xT, r.xT_b.at[:, tokens], r.rxt.at[e], bb, 1)
    r.idcol[...] = jnp.broadcast_to(r.ids[...].astype(F32), (128, tok)).T

    def ids_of(block):
        return jnp.concatenate(
            [r.id_all[2 * block, 0:1, :], r.id_all[2 * block + 1, 0:1, :]], axis=1
        ).astype(F32)

    def set_bias(block, local_is_query):
        shape = (tok, 2 * tok)
        mine = s * tok + lax.broadcasted_iota(jnp.int32, shape, 0)
        theirs = block * (2 * tok) + lax.broadcasted_iota(jnp.int32, shape, 1)
        my_id = twice(r.idcol[...])
        their_id = jnp.broadcast_to(ids_of(block), shape)
        causal = (theirs <= mine) if local_is_query else (mine <= theirs)
        allowed = (my_id == their_id) & causal & ((my_id != 0.0) | (mine == theirs))
        bias = jnp.where(allowed, 0.0, MASKED)
        r.bias[...] = jnp.concatenate([bias, bias], axis=0)

    units = fs // n

    def quarter_weights():
        for src, dst in ((r.wg, r.wgT), (r.wu, r.wuT)):
            for t in range(n):
                tile = src[:, pl.ds(pl.multiple_of((2 * t + by) * 128, 128), 128)].astype(F32)
                for p in range(pairs):
                    r.tmpT[:, p * 128:(p + 1) * 128] = tile[p * 128:(p + 1) * 128].T.astype(BF16)
                dst[t * units:(t + 1) * units, :] = r.tmpT[pl.ds(pl.multiple_of(bx * units, units), units), :]

    r.m[...] = jnp.full(r.m.shape, MASKED, F32)
    r.l[...] = jnp.zeros(r.l.shape, F32)
    r.acc[...] = jnp.zeros(r.acc.shape, F32)
    loads["wk"].wait()
    loads["wv"].wait()

    def forward_step(j, _):
        kb = z - j
        mine, other = 2 * kb + c, 2 * kb + 1 - c

        @pl.when(j > 0)
        def _():
            for ch in range(2):
                got = rows_of(r.x_all, mine, ch)
                arrived(got, r.rx.at[ch, mine])

                @pl.when(z + 1 < nz)
                def _():
                    remote(got, got, r.fsem.at[ch, mine], r.rx.at[ch, mine], right).start()

                remote(got, got, r.bsem.at[ch, mine], r.rx.at[ch, mine], sib).start()

            arrived(r.id_all.at[mine], r.rid.at[mine])

        for ch in range(2):
            arrived(rows_of(r.x_all, other, ch), r.rx.at[ch, other])
        arrived(r.id_all.at[other], r.rid.at[other])
        set_bias(kb, True)

        xb = r.x_all[pl.ds(2 * kb, 2)].reshape(2 * tok, d)
        u = mm(xb, r.wk[...])
        co, si = r.cos[kb], r.sin[kb]
        for p in range(pairs):
            part = u[:, p * 128:(p + 1) * 128]
            r.k_all[kb, :, p * 128:(p + 1) * 128] = (part * co + turn(part) * si).astype(BF16)
        r.v_all[kb] = mm(xb, r.wv[...]).astype(BF16)

        def pair(p, _):
            lanes = pl.ds(pl.multiple_of(p * 128, 128), 128)
            qp, kp, vp = r.q_all[s, :, lanes], r.k_all[kb, :, lanes], r.v_all[kb, :, lanes]
            sc = mm_nt(stack(qp), kp) + r.bias[...]
            m_old = r.m[p]
            m_new = jnp.maximum(m_old, jnp.max(sc, axis=1, keepdims=True))
            alpha = jnp.exp(m_old - m_new)
            ex = jnp.exp(sc - twice(m_new))
            r.m[p] = m_new
            r.l[p] = r.l[p] * alpha + jnp.sum(ex, axis=1, keepdims=True)
            r.acc[:, lanes] = r.acc[:, lanes] * unstack(alpha) + unstack(mm(ex.astype(BF16), vp))
            return 0

        lax.fori_loop(0, pairs, pair, 0, unroll=True)

        @pl.when((j == 0) & (c == 0))
        def _():
            loads["wg"].wait()
            loads["wu"].wait()
            quarter_weights()

        return 0

    lax.fori_loop(0, z + 1, forward_step, 0)

    def finish(p, _):
        lanes = pl.ds(pl.multiple_of(p * 128, 128), 128)
        r.acc[:, lanes] = r.acc[:, lanes] / unstack(r.l[p])
        r.m[p] = r.m[p] + jnp.log(r.l[p])
        return 0

    lax.fori_loop(0, pairs, finish, 0, unroll=True)
    r.olow[...] = r.acc[...].astype(BF16)

    loads["wo"].wait()
    loads["ga"].wait()
    loads["gf"].wait()
    loads["cot"].wait()
    gain_a, gain_f = r.ga[...].reshape(1, d), r.gf[...].reshape(1, d)
    r1 = r.x_all[s].astype(F32) + mm(r.olow[...], r.wo[...])
    ri1 = lax.rsqrt(jnp.mean(r1 * r1, axis=1, keepdims=True) + EPSILON)
    r.ri1[...] = jnp.broadcast_to(ri1, (tok, 128))
    n1 = r1 * ri1
    r.n1[...] = n1
    h1 = n1 * gain_a
    r.h1[...] = h1
    r.hb[...] = h1.astype(BF16)
    transpose_into(r.hT, h1)
    for to_b in (b, side, across):
        plane_send(r.hT, r.hT_b.at[:, tokens], r.rh.at[e], to_b, 0)

    @pl.when(c == 1)
    def _():
        loads["wg"].wait()
        loads["wu"].wait()

    def gate_at(i):
        return (slice((i // 2) * tok, (i // 2 + 1) * tok), slice((i % 2) * 512, (i % 2 + 1) * 512))

    def up_at(i):
        return gate_at(i + f // 512)

    for i in range(f // 512):
        at = slice(i * 512, (i + 1) * 512)
        g = mm(r.hb[...], r.wg[:, at])
        u = mm(r.hb[...], r.wu[:, at])
        r.fa[gate_at(i)] = g
        r.fa[up_at(i)] = u
        a = g / (1.0 + jnp.exp(-g)) * u
        r.act[:, at] = a.astype(BF16)
    loads["wd"].wait()
    r2 = r.h1[...] + mm(r.act[...], r.wd[...])
    ri2 = lax.rsqrt(jnp.mean(r2 * r2, axis=1, keepdims=True) + EPSILON)
    n2 = r2 * ri2
    ct = r.cot[...].astype(F32)
    t2 = ct * gain_f
    dr2 = ri2 * (t2 - n2 * jnp.mean(n2 * t2, axis=1, keepdims=True))
    r.dr[...] = dr2
    r.dmo[...] = dr2.astype(BF16)
    for to_b in (b, side, across):
        plane_send(r.dmo, r.dmo_b.at[tokens, :], r.rdmo.at[e], to_b, 1)

    r.out_v[...] = n2 * gain_f
    out_copy = pltpu.make_async_copy(r.out_v, r.out_h, r.osem.at[0])
    out_copy.start()
    gain_ffn = jnp.sum(ct * n2, axis=0, keepdims=True)
    transpose_into(r.oT, r.acc[...])

    for i in range(f // 512):
        at = slice(i * 512, (i + 1) * 512)
        da = mm_nt(r.dmo[...], r.wd[at, :])
        g, u = r.fa[gate_at(i)], r.fa[up_at(i)]
        sg = 1.0 / (1.0 + jnp.exp(-g))
        r.dg[:, at] = (da * u * (sg * (1.0 + g * (1.0 - sg)))).astype(BF16)
        r.du[:, at] = (da * (g * sg)).astype(BF16)
    dh1 = r.dr[...] + mm_nt(r.dg[...], r.wg[...]) + mm_nt(r.du[...], r.wu[...])
    n1 = r.n1[...]
    gain_attn = jnp.sum(dh1 * n1, axis=0, keepdims=True)
    t1 = dh1 * gain_a
    dr1 = r.ri1[:, 0:1] * (t1 - n1 * jnp.mean(n1 * t1, axis=1, keepdims=True))
    r.dr[...] = dr1
    r.dattn[...] = dr1.astype(BF16)
    r.gl[...] = jnp.concatenate([gain_attn, gain_ffn, jnp.zeros((6, d), F32)], axis=0)
    plane_send(r.gl, r.gl_b.at[e], r.rgl.at[e], 0, 0)
    plane_send_lazy(lambda: (r.oT, r.o2.at[:, own], r.ro2.at[c]), b, 1)
    plane_send_lazy(lambda: (r.dattn, r.da2.at[own, :], r.rda2.at[c]), b, 1)

    r.do_all[s] = mm_nt(r.dattn[...], r.wo[...]).astype(BF16)
    for ch in range(2):
        mine = rows_of(r.do_all, s, ch)
        send(z > 0, mine, mine, r.rdo.at[ch, s], left)
        send(always, mine, mine, r.rdo.at[ch, s], sib)

    stats = jnp.zeros((tok, 128), F32)
    for p in range(pairs):
        prod = r.do_all[s, :, p * 128:(p + 1) * 128].astype(F32) * r.acc[:, p * 128:(p + 1) * 128]
        for h in range(2):
            head = 2 * p + h
            part = jnp.sum(jnp.where(first == (h == 0), prod, 0.0), axis=1, keepdims=True)
            part = jnp.broadcast_to(part, (tok, 128))
            r.delta[p, h * tok:(h + 1) * tok] = part
            stats = jnp.where(lane == head, r.m[p, h * tok:(h + 1) * tok], stats)
            stats = jnp.where(lane == 16 + head, part, stats)
    r.st_all[s] = stats.T[0:32, :]
    send(z > 0, r.st_all.at[s], r.st_all.at[s], r.rst.at[s], left)
    send(always, r.st_all.at[s], r.st_all.at[s], r.rst.at[s], sib)

    def each_source(dst_of, rsem, count):
        for i in range(count):
            arrived(dst_of(i), rsem.at[i])

    end = (z == 0) | (z == nz - 1)

    def on(to_c, some):
        return c == to_c

    def share(src_of, dst_of, far_of, to_c, some=False):
        near = lambda: jnp.where(z < nz // 2, 0, nz - 1)
        for i in range(2):
            send_lazy(
                lambda i=i: (
                    on(to_c, some) & end, src_of(jnp.abs(nz - 1 - i - z)), *far_of(i),
                    (b, 2 * jnp.where(z == 0, 1, nz - 2) + to_c),
                )
            )
        send_lazy(
            lambda: (on(to_c, some) & jnp.logical_not(end), src_of(near()), *dst_of(), (b, 2 * near() + to_c))
        )

    def share_near(src_of, dst_of, far_of, to_c, some=False):
        send_lazy(
            lambda: (on(to_c, some) & end, src_of(jnp.where(z == 0, 1, nz - 2)), *dst_of(),
                     (b, 2 * jnp.where(z == 0, 1, nz - 2) + to_c))
        )

    def pass_on(own_of, dst_of, far_of, to_c, some=False):
        def here():
            return on(to_c, some) & jnp.logical_not(end)

        for i in range(2):
            def target(i=i):
                return nz - 1 - z if i else jnp.where(z == 1, nz - 1, 0)

            @pl.when(here())
            def _(i=i, target=target):
                far, sem = far_of(i)
                arrived(far, sem)
                far[...] = (own_of(target())[...].astype(F32) + far[...].astype(F32)).astype(BF16)

            send_lazy(lambda i=i, target=target: (here(), far_of(i)[0], *dst_of(), (b, 2 * target() + to_c)))

    pieces = ((0, pl.ds(fs * 0 // 4, fs * 4 // 4)), (1, pl.ds(fs * 0 // 4, fs * 2 // 4)), (1, pl.ds(fs * 2 // 4, fs * 2 // 4)))
    gate_up = [
        (
            lambda zz, k=k, at=at: r.pgu.at[k, pl.ds(pl.multiple_of(zz * blk, blk), blk), at],
            lambda p=p, k=k, at=at: (r.rgu.at[k, z, :, at], r.zgu.at[p, z]),
            lambda i, p=p, k=k, at=at: (r.ugu.at[k, i, :, at], r.zfar.at[p, i]),
            0,
        )
        for p, (k, at) in enumerate(pieces)
    ]
    down = (
        lambda zz: r.pdn.at[pl.ds(2 * zz, 2)],
        lambda: (r.rdn.at[z], r.zdn.at[z]),
        lambda i: (r.udn.at[i], r.zfar.at[3, i]),
        1,
    )
    outp = (
        lambda zz: r.pout.at[pl.ds(pl.multiple_of(zz * blk, blk), blk), :],
        lambda: (r.rout.at[z], r.zout.at[z]),
        lambda i: (r.uout.at[i], r.zfar.at[4, i]),
        1,
    )
    early = (
        lambda zz: r.pq.at[pl.ds(2 * zz, 2)],
        lambda: (r.rqz.at[z], r.zq.at[z]),
        lambda i: (r.uq.at[i], r.zfar.at[5, i]),
        1,
    )
    late = (
        lambda zz: r.pat.at[pl.ds(pl.multiple_of(zz * blk, blk), blk), :],
        lambda: (r.rat.at[z], r.zat.at[z]),
        lambda i: (r.uat.at[i], r.zfar.at[6, i]),
        1,
    )

    def hidden_again():
        @pl.when(c == 0)
        def _():
            for i in range(2 * nb):
                @pl.when((i != 2 * side) & (i != 2 * across + 1))
                def _(i=i):
                    arrived(hT_slot(i), r.rh.at[i])

            for i in range(2 * nb * tok // 512):
                at = slice(i * 512, (i + 1) * 512)
                g = mm(r.wgT[...], r.hT_b[:, at])
                u = mm(r.wuT[...], r.hT_b[:, at])
                sg = 1.0 / (1.0 + jnp.exp(-g))
                r.act_x[:, at] = (g * sg * u).astype(BF16)
                r.fa[:, at] = u * (sg * (1.0 + g * (1.0 - sg)))
                r.fb[:, at] = g * sg

        send_lazy(lambda: (c == 0, r.act_x, r.act_x, r.rax.at[0], sib))

    def hidden_sums():
        @pl.when(c == 1)
        def _():
            for i in range(2 * nb):
                @pl.when((i != 2 * side) & (i != 2 * across + 1))
                def _(i=i):
                    arrived(dmo_slot(i), r.rdmo.at[i])

            rows_d = jnp.concatenate(
                [r.wd[pl.ds(pl.multiple_of(t * nb * units + b * units, units), units), :] for t in range(n)], axis=0
            )
            r.da_x[...] = mm_nt(rows_d, r.dmo_b[...]).astype(BF16)

        send_lazy(lambda: (c == 1, r.da_x, r.da_x, r.rda.at[0], sib))

        @pl.when(c == 1)
        def _():
            arrived(r.act_x, r.rax.at[0])
            r.pdn[...] = mm(r.act_x[...], r.dmo_b[...]).astype(BF16).reshape(n, units, d)

        share(*down)
        share_near(*down)
        for k in range(2):
            @pl.when(c == 0)
            def _(k=k):
                if k == 0:
                    arrived(r.da_x, r.rda.at[0])
                r.dgu[k] = (r.da_x[...].astype(F32) * (r.fb if k else r.fa)[...]).astype(BF16)
                r.pgu[k] = mm_nt(r.hT_b[...], r.dgu[k]).astype(BF16)

            for p, (of, _) in enumerate(pieces):
                if of == k:
                    share(*gate_up[p])
                    share_near(*gate_up[p])
        pass_on(*outp)


    relay(hT_slot, r.rh, 0)

    r.acc[...] = jnp.zeros(r.acc.shape, F32)

    def query_step(kb, _):
        @pl.when(kb == jnp.maximum(z - 1, 0))
        def _():
            relay(dmo_slot, r.rdmo, 1)

            @pl.when(c == 1)
            def _():
                for i in range(2):
                    arrived(r.o2.at[:, pl.ds(i * tok, tok)], r.ro2.at[i])
                    arrived(r.da2.at[pl.ds(i * tok, tok), :], r.rda2.at[i])
                r.pout[...] = mm(r.o2[...], r.da2[...]).astype(BF16)

            share(*outp)
            share_near(*outp)

        set_bias(kb, True)

        def pair(p, _):
            lanes = pl.ds(pl.multiple_of(p * 128, 128), 128)
            qp, kp, vp = r.q_all[s, :, lanes], r.k_all[kb, :, lanes], r.v_all[kb, :, lanes]
            dop = r.do_all[s, :, lanes]
            pf = jnp.exp(mm_nt(stack(qp), kp) + r.bias[...] - twice(r.m[p]))
            dp = mm_nt(stack(dop), vp)
            ds = (pf * (dp - twice(r.delta[p]))).astype(BF16)
            r.acc[:, lanes] += unstack(mm(ds, kp))
            return 0

        lax.fori_loop(0, pairs, pair, 0, unroll=True)
        return 0

    lax.fori_loop(0, z + 1, query_step, 0)

    def turn_back(src, dst, factor):
        co, si = r.cos[z, own, :], r.sin[z, own, :]
        for p in range(pairs):
            g = src[:, p * 128:(p + 1) * 128] * factor
            dst[:, p * 128:(p + 1) * 128] = (g * co - turn(g) * si).astype(BF16)

    turn_back(r.acc, r.dq, 0.125)

    def half_send(k, value, h, bb):
        plane_send_lazy(
            lambda: (value.at[:, pl.ds(h * dh, dh)], r.at_b.at[k, tokens, :], r.rat_in.at[k, e]), bb, 1
        )

    for bb in range(nb):
        half_send(0, r.dq, bb % 2, bb)
    hidden_again()

    r.acc[...] = jnp.zeros(r.acc.shape, F32)
    r.acc2[...] = jnp.zeros(r.acc2.shape, F32)

    def key_step(j):
        qb = z + j
        mine, other = 2 * qb + c, 2 * qb + 1 - c

        @pl.when(j > 0)
        def _():
            arrived(r.id_all.at[mine], r.rid.at[mine])
            arrived(r.id_all.at[other], r.rid.at[other])
            arrived(r.q_all.at[mine], r.rq.at[mine])
            remote(r.q_all.at[mine], r.q_all.at[mine], r.bsem.at[2, mine], r.rq.at[mine], sib).start()
            blocks = [(rows_of(r.do_all, mine, ch), r.rdo.at[ch, mine]) for ch in range(2)]
            blocks.append((r.st_all.at[mine], r.rst.at[mine]))
            for i, (got, sem) in enumerate(blocks):
                arrived(got, sem)

                @pl.when(z > 0)
                def _():
                    remote(got, got, r.fsem.at[2 + i, mine], sem, left).start()

                remote(got, got, r.bsem.at[3 + i, mine], sem, sib).start()

        arrived(r.q_all.at[other], r.rq.at[other])
        for ch in range(2):
            arrived(rows_of(r.do_all, other, ch), r.rdo.at[ch, other])
        arrived(r.st_all.at[other], r.rst.at[other])
        set_bias(qb, False)

        def pair(p, _):
            lanes = pl.ds(pl.multiple_of(p * 128, 128), 128)
            kp, vp = r.k_all[z, own, lanes], r.v_all[z, own, lanes]
            qp = r.q_all[pl.ds(2 * qb, 2), :, lanes].reshape(2 * tok, 128)
            dop = r.do_all[pl.ds(2 * qb, 2), :, lanes].reshape(2 * tok, 128)

            def row(base):
                return jnp.concatenate(
                    [
                        jnp.broadcast_to(
                            jnp.concatenate(
                                [r.st_all[2 * qb + i, pl.ds(base + 2 * p + h, 1), :] for i in range(2)], axis=1
                            ),
                            (tok, 2 * tok),
                        )
                        for h in range(2)
                    ],
                    axis=0,
                )

            pf = jnp.exp(mm_nt(stack(kp), qp) + r.bias[...] - row(0))
            dp = mm_nt(stack(vp), dop)
            ds = (pf * (dp - row(16))).astype(BF16)
            r.acc2[:, lanes] += unstack(mm(pf.astype(BF16), dop))
            r.acc[:, lanes] += unstack(mm(ds, qp))
            return 0

        lax.fori_loop(0, pairs, pair, 0, unroll=True)

    def keys_done():
        turn_back(r.acc, r.dk, 1.0)
        r.dv[...] = r.acc2[...].astype(BF16)
        for bb in range(nb):
            half_send(1, r.dv if bb >= 2 else r.dk, bb % 2, bb)
    last = nz - z
    sums_at = jnp.where(z == 0, 2, jnp.where(z == nz - 1, 0, last))

    def key_loop(j, _):
        pl.when(j == sums_at)(hidden_sums)

        @pl.when(j < last)
        def _():
            key_step(j)

        pl.when(j == last - 1)(keys_done)
        return 0

    lax.fori_loop(0, last + 1, key_loop, 0)
    r.gin_v[...] = (
        r.dr[...] + mm_nt(r.dq[...], r.wq[...]) + mm_nt(r.dk[...], r.wk[...]) + mm_nt(r.dv[...], r.wv[...])
    )
    pltpu.make_async_copy(r.gin_v, r.gin_h, r.osem.at[1]).start()


    @pl.when(c == 1)
    def _():
        each_source(lambda i: r.xT_b.at[:, pl.ds(i * tok, tok)], r.rxt, 2 * nb)

    def attn_sum(k):
        @pl.when(c == 1)
        def _():
            each_source(lambda i: r.at_b.at[k, pl.ds(i * tok, tok), :], r.rat_in.at[k], 2 * nb)
            if k:
                r.pat[...] = mm(r.xT_b[...], r.at_b[k]).astype(BF16)
            else:
                part = d // (2 * n)
                some = jnp.concatenate(
                    [r.xT_b[pl.ds(pl.multiple_of((2 * t + by) * part, part), part), :] for t in range(n)], axis=0
                )
                r.pq[...] = mm(some, r.at_b[k]).astype(BF16).reshape(n, part, dh)

        share(*(late if k else early))

    def totals(total_of, own, recv_of, rsem_of):
        def add(slots):
            total = own().astype(F32)
            for at in slots:
                arrived(recv_of(at), rsem_of(at))
                total = total + recv_of(at)[...].astype(F32)
            total_of()[...] = total.astype(BF16).reshape(total_of().shape)

        pl.when(end)(lambda: add((1, 2)))
        pl.when(jnp.logical_not(end))(lambda: add((jnp.where(z == 1, 0, nz - 1), nz - 1 - z)))

    def spread(src_of, dst_of, from_c, some=False):
        for bb in range(nb):
            for cc in range(2):
                def here(bb=bb, cc=cc):
                    return (b == bb) & (c == cc)

                send_lazy(
                    lambda bb=bb, cc=cc, here=here: (
                        on(from_c, some) & jnp.logical_not(here()), src_of(cc), *dst_of(), (bb, 2 * z + cc)
                    )
                )

                @pl.when(on(from_c, some) & here())
                def _(cc=cc):
                    pltpu.make_async_copy(src_of(cc), *dst_of()).start()

    rows = pl.ds(pl.multiple_of(z * blk, blk), blk)
    quarter = blk // 4

    def out_total():
        @pl.when(c == 1)
        def _():
            total = None
            for bb in range(nb):
                arrived(r.rso.at[bb], r.rrso.at[bb])
                part = r.rso[bb].astype(F32)
                total = part if total is None else total + part
            r.fso[...] = total.astype(BF16)

        spread(lambda cc: r.fso.at[cc], lambda: (r.oout_h.at[b], r.fout.at[b]), 1)

    def gate_up_total(p):
        k, cols = pieces[p]

        @pl.when(c == 0)
        def _():
            totals(
                lambda: r.sgu.at[k, :, cols], lambda: r.pgu[k, rows, cols], lambda at: r.rgu.at[k, at, :, cols],
                lambda at: r.zgu.at[p, at],
            )

        spread(
            lambda cc: r.sgu.at[k, pl.ds(cc * (blk // 2), blk // 2), cols],
            lambda: (r.ogu_h.at[b, k, :, cols], r.fgu.at[p, b]),
            0,
        )

    attn_sum(0)
    @pl.when(c == 1)
    def _():
        totals(lambda: r.sout, lambda: r.pout[rows, :], lambda at: r.rout.at[at], lambda at: r.zout.at[at])

    for bb in range(nb):
        at = (slice(None), pl.ds((bb // 2) * quarter, quarter), pl.ds((bb % 2) * dh, dh))
        send((c == 1) & (b != bb), r.sout.at[at], r.rso.at[b], r.rrso.at[b], (bb, s))

        @pl.when((c == 1) & (b == bb))
        def _(at=at):
            pltpu.make_async_copy(r.sout.at[at], r.rso.at[b], r.rrso.at[b]).start()

    pass_on(*gate_up[0])
    gate_up_total(0)
    for part in gate_up[1:]:
        pass_on(*part)
    for p in range(1, len(pieces)):
        gate_up_total(p)
    pass_on(*down)
    attn_sum(1)
    for part in (early, late):
        share_near(*part)
    pass_on(*early)
    out_total()

    adds = (b == 0) & (c == 0)

    @pl.when(adds)
    def _():
        total = None
        for i in range(2 * nb):
            arrived(r.gl_b.at[i], r.rgl.at[i])
            total = r.gl_b[i] if total is None else total + r.gl_b[i]
        r.gz[z] = total

    for zz in range(nz):
        send(adds & (z != zz), r.gz.at[z], r.gz.at[z], r.zgl.at[z], (0, 2 * zz))

    @pl.when(adds)
    def _():
        total = r.gz[z]
        for dz in range(1, nz):
            at = lax.rem(z + dz, nz)
            arrived(r.gz.at[at], r.zgl.at[at])
            total = total + r.gz[at]
        r.gsum[...] = total

    for bb in range(nb):
        for cc in range(2):
            here = (bb == 0) and (cc == 0)
            if not here:
                send(adds, r.gsum, r.ogl_h, r.fgl.at[0], (bb, 2 * z + cc))

    @pl.when(adds)
    def _():
        pltpu.make_async_copy(r.gsum, r.ogl_h, r.fgl.at[0]).start()

    @pl.when(c == 1)
    def _():
        totals(lambda: r.sdn, lambda: r.pdn[pl.ds(2 * z, 2)], lambda at: r.rdn.at[at], lambda at: r.zdn.at[at])

    spread(lambda cc: r.sdn.at[cc], lambda: (r.odn_h.at[b], r.fdn.at[b]), 1)
    pass_on(*late)

    @pl.when(c == 1)
    def _():
        totals(lambda: r.sq, lambda: r.pq[pl.ds(2 * z, 2)], lambda at: r.rqz.at[at], lambda at: r.zq.at[at])

    spread(lambda cc: r.sq.at[cc], lambda: (r.oq_h.at[b], r.fq.at[b]), 1)

    @pl.when(c == 1)
    def _():
        totals(lambda: r.sat, lambda: r.pat[rows, :], lambda at: r.rat.at[at], lambda at: r.zat.at[at])

    spread(
        lambda cc: r.sat.at[pl.ds(cc * (blk // 2), blk // 2), :], lambda: (r.oat_h.at[b], r.fat.at[b]), 1
    )

    for bb in range(nb):
        for p, (k, at) in enumerate(pieces):
            arrived(r.ogu_h.at[bb, k, :, at], r.fgu.at[p, bb])
        arrived(r.odn_h.at[bb], r.fdn.at[bb])
        arrived(r.oq_h.at[bb], r.fq.at[bb])
        arrived(r.oout_h.at[bb], r.fout.at[bb])
        arrived(r.oat_h.at[bb], r.fat.at[bb])
    arrived(r.ogl_h, r.fgl.at[0])
    out_copy.wait()
    pltpu.make_async_copy(r.gin_v, r.gin_h, r.osem.at[1]).wait()
    assert used[0] <= r.ssem.shape[0], used
    for make, at in pending:
        cond, src, dst, rsem, dev = make()

        @pl.when(cond)
        def _():
            remote(src, dst, r.ssem.at[at], rsem, dev).wait_send()

    def sent_on(t, _):
        @pl.when((lax.rem(t, 2) == c) & (t < s))
        def _():
            for ch in range(2):
                got = rows_of(r.x_all, t, ch)
                remote(got, got, r.bsem.at[ch, t], r.rx.at[ch, t], sib).wait_send()

                @pl.when(z + 1 < nz)
                def _():
                    remote(got, got, r.fsem.at[ch, t], r.rx.at[ch, t], right).wait_send()

        @pl.when((lax.rem(t, 2) == c) & (t > s))
        def _():
            remote(r.q_all.at[t], r.q_all.at[t], r.bsem.at[2, t], r.rq.at[t], sib).wait_send()
            blocks = [(rows_of(r.do_all, t, ch), r.rdo.at[ch, t]) for ch in range(2)]
            blocks.append((r.st_all.at[t], r.rst.at[t]))
            for i, (got, sem) in enumerate(blocks):
                remote(got, got, r.bsem.at[3 + i, t], sem, sib).wait_send()

                @pl.when(z > 0)
                def _():
                    remote(got, got, r.fsem.at[2 + i, t], sem, left).wait_send()
        return 0

    lax.fori_loop(0, n, sent_on, 0)


def unpack_kernel(
    n, nb, out_in, gin_in, oat_h, ogu_h, odn_h, oout_h, oq_h, ogl_h,
    out, gin, gq_h, gk_h, gv_h, go_h, gg_h, gu_h, gd_h, g1_h, g2_h,
    oat, ogu, odn, oout, oq, ogl, gq, gk, gv, go, gg, gu, gd, out_v, gin_v, g1, g2, isem, osem,
):
    s = lax.axis_index("seq")
    fs = ogu.shape[3]
    units, dh = odn.shape[1], odn.shape[2] // 2
    copy = pltpu.make_async_copy
    loads = [copy(a, b, isem.at[i]) for i, (a, b) in enumerate(
        ((ogu_h, ogu), (oat_h, oat), (odn_h, odn), (ogl_h, ogl), (out_in, out_v), (gin_in, gin_v), (oout_h, oout), (oq_h, oq)))]
    stores = [copy(a, b, osem.at[i]) for i, (a, b) in enumerate(
        ((gg, gg_h), (gu, gu_h), (gq, gq_h), (gk, gk_h), (gv, gv_h), (go, go_h), (gd, gd_h),
         (out_v, out.at[0]), (gin_v, gin.at[0]), (g1, g1_h), (g2, g2_h)))]
    for load in loads:
        load.start()
    loads[0].wait()
    low = lax.broadcasted_iota(jnp.int32, (ogu.shape[2], 128), 1) < 64

    def interleave(k, dst):
        for t in range(n):
            for y in range(2):
                at = slice((t // 2) * 128, (t // 2 + 1) * 128)
                one, two = ogu[2 * y, k, :, at].astype(F32), ogu[2 * y + 1, k, :, at].astype(F32)
                if t % 2:
                    one = pltpu.roll(one, 64, 1)
                else:
                    two = pltpu.roll(two, 64, 1)
                dst[:, (2 * t + y) * 128:(2 * t + y + 1) * 128] = jnp.where(low, one, two)

    interleave(0, gg)
    stores[0].start()
    interleave(1, gu)
    stores[1].start()
    loads[1].wait()
    for m, (ref, bb) in enumerate(((gk, 0), (gv, 2))):
        ref[:, :dh] = oat[bb].astype(F32)
        ref[:, dh:] = oat[bb + 1].astype(F32)
        stores[3 + m].start()
    loads[6].wait()
    loads[7].wait()
    part = oout.shape[1]
    for m, (src, dst) in enumerate(((oq, gq), (oout, go))):
        for bb in range(nb):
            dst[(bb // 2) * part:(bb // 2 + 1) * part, (bb % 2) * dh:(bb % 2 + 1) * dh] = src[bb].astype(F32)
        stores[5 if m else 2].start()
    loads[2].wait()
    for bb in range(nb):
        gd[bb * units:(bb + 1) * units, :] = odn[bb].astype(F32)
    stores[6].start()
    for i in (4, 5):
        loads[i].wait()
        stores[3 + i].start()
    loads[3].wait()
    d = ogl.shape[1]
    own = d // n
    gains = pltpu.roll(ogl[...], lax.rem(d - s * own, d), 1)
    g1[...] = gains[0:1, :own]
    g2[...] = gains[1:2, :own]
    stores[9].start()
    stores[10].start()
    for store in stores:
        store.wait()


def rope_constants(length, head_dim):
    half = head_dim // 2
    inverse = np.exp(-2.0 * math.log(THETA) / head_dim * np.arange(half)).astype(np.float32)
    angle = np.arange(length, dtype=np.float32)[:, None] * inverse
    cos, sin = np.cos(angle.astype(np.float64)), np.sin(angle.astype(np.float64))
    return (
        np.concatenate([cos, cos, cos, cos], 1).astype(np.float32),
        np.concatenate([-sin, sin, -sin, sin], 1).astype(np.float32),
    )


def fused_local(n, nb, tokens, doc_ids, w_query, w_key, w_value, w_out, w_gate, w_up, w_down, gain_attn, gain_ffn, cotangent):
    _, tok, d = tokens.shape
    f = w_gate.shape[1]
    nz = n // 2
    cos, sin = rope_constants(n * tok, d // HEADS)
    cos = jnp.asarray(cos.reshape(nz, 2 * tok, 128))
    sin = jnp.asarray(sin.reshape(nz, 2 * tok, 128))
    plan = scratch_plan(tok, d, f, n, nb)
    vmem, anywhere = pl.BlockSpec(memory_space=pltpu.VMEM), pl.BlockSpec(memory_space=pl.ANY)
    shape = jax.ShapeDtypeStruct
    parts = pl.pallas_call(
        functools.partial(layer_kernel, tuple(plan), tok, d, f, n, nb),
        out_shape=(
            shape((tok, d), F32), shape((tok, d), F32), shape((nb, d // n, d // 2), BF16),
            shape((nb, 2, d // n, f // nb), BF16), shape((nb, f // (nb * n), d), BF16), shape((nb, d // (2 * n), d // 2), BF16),
            shape((nb, d // (2 * n), d // 2), BF16), shape((8, d), F32),
        ),
        in_specs=[anywhere] * 14,
        out_specs=[anywhere] * 8,
        scratch_shapes=list(plan.values()),
        compiler_params=pltpu.CompilerParams(
            collective_id=0, has_side_effects=True, vmem_limit_bytes=62 * 2**20
        ),
        name="layer",
    )(
        doc_ids, tokens, cotangent, gain_attn, gain_ffn, cos, sin,
        w_query, w_key, w_value, w_out, w_gate, w_up, w_down,
    )
    own = d // n
    grads = [shape((own, d), F32)] * 4 + [shape((own, f), F32)] * 2 + [shape((f // n, d), F32)]
    results = pl.pallas_call(
        functools.partial(unpack_kernel, n, nb),
        out_shape=(shape((1, tok, d), F32), shape((1, tok, d), F32), *grads, shape((1, own), F32), shape((1, own), F32)),
        in_specs=[pl.BlockSpec(memory_space=pltpu.HBM)] * 8,
        out_specs=[anywhere] * 11,
        scratch_shapes=[pltpu.VMEM(parts[i].shape, parts[i].dtype) for i in (2, 3, 4, 5, 6, 7)]
        + [pltpu.VMEM(g.shape, g.dtype) for g in grads]
        + [pltpu.VMEM((tok, d), F32)] * 2
        + [pltpu.VMEM((1, own), F32)] * 2
        + [pltpu.SemaphoreType.DMA((8,)), pltpu.SemaphoreType.DMA((11,))],
        compiler_params=pltpu.CompilerParams(vmem_limit_bytes=62 * 2**20),
        name="unpack",
    )(*parts)
    return results[:9] + (results[9].reshape(own), results[10].reshape(own))


def fits(shapes, n, nb):
    (_, tok, d), f = shapes[0], shapes[6][1]
    return (
        nb == 4 and n == 8 and n * tok <= 1024 and tok == 128 and shapes[0][0] == 1
        and d == HEADS * 64 and d % 256 == 0 and d % (32 * n) == 0 and f == 2 * tok * n and f % 512 == 0
    )


def solution(mesh):
    nb, n = mesh.shape["batch"], mesh.shape["seq"]

    def either(*args):
        shapes = [a.shape for a in args]
        if fits(shapes, n, nb):
            return fused_local(n, nb, *args)
        return local(*args)

    return jax.shard_map(
        either,
        mesh=mesh,
        in_specs=(
            P("batch", "seq", None),
            P("batch", "seq"),
            P(),
            P(),
            P(),
            P(),
            P(),
            P(),
            P(),
            P(),
            P(),
            P("batch", "seq", None),
        ),
        out_specs=(
            P("batch", "seq", None),
            P("batch", "seq", None),
            P("seq", None),
            P("seq", None),
            P("seq", None),
            P("seq", None),
            P("seq", None),
            P("seq", None),
            P("seq", None),
            P("seq"),
            P("seq"),
        ),
        check_vma=False,
    )
```
